32 devices in a mesh: ctx: 4 (over y, x), head: 8 (over z, core).
Axes of the slice: x: 2, y: 2, z: 4, core: 2. Of those that a mesh axis runs over, the one named last changes fastest.
Arguments:
- queries: bfloat16 [4096, 4096], P('ctx', 'head'), as said below
- keys: bfloat16 [4096, 4096], P('ctx', 'head'), as said below
- values: bfloat16 [4096, 4096], P('ctx', 'head'), may hold values from -6 to 6
- doc_ids: int32 [4096], P('ctx'), may hold values from 0 to 7, as said below
- w_out: bfloat16 [4096, 4096], P('head'), may hold values from -0.125 to 0.125
Outputs:
- mixed: bfloat16 [4096, 4096], P('ctx', 'head')
The draws below stay inside these ranges and needn't reach their ends.
Inputs may be any that keep to these rules, and one draw needn't show every extreme that they name: `doc_ids`: within every draw the numbers never fall along sequence positions pos(g), so each document is a contiguous run of positions; every number from 0 to the largest names a document; documents have no fixed length. Entries of the queries lie within the stated range. Entries of the keys lie within the stated range.
All inputs are finite; a program needn't handle non-finite values.
Results may differ from the reference program's by a relative error of at most 0.018.
Values may be sent and summed in bfloat16 or wider, within the bound.
No kernel may reach another device: no remote copies, remote signals or barrier semaphores. Data moves between devices by JAX's collectives and lax.ppermute only.
A program may use at most 128 MiB of HBM per device.

```python
import math
import jax
import jax.numpy as jnp
from jax import lax

D = 4096
HEADS = 32
HD = 128
TOK_DEV = 1024
SEQ = 4096
N_CTX = 4


def draw_queries(key, part):
    key = jax.random.fold_in(key, 1)
    drawn = jnp.clip(jax.random.normal(key, (SEQ, HEADS * HD), jnp.float32), -6.0, 6.0)
    return drawn.astype(jnp.bfloat16)


def draw_keys(key, part):
    key = jax.random.fold_in(key, 2)
    drawn = jnp.clip(jax.random.normal(key, (SEQ, HEADS * HD), jnp.float32), -6.0, 6.0)
    return drawn.astype(jnp.bfloat16)


def draw_doc_ids(key, part):
    key = jax.random.fold_in(key, 3)
    order = jax.random.permutation(key, SEQ - 1).astype(jnp.int32) + 1
    marked = order[:2 * N_CTX - 1]
    flags = jnp.zeros((SEQ,), jnp.int32).at[marked].set(1)
    by_position = jnp.cumsum(flags).astype(jnp.int32)
    flat_index = jnp.arange(SEQ, dtype=jnp.int32)
    owner_dev = flat_index // TOK_DEV
    within = flat_index % TOK_DEV
    half_rows = TOK_DEV // 2
    fold_block = jnp.where(within < half_rows, owner_dev, 2 * N_CTX - 1 - owner_dev)
    positions = fold_block * half_rows + within % half_rows
    return by_position[positions]


def spiked(array, rng, source, target, shards_of, factor):
    def block_of(axis_at):
        return (jnp.arange(array.shape[axis_at]) // (array.shape[axis_at] // shards_of)).reshape((-1,) + (1,) * (array.ndim - 1 - axis_at))

    first = jax.random.permutation(rng, shards_of)[block_of(target)]
    second = (block_of(target) + shards_of // 2) % shards_of
    return jnp.where((block_of(source) == first) | (block_of(source) == second), factor * array, array)


def block_levels(own_key, dims, shards, least, high):
    loudness = 1.0
    for position, blocks in shards:
        heights = jax.random.uniform(jax.random.fold_in(jax.random.fold_in(own_key, 6), position), (blocks,), jnp.float32, least / len(shards), high / len(shards))
        loudness = loudness * jnp.repeat(jnp.exp(heights), dims[position] // blocks).reshape((-1,) + (1,) * (len(dims) - 1 - position))
    return loudness


def noise(key, shape, width, reach, split=(), held_as=jnp.bfloat16):
    values = width * jax.random.normal(key, shape, jnp.float32)
    if split:
        values = values * block_levels(key, shape, split, -0.22, 0.18)
    return jnp.clip(values, -reach, reach).astype(held_as)


def gaussian_with(key, shape, width, most, shards, heavy, kind=jnp.bfloat16):
    values = width * jax.random.normal(key, shape, jnp.float32)
    if shards:
        values = values * block_levels(key, shape, shards, -0.22, 0.18)
    return jnp.clip(spiked(values, jax.random.fold_in(key, 3), *heavy), -most, most).astype(kind)


def setup_inputs(seed: int = 0) -> dict:
    key_of = jax.random.split(jax.random.key(seed), 6)
    return {
        "queries": draw_queries(jax.random.fold_in(key_of[5], 71), 0),
        "keys": draw_keys(jax.random.fold_in(key_of[5], 71), 0),
        "values": noise(key_of[2], (SEQ, HEADS * HD), 1.0, 6.0, ((0, 4), (1, 8))),
        "doc_ids": draw_doc_ids(jax.random.fold_in(key_of[5], 71), 0),
        "w_out": gaussian_with(key_of[4], (HEADS * HD, D), (HEADS * HD) ** -0.5, 0.125, ((0, 8),), (0, 1, 8, 2.0)),
    }


MASKED_SCORE = -1e+30

def stored_positions(total_rows):
    flat_index = jnp.arange(total_rows, dtype=jnp.int32)
    owner_dev = flat_index // TOK_DEV
    within = flat_index % TOK_DEV
    half_rows = TOK_DEV // 2
    fold_block = jnp.where(within < half_rows, owner_dev, 2 * N_CTX - 1 - owner_dev)
    return fold_block * half_rows + within % half_rows

def reference(queries, keys, values, doc_ids, w_out):
    positions = stored_positions(SEQ)
    scaling = 1.0 / math.sqrt(HD)
    query_heads = queries.astype(jnp.float32).reshape(SEQ, HEADS, HD).transpose(1, 0, 2)
    key_heads = keys.astype(jnp.float32).reshape(SEQ, HEADS, HD).transpose(1, 0, 2)
    value_heads = values.astype(jnp.float32).reshape(SEQ, HEADS, HD).transpose(1, 0, 2)
    block_rows = min(512, SEQ)
    block_count = SEQ // block_rows

    def one_head(operands):
        query_one, key_one, value_one = operands

        def one_block(block_index):
            first = (block_index * block_rows).astype(jnp.int32)
            query_block = lax.dynamic_slice_in_dim(query_one, first, block_rows, 0)
            query_pos = lax.dynamic_slice_in_dim(positions, first, block_rows, 0)
            query_doc = lax.dynamic_slice_in_dim(doc_ids, first, block_rows, 0)
            scores = jnp.dot(query_block, key_one.T, precision=lax.Precision.HIGHEST) * scaling
            allowed = (query_doc[:, None] == doc_ids[None, :]) & (positions[None, :] <= query_pos[:, None])
            scores = jnp.where(allowed, scores, MASKED_SCORE)
            row_max = lax.optimization_barrier(jnp.max(scores, axis=1, keepdims=True))
            weights = jnp.where(allowed, jnp.exp(scores - row_max), 0.0)
            totals = lax.optimization_barrier(jnp.sum(weights, axis=1, keepdims=True))
            rounded = lax.optimization_barrier(weights.astype(jnp.bfloat16)).astype(jnp.float32)
            return jnp.dot(rounded, value_one, precision=lax.Precision.HIGHEST) / totals
        blocks = lax.map(one_block, jnp.arange(block_count, dtype=jnp.int32))
        return blocks.reshape(SEQ, HD)
    head_outs = lax.map(one_head, (query_heads, key_heads, value_heads))
    attended = head_outs.transpose(1, 0, 2).reshape(SEQ, HEADS * HD).astype(jnp.bfloat16)
    return jnp.dot(attended, w_out, preferred_element_type=jnp.float32).astype(jnp.bfloat16)
```

```python
import functools
import math

import jax
import jax.numpy as jnp
from jax import lax
from jax.experimental import pallas as pl
from jax.experimental.pallas import tpu as pltpu
from jax.sharding import PartitionSpec as P

HD = 128


MASKED_SCORE = -1e30
LOG2E = 1.4426950408889634


def passed_along(value, axis, steps):
    count = lax.axis_size(axis)
    pairs = [(source, (source + steps) % count) for source in range(count)]
    return lax.ppermute(value, axis, pairs)


def folded_positions(row_total, offset, shard_rows, devices_ctx):
    flat_index = offset + lax.iota(jnp.int32, row_total)
    owner_dev = flat_index // shard_rows
    within = flat_index % shard_rows
    half_rows = shard_rows // 2
    fold_block = jnp.where(within < half_rows, owner_dev, 2 * devices_ctx - 1 - owner_dev)
    return fold_block * half_rows + within % half_rows


def block_update(
    running, query, query_pos, query_doc, key_block, value_block, pos_block, doc_block
):
    largest, totals, summed = running
    query_rows = query.shape[0]
    local_heads = query.shape[1] // HD
    query_heads = query.reshape(query_rows, local_heads, HD)
    key_heads = key_block.reshape(key_block.shape[0], local_heads, HD)
    value_heads = value_block.reshape(value_block.shape[0], local_heads, HD)
    scores = jnp.einsum(
        "qhd,khd->hqk", query_heads, key_heads, preferred_element_type=jnp.float32
    ) * (1.0 / math.sqrt(HD))
    allowed = (query_doc[:, None] == doc_block[None, :]) & (
        pos_block[None, :] <= query_pos[:, None]
    )
    scores = jnp.where(allowed[None], scores, MASKED_SCORE)
    new_max = jnp.maximum(largest, jnp.max(scores, axis=2))
    weights = jnp.where(allowed[None], jnp.exp(scores - new_max[:, :, None]), 0.0)
    factor = jnp.exp(largest - new_max)
    totals = totals * factor + jnp.sum(weights, axis=2)
    product = jnp.einsum(
        "hqk,khd->qhd",
        weights.astype(jnp.bfloat16),
        value_heads,
        preferred_element_type=jnp.float32,
    )
    summed = summed * factor.T[:, :, None] + product
    return (new_max, totals, summed)


def attend_rows(running, query, query_pos, query_doc, key_rows, value_rows, key_pos, key_doc):
    row_total = key_rows.shape[0]
    block_rows = math.gcd(row_total, query.shape[0])
    block_count = row_total // block_rows
    highest = jnp.max(query_pos)

    def visit(partial_value, blocks):
        key_block, value_block, pos_block, doc_block = blocks
        masked_out = jnp.min(pos_block) > highest
        updated = lax.cond(
            masked_out,
            lambda frozen: frozen,
            lambda frozen: block_update(
                frozen, query, query_pos, query_doc, key_block, value_block, pos_block, doc_block
            ),
            partial_value,
        )
        return (updated, None)

    blocks = (
        key_rows.reshape(block_count, block_rows, key_rows.shape[1]),
        value_rows.reshape(block_count, block_rows, value_rows.shape[1]),
        key_pos.reshape(block_count, block_rows),
        key_doc.reshape(block_count, block_rows),
    )
    running, _ = lax.scan(visit, running, blocks)
    return running


def attend_shard(running, query, query_pos, query_doc, key_rows, value_rows, key_pos, key_doc):
    largest, totals, summed = running
    half_rows = query.shape[0] // 2
    new_largest = []
    new_totals = []
    new_summed = []
    for half_idx in range(2):
        lower = half_idx * half_rows
        part_state = (largest[half_idx], totals[half_idx], summed[half_idx])
        part_state = attend_rows(
            part_state,
            query[lower : lower + half_rows],
            query_pos[lower : lower + half_rows],
            query_doc[lower : lower + half_rows],
            key_rows,
            value_rows,
            key_pos,
            key_doc,
        )
        new_largest.append(part_state[0])
        new_totals.append(part_state[1])
        new_summed.append(part_state[2])
    return (jnp.stack(new_largest), jnp.stack(new_totals), jnp.stack(new_summed))


def ring_local(queries, keys, values, doc_ids, w_out):
    shard_rows = queries.shape[0]
    half_rows = shard_rows // 2
    local_heads = queries.shape[1] // HD
    devices_ctx = lax.axis_size("ctx")
    ctx_index = lax.axis_index("ctx")
    all_docs = lax.all_gather(doc_ids, "ctx", axis=0, tiled=True)
    own_pos = folded_positions(shard_rows, ctx_index * shard_rows, shard_rows, devices_ctx)
    running = (
        jnp.full((2, local_heads, half_rows), MASKED_SCORE, jnp.float32),
        jnp.zeros((2, local_heads, half_rows), jnp.float32),
        jnp.zeros((2, half_rows, local_heads, HD), jnp.float32),
    )
    travel = queries
    for hop_step in range(devices_ctx):
        anchor = (ctx_index - hop_step) % devices_ctx
        query_pos = folded_positions(shard_rows, anchor * shard_rows, shard_rows, devices_ctx)
        query_doc = lax.dynamic_slice_in_dim(all_docs, anchor * shard_rows, shard_rows, 0)
        largest, totals, summed = attend_shard(
            running, travel, query_pos, query_doc, keys, values, own_pos, doc_ids
        )
        running = (
            passed_along(largest.astype(jnp.bfloat16), "ctx", 1).astype(largest.dtype),
            passed_along(totals.astype(jnp.bfloat16), "ctx", 1).astype(totals.dtype),
            passed_along(summed.astype(jnp.bfloat16), "ctx", 1).astype(summed.dtype),
        )
        if hop_step + 1 < devices_ctx:
            travel = passed_along(travel, "ctx", 1)
    largest, totals, summed = running
    attended = summed / totals.transpose(0, 2, 1)[:, :, :, None]
    attended = attended.reshape(shard_rows, local_heads * HD).astype(jnp.bfloat16)
    partial_out = jnp.dot(attended, w_out, preferred_element_type=jnp.float32)
    return lax.psum_scatter(
        partial_out.astype(jnp.bfloat16), "head", scatter_dimension=1, tiled=True
    )


def params(mib):
    return pltpu.CompilerParams(vmem_limit_bytes=mib * 1024 * 1024)


def cost(flops, moved):
    return pl.CostEstimate(flops=flops, bytes_accessed=moved, transcendentals=0)


def pack(ctx_index, half, queries, keys, values, docs):
    rows = queries.shape[0] // 2
    group = queries.shape[1] // HD
    doc_rows = 0 if docs is None else docs.shape[0]
    total = 3 * rows + doc_rows

    def kernel(ctx_ref, *refs):
        outs = refs[len(refs) - (group - 1) :]
        for place in range(group - 1):
            for part in range(3):
                outs[place][part * rows : (part + 1) * rows, :] = refs[place * 3 + part][...]
            if docs is not None:
                outs[place][3 * rows :, :] = refs[3 * (group - 1)][...]

    def piece(distance):
        return pl.BlockSpec((rows, HD), lambda step, ctx: (half, ctx[0] ^ distance))

    in_specs = []
    operands = []
    for distance in range(1, group):
        for array in (queries, keys, values):
            in_specs.append(piece(distance))
            operands.append(array)
    if docs is not None:
        in_specs.append(pl.BlockSpec(docs.shape, lambda step, ctx: (0, 0)))
        operands.append(docs)
    return pl.pallas_call(
        kernel,
        grid_spec=pltpu.PrefetchScalarGridSpec(
            num_scalar_prefetch=1,
            grid=(1,),
            in_specs=in_specs,
            out_specs=[pl.BlockSpec((total, HD), lambda step, ctx: (0, 0))] * (group - 1),
        ),
        out_shape=[jax.ShapeDtypeStruct((total, HD), jnp.bfloat16)] * (group - 1),
        compiler_params=params(24),
        cost_estimate=cost(0, 6 * (group - 1) * rows * HD * 2),
        name="pack",
    )(ctx_index, *operands)


def attend(ctx_index, queries, keys, values, docs, low, high):
    rows = queries.shape[0] // 2
    group = queries.shape[1] // HD
    with_high = high is not None
    blocks = 2 * group if with_high else group
    lanes = rows // HD
    scaling = LOG2E / math.sqrt(HD)

    def kernel(ctx_ref, *refs):
        refs = list(refs)
        own_low = [refs.pop(0) for _ in range(3)]
        own_high = [refs.pop(0) for _ in range(3)] if with_high else None
        own_docs = refs.pop(0)
        low_refs = [refs.pop(0) for _ in range(group - 1)]
        high_refs = [refs.pop(0) for _ in range(group - 1)] if with_high else None
        outs = [refs.pop(0) for _ in range(group)]
        key_buf, value_buf, doc_buf = refs
        ctx = ctx_ref[0]

        def part(upper, distance, index):
            if distance == 0:
                return (own_high if upper else own_low)[index][...]
            source = (high_refs if upper else low_refs)[distance - 1]
            return source[index * rows : (index + 1) * rows, :]

        first_doc = {}
        last_doc = {}
        place = {}
        doc_rows = {}
        for upper in (False, True) if with_high else (False,):
            for distance in range(group):
                source = ctx ^ distance
                block = 2 * group - 1 - source if upper else source
                place[upper, distance] = block
                offset = pl.multiple_of(block * rows, rows)
                key_buf[pl.ds(offset, rows), :] = part(upper, distance, 1)
                value_buf[pl.ds(offset, rows), :] = part(upper, distance, 2)
                if distance == 0:
                    both = own_docs[...]
                else:
                    both = low_refs[distance - 1][3 * rows :, :]
                both = both.astype(jnp.float32)
                begin = lanes if upper else 0
                mine = both[begin : begin + lanes, :]
                doc_rows[upper, distance] = mine
                doc_buf[pl.ds(block, 1), :] = jnp.concatenate(
                    [mine[line : line + 1, :] for line in range(lanes)], axis=1
                )
                first_doc[upper, distance] = jnp.min(mine)
                last_doc[upper, distance] = jnp.max(mine)

        row_index = lax.broadcasted_iota(jnp.int32, (rows, rows), 0)
        column_index = lax.broadcasted_iota(jnp.int32, (rows, rows), 1)
        for distance in range(group):
            me = (with_high, distance)
            block = place[me]
            query = part(with_high, distance, 0)
            mine = doc_rows[me]
            query_doc = jnp.concatenate(
                [
                    jnp.transpose(jnp.broadcast_to(mine[line : line + 1, :], (HD, HD)))
                    for line in range(lanes)
                ],
                axis=0,
            )[:, :1]
            start = jnp.int32(0)
            for other, last in last_doc.items():
                skip = jnp.logical_and(place[other] < block, last < first_doc[me])
                start = start + skip.astype(jnp.int32)

            def scores_of(index):
                offset = pl.multiple_of(index * rows, rows)
                raw = lax.dot_general(
                    query,
                    key_buf[pl.ds(offset, rows), :],
                    (((1,), (1,)), ((), ())),
                    preferred_element_type=jnp.float32,
                )
                same = query_doc == doc_buf[pl.ds(index, 1), :]
                return raw * scaling, same

            def weighted(weights, index):
                offset = pl.multiple_of(index * rows, rows)
                return jnp.dot(
                    weights.astype(jnp.bfloat16),
                    value_buf[pl.ds(offset, rows), :],
                    preferred_element_type=jnp.float32,
                )

            scores, same = scores_of(block)
            scores = jnp.where(same & (column_index <= row_index), scores, MASKED_SCORE)
            largest = jnp.max(scores, axis=1, keepdims=True)
            weights = jnp.exp2(scores - largest)
            totals = jnp.sum(weights, axis=1, keepdims=True)
            summed = weighted(weights, block)

            def visit(index, running):
                largest, totals, summed = running
                scores, same = scores_of(index)
                scores = jnp.where(same, scores, MASKED_SCORE)
                new_max = jnp.maximum(largest, jnp.max(scores, axis=1, keepdims=True))
                factor = jnp.exp2(largest - new_max)
                weights = jnp.exp2(scores - new_max)
                totals = totals * factor + jnp.sum(weights, axis=1, keepdims=True)
                summed = summed * factor + weighted(weights, index)
                return new_max, totals, summed

            largest, totals, summed = lax.fori_loop(
                start, block, visit, (largest, totals, summed)
            )
            outs[distance][...] = (summed / totals).astype(jnp.bfloat16)

    def own(upper):
        return pl.BlockSpec((rows, HD), lambda step, ctx: (int(upper), ctx[0]))

    def whole(array):
        return pl.BlockSpec(array.shape, lambda step, ctx: (0, 0))

    in_specs = [own(False)] * 3
    operands = [queries, keys, values]
    if with_high:
        in_specs += [own(True)] * 3
        operands += [queries, keys, values]
    operands += [docs, *low]
    in_specs += [whole(array) for array in (docs, *low)]
    if with_high:
        operands += list(high)
        in_specs += [whole(array) for array in high]
    pairs = group * 2 * rows * rows * HD * 2 * (3 if with_high else 2)
    return pl.pallas_call(
        kernel,
        grid_spec=pltpu.PrefetchScalarGridSpec(
            num_scalar_prefetch=1,
            grid=(1,),
            in_specs=in_specs,
            out_specs=[pl.BlockSpec((rows, HD), lambda step, ctx: (0, 0))] * group,
            scratch_shapes=[
                pltpu.VMEM((blocks * rows, HD), jnp.bfloat16),
                pltpu.VMEM((blocks * rows, HD), jnp.bfloat16),
                pltpu.VMEM((max(blocks, 8), rows), jnp.float32),
            ],
        ),
        out_shape=[jax.ShapeDtypeStruct((rows, HD), jnp.bfloat16)] * group,
        compiler_params=params(40),
        cost_estimate=cost(pairs, 8 * rows * HD * 2 * group),
        name="attend_high" if with_high else "attend_low",
    )(ctx_index, *operands)


def assemble(ctx_index, pieces):
    rows = pieces[0].shape[0]
    group = len(pieces)

    def kernel(ctx_ref, *refs):
        for distance in range(group):
            column = pl.multiple_of((ctx_ref[0] ^ distance) * HD, HD)
            refs[-1][:, pl.ds(column, HD)] = refs[distance][...]

    return pl.pallas_call(
        kernel,
        grid_spec=pltpu.PrefetchScalarGridSpec(
            num_scalar_prefetch=1,
            grid=(1,),
            in_specs=[pl.BlockSpec((rows, HD), lambda step, ctx: (0, 0))] * group,
            out_specs=pl.BlockSpec((rows, group * HD), lambda step, ctx: (0, 0)),
        ),
        out_shape=jax.ShapeDtypeStruct((rows, group * HD), jnp.bfloat16),
        compiler_params=params(16),
        cost_estimate=cost(0, 4 * rows * group * HD),
        name="assemble",
    )(ctx_index, *pieces)


def project(core, mine, sibling, w_mine, w_sibling, chips):
    rows, depth = mine.shape
    columns = w_mine.shape[1] // (2 * chips)

    def kernel(core_ref, mine_ref, sibling_ref, w_mine_ref, w_sibling_ref, out_ref):
        total = jnp.dot(mine_ref[...], w_mine_ref[...], preferred_element_type=jnp.float32)
        total += jnp.dot(sibling_ref[...], w_sibling_ref[...], preferred_element_type=jnp.float32)
        out_ref[0] = total.astype(jnp.bfloat16)

    return pl.pallas_call(
        kernel,
        grid_spec=pltpu.PrefetchScalarGridSpec(
            num_scalar_prefetch=1,
            grid=(chips,),
            in_specs=[
                pl.BlockSpec((rows, depth), lambda chip, core: (0, 0)),
                pl.BlockSpec((rows, depth), lambda chip, core: (0, 0)),
                pl.BlockSpec((depth, columns), lambda chip, core: (0, 2 * chip + core[0])),
                pl.BlockSpec((depth, columns), lambda chip, core: (0, chip)),
            ],
            out_specs=pl.BlockSpec((1, rows, columns), lambda chip, core: (chip, 0, 0)),
        ),
        out_shape=jax.ShapeDtypeStruct((chips, rows, columns), jnp.bfloat16),
        compiler_params=params(24),
        cost_estimate=cost(
            4 * rows * depth * columns * chips, 2 * chips * (rows + 2 * depth) * columns
        ),
        name="project",
    )(core, mine, sibling, w_mine, w_sibling)


def swap(value, axis, distance):
    count = lax.axis_size(axis)
    return lax.ppermute(value, axis, [(source, source ^ distance) for source in range(count)])


def line_reduce_scatter(shares, chip, chips):
    def share(index):
        return lax.dynamic_index_in_dim(shares, jnp.clip(index, 0, chips - 1), 0, keepdims=False)

    from_left = None
    from_right = None
    for step in range(1, chips):
        to_right = share(chips - step + chip)
        to_left = share(chip + step - chips)
        if step > 1:
            to_right = (to_right.astype(jnp.float32) + from_left.astype(jnp.float32)).astype(
                jnp.bfloat16
            )
            to_left = (to_left.astype(jnp.float32) + from_right.astype(jnp.float32)).astype(
                jnp.bfloat16
            )
        right_pairs = []
        left_pairs = []
        for source in range(step):
            for core in range(2):
                right_pairs.append((2 * source + core, 2 * source + 2 + core))
                mirrored = chips - 1 - source
                left_pairs.append((2 * mirrored + core, 2 * mirrored - 2 + core))
        from_left = lax.ppermute(to_right, "head", right_pairs)
        from_right = lax.ppermute(to_left, "head", left_pairs)
    total = share(chip).astype(jnp.float32)
    total = total + from_left.astype(jnp.float32) + from_right.astype(jnp.float32)
    return total.astype(jnp.bfloat16)


def exchange_local(queries, keys, values, doc_ids, w_out):
    shard_rows = queries.shape[0]
    group = queries.shape[1] // HD
    chips = lax.axis_size("head") // 2
    ctx_index = lax.axis_index("ctx").astype(jnp.int32).reshape(1)
    head_index = lax.axis_index("head").astype(jnp.int32)
    chip = head_index // 2
    core = head_index % 2

    docs = doc_ids.astype(jnp.bfloat16).reshape(shard_rows // HD, HD)
    docs = jnp.pad(docs, ((0, -docs.shape[0] % 16), (0, 0)))

    low_out = pack(ctx_index, 0, queries, keys, values, docs)
    low = [swap(low_out[distance - 1], "ctx", distance) for distance in range(1, group)]

    depth, width = w_out.shape
    w_split = w_out.reshape(depth, chips, 2, width // (2 * chips))
    w_give = lax.dynamic_index_in_dim(w_split, 1 - core, 2, keepdims=False)
    w_sibling = swap(w_give.reshape(depth, width // 2), "head", 1)

    high_out = pack(ctx_index, 1, queries, keys, values, None)
    *high_out, low[0], low[1], low[2] = lax.optimization_barrier((*high_out, *low))
    high = [swap(high_out[distance - 1], "ctx", distance) for distance in range(1, group)]

    results = []
    for half in range(2):
        pieces = attend(ctx_index, queries, keys, values, docs, low, high if half else None)
        back = [swap(pieces[distance], "ctx", distance) for distance in range(1, group)]
        mine = assemble(ctx_index, [pieces[0], *back])
        sibling = swap(mine, "head", 1)
        shares = project(core.reshape(1), mine, sibling, w_out, w_sibling, chips)
        results.append(line_reduce_scatter(shares, chip, chips))
    return jnp.concatenate(results, axis=0)


def solution(mesh):
    in_specs = (P("ctx", "head"), P("ctx", "head"), P("ctx", "head"), P("ctx"), P("head", None))
    out_specs = P("ctx", "head")
    ctx_count = mesh.shape["ctx"]
    head_count = mesh.shape["head"]

    def local(queries, keys, values, doc_ids, w_out):
        heads = queries.shape[1] // HD
        exchange = heads == ctx_count and heads == 4 and head_count % 2 == 0 and head_count > 2
        body = exchange_local if exchange else ring_local
        return body(queries, keys, values, doc_ids, w_out)

    return jax.shard_map(
        local, mesh=mesh, in_specs=in_specs, out_specs=out_specs, check_vma=False
    )
```

```python
import functools
import math

import jax
import jax.numpy as jnp
from jax import lax
from jax.experimental import pallas as pl
from jax.experimental.pallas import tpu as pltpu
from jax.sharding import PartitionSpec as P

HD = 128


MASKED_SCORE = -1e30
LOG2E = 1.4426950408889634


def passed_along(value, axis, steps):
    count = lax.axis_size(axis)
    pairs = [(source, (source + steps) % count) for source in range(count)]
    return lax.ppermute(value, axis, pairs)


def folded_positions(row_total, offset, shard_rows, devices_ctx):
    flat_index = offset + lax.iota(jnp.int32, row_total)
    owner_dev = flat_index // shard_rows
    within = flat_index % shard_rows
    half_rows = shard_rows // 2
    fold_block = jnp.where(within < half_rows, owner_dev, 2 * devices_ctx - 1 - owner_dev)
    return fold_block * half_rows + within % half_rows


def block_update(
    running, query, query_pos, query_doc, key_block, value_block, pos_block, doc_block
):
    largest, totals, summed = running
    query_rows = query.shape[0]
    local_heads = query.shape[1] // HD
    query_heads = query.reshape(query_rows, local_heads, HD)
    key_heads = key_block.reshape(key_block.shape[0], local_heads, HD)
    value_heads = value_block.reshape(value_block.shape[0], local_heads, HD)
    scores = jnp.einsum(
        "qhd,khd->hqk", query_heads, key_heads, preferred_element_type=jnp.float32
    ) * (1.0 / math.sqrt(HD))
    allowed = (query_doc[:, None] == doc_block[None, :]) & (
        pos_block[None, :] <= query_pos[:, None]
    )
    scores = jnp.where(allowed[None], scores, MASKED_SCORE)
    new_max = jnp.maximum(largest, jnp.max(scores, axis=2))
    weights = jnp.where(allowed[None], jnp.exp(scores - new_max[:, :, None]), 0.0)
    factor = jnp.exp(largest - new_max)
    totals = totals * factor + jnp.sum(weights, axis=2)
    product = jnp.einsum(
        "hqk,khd->qhd",
        weights.astype(jnp.bfloat16),
        value_heads,
        preferred_element_type=jnp.float32,
    )
    summed = summed * factor.T[:, :, None] + product
    return (new_max, totals, summed)


def attend_rows(running, query, query_pos, query_doc, key_rows, value_rows, key_pos, key_doc):
    row_total = key_rows.shape[0]
    block_rows = math.gcd(row_total, query.shape[0])
    block_count = row_total // block_rows
    highest = jnp.max(query_pos)

    def visit(partial_value, blocks):
        key_block, value_block, pos_block, doc_block = blocks
        masked_out = jnp.min(pos_block) > highest
        updated = lax.cond(
            masked_out,
            lambda frozen: frozen,
            lambda frozen: block_update(
                frozen, query, query_pos, query_doc, key_block, value_block, pos_block, doc_block
            ),
            partial_value,
        )
        return (updated, None)

    blocks = (
        key_rows.reshape(block_count, block_rows, key_rows.shape[1]),
        value_rows.reshape(block_count, block_rows, value_rows.shape[1]),
        key_pos.reshape(block_count, block_rows),
        key_doc.reshape(block_count, block_rows),
    )
    running, _ = lax.scan(visit, running, blocks)
    return running


def attend_shard(running, query, query_pos, query_doc, key_rows, value_rows, key_pos, key_doc):
    largest, totals, summed = running
    half_rows = query.shape[0] // 2
    new_largest = []
    new_totals = []
    new_summed = []
    for half_idx in range(2):
        lower = half_idx * half_rows
        part_state = (largest[half_idx], totals[half_idx], summed[half_idx])
        part_state = attend_rows(
            part_state,
            query[lower : lower + half_rows],
            query_pos[lower : lower + half_rows],
            query_doc[lower : lower + half_rows],
            key_rows,
            value_rows,
            key_pos,
            key_doc,
        )
        new_largest.append(part_state[0])
        new_totals.append(part_state[1])
        new_summed.append(part_state[2])
    return (jnp.stack(new_largest), jnp.stack(new_totals), jnp.stack(new_summed))


def ring_local(queries, keys, values, doc_ids, w_out):
    shard_rows = queries.shape[0]
    half_rows = shard_rows // 2
    local_heads = queries.shape[1] // HD
    devices_ctx = lax.axis_size("ctx")
    ctx_index = lax.axis_index("ctx")
    all_docs = lax.all_gather(doc_ids, "ctx", axis=0, tiled=True)
    own_pos = folded_positions(shard_rows, ctx_index * shard_rows, shard_rows, devices_ctx)
    running = (
        jnp.full((2, local_heads, half_rows), MASKED_SCORE, jnp.float32),
        jnp.zeros((2, local_heads, half_rows), jnp.float32),
        jnp.zeros((2, half_rows, local_heads, HD), jnp.float32),
    )
    travel = queries
    for hop_step in range(devices_ctx):
        anchor = (ctx_index - hop_step) % devices_ctx
        query_pos = folded_positions(shard_rows, anchor * shard_rows, shard_rows, devices_ctx)
        query_doc = lax.dynamic_slice_in_dim(all_docs, anchor * shard_rows, shard_rows, 0)
        largest, totals, summed = attend_shard(
            running, travel, query_pos, query_doc, keys, values, own_pos, doc_ids
        )
        running = (
            passed_along(largest.astype(jnp.bfloat16), "ctx", 1).astype(largest.dtype),
            passed_along(totals.astype(jnp.bfloat16), "ctx", 1).astype(totals.dtype),
            passed_along(summed.astype(jnp.bfloat16), "ctx", 1).astype(summed.dtype),
        )
        if hop_step + 1 < devices_ctx:
            travel = passed_along(travel, "ctx", 1)
    largest, totals, summed = running
    attended = summed / totals.transpose(0, 2, 1)[:, :, :, None]
    attended = attended.reshape(shard_rows, local_heads * HD).astype(jnp.bfloat16)
    partial_out = jnp.dot(attended, w_out, preferred_element_type=jnp.float32)
    return lax.psum_scatter(
        partial_out.astype(jnp.bfloat16), "head", scatter_dimension=1, tiled=True
    )


def params(mib):
    return pltpu.CompilerParams(vmem_limit_bytes=mib * 1024 * 1024)


SMALL = pl.CostEstimate(flops=1024, bytes_accessed=1024, transcendentals=0)


def pack(ctx_index, half, queries, keys, values, docs):
    rows = queries.shape[0] // 2
    group = queries.shape[1] // HD
    doc_rows = 0 if docs is None else 16 * pl.cdiv(docs.shape[0], 16)
    total = 3 * rows + doc_rows

    def kernel(ctx_ref, *refs):
        outs = refs[len(refs) - (group - 1) :]
        if docs is not None:
            mine = refs[3 * (group - 1)][...].astype(jnp.float32)
            empty = jnp.zeros((doc_rows - mine.shape[0], HD), jnp.float32)
            mine = jnp.concatenate([mine, empty], axis=0).astype(jnp.bfloat16)
        for place in range(group - 1):
            for part in range(3):
                outs[place][part * rows : (part + 1) * rows, :] = refs[place * 3 + part][...]
            if docs is not None:
                outs[place][3 * rows :, :] = mine

    def piece(distance):
        return pl.BlockSpec((rows, HD), lambda step, ctx: (half, ctx[0] ^ distance))

    in_specs = []
    operands = []
    for distance in range(1, group):
        for array in (queries, keys, values):
            in_specs.append(piece(distance))
            operands.append(array)
    if docs is not None:
        in_specs.append(pl.BlockSpec(docs.shape, lambda step, ctx: (0, 0)))
        operands.append(docs)
    return pl.pallas_call(
        kernel,
        grid_spec=pltpu.PrefetchScalarGridSpec(
            num_scalar_prefetch=1,
            grid=(1,),
            in_specs=in_specs,
            out_specs=[pl.BlockSpec((total, HD), lambda step, ctx: (0, 0))] * (group - 1),
        ),
        out_shape=[jax.ShapeDtypeStruct((total, HD), jnp.bfloat16)] * (group - 1),
        compiler_params=params(24),
        cost_estimate=SMALL,
        name="pack",
    )(ctx_index, *operands)


def pack_projection(core, w_out, chips):
    depth, width = w_out.shape
    columns = width // (2 * chips)

    def kernel(core_ref, w_ref, out_ref):
        out_ref[...] = w_ref[...]

    return pl.pallas_call(
        kernel,
        grid_spec=pltpu.PrefetchScalarGridSpec(
            num_scalar_prefetch=1,
            grid=(chips,),
            in_specs=[pl.BlockSpec((depth, columns), lambda chip, c: (0, 2 * chip + 1 - c[0]))],
            out_specs=pl.BlockSpec((depth, columns), lambda chip, c: (0, chip)),
        ),
        out_shape=jax.ShapeDtypeStruct((depth, chips * columns), w_out.dtype),
        compiler_params=params(16),
        cost_estimate=SMALL,
        name="pack_projection",
    )(core, w_out)


def attend(ctx_index, queries, keys, values, docs, low, high):
    rows = queries.shape[0] // 2
    group = queries.shape[1] // HD
    with_high = high is not None
    blocks = 2 * group if with_high else group
    lanes = rows // HD
    scaling = LOG2E / math.sqrt(HD)

    def kernel(ctx_ref, *refs):
        refs = list(refs)
        own_low = [refs.pop(0) for _ in range(3)]
        own_high = [refs.pop(0) for _ in range(3)] if with_high else None
        own_docs = refs.pop(0)
        low_refs = [refs.pop(0) for _ in range(group - 1)]
        high_refs = [refs.pop(0) for _ in range(group - 1)] if with_high else None
        outs = [refs.pop(0) for _ in range(group)]
        key_buf, value_buf, doc_buf = refs
        ctx = ctx_ref[0]

        def part(upper, distance, index):
            if distance == 0:
                return (own_high if upper else own_low)[index][...]
            source = (high_refs if upper else low_refs)[distance - 1]
            return source[index * rows : (index + 1) * rows, :]

        first_doc = {}
        last_doc = {}
        place = {}
        doc_rows = {}
        for upper in (False, True) if with_high else (False,):
            for distance in range(group):
                source = ctx ^ distance
                block = 2 * group - 1 - source if upper else source
                place[upper, distance] = block
                offset = pl.multiple_of(block * rows, rows)
                key_buf[pl.ds(offset, rows), :] = part(upper, distance, 1)
                value_buf[pl.ds(offset, rows), :] = part(upper, distance, 2)
                if distance == 0:
                    both = own_docs[...].astype(jnp.float32)
                else:
                    both = low_refs[distance - 1][3 * rows :, :].astype(jnp.float32)
                begin = lanes if upper else 0
                mine = both[begin : begin + lanes, :]
                doc_rows[upper, distance] = mine
                doc_buf[pl.ds(block, 1), :] = jnp.concatenate(
                    [mine[line : line + 1, :] for line in range(lanes)], axis=1
                )
                first_doc[upper, distance] = jnp.min(mine)
                last_doc[upper, distance] = jnp.max(mine)

        row_index = lax.broadcasted_iota(jnp.int32, (rows, rows), 0)
        column_index = lax.broadcasted_iota(jnp.int32, (rows, rows), 1)
        for distance in range(group):
            me = (with_high, distance)
            block = place[me]
            query = part(with_high, distance, 0)
            mine = doc_rows[me]
            query_doc = jnp.concatenate(
                [
                    jnp.transpose(jnp.broadcast_to(mine[line : line + 1, :], (HD, HD)))
                    for line in range(lanes)
                ],
                axis=0,
            )[:, :1]
            start = jnp.int32(0)
            for other, last in last_doc.items():
                skip = jnp.logical_and(place[other] < block, last < first_doc[me])
                start = start + skip.astype(jnp.int32)

            def scores_of(index):
                offset = pl.multiple_of(index * rows, rows)
                raw = lax.dot_general(
                    query,
                    key_buf[pl.ds(offset, rows), :],
                    (((1,), (1,)), ((), ())),
                    preferred_element_type=jnp.float32,
                )
                same = query_doc == doc_buf[pl.ds(index, 1), :]
                return raw * scaling, same

            def weighted(weights, index):
                offset = pl.multiple_of(index * rows, rows)
                return jnp.dot(
                    weights.astype(jnp.bfloat16),
                    value_buf[pl.ds(offset, rows), :],
                    preferred_element_type=jnp.float32,
                )

            scores, same = scores_of(block)
            scores = jnp.where(same & (column_index <= row_index), scores, MASKED_SCORE)
            largest = jnp.max(scores, axis=1, keepdims=True)
            weights = jnp.exp2(scores - largest)
            totals = jnp.sum(weights, axis=1, keepdims=True)
            summed = weighted(weights, block)

            def visit(index, running):
                largest, totals, summed = running
                scores, same = scores_of(index)
                scores = jnp.where(same, scores, MASKED_SCORE)
                new_max = jnp.maximum(largest, jnp.max(scores, axis=1, keepdims=True))
                factor = jnp.exp2(largest - new_max)
                weights = jnp.exp2(scores - new_max)
                totals = totals * factor + jnp.sum(weights, axis=1, keepdims=True)
                summed = summed * factor + weighted(weights, index)
                return new_max, totals, summed

            largest, totals, summed = lax.fori_loop(
                start, block, visit, (largest, totals, summed)
            )
            outs[distance][...] = (summed / totals).astype(jnp.bfloat16)

    def own(upper):
        return pl.BlockSpec((rows, HD), lambda step, ctx: (int(upper), ctx[0]))

    def whole(array):
        return pl.BlockSpec(array.shape, lambda step, ctx: (0, 0))

    in_specs = [own(False)] * 3
    operands = [queries, keys, values]
    if with_high:
        in_specs += [own(True)] * 3
        operands += [queries, keys, values]
    operands += [docs, *low]
    in_specs += [whole(array) for array in (docs, *low)]
    if with_high:
        operands += list(high)
        in_specs += [whole(array) for array in high]
    return pl.pallas_call(
        kernel,
        grid_spec=pltpu.PrefetchScalarGridSpec(
            num_scalar_prefetch=1,
            grid=(1,),
            in_specs=in_specs,
            out_specs=[pl.BlockSpec((rows, HD), lambda step, ctx: (0, 0))] * group,
            scratch_shapes=[
                pltpu.VMEM((blocks * rows, HD), jnp.bfloat16),
                pltpu.VMEM((blocks * rows, HD), jnp.bfloat16),
                pltpu.VMEM((max(blocks, 8), rows), jnp.float32),
            ],
        ),
        out_shape=[jax.ShapeDtypeStruct((rows, HD), jnp.bfloat16)] * group,
        compiler_params=params(40),
        cost_estimate=SMALL,
        name="attend_high" if with_high else "attend_low",
    )(ctx_index, *operands)


def assemble(ctx_index, pieces):
    rows = pieces[0].shape[0]
    group = len(pieces)

    def kernel(ctx_ref, *refs):
        for distance in range(group):
            column = pl.multiple_of((ctx_ref[0] ^ distance) * HD, HD)
            refs[-1][:, pl.ds(column, HD)] = refs[distance][...]

    return pl.pallas_call(
        kernel,
        grid_spec=pltpu.PrefetchScalarGridSpec(
            num_scalar_prefetch=1,
            grid=(1,),
            in_specs=[pl.BlockSpec((rows, HD), lambda step, ctx: (0, 0))] * group,
            out_specs=pl.BlockSpec((rows, group * HD), lambda step, ctx: (0, 0)),
        ),
        out_shape=jax.ShapeDtypeStruct((rows, group * HD), jnp.bfloat16),
        compiler_params=params(16),
        cost_estimate=SMALL,
        name="assemble",
    )(ctx_index, *pieces)


def project(places, slot, mine, sibling, w_mine, w_sibling, chips):
    rows, depth = mine.shape
    columns = w_mine.shape[1] // (2 * chips)

    def kernel(places_ref, mine_ref, sibling_ref, w_mine_ref, w_sibling_ref, out_ref):
        total = jnp.dot(mine_ref[...], w_mine_ref[...], preferred_element_type=jnp.float32)
        total += jnp.dot(sibling_ref[...], w_sibling_ref[...], preferred_element_type=jnp.float32)
        out_ref[...] = total.astype(jnp.bfloat16)

    return pl.pallas_call(
        kernel,
        grid_spec=pltpu.PrefetchScalarGridSpec(
            num_scalar_prefetch=1,
            grid=(1,),
            in_specs=[
                pl.BlockSpec((rows, depth), lambda step, at: (0, 0)),
                pl.BlockSpec((rows, depth), lambda step, at: (0, 0)),
                pl.BlockSpec((depth, columns), lambda step, at: (0, 2 * at[slot] + at[chips])),
                pl.BlockSpec((depth, columns), lambda step, at: (0, at[slot])),
            ],
            out_specs=pl.BlockSpec((rows, columns), lambda step, at: (0, 0)),
        ),
        out_shape=jax.ShapeDtypeStruct((rows, columns), jnp.bfloat16),
        compiler_params=params(16),
        cost_estimate=SMALL,
        name="project",
    )(places, mine, sibling, w_mine, w_sibling)


def swap(value, axis, distance):
    count = lax.axis_size(axis)
    return lax.ppermute(value, axis, [(source, source ^ distance) for source in range(count)])


def between_chips(value, pairs):
    both = [(2 * source + core, 2 * target + core) for source, target in pairs for core in (0, 1)]
    return lax.ppermute(value, "head", both)


def add(*terms):
    total = terms[0].astype(jnp.float32)
    for term in terms[1:]:
        total = total + term.astype(jnp.float32)
    return total.astype(jnp.bfloat16)


SENDING = ((3, 2, 1, 0), (3, 2, 0, 1), (0, 1, 3, 2), (0, 1, 2, 3))
TO_MIDDLE = ((0, 1), (3, 2))
ACROSS = ((1, 2), (2, 1))
TO_ENDS = ((2, 3), (1, 0))


def line_reduce_scatter(shares):
    end = [between_chips(share, TO_MIDDLE) for share in shares[:3]]
    across = [between_chips(add(shares[turn], end[turn]), ACROSS) for turn in range(2)]
    outer = between_chips(add(shares[2], across[0]), TO_ENDS)
    return add(shares[3], end[2], across[1], outer)


def exchange_local(queries, keys, values, doc_ids, w_out):
    shard_rows = queries.shape[0]
    group = queries.shape[1] // HD
    chips = lax.axis_size("head") // 2
    ctx_index = lax.axis_index("ctx").astype(jnp.int32).reshape(1)
    head_index = lax.axis_index("head").astype(jnp.int32)
    chip = head_index // 2
    core = (head_index % 2).reshape(1)
    places = jnp.concatenate([jnp.array(SENDING, jnp.int32)[chip], core])
    docs = doc_ids.reshape(shard_rows // HD, HD)

    low_out = pack(ctx_index, 0, queries, keys, values, docs)
    *low_out, w_later = lax.optimization_barrier((*low_out, w_out))
    low = [swap(low_out[distance - 1], "ctx", distance) for distance in range(1, group)]
    w_sibling = swap(pack_projection(core, w_later, chips), "head", 1)
    high_out = pack(ctx_index, 1, queries, keys, values, None)
    high_out, low = lax.optimization_barrier((high_out, low))
    high = [swap(high_out[distance - 1], "ctx", distance) for distance in range(1, group - 1)]

    pieces = attend(ctx_index, queries, keys, values, docs, low, None)
    back = [swap(pieces[distance], "ctx", distance) for distance in range(1, group)]
    back, high, diagonal_out = lax.optimization_barrier((back, high, high_out[group - 2]))
    high = [*high, swap(diagonal_out, "ctx", group - 1)]
    mine = assemble(ctx_index, [pieces[0], *back])
    sibling = swap(mine, "head", 1)
    shares = [
        project(places, slot, mine, sibling, w_out, w_sibling, chips) for slot in range(chips)
    ]
    end = [between_chips(share, TO_MIDDLE) for share in shares[:3]]
    passed = add(shares[0], end[0])

    high, passed, shares = lax.optimization_barrier((high, passed, shares))
    across = [between_chips(passed, ACROSS)]
    pieces = attend(ctx_index, queries, keys, values, docs, low, high)
    back = [swap(pieces[distance], "ctx", distance) for distance in range(1, group)]
    back, passed = lax.optimization_barrier((back, add(shares[1], end[1])))
    across.append(between_chips(passed, ACROSS))
    outer = between_chips(add(shares[2], across[0]), TO_ENDS)
    mine = assemble(ctx_index, [pieces[0], *back])
    sibling = swap(mine, "head", 1)
    late_shares = [
        project(places, slot, mine, sibling, w_out, w_sibling, chips) for slot in range(chips)
    ]
    late_shares[1], end[2] = lax.optimization_barrier((late_shares[1], end[2]))
    first = add(shares[3], end[2], across[1], outer)
    return jnp.concatenate([first, line_reduce_scatter(late_shares)], axis=0)


def solution(mesh):
    in_specs = (P("ctx", "head"), P("ctx", "head"), P("ctx", "head"), P("ctx"), P("head", None))
    out_specs = P("ctx", "head")
    ctx_count = mesh.shape["ctx"]
    head_count = mesh.shape["head"]

    def local(queries, keys, values, doc_ids, w_out):
        heads = queries.shape[1] // HD
        exchange = heads == ctx_count and heads == 4 and head_count == 2 * len(SENDING)
        body = exchange_local if exchange else ring_local
        return body(queries, keys, values, doc_ids, w_out)

    return jax.shard_map(
        local, mesh=mesh, in_specs=in_specs, out_specs=out_specs, check_vma=False
    )
```

```python
import functools
import math

import jax
import jax.numpy as jnp
from jax import lax
from jax.experimental import pallas as pl
from jax.experimental.pallas import tpu as pltpu
from jax.sharding import PartitionSpec as P

HD = 128


MASKED_SCORE = -1e30
LOG2E = 1.4426950408889634


def passed_along(value, axis, steps):
    count = lax.axis_size(axis)
    pairs = [(source, (source + steps) % count) for source in range(count)]
    return lax.ppermute(value, axis, pairs)


def folded_positions(row_total, offset, shard_rows, devices_ctx):
    flat_index = offset + lax.iota(jnp.int32, row_total)
    owner_dev = flat_index // shard_rows
    within = flat_index % shard_rows
    half_rows = shard_rows // 2
    fold_block = jnp.where(within < half_rows, owner_dev, 2 * devices_ctx - 1 - owner_dev)
    return fold_block * half_rows + within % half_rows


def block_update(
    running, query, query_pos, query_doc, key_block, value_block, pos_block, doc_block
):
    largest, totals, summed = running
    query_rows = query.shape[0]
    local_heads = query.shape[1] // HD
    query_heads = query.reshape(query_rows, local_heads, HD)
    key_heads = key_block.reshape(key_block.shape[0], local_heads, HD)
    value_heads = value_block.reshape(value_block.shape[0], local_heads, HD)
    scores = jnp.einsum(
        "qhd,khd->hqk", query_heads, key_heads, preferred_element_type=jnp.float32
    ) * (1.0 / math.sqrt(HD))
    allowed = (query_doc[:, None] == doc_block[None, :]) & (
        pos_block[None, :] <= query_pos[:, None]
    )
    scores = jnp.where(allowed[None], scores, MASKED_SCORE)
    new_max = jnp.maximum(largest, jnp.max(scores, axis=2))
    weights = jnp.where(allowed[None], jnp.exp(scores - new_max[:, :, None]), 0.0)
    factor = jnp.exp(largest - new_max)
    totals = totals * factor + jnp.sum(weights, axis=2)
    product = jnp.einsum(
        "hqk,khd->qhd",
        weights.astype(jnp.bfloat16),
        value_heads,
        preferred_element_type=jnp.float32,
    )
    summed = summed * factor.T[:, :, None] + product
    return (new_max, totals, summed)


def attend_rows(running, query, query_pos, query_doc, key_rows, value_rows, key_pos, key_doc):
    row_total = key_rows.shape[0]
    block_rows = math.gcd(row_total, query.shape[0])
    block_count = row_total // block_rows
    highest = jnp.max(query_pos)

    def visit(partial_value, blocks):
        key_block, value_block, pos_block, doc_block = blocks
        masked_out = jnp.min(pos_block) > highest
        updated = lax.cond(
            masked_out,
            lambda frozen: frozen,
            lambda frozen: block_update(
                frozen, query, query_pos, query_doc, key_block, value_block, pos_block, doc_block
            ),
            partial_value,
        )
        return (updated, None)

    blocks = (
        key_rows.reshape(block_count, block_rows, key_rows.shape[1]),
        value_rows.reshape(block_count, block_rows, value_rows.shape[1]),
        key_pos.reshape(block_count, block_rows),
        key_doc.reshape(block_count, block_rows),
    )
    running, _ = lax.scan(visit, running, blocks)
    return running


def attend_shard(running, query, query_pos, query_doc, key_rows, value_rows, key_pos, key_doc):
    largest, totals, summed = running
    half_rows = query.shape[0] // 2
    new_largest = []
    new_totals = []
    new_summed = []
    for half_idx in range(2):
        lower = half_idx * half_rows
        part_state = (largest[half_idx], totals[half_idx], summed[half_idx])
        part_state = attend_rows(
            part_state,
            query[lower : lower + half_rows],
            query_pos[lower : lower + half_rows],
            query_doc[lower : lower + half_rows],
            key_rows,
            value_rows,
            key_pos,
            key_doc,
        )
        new_largest.append(part_state[0])
        new_totals.append(part_state[1])
        new_summed.append(part_state[2])
    return (jnp.stack(new_largest), jnp.stack(new_totals), jnp.stack(new_summed))


def ring_local(queries, keys, values, doc_ids, w_out):
    shard_rows = queries.shape[0]
    half_rows = shard_rows // 2
    local_heads = queries.shape[1] // HD
    devices_ctx = lax.axis_size("ctx")
    ctx_index = lax.axis_index("ctx")
    all_docs = lax.all_gather(doc_ids, "ctx", axis=0, tiled=True)
    own_pos = folded_positions(shard_rows, ctx_index * shard_rows, shard_rows, devices_ctx)
    running = (
        jnp.full((2, local_heads, half_rows), MASKED_SCORE, jnp.float32),
        jnp.zeros((2, local_heads, half_rows), jnp.float32),
        jnp.zeros((2, half_rows, local_heads, HD), jnp.float32),
    )
    travel = queries
    for hop_step in range(devices_ctx):
        anchor = (ctx_index - hop_step) % devices_ctx
        query_pos = folded_positions(shard_rows, anchor * shard_rows, shard_rows, devices_ctx)
        query_doc = lax.dynamic_slice_in_dim(all_docs, anchor * shard_rows, shard_rows, 0)
        largest, totals, summed = attend_shard(
            running, travel, query_pos, query_doc, keys, values, own_pos, doc_ids
        )
        running = (
            passed_along(largest.astype(jnp.bfloat16), "ctx", 1).astype(largest.dtype),
            passed_along(totals.astype(jnp.bfloat16), "ctx", 1).astype(totals.dtype),
            passed_along(summed.astype(jnp.bfloat16), "ctx", 1).astype(summed.dtype),
        )
        if hop_step + 1 < devices_ctx:
            travel = passed_along(travel, "ctx", 1)
    largest, totals, summed = running
    attended = summed / totals.transpose(0, 2, 1)[:, :, :, None]
    attended = attended.reshape(shard_rows, local_heads * HD).astype(jnp.bfloat16)
    partial_out = jnp.dot(attended, w_out, preferred_element_type=jnp.float32)
    return lax.psum_scatter(
        partial_out.astype(jnp.bfloat16), "head", scatter_dimension=1, tiled=True
    )


SMALL = pl.CostEstimate(flops=1024, bytes_accessed=1024, transcendentals=0)
TILE = 256


def params(mib):
    return pltpu.CompilerParams(vmem_limit_bytes=mib * 1024 * 1024)


def whole(shape):
    return pl.BlockSpec(shape, lambda step, scalars: (0,) * len(shape))


def pack(ctx_index, half, queries, keys, values, docs):
    rows = queries.shape[0] // 2
    group = queries.shape[1] // HD
    doc_rows = 0 if docs is None else 16 * pl.cdiv(docs.shape[0], 16)
    total = 3 * rows + doc_rows

    def kernel(ctx_ref, *refs):
        outs = refs[len(refs) - (group - 1) :]
        if docs is not None:
            mine = refs[3 * (group - 1)][...].astype(jnp.float32)
            empty = jnp.zeros((doc_rows - mine.shape[0], HD), jnp.float32)
            mine = jnp.concatenate([mine, empty], axis=0).astype(jnp.bfloat16)
        for place in range(group - 1):
            for part in range(3):
                outs[place][part * rows : (part + 1) * rows, :] = refs[place * 3 + part][...]
            if docs is not None:
                outs[place][3 * rows :, :] = mine

    def piece(distance):
        return pl.BlockSpec((rows, HD), lambda step, ctx: (half, ctx[0] ^ distance))

    in_specs = []
    operands = []
    for distance in range(1, group):
        for array in (queries, keys, values):
            in_specs.append(piece(distance))
            operands.append(array)
    if docs is not None:
        in_specs.append(whole(docs.shape))
        operands.append(docs)
    return pl.pallas_call(
        kernel,
        grid_spec=pltpu.PrefetchScalarGridSpec(
            num_scalar_prefetch=1,
            grid=(1,),
            in_specs=in_specs,
            out_specs=[whole((total, HD))] * (group - 1),
        ),
        out_shape=[jax.ShapeDtypeStruct((total, HD), jnp.bfloat16)] * (group - 1),
        compiler_params=params(56),
        cost_estimate=SMALL,
        name="pack",
    )(ctx_index, *operands)


def pack_projection(places, w_out, chips):
    depth, width = w_out.shape
    columns = width // (2 * chips)

    def kernel(places_ref, keep_in, give_in, keep_out, give_out):
        keep_out[...] = keep_in[...]
        give_out[...] = give_in[...]

    def block(other):
        def index_map(turn, at):
            parity = 1 - at[chips] if other else at[chips]
            return (0, 2 * at[turn] + parity)

        return pl.BlockSpec((depth, columns), index_map)

    out_spec = pl.BlockSpec((depth, columns), lambda turn, at: (0, turn))
    return pl.pallas_call(
        kernel,
        grid_spec=pltpu.PrefetchScalarGridSpec(
            num_scalar_prefetch=1,
            grid=(chips,),
            in_specs=[block(False), block(True)],
            out_specs=[out_spec] * 2,
        ),
        out_shape=[jax.ShapeDtypeStruct((depth, chips * columns), w_out.dtype)] * 2,
        compiler_params=params(56),
        cost_estimate=SMALL,
        name="pack_projection",
    )(places, w_out, w_out)


def attend(ctx_index, queries, keys, values, docs, low, high, tiles):
    rows = queries.shape[0] // 2
    group = queries.shape[1] // HD
    with_high = high is not None
    per_block = rows // TILE
    key_rows = (2 * group if with_high else group) * rows
    key_tiles = key_rows // TILE
    lanes = TILE // HD
    scaling = LOG2E / math.sqrt(HD)

    def kernel(ctx_ref, *refs):
        refs = list(refs)
        own_low = [refs.pop(0) for _ in range(3)]
        own_high = [refs.pop(0) for _ in range(3)] if with_high else None
        own_docs = refs.pop(0)
        low_refs = [refs.pop(0) for _ in range(group - 1)]
        high_refs = [refs.pop(0) for _ in range(group - 1)] if with_high else None
        outs = [refs.pop(0) for _ in range(group)]
        key_buf, value_buf, doc_buf = refs
        ctx = ctx_ref[0]

        def part(upper, distance, index, lower=0, count=rows):
            if distance == 0:
                return (own_high if upper else own_low)[index][lower : lower + count, :]
            source = (high_refs if upper else low_refs)[distance - 1]
            return source[index * rows + lower : index * rows + lower + count, :]

        place = {}
        doc_lines = {}
        for upper in (False, True) if with_high else (False,):
            for distance in range(group):
                source = ctx ^ distance
                block = 2 * group - 1 - source if upper else source
                place[upper, distance] = block
                offset = pl.multiple_of(block * rows, rows)
                key_buf[pl.ds(offset, rows), :] = part(upper, distance, 1)
                value_buf[pl.ds(offset, rows), :HD] = part(upper, distance, 2)
                if distance == 0:
                    both = own_docs[...].astype(jnp.float32)
                else:
                    both = low_refs[distance - 1][3 * rows :, :].astype(jnp.float32)
                begin = rows // HD if upper else 0
                for tile in range(per_block):
                    first = begin + tile * lanes
                    lines = [both[line : line + 1, :] for line in range(first, first + lanes)]
                    doc_lines[upper, distance, tile] = lines
                    doc_buf[pl.ds(block * per_block + tile, 1), :] = jnp.concatenate(lines, axis=1)
        value_buf[:, HD:] = jnp.ones((key_rows, HD), jnp.bfloat16)
        last_docs = doc_buf[:, TILE - 1 : TILE]

        def scores_of(query, index):
            offset = pl.multiple_of(index * TILE, TILE)
            raw = lax.dot_general(
                query,
                key_buf[pl.ds(offset, TILE), :],
                (((1,), (1,)), ((), ())),
                preferred_element_type=jnp.float32,
            )
            return raw * scaling

        def weighted(weights, index):
            offset = pl.multiple_of(index * TILE, TILE)
            return jnp.dot(
                weights.astype(jnp.bfloat16),
                value_buf[pl.ds(offset, TILE), :],
                preferred_element_type=jnp.float32,
            )

        causal = lax.broadcasted_iota(jnp.int32, (TILE, TILE), 1) <= lax.broadcasted_iota(
            jnp.int32, (TILE, TILE), 0
        )
        for number, tile in enumerate(tiles):
            state = []
            starts = []
            ends = []
            queries_of = []
            docs_of = []
            for distance in range(group):
                lines = doc_lines[with_high, distance, tile]
                column = jnp.concatenate(
                    [jnp.transpose(jnp.broadcast_to(line, (HD, HD))) for line in lines], axis=0
                )
                query_doc = jnp.concatenate([column] * lanes, axis=1)
                end = place[with_high, distance] * per_block + tile
                earlier = last_docs < lines[0][:, :1]
                starts.append(jnp.sum(earlier.astype(jnp.int32)))
                ends.append(end)
                query = part(with_high, distance, 0, tile * TILE, TILE)
                queries_of.append(query)
                docs_of.append(query_doc)
                same = query_doc == jnp.concatenate(lines, axis=1)
                scores = jnp.where(same & causal, scores_of(query, end), MASKED_SCORE)
                largest = jnp.max(scores, axis=1, keepdims=True)
                summed = weighted(jnp.exp2(scores - largest), end)
                state.append((largest, summed))

            longest = ends[0] - starts[0]
            for distance in range(1, group):
                longest = jnp.maximum(longest, ends[distance] - starts[distance])

            def visit(step, running):
                renewed = []
                for distance in range(group):
                    largest, summed = running[distance]
                    wanted = starts[distance] + step
                    index = jnp.minimum(wanted, ends[distance])
                    key_doc = doc_buf[pl.ds(index, 1), :]
                    key_doc = jnp.where(wanted < ends[distance], key_doc, -1.0)
                    scores = scores_of(queries_of[distance], index)
                    scores = jnp.where(docs_of[distance] == key_doc, scores, MASKED_SCORE)
                    new_max = jnp.maximum(largest, jnp.max(scores, axis=1, keepdims=True))
                    factor = jnp.exp2(largest - new_max)
                    product = weighted(jnp.exp2(scores - new_max), index)
                    renewed.append((new_max, summed * factor + product))
                return tuple(renewed)

            state = lax.fori_loop(0, longest, visit, tuple(state))
            for distance in range(group):
                summed = state[distance][1]
                outs[distance][number * TILE : (number + 1) * TILE, :] = (
                    summed[:, :HD] / summed[:, HD:]
                ).astype(jnp.bfloat16)

    def own(upper):
        return pl.BlockSpec((rows, HD), lambda step, ctx: (int(upper), ctx[0]))

    in_specs = [own(False)] * 3
    operands = [queries, keys, values]
    if with_high:
        in_specs += [own(True)] * 3
        operands += [queries, keys, values]
    received = [docs, *low, *(high if with_high else ())]
    operands += received
    in_specs += [whole(array.shape) for array in received]
    out_rows = len(tiles) * TILE
    return pl.pallas_call(
        kernel,
        grid_spec=pltpu.PrefetchScalarGridSpec(
            num_scalar_prefetch=1,
            grid=(1,),
            in_specs=in_specs,
            out_specs=[whole((out_rows, HD))] * group,
            scratch_shapes=[
                pltpu.VMEM((key_rows, HD), jnp.bfloat16),
                pltpu.VMEM((key_rows, 2 * HD), jnp.bfloat16),
                pltpu.VMEM((key_tiles, TILE), jnp.float32),
            ],
        ),
        out_shape=[jax.ShapeDtypeStruct((out_rows, HD), jnp.bfloat16)] * group,
        compiler_params=params(40),
        cost_estimate=SMALL,
        name="attend",
    )(ctx_index, *operands)


def assemble(ctx_index, pieces):
    rows = pieces[0].shape[0]
    group = len(pieces)

    def kernel(ctx_ref, *refs):
        for distance in range(group):
            column = pl.multiple_of((ctx_ref[0] ^ distance) * HD, HD)
            refs[-1][:, pl.ds(column, HD)] = refs[distance][...]

    return pl.pallas_call(
        kernel,
        grid_spec=pltpu.PrefetchScalarGridSpec(
            num_scalar_prefetch=1,
            grid=(1,),
            in_specs=[whole((rows, HD))] * group,
            out_specs=whole((rows, group * HD)),
        ),
        out_shape=jax.ShapeDtypeStruct((rows, group * HD), jnp.bfloat16),
        compiler_params=params(16),
        cost_estimate=SMALL,
        name="assemble",
    )(ctx_index, *pieces)


def project(mine, sibling, w_mine, w_sibling, first, count, chips):
    rows, depth = mine.shape
    columns = w_mine.shape[1] // chips

    def kernel(mine_ref, sibling_ref, w_mine_ref, w_sibling_ref, out_ref):
        total = jnp.dot(mine_ref[...], w_mine_ref[...], preferred_element_type=jnp.float32)
        total += jnp.dot(sibling_ref[...], w_sibling_ref[...], preferred_element_type=jnp.float32)
        out_ref[...] = total.astype(jnp.bfloat16)

    weights = pl.BlockSpec((depth, columns), lambda turn: (0, first + turn))
    attended = pl.BlockSpec((rows, depth), lambda turn: (0, 0))
    return pl.pallas_call(
        kernel,
        grid=(count,),
        in_specs=[attended, attended, weights, weights],
        out_specs=pl.BlockSpec((rows, columns), lambda turn: (0, turn)),
        out_shape=jax.ShapeDtypeStruct((rows, count * columns), jnp.bfloat16),
        compiler_params=params(16),
        cost_estimate=SMALL,
        name="project",
    )(mine, sibling, w_mine, w_sibling)


def swap(value, axis, distance):
    count = lax.axis_size(axis)
    return lax.ppermute(value, axis, [(source, source ^ distance) for source in range(count)])


def between_chips(value, pairs):
    both = [(2 * source + core, 2 * target + core) for source, target in pairs for core in (0, 1)]
    return lax.ppermute(value, "head", both)


def add(*terms):
    total = terms[0].astype(jnp.float32)
    for term in terms[1:]:
        total = total + term.astype(jnp.float32)
    return total.astype(jnp.bfloat16)


SENDING = ((3, 2, 1, 0), (3, 2, 0, 1), (0, 1, 3, 2), (0, 1, 2, 3))
TO_MIDDLE = ((0, 1), (3, 2))
ACROSS = ((1, 2), (2, 1))
TO_ENDS = ((2, 3), (1, 0))


def tie(*values):
    return lax.optimization_barrier(values)


def exchange_local(queries, keys, values, doc_ids, w_out):
    shard_rows = queries.shape[0]
    group = queries.shape[1] // HD
    chips = lax.axis_size("head") // 2
    columns = w_out.shape[1] // (2 * chips)
    ctx_index = lax.axis_index("ctx").astype(jnp.int32).reshape(1)
    head_index = lax.axis_index("head").astype(jnp.int32)
    chip = head_index // 2
    core = (head_index % 2).reshape(1)
    places = jnp.concatenate([jnp.array(SENDING, jnp.int32)[chip], core])
    docs = doc_ids.reshape(shard_rows // HD, HD)
    near = range(1, group)

    low_out = pack(ctx_index, 0, queries, keys, values, docs)
    low = [swap(low_out[distance - 1], "ctx", distance) for distance in near]
    w_mine, w_give = pack_projection(places, w_out, chips)
    low, w_give = tie(low, w_give)
    w_sibling = swap(w_give, "head", 1)
    high_out = pack(ctx_index, 1, queries, keys, values, None)

    def attend_rows(high, tiles):
        return attend(ctx_index, queries, keys, values, docs, low, high, tiles)

    def send_back(pieces):
        return [swap(pieces[distance], "ctx", distance) for distance in near]

    def share_of(mine, sibling, first, count):
        return project(mine, sibling, w_mine, w_sibling, first, count, chips)

    pieces = attend_rows(None, (0,))
    back = send_back(pieces)
    pieces, high_out = tie(pieces, high_out)
    high = [swap(high_out[0], "ctx", 1), swap(high_out[1], "ctx", 2)]
    mine = [assemble(ctx_index, [pieces[0], *back])]
    mine[0], diagonal_out = tie(mine[0], high_out[2])
    high.append(swap(diagonal_out, "ctx", 3))
    sibling = [swap(mine[0], "head", 1)]
    shares = [share_of(mine[0], sibling[0], 0, 2)]
    end = [between_chips(shares[0], TO_MIDDLE)]

    pieces = attend_rows(None, tuple(range(1, shard_rows // 2 // TILE)))
    back = send_back(pieces)
    back, shares, high = tie(back, shares, high)
    mine.append(assemble(ctx_index, [pieces[0], *back]))
    sibling.append(swap(mine[1], "head", 1))
    shares.append(share_of(mine[1], sibling[1], 0, 2))
    end.append(between_chips(shares[1], TO_MIDDLE))
    rest = [share_of(mine[turn], sibling[turn], 2, 2) for turn in range(2)]
    rest = jnp.concatenate(rest, axis=0)
    passed = add(shares[0], end[0])

    high, passed, rest, shares = tie(high, passed, rest, shares)
    across = [between_chips(passed, ACROSS)]
    pieces = attend_rows(high, tuple(range(shard_rows // 2 // TILE)))
    back = send_back(pieces)
    passed = add(shares[1], end[1])
    back, passed, kept, across[0] = tie(back, passed, rest[:, :columns], across[0])
    across.append(between_chips(passed, ACROSS))
    end_low = between_chips(kept, TO_MIDDLE)
    mine_high = assemble(ctx_index, [pieces[0], *back])
    sibling_high = swap(mine_high, "head", 1)
    late = [share_of(mine_high, sibling_high, turn, 1) for turn in range(4)]
    end_high = [between_chips(late[0], TO_MIDDLE)]
    across_low = jnp.concatenate(across, axis=0)
    outer_low = between_chips(add(rest[:, :columns], across_low[:, :columns]), TO_ENDS)
    passed = add(late[0], end_high[0])
    late[1], passed = tie(late[1], passed)
    across_high = [between_chips(passed, ACROSS)]
    end_high.append(between_chips(late[1], TO_MIDDLE))
    passed = add(late[1], end_high[1])
    late[2], passed = tie(late[2], passed)
    across_high.append(between_chips(passed, ACROSS))
    end_high.append(between_chips(late[2], TO_MIDDLE))
    outer_high = between_chips(add(late[2], across_high[0]), TO_ENDS)
    first = add(rest[:, columns:], end_low, across_low[:, columns:], outer_low)
    second = add(late[3], end_high[2], across_high[1], outer_high)
    return jnp.concatenate([first, second], axis=0)


def solution(mesh):
    in_specs = (P("ctx", "head"), P("ctx", "head"), P("ctx", "head"), P("ctx"), P("head", None))
    out_specs = P("ctx", "head")
    ctx_count = mesh.shape["ctx"]
    head_count = mesh.shape["head"]

    def local(queries, keys, values, doc_ids, w_out):
        heads = queries.shape[1] // HD
        exchange = heads == ctx_count and heads == 4 and head_count == 2 * len(SENDING)
        exchange = exchange and queries.shape[0] % (4 * TILE) == 0
        body = exchange_local if exchange else ring_local
        return body(queries, keys, values, doc_ids, w_out)

    return jax.shard_map(
        local, mesh=mesh, in_specs=in_specs, out_specs=out_specs, check_vma=False
    )
```

```python
import functools
import math

import jax
import jax.numpy as jnp
from jax import lax
from jax.experimental import pallas as pl
from jax.experimental.pallas import tpu as pltpu
from jax.sharding import PartitionSpec as P

HD = 128


MASKED_SCORE = -1e30
LOG2E = 1.4426950408889634


def passed_along(value, axis, steps):
    count = lax.axis_size(axis)
    pairs = [(source, (source + steps) % count) for source in range(count)]
    return lax.ppermute(value, axis, pairs)


def folded_positions(row_total, offset, shard_rows, devices_ctx):
    flat_index = offset + lax.iota(jnp.int32, row_total)
    owner_dev = flat_index // shard_rows
    within = flat_index % shard_rows
    half_rows = shard_rows // 2
    fold_block = jnp.where(within < half_rows, owner_dev, 2 * devices_ctx - 1 - owner_dev)
    return fold_block * half_rows + within % half_rows


def block_update(
    running, query, query_pos, query_doc, key_block, value_block, pos_block, doc_block
):
    largest, totals, summed = running
    query_rows = query.shape[0]
    local_heads = query.shape[1] // HD
    query_heads = query.reshape(query_rows, local_heads, HD)
    key_heads = key_block.reshape(key_block.shape[0], local_heads, HD)
    value_heads = value_block.reshape(value_block.shape[0], local_heads, HD)
    scores = jnp.einsum(
        "qhd,khd->hqk", query_heads, key_heads, preferred_element_type=jnp.float32
    ) * (1.0 / math.sqrt(HD))
    allowed = (query_doc[:, None] == doc_block[None, :]) & (
        pos_block[None, :] <= query_pos[:, None]
    )
    scores = jnp.where(allowed[None], scores, MASKED_SCORE)
    new_max = jnp.maximum(largest, jnp.max(scores, axis=2))
    weights = jnp.where(allowed[None], jnp.exp(scores - new_max[:, :, None]), 0.0)
    factor = jnp.exp(largest - new_max)
    totals = totals * factor + jnp.sum(weights, axis=2)
    product = jnp.einsum(
        "hqk,khd->qhd",
        weights.astype(jnp.bfloat16),
        value_heads,
        preferred_element_type=jnp.float32,
    )
    summed = summed * factor.T[:, :, None] + product
    return (new_max, totals, summed)


def attend_rows(running, query, query_pos, query_doc, key_rows, value_rows, key_pos, key_doc):
    row_total = key_rows.shape[0]
    block_rows = math.gcd(row_total, query.shape[0])
    block_count = row_total // block_rows
    highest = jnp.max(query_pos)

    def visit(partial_value, blocks):
        key_block, value_block, pos_block, doc_block = blocks
        masked_out = jnp.min(pos_block) > highest
        updated = lax.cond(
            masked_out,
            lambda frozen: frozen,
            lambda frozen: block_update(
                frozen, query, query_pos, query_doc, key_block, value_block, pos_block, doc_block
            ),
            partial_value,
        )
        return (updated, None)

    blocks = (
        key_rows.reshape(block_count, block_rows, key_rows.shape[1]),
        value_rows.reshape(block_count, block_rows, value_rows.shape[1]),
        key_pos.reshape(block_count, block_rows),
        key_doc.reshape(block_count, block_rows),
    )
    running, _ = lax.scan(visit, running, blocks)
    return running


def attend_shard(running, query, query_pos, query_doc, key_rows, value_rows, key_pos, key_doc):
    largest, totals, summed = running
    half_rows = query.shape[0] // 2
    new_largest = []
    new_totals = []
    new_summed = []
    for half_idx in range(2):
        lower = half_idx * half_rows
        part_state = (largest[half_idx], totals[half_idx], summed[half_idx])
        part_state = attend_rows(
            part_state,
            query[lower : lower + half_rows],
            query_pos[lower : lower + half_rows],
            query_doc[lower : lower + half_rows],
            key_rows,
            value_rows,
            key_pos,
            key_doc,
        )
        new_largest.append(part_state[0])
        new_totals.append(part_state[1])
        new_summed.append(part_state[2])
    return (jnp.stack(new_largest), jnp.stack(new_totals), jnp.stack(new_summed))


def ring_local(queries, keys, values, doc_ids, w_out):
    shard_rows = queries.shape[0]
    half_rows = shard_rows // 2
    local_heads = queries.shape[1] // HD
    devices_ctx = lax.axis_size("ctx")
    ctx_index = lax.axis_index("ctx")
    all_docs = lax.all_gather(doc_ids, "ctx", axis=0, tiled=True)
    own_pos = folded_positions(shard_rows, ctx_index * shard_rows, shard_rows, devices_ctx)
    running = (
        jnp.full((2, local_heads, half_rows), MASKED_SCORE, jnp.float32),
        jnp.zeros((2, local_heads, half_rows), jnp.float32),
        jnp.zeros((2, half_rows, local_heads, HD), jnp.float32),
    )
    travel = queries
    for hop_step in range(devices_ctx):
        anchor = (ctx_index - hop_step) % devices_ctx
        query_pos = folded_positions(shard_rows, anchor * shard_rows, shard_rows, devices_ctx)
        query_doc = lax.dynamic_slice_in_dim(all_docs, anchor * shard_rows, shard_rows, 0)
        largest, totals, summed = attend_shard(
            running, travel, query_pos, query_doc, keys, values, own_pos, doc_ids
        )
        running = (
            passed_along(largest.astype(jnp.bfloat16), "ctx", 1).astype(largest.dtype),
            passed_along(totals.astype(jnp.bfloat16), "ctx", 1).astype(totals.dtype),
            passed_along(summed.astype(jnp.bfloat16), "ctx", 1).astype(summed.dtype),
        )
        if hop_step + 1 < devices_ctx:
            travel = passed_along(travel, "ctx", 1)
    largest, totals, summed = running
    attended = summed / totals.transpose(0, 2, 1)[:, :, :, None]
    attended = attended.reshape(shard_rows, local_heads * HD).astype(jnp.bfloat16)
    partial_out = jnp.dot(attended, w_out, preferred_element_type=jnp.float32)
    return lax.psum_scatter(
        partial_out.astype(jnp.bfloat16), "head", scatter_dimension=1, tiled=True
    )


SMALL = pl.CostEstimate(flops=1024, bytes_accessed=1024, transcendentals=0)
TILE = 256


def params(mib):
    return pltpu.CompilerParams(vmem_limit_bytes=mib * 1024 * 1024)


def whole(shape):
    return pl.BlockSpec(shape, lambda step, scalars: (0,) * len(shape))


def pack(ctx_index, half, queries, keys, values, docs):
    rows = queries.shape[0] // 2
    group = queries.shape[1] // HD
    doc_rows = 0 if docs is None else 16 * pl.cdiv(docs.shape[0], 16)
    total = 3 * rows + doc_rows

    def kernel(ctx_ref, *refs):
        outs = refs[len(refs) - (group - 1) :]
        if docs is not None:
            mine = refs[3 * (group - 1)][...].astype(jnp.float32)
            empty = jnp.zeros((doc_rows - mine.shape[0], HD), jnp.float32)
            mine = jnp.concatenate([mine, empty], axis=0).astype(jnp.bfloat16)
        for place in range(group - 1):
            for part in range(3):
                outs[place][part * rows : (part + 1) * rows, :] = refs[place * 3 + part][...]
            if docs is not None:
                outs[place][3 * rows :, :] = mine

    def piece(distance):
        return pl.BlockSpec((rows, HD), lambda step, ctx: (half, ctx[0] ^ distance))

    in_specs = []
    operands = []
    for distance in range(1, group):
        for array in (queries, keys, values):
            in_specs.append(piece(distance))
            operands.append(array)
    if docs is not None:
        in_specs.append(whole(docs.shape))
        operands.append(docs)
    return pl.pallas_call(
        kernel,
        grid_spec=pltpu.PrefetchScalarGridSpec(
            num_scalar_prefetch=1,
            grid=(1,),
            in_specs=in_specs,
            out_specs=[whole((total, HD))] * (group - 1),
        ),
        out_shape=[jax.ShapeDtypeStruct((total, HD), jnp.bfloat16)] * (group - 1),
        compiler_params=params(56),
        cost_estimate=SMALL,
        name="pack",
    )(ctx_index, *operands)


def pack_projection(places, w_out, chips):
    depth, width = w_out.shape
    columns = width // (2 * chips)

    def kernel(places_ref, keep_in, give_in, keep_out, give_out):
        keep_out[...] = keep_in[...]
        give_out[...] = give_in[...]

    def block(other):
        def index_map(turn, at):
            parity = 1 - at[chips] if other else at[chips]
            return (0, 2 * at[turn] + parity)

        return pl.BlockSpec((depth, columns), index_map)

    out_spec = pl.BlockSpec((depth, columns), lambda turn, at: (0, turn))
    return pl.pallas_call(
        kernel,
        grid_spec=pltpu.PrefetchScalarGridSpec(
            num_scalar_prefetch=1,
            grid=(chips,),
            in_specs=[block(False), block(True)],
            out_specs=[out_spec] * 2,
        ),
        out_shape=[jax.ShapeDtypeStruct((depth, chips * columns), w_out.dtype)] * 2,
        compiler_params=params(56),
        cost_estimate=SMALL,
        name="pack_projection",
    )(places, w_out, w_out)


def attend(ctx_index, queries, keys, values, docs, low, high, tiles):
    rows = queries.shape[0] // 2
    group = queries.shape[1] // HD
    with_high = high is not None
    per_block = rows // TILE
    key_rows = (2 * group if with_high else group) * rows
    key_tiles = key_rows // TILE
    lanes = TILE // HD
    scaling = LOG2E / math.sqrt(HD)

    def kernel(ctx_ref, *refs):
        refs = list(refs)
        own_low = [refs.pop(0) for _ in range(3)]
        own_high = [refs.pop(0) for _ in range(3)] if with_high else None
        own_docs = refs.pop(0)
        low_refs = [refs.pop(0) for _ in range(group - 1)]
        high_refs = [refs.pop(0) for _ in range(group - 1)] if with_high else None
        outs = [refs.pop(0) for _ in range(group)]
        key_buf, value_buf, doc_buf = refs
        ctx = ctx_ref[0]

        def part(upper, distance, index, lower=0, count=rows):
            if distance == 0:
                return (own_high if upper else own_low)[index][lower : lower + count, :]
            source = (high_refs if upper else low_refs)[distance - 1]
            return source[index * rows + lower : index * rows + lower + count, :]

        place = {}
        doc_lines = {}
        for upper in (False, True) if with_high else (False,):
            for distance in range(group):
                source = ctx ^ distance
                block = 2 * group - 1 - source if upper else source
                place[upper, distance] = block
                offset = pl.multiple_of(block * rows, rows)
                key_buf[pl.ds(offset, rows), :] = part(upper, distance, 1)
                value_buf[pl.ds(offset, rows), :HD] = part(upper, distance, 2)
                if distance == 0:
                    both = own_docs[...].astype(jnp.float32)
                else:
                    both = low_refs[distance - 1][3 * rows :, :].astype(jnp.float32)
                begin = rows // HD if upper else 0
                for tile in range(per_block):
                    first = begin + tile * lanes
                    lines = [both[line : line + 1, :] for line in range(first, first + lanes)]
                    doc_lines[upper, distance, tile] = lines
                    doc_buf[pl.ds(block * per_block + tile, 1), :] = jnp.concatenate(lines, axis=1)
        value_buf[:, HD:] = jnp.ones((key_rows, HD), jnp.bfloat16)
        last_docs = doc_buf[:, TILE - 1 : TILE]

        def scores_of(query, index):
            offset = pl.multiple_of(index * TILE, TILE)
            raw = lax.dot_general(
                query,
                key_buf[pl.ds(offset, TILE), :],
                (((1,), (1,)), ((), ())),
                preferred_element_type=jnp.float32,
            )
            return raw * scaling

        def weighted(weights, index):
            offset = pl.multiple_of(index * TILE, TILE)
            return jnp.dot(
                weights.astype(jnp.bfloat16),
                value_buf[pl.ds(offset, TILE), :],
                preferred_element_type=jnp.float32,
            )

        causal = lax.broadcasted_iota(jnp.int32, (TILE, TILE), 1) <= lax.broadcasted_iota(
            jnp.int32, (TILE, TILE), 0
        )
        for number, tile in enumerate(tiles):
            state = []
            starts = []
            ends = []
            queries_of = []
            docs_of = []
            for distance in range(group):
                lines = doc_lines[with_high, distance, tile]
                column = jnp.concatenate(
                    [jnp.transpose(jnp.broadcast_to(line, (HD, HD))) for line in lines], axis=0
                )
                query_doc = jnp.concatenate([column] * lanes, axis=1)
                end = place[with_high, distance] * per_block + tile
                earlier = last_docs < lines[0][:, :1]
                starts.append(jnp.sum(earlier.astype(jnp.int32)))
                ends.append(end)
                query = part(with_high, distance, 0, tile * TILE, TILE)
                queries_of.append(query)
                docs_of.append(query_doc)
                same = query_doc == jnp.concatenate(lines, axis=1)
                scores = jnp.where(same & causal, scores_of(query, end), MASKED_SCORE)
                largest = jnp.max(scores, axis=1, keepdims=True)
                summed = weighted(jnp.exp2(scores - largest), end)
                state.append((largest, summed))

            longest = ends[0] - starts[0]
            for distance in range(1, group):
                longest = jnp.maximum(longest, ends[distance] - starts[distance])

            def visit(step, running):
                renewed = []
                for distance in range(group):
                    largest, summed = running[distance]
                    wanted = starts[distance] + step
                    index = jnp.minimum(wanted, ends[distance])
                    key_doc = doc_buf[pl.ds(index, 1), :]
                    key_doc = jnp.where(wanted < ends[distance], key_doc, -1.0)
                    scores = scores_of(queries_of[distance], index)
                    scores = jnp.where(docs_of[distance] == key_doc, scores, MASKED_SCORE)
                    new_max = jnp.maximum(largest, jnp.max(scores, axis=1, keepdims=True))
                    factor = jnp.exp2(largest - new_max)
                    product = weighted(jnp.exp2(scores - new_max), index)
                    renewed.append((new_max, summed * factor + product))
                return tuple(renewed)

            state = lax.fori_loop(0, longest, visit, tuple(state))
            for distance in range(group):
                summed = state[distance][1]
                outs[distance][number * TILE : (number + 1) * TILE, :] = (
                    summed[:, :HD] / summed[:, HD:]
                ).astype(jnp.bfloat16)

    def own(upper):
        return pl.BlockSpec((rows, HD), lambda step, ctx: (int(upper), ctx[0]))

    in_specs = [own(False)] * 3
    operands = [queries, keys, values]
    if with_high:
        in_specs += [own(True)] * 3
        operands += [queries, keys, values]
    received = [docs, *low, *(high if with_high else ())]
    operands += received
    in_specs += [whole(array.shape) for array in received]
    out_rows = len(tiles) * TILE
    return pl.pallas_call(
        kernel,
        grid_spec=pltpu.PrefetchScalarGridSpec(
            num_scalar_prefetch=1,
            grid=(1,),
            in_specs=in_specs,
            out_specs=[whole((out_rows, HD))] * group,
            scratch_shapes=[
                pltpu.VMEM((key_rows, HD), jnp.bfloat16),
                pltpu.VMEM((key_rows, 2 * HD), jnp.bfloat16),
                pltpu.VMEM((key_tiles, TILE), jnp.float32),
            ],
        ),
        out_shape=[jax.ShapeDtypeStruct((out_rows, HD), jnp.bfloat16)] * group,
        compiler_params=params(40),
        cost_estimate=SMALL,
        name="attend",
    )(ctx_index, *operands)


def assemble(ctx_index, pieces):
    rows = pieces[0].shape[0]
    group = len(pieces)

    def kernel(ctx_ref, *refs):
        for distance in range(group):
            column = pl.multiple_of((ctx_ref[0] ^ distance) * HD, HD)
            refs[-1][:, pl.ds(column, HD)] = refs[distance][...]

    return pl.pallas_call(
        kernel,
        grid_spec=pltpu.PrefetchScalarGridSpec(
            num_scalar_prefetch=1,
            grid=(1,),
            in_specs=[whole((rows, HD))] * group,
            out_specs=whole((rows, group * HD)),
        ),
        out_shape=jax.ShapeDtypeStruct((rows, group * HD), jnp.bfloat16),
        compiler_params=params(16),
        cost_estimate=SMALL,
        name="assemble",
    )(ctx_index, *pieces)


def project(mine, sibling, w_mine, w_sibling, first, count, chips):
    rows, depth = mine.shape
    columns = w_mine.shape[1] // chips

    def kernel(mine_ref, sibling_ref, w_mine_ref, w_sibling_ref, out_ref):
        total = jnp.dot(mine_ref[...], w_mine_ref[...], preferred_element_type=jnp.float32)
        total += jnp.dot(sibling_ref[...], w_sibling_ref[...], preferred_element_type=jnp.float32)
        out_ref[...] = total.astype(jnp.bfloat16)

    weights = pl.BlockSpec((depth, columns), lambda turn: (0, first + turn))
    attended = pl.BlockSpec((rows, depth), lambda turn: (0, 0))
    return pl.pallas_call(
        kernel,
        grid=(count,),
        in_specs=[attended, attended, weights, weights],
        out_specs=pl.BlockSpec((rows, columns), lambda turn: (0, turn)),
        out_shape=jax.ShapeDtypeStruct((rows, count * columns), jnp.bfloat16),
        compiler_params=params(16),
        cost_estimate=SMALL,
        name="project",
    )(mine, sibling, w_mine, w_sibling)


def swap(value, axis, distance):
    count = lax.axis_size(axis)
    return lax.ppermute(value, axis, [(source, source ^ distance) for source in range(count)])


def between_chips(value, pairs):
    both = [(2 * source + core, 2 * target + core) for source, target in pairs for core in (0, 1)]
    return lax.ppermute(value, "head", both)


def add(*terms):
    total = terms[0].astype(jnp.float32)
    for term in terms[1:]:
        total = total + term.astype(jnp.float32)
    return total.astype(jnp.bfloat16)


SENDING = ((3, 2, 1, 0), (3, 2, 0, 1), (0, 1, 3, 2), (0, 1, 2, 3))
TO_MIDDLE = ((0, 1), (3, 2))
ACROSS = ((1, 2), (2, 1))
TO_ENDS = ((2, 3), (1, 0))


def tie(*values):
    return lax.optimization_barrier(values)


def exchange_local(queries, keys, values, doc_ids, w_out):
    shard_rows = queries.shape[0]
    group = queries.shape[1] // HD
    chips = lax.axis_size("head") // 2
    columns = w_out.shape[1] // (2 * chips)
    ctx_index = lax.axis_index("ctx").astype(jnp.int32).reshape(1)
    head_index = lax.axis_index("head").astype(jnp.int32)
    chip = head_index // 2
    core = (head_index % 2).reshape(1)
    places = jnp.concatenate([jnp.array(SENDING, jnp.int32)[chip], core])
    docs = doc_ids.reshape(shard_rows // HD, HD)
    near = range(1, group)

    low_out = pack(ctx_index, 0, queries, keys, values, docs)
    low = [swap(low_out[distance - 1], "ctx", distance) for distance in near]
    w_mine, w_give = pack_projection(places, w_out, chips)
    low, w_give = tie(low, w_give)
    w_sibling = swap(w_give, "head", 1)
    high_out = pack(ctx_index, 1, queries, keys, values, None)
    tiles = tuple(range(shard_rows // 2 // TILE))

    def send_back(pieces):
        return [swap(pieces[distance], "ctx", distance) for distance in near]

    def share_of(mine, sibling, turn):
        return project(mine, sibling, w_mine, w_sibling, turn, 1, chips)

    pieces = attend(ctx_index, queries, keys, values, docs, low, None, tiles)
    back = send_back(pieces)
    pieces, high_out = tie(pieces, high_out)
    high = [swap(high_out[0], "ctx", 1), swap(high_out[1], "ctx", 2)]
    mine = assemble(ctx_index, [pieces[0], *back])
    mine, diagonal_out = tie(mine, high_out[2])
    high.append(swap(diagonal_out, "ctx", 3))
    sibling = swap(mine, "head", 1)
    shares = [share_of(mine, sibling, turn) for turn in range(chips)]
    end = [between_chips(shares[0], TO_MIDDLE)]
    end[0], shares[1] = tie(end[0], shares[1])
    end.append(between_chips(shares[1], TO_MIDDLE))
    passed = add(shares[0], end[0])

    high, passed, shares[1:] = tie(high, passed, shares[1:])
    across = [between_chips(passed, ACROSS)]
    pieces = attend(ctx_index, queries, keys, values, docs, low, high, tiles)
    back = send_back(pieces)
    passed = add(shares[1], end[1])
    back, passed, shares[2] = tie(back, passed, shares[2])
    across.append(between_chips(passed, ACROSS))
    end.append(between_chips(shares[2], TO_MIDDLE))
    mine = assemble(ctx_index, [pieces[0], *back])
    mine, across[0] = tie(mine, across[0])
    sibling = swap(mine, "head", 1)
    outer = between_chips(add(shares[2], across[0]), TO_ENDS)
    late = [share_of(mine, sibling, turn) for turn in range(chips)]
    late[0], end[2] = tie(late[0], end[2])
    end_high = [between_chips(late[0], TO_MIDDLE)]
    passed = add(late[0], end_high[0])
    late[1], passed, across[1], outer = tie(late[1], passed, across[1], outer)
    across_high = [between_chips(passed, ACROSS)]
    end_high.append(between_chips(late[1], TO_MIDDLE))
    first = add(shares[3], end[2], across[1], outer)
    passed = add(late[1], end_high[1])
    late[2], passed, first = tie(late[2], passed, first)
    across_high.append(between_chips(passed, ACROSS))
    end_high.append(between_chips(late[2], TO_MIDDLE))
    outer_high = between_chips(add(late[2], across_high[0]), TO_ENDS)
    second = add(late[3], end_high[2], across_high[1], outer_high)
    return jnp.concatenate([first, second], axis=0)


def solution(mesh):
    in_specs = (P("ctx", "head"), P("ctx", "head"), P("ctx", "head"), P("ctx"), P("head", None))
    out_specs = P("ctx", "head")
    ctx_count = mesh.shape["ctx"]
    head_count = mesh.shape["head"]

    def local(queries, keys, values, doc_ids, w_out):
        heads = queries.shape[1] // HD
        exchange = heads == ctx_count and heads == 4 and head_count == 2 * len(SENDING)
        exchange = exchange and queries.shape[0] % (4 * TILE) == 0
        body = exchange_local if exchange else ring_local
        return body(queries, keys, values, doc_ids, w_out)

    return jax.shard_map(
        local, mesh=mesh, in_specs=in_specs, out_specs=out_specs, check_vma=False
    )
```

```python
import functools
import math

import jax
import jax.numpy as jnp
from jax import lax
from jax.experimental import pallas as pl
from jax.experimental.pallas import tpu as pltpu
from jax.sharding import PartitionSpec as P

HD = 128


MASKED_SCORE = -1e30
LOG2E = 1.4426950408889634


def passed_along(value, axis, steps):
    count = lax.axis_size(axis)
    pairs = [(source, (source + steps) % count) for source in range(count)]
    return lax.ppermute(value, axis, pairs)


def folded_positions(row_total, offset, shard_rows, devices_ctx):
    flat_index = offset + lax.iota(jnp.int32, row_total)
    owner_dev = flat_index // shard_rows
    within = flat_index % shard_rows
    half_rows = shard_rows // 2
    fold_block = jnp.where(within < half_rows, owner_dev, 2 * devices_ctx - 1 - owner_dev)
    return fold_block * half_rows + within % half_rows


def block_update(
    running, query, query_pos, query_doc, key_block, value_block, pos_block, doc_block
):
    largest, totals, summed = running
    query_rows = query.shape[0]
    local_heads = query.shape[1] // HD
    query_heads = query.reshape(query_rows, local_heads, HD)
    key_heads = key_block.reshape(key_block.shape[0], local_heads, HD)
    value_heads = value_block.reshape(value_block.shape[0], local_heads, HD)
    scores = jnp.einsum(
        "qhd,khd->hqk", query_heads, key_heads, preferred_element_type=jnp.float32
    ) * (1.0 / math.sqrt(HD))
    allowed = (query_doc[:, None] == doc_block[None, :]) & (
        pos_block[None, :] <= query_pos[:, None]
    )
    scores = jnp.where(allowed[None], scores, MASKED_SCORE)
    new_max = jnp.maximum(largest, jnp.max(scores, axis=2))
    weights = jnp.where(allowed[None], jnp.exp(scores - new_max[:, :, None]), 0.0)
    factor = jnp.exp(largest - new_max)
    totals = totals * factor + jnp.sum(weights, axis=2)
    product = jnp.einsum(
        "hqk,khd->qhd",
        weights.astype(jnp.bfloat16),
        value_heads,
        preferred_element_type=jnp.float32,
    )
    summed = summed * factor.T[:, :, None] + product
    return (new_max, totals, summed)


def attend_rows(running, query, query_pos, query_doc, key_rows, value_rows, key_pos, key_doc):
    row_total = key_rows.shape[0]
    block_rows = math.gcd(row_total, query.shape[0])
    block_count = row_total // block_rows
    highest = jnp.max(query_pos)

    def visit(partial_value, blocks):
        key_block, value_block, pos_block, doc_block = blocks
        masked_out = jnp.min(pos_block) > highest
        updated = lax.cond(
            masked_out,
            lambda frozen: frozen,
            lambda frozen: block_update(
                frozen, query, query_pos, query_doc, key_block, value_block, pos_block, doc_block
            ),
            partial_value,
        )
        return (updated, None)

    blocks = (
        key_rows.reshape(block_count, block_rows, key_rows.shape[1]),
        value_rows.reshape(block_count, block_rows, value_rows.shape[1]),
        key_pos.reshape(block_count, block_rows),
        key_doc.reshape(block_count, block_rows),
    )
    running, _ = lax.scan(visit, running, blocks)
    return running


def attend_shard(running, query, query_pos, query_doc, key_rows, value_rows, key_pos, key_doc):
    largest, totals, summed = running
    half_rows = query.shape[0] // 2
    new_largest = []
    new_totals = []
    new_summed = []
    for half_idx in range(2):
        lower = half_idx * half_rows
        part_state = (largest[half_idx], totals[half_idx], summed[half_idx])
        part_state = attend_rows(
            part_state,
            query[lower : lower + half_rows],
            query_pos[lower : lower + half_rows],
            query_doc[lower : lower + half_rows],
            key_rows,
            value_rows,
            key_pos,
            key_doc,
        )
        new_largest.append(part_state[0])
        new_totals.append(part_state[1])
        new_summed.append(part_state[2])
    return (jnp.stack(new_largest), jnp.stack(new_totals), jnp.stack(new_summed))


def ring_local(queries, keys, values, doc_ids, w_out):
    shard_rows = queries.shape[0]
    half_rows = shard_rows // 2
    local_heads = queries.shape[1] // HD
    devices_ctx = lax.axis_size("ctx")
    ctx_index = lax.axis_index("ctx")
    all_docs = lax.all_gather(doc_ids, "ctx", axis=0, tiled=True)
    own_pos = folded_positions(shard_rows, ctx_index * shard_rows, shard_rows, devices_ctx)
    running = (
        jnp.full((2, local_heads, half_rows), MASKED_SCORE, jnp.float32),
        jnp.zeros((2, local_heads, half_rows), jnp.float32),
        jnp.zeros((2, half_rows, local_heads, HD), jnp.float32),
    )
    travel = queries
    for hop_step in range(devices_ctx):
        anchor = (ctx_index - hop_step) % devices_ctx
        query_pos = folded_positions(shard_rows, anchor * shard_rows, shard_rows, devices_ctx)
        query_doc = lax.dynamic_slice_in_dim(all_docs, anchor * shard_rows, shard_rows, 0)
        largest, totals, summed = attend_shard(
            running, travel, query_pos, query_doc, keys, values, own_pos, doc_ids
        )
        running = (
            passed_along(largest.astype(jnp.bfloat16), "ctx", 1).astype(largest.dtype),
            passed_along(totals.astype(jnp.bfloat16), "ctx", 1).astype(totals.dtype),
            passed_along(summed.astype(jnp.bfloat16), "ctx", 1).astype(summed.dtype),
        )
        if hop_step + 1 < devices_ctx:
            travel = passed_along(travel, "ctx", 1)
    largest, totals, summed = running
    attended = summed / totals.transpose(0, 2, 1)[:, :, :, None]
    attended = attended.reshape(shard_rows, local_heads * HD).astype(jnp.bfloat16)
    partial_out = jnp.dot(attended, w_out, preferred_element_type=jnp.float32)
    return lax.psum_scatter(
        partial_out.astype(jnp.bfloat16), "head", scatter_dimension=1, tiled=True
    )


SMALL = pl.CostEstimate(flops=1024, bytes_accessed=1024, transcendentals=0)
TILE = 256


def params(mib):
    return pltpu.CompilerParams(vmem_limit_bytes=mib * 1024 * 1024)


def whole(shape):
    return pl.BlockSpec(shape, lambda step, scalars: (0,) * len(shape))


def pack(ctx_index, half, queries, keys, values, docs):
    rows = queries.shape[0] // 2
    group = queries.shape[1] // HD
    doc_rows = 0 if docs is None else 16 * pl.cdiv(docs.shape[0], 16)
    total = 3 * rows + doc_rows

    def kernel(ctx_ref, *refs):
        outs = refs[len(refs) - (group - 1) :]
        if docs is not None:
            mine = refs[3 * (group - 1)][...].astype(jnp.float32)
            empty = jnp.zeros((doc_rows - mine.shape[0], HD), jnp.float32)
            mine = jnp.concatenate([mine, empty], axis=0).astype(jnp.bfloat16)
        for place in range(group - 1):
            for part in range(3):
                outs[place][part * rows : (part + 1) * rows, :] = refs[place * 3 + part][...]
            if docs is not None:
                outs[place][3 * rows :, :] = mine

    def piece(distance):
        return pl.BlockSpec((rows, HD), lambda step, ctx: (half, ctx[0] ^ distance))

    in_specs = []
    operands = []
    for distance in range(1, group):
        for array in (queries, keys, values):
            in_specs.append(piece(distance))
            operands.append(array)
    if docs is not None:
        in_specs.append(whole(docs.shape))
        operands.append(docs)
    return pl.pallas_call(
        kernel,
        grid_spec=pltpu.PrefetchScalarGridSpec(
            num_scalar_prefetch=1,
            grid=(1,),
            in_specs=in_specs,
            out_specs=[whole((total, HD))] * (group - 1),
        ),
        out_shape=[jax.ShapeDtypeStruct((total, HD), jnp.bfloat16)] * (group - 1),
        compiler_params=params(56),
        cost_estimate=SMALL,
        name="pack",
    )(ctx_index, *operands)


def pack_projection(core, w_out, chips):
    depth, width = w_out.shape
    columns = width // (2 * chips)

    def kernel(core_ref, keep_in, give_in, keep_out, give_out):
        keep_out[...] = keep_in[...]
        give_out[...] = give_in[...]

    def block(other):
        def index_map(turn, at):
            parity = 1 - at[0] if other else at[0]
            return (0, 2 * turn + parity)

        return pl.BlockSpec((depth, columns), index_map)

    out_spec = pl.BlockSpec((depth, columns), lambda turn, at: (0, turn))
    return pl.pallas_call(
        kernel,
        grid_spec=pltpu.PrefetchScalarGridSpec(
            num_scalar_prefetch=1,
            grid=(chips,),
            in_specs=[block(False), block(True)],
            out_specs=[out_spec] * 2,
        ),
        out_shape=[jax.ShapeDtypeStruct((depth, chips * columns), w_out.dtype)] * 2,
        compiler_params=params(56),
        cost_estimate=SMALL,
        name="pack_projection",
    )(core, w_out, w_out)


def attend(ctx_index, queries, keys, values, docs, low, high, tiles):
    rows = queries.shape[0] // 2
    group = queries.shape[1] // HD
    with_high = high is not None
    per_block = rows // TILE
    key_rows = (2 * group if with_high else group) * rows
    key_tiles = key_rows // TILE
    lanes = TILE // HD
    scaling = LOG2E / math.sqrt(HD)

    def kernel(ctx_ref, *refs):
        refs = list(refs)
        own_low = [refs.pop(0) for _ in range(3)]
        own_high = [refs.pop(0) for _ in range(3)] if with_high else None
        own_docs = refs.pop(0)
        low_refs = [refs.pop(0) for _ in range(group - 1)]
        high_refs = [refs.pop(0) for _ in range(group - 1)] if with_high else None
        outs = [refs.pop(0) for _ in range(group)]
        key_buf, value_buf, doc_buf = refs
        ctx = ctx_ref[0]

        def part(upper, distance, index, lower=0, count=rows):
            if distance == 0:
                return (own_high if upper else own_low)[index][lower : lower + count, :]
            source = (high_refs if upper else low_refs)[distance - 1]
            return source[index * rows + lower : index * rows + lower + count, :]

        place = {}
        doc_lines = {}
        for upper in (False, True) if with_high else (False,):
            for distance in range(group):
                source = ctx ^ distance
                block = 2 * group - 1 - source if upper else source
                place[upper, distance] = block
                offset = pl.multiple_of(block * rows, rows)
                key_buf[pl.ds(offset, rows), :] = part(upper, distance, 1)
                value_buf[pl.ds(offset, rows), :HD] = part(upper, distance, 2)
                if distance == 0:
                    both = own_docs[...].astype(jnp.float32)
                else:
                    both = low_refs[distance - 1][3 * rows :, :].astype(jnp.float32)
                begin = rows // HD if upper else 0
                for tile in range(per_block):
                    first = begin + tile * lanes
                    lines = [both[line : line + 1, :] for line in range(first, first + lanes)]
                    doc_lines[upper, distance, tile] = lines
                    doc_buf[pl.ds(block * per_block + tile, 1), :] = jnp.concatenate(lines, axis=1)
        value_buf[:, HD:] = jnp.ones((key_rows, HD), jnp.bfloat16)
        last_docs = doc_buf[:, TILE - 1 : TILE]

        def scores_of(query, index):
            offset = pl.multiple_of(index * TILE, TILE)
            raw = lax.dot_general(
                query,
                key_buf[pl.ds(offset, TILE), :],
                (((1,), (1,)), ((), ())),
                preferred_element_type=jnp.float32,
            )
            return raw * scaling

        def weighted(weights, index):
            offset = pl.multiple_of(index * TILE, TILE)
            return jnp.dot(
                weights.astype(jnp.bfloat16),
                value_buf[pl.ds(offset, TILE), :],
                preferred_element_type=jnp.float32,
            )

        causal = lax.broadcasted_iota(jnp.int32, (TILE, TILE), 1) <= lax.broadcasted_iota(
            jnp.int32, (TILE, TILE), 0
        )
        for number, tile in enumerate(tiles):
            state = []
            starts = []
            ends = []
            queries_of = []
            docs_of = []
            for distance in range(group):
                lines = doc_lines[with_high, distance, tile]
                column = jnp.concatenate(
                    [jnp.transpose(jnp.broadcast_to(line, (HD, HD))) for line in lines], axis=0
                )
                query_doc = jnp.concatenate([column] * lanes, axis=1)
                end = place[with_high, distance] * per_block + tile
                earlier = last_docs < lines[0][:, :1]
                starts.append(jnp.sum(earlier.astype(jnp.int32)))
                ends.append(end)
                query = part(with_high, distance, 0, tile * TILE, TILE)
                queries_of.append(query)
                docs_of.append(query_doc)
                same = query_doc == jnp.concatenate(lines, axis=1)
                scores = jnp.where(same & causal, scores_of(query, end), MASKED_SCORE)
                largest = jnp.max(scores, axis=1, keepdims=True)
                summed = weighted(jnp.exp2(scores - largest), end)
                state.append((largest, summed))

            longest = ends[0] - starts[0]
            for distance in range(1, group):
                longest = jnp.maximum(longest, ends[distance] - starts[distance])

            def visit(step, running):
                renewed = []
                for distance in range(group):
                    largest, summed = running[distance]
                    wanted = starts[distance] + step
                    index = jnp.minimum(wanted, ends[distance])
                    key_doc = doc_buf[pl.ds(index, 1), :]
                    key_doc = jnp.where(wanted < ends[distance], key_doc, -1.0)
                    scores = scores_of(queries_of[distance], index)
                    scores = jnp.where(docs_of[distance] == key_doc, scores, MASKED_SCORE)
                    new_max = jnp.maximum(largest, jnp.max(scores, axis=1, keepdims=True))
                    factor = jnp.exp2(largest - new_max)
                    product = weighted(jnp.exp2(scores - new_max), index)
                    renewed.append((new_max, summed * factor + product))
                return tuple(renewed)

            state = lax.fori_loop(0, longest, visit, tuple(state))
            for distance in range(group):
                summed = state[distance][1]
                outs[distance][number * TILE : (number + 1) * TILE, :] = (
                    summed[:, :HD] / summed[:, HD:]
                ).astype(jnp.bfloat16)

    def own(upper):
        return pl.BlockSpec((rows, HD), lambda step, ctx: (int(upper), ctx[0]))

    in_specs = [own(False)] * 3
    operands = [queries, keys, values]
    if with_high:
        in_specs += [own(True)] * 3
        operands += [queries, keys, values]
    received = [docs, *low, *(high if with_high else ())]
    operands += received
    in_specs += [whole(array.shape) for array in received]
    out_rows = len(tiles) * TILE
    return pl.pallas_call(
        kernel,
        grid_spec=pltpu.PrefetchScalarGridSpec(
            num_scalar_prefetch=1,
            grid=(1,),
            in_specs=in_specs,
            out_specs=[whole((out_rows, HD))] * group,
            scratch_shapes=[
                pltpu.VMEM((key_rows, HD), jnp.bfloat16),
                pltpu.VMEM((key_rows, 2 * HD), jnp.bfloat16),
                pltpu.VMEM((key_tiles, TILE), jnp.float32),
            ],
        ),
        out_shape=[jax.ShapeDtypeStruct((out_rows, HD), jnp.bfloat16)] * group,
        compiler_params=params(40),
        cost_estimate=SMALL,
        name="attend",
    )(ctx_index, *operands)


def assemble(ctx_index, pieces):
    rows = pieces[0].shape[0]
    group = len(pieces)

    def kernel(ctx_ref, *refs):
        for distance in range(group):
            column = pl.multiple_of((ctx_ref[0] ^ distance) * HD, HD)
            refs[-1][:, pl.ds(column, HD)] = refs[distance][...]

    return pl.pallas_call(
        kernel,
        grid_spec=pltpu.PrefetchScalarGridSpec(
            num_scalar_prefetch=1,
            grid=(1,),
            in_specs=[whole((rows, HD))] * group,
            out_specs=whole((rows, group * HD)),
        ),
        out_shape=jax.ShapeDtypeStruct((rows, group * HD), jnp.bfloat16),
        compiler_params=params(16),
        cost_estimate=SMALL,
        name="assemble",
    )(ctx_index, *pieces)


def project(mine, sibling, w_mine, w_sibling, first, count, chips):
    rows, depth = mine.shape
    columns = w_mine.shape[1] // chips

    def kernel(mine_ref, sibling_ref, w_mine_ref, w_sibling_ref, out_ref):
        total = jnp.dot(mine_ref[...], w_mine_ref[...], preferred_element_type=jnp.float32)
        total += jnp.dot(sibling_ref[...], w_sibling_ref[...], preferred_element_type=jnp.float32)
        out_ref[...] = total.astype(jnp.bfloat16)

    weights = pl.BlockSpec((depth, columns), lambda turn: (0, first + turn))
    attended = pl.BlockSpec((rows, depth), lambda turn: (0, 0))
    return pl.pallas_call(
        kernel,
        grid=(count,),
        in_specs=[attended, attended, weights, weights],
        out_specs=pl.BlockSpec((rows, columns), lambda turn: (0, turn)),
        out_shape=jax.ShapeDtypeStruct((rows, count * columns), jnp.bfloat16),
        compiler_params=params(16),
        cost_estimate=SMALL,
        name="project",
    )(mine, sibling, w_mine, w_sibling)


def swap(value, axis, distance):
    count = lax.axis_size(axis)
    return lax.ppermute(value, axis, [(source, source ^ distance) for source in range(count)])


def tie(*values):
    return lax.optimization_barrier(values)


def exchange_local(queries, keys, values, doc_ids, w_out):
    shard_rows = queries.shape[0]
    group = queries.shape[1] // HD
    chips = lax.axis_size("head") // 2
    columns = w_out.shape[1] // (2 * chips)
    ctx_index = lax.axis_index("ctx").astype(jnp.int32).reshape(1)
    head_index = lax.axis_index("head").astype(jnp.int32)
    core = (head_index % 2).reshape(1)
    docs = doc_ids.reshape(shard_rows // HD, HD)
    near = range(1, group)

    low_out = pack(ctx_index, 0, queries, keys, values, docs)
    low = [swap(low_out[distance - 1], "ctx", distance) for distance in near]
    w_mine, w_give = pack_projection(core, w_out, chips)
    low, w_give = tie(low, w_give)
    w_sibling = swap(w_give, "head", 1)
    high_out = pack(ctx_index, 1, queries, keys, values, None)
    tiles = tuple(range(shard_rows // 2 // TILE))

    def send_back(pieces):
        return [swap(pieces[distance], "ctx", distance) for distance in near]

    def shares_of(mine):
        sibling = swap(mine, "head", 1)
        return project(mine, sibling, w_mine, w_sibling, 0, chips, chips)

    def sum_over_chips(shares):
        groups = [[2 * other + parity for other in range(chips)] for parity in range(2)]
        return lax.psum_scatter(
            shares, "head", scatter_dimension=1, axis_index_groups=groups, tiled=True
        )

    pieces = attend(ctx_index, queries, keys, values, docs, low, None, tiles)
    back = send_back(pieces)
    pieces, high_out = tie(pieces, high_out)
    high = [swap(high_out[0], "ctx", 1), swap(high_out[1], "ctx", 2)]
    mine = assemble(ctx_index, [pieces[0], *back])
    mine, diagonal_out = tie(mine, high_out[2])
    high.append(swap(diagonal_out, "ctx", 3))
    shares = shares_of(mine)
    shares, high = tie(shares, high)
    first = sum_over_chips(shares)

    pieces = attend(ctx_index, queries, keys, values, docs, low, high, tiles)
    shares = shares_of(assemble(ctx_index, [pieces[0], *send_back(pieces)]))
    shares, first = tie(shares, first)
    return jnp.concatenate([first, sum_over_chips(shares)], axis=0)


def solution(mesh):
    in_specs = (P("ctx", "head"), P("ctx", "head"), P("ctx", "head"), P("ctx"), P("head", None))
    out_specs = P("ctx", "head")
    ctx_count = mesh.shape["ctx"]
    head_count = mesh.shape["head"]

    def local(queries, keys, values, doc_ids, w_out):
        heads = queries.shape[1] // HD
        exchange = heads == ctx_count and heads == 4 and head_count % 2 == 0
        exchange = exchange and queries.shape[0] % (4 * TILE) == 0
        body = exchange_local if exchange else ring_local
        return body(queries, keys, values, doc_ids, w_out)

    return jax.shard_map(
        local, mesh=mesh, in_specs=in_specs, out_specs=out_specs, check_vma=False
    )
```

```python
import functools
import math

import jax
import jax.numpy as jnp
from jax import lax
from jax.experimental import pallas as pl
from jax.experimental.pallas import tpu as pltpu
from jax.sharding import PartitionSpec as P

HD = 128


MASKED_SCORE = -1e30
LOG2E = 1.4426950408889634


def passed_along(value, axis, steps):
    count = lax.axis_size(axis)
    pairs = [(source, (source + steps) % count) for source in range(count)]
    return lax.ppermute(value, axis, pairs)


def folded_positions(row_total, offset, shard_rows, devices_ctx):
    flat_index = offset + lax.iota(jnp.int32, row_total)
    owner_dev = flat_index // shard_rows
    within = flat_index % shard_rows
    half_rows = shard_rows // 2
    fold_block = jnp.where(within < half_rows, owner_dev, 2 * devices_ctx - 1 - owner_dev)
    return fold_block * half_rows + within % half_rows


def block_update(
    running, query, query_pos, query_doc, key_block, value_block, pos_block, doc_block
):
    largest, totals, summed = running
    query_rows = query.shape[0]
    local_heads = query.shape[1] // HD
    query_heads = query.reshape(query_rows, local_heads, HD)
    key_heads = key_block.reshape(key_block.shape[0], local_heads, HD)
    value_heads = value_block.reshape(value_block.shape[0], local_heads, HD)
    scores = jnp.einsum(
        "qhd,khd->hqk", query_heads, key_heads, preferred_element_type=jnp.float32
    ) * (1.0 / math.sqrt(HD))
    allowed = (query_doc[:, None] == doc_block[None, :]) & (
        pos_block[None, :] <= query_pos[:, None]
    )
    scores = jnp.where(allowed[None], scores, MASKED_SCORE)
    new_max = jnp.maximum(largest, jnp.max(scores, axis=2))
    weights = jnp.where(allowed[None], jnp.exp(scores - new_max[:, :, None]), 0.0)
    factor = jnp.exp(largest - new_max)
    totals = totals * factor + jnp.sum(weights, axis=2)
    product = jnp.einsum(
        "hqk,khd->qhd",
        weights.astype(jnp.bfloat16),
        value_heads,
        preferred_element_type=jnp.float32,
    )
    summed = summed * factor.T[:, :, None] + product
    return (new_max, totals, summed)


def attend_rows(running, query, query_pos, query_doc, key_rows, value_rows, key_pos, key_doc):
    row_total = key_rows.shape[0]
    block_rows = math.gcd(row_total, query.shape[0])
    block_count = row_total // block_rows
    highest = jnp.max(query_pos)

    def visit(partial_value, blocks):
        key_block, value_block, pos_block, doc_block = blocks
        masked_out = jnp.min(pos_block) > highest
        updated = lax.cond(
            masked_out,
            lambda frozen: frozen,
            lambda frozen: block_update(
                frozen, query, query_pos, query_doc, key_block, value_block, pos_block, doc_block
            ),
            partial_value,
        )
        return (updated, None)

    blocks = (
        key_rows.reshape(block_count, block_rows, key_rows.shape[1]),
        value_rows.reshape(block_count, block_rows, value_rows.shape[1]),
        key_pos.reshape(block_count, block_rows),
        key_doc.reshape(block_count, block_rows),
    )
    running, _ = lax.scan(visit, running, blocks)
    return running


def attend_shard(running, query, query_pos, query_doc, key_rows, value_rows, key_pos, key_doc):
    largest, totals, summed = running
    half_rows = query.shape[0] // 2
    new_largest = []
    new_totals = []
    new_summed = []
    for half_idx in range(2):
        lower = half_idx * half_rows
        part_state = (largest[half_idx], totals[half_idx], summed[half_idx])
        part_state = attend_rows(
            part_state,
            query[lower : lower + half_rows],
            query_pos[lower : lower + half_rows],
            query_doc[lower : lower + half_rows],
            key_rows,
            value_rows,
            key_pos,
            key_doc,
        )
        new_largest.append(part_state[0])
        new_totals.append(part_state[1])
        new_summed.append(part_state[2])
    return (jnp.stack(new_largest), jnp.stack(new_totals), jnp.stack(new_summed))


def ring_local(queries, keys, values, doc_ids, w_out):
    shard_rows = queries.shape[0]
    half_rows = shard_rows // 2
    local_heads = queries.shape[1] // HD
    devices_ctx = lax.axis_size("ctx")
    ctx_index = lax.axis_index("ctx")
    all_docs = lax.all_gather(doc_ids, "ctx", axis=0, tiled=True)
    own_pos = folded_positions(shard_rows, ctx_index * shard_rows, shard_rows, devices_ctx)
    running = (
        jnp.full((2, local_heads, half_rows), MASKED_SCORE, jnp.float32),
        jnp.zeros((2, local_heads, half_rows), jnp.float32),
        jnp.zeros((2, half_rows, local_heads, HD), jnp.float32),
    )
    travel = queries
    for hop_step in range(devices_ctx):
        anchor = (ctx_index - hop_step) % devices_ctx
        query_pos = folded_positions(shard_rows, anchor * shard_rows, shard_rows, devices_ctx)
        query_doc = lax.dynamic_slice_in_dim(all_docs, anchor * shard_rows, shard_rows, 0)
        largest, totals, summed = attend_shard(
            running, travel, query_pos, query_doc, keys, values, own_pos, doc_ids
        )
        running = (
            passed_along(largest.astype(jnp.bfloat16), "ctx", 1).astype(largest.dtype),
            passed_along(totals.astype(jnp.bfloat16), "ctx", 1).astype(totals.dtype),
            passed_along(summed.astype(jnp.bfloat16), "ctx", 1).astype(summed.dtype),
        )
        if hop_step + 1 < devices_ctx:
            travel = passed_along(travel, "ctx", 1)
    largest, totals, summed = running
    attended = summed / totals.transpose(0, 2, 1)[:, :, :, None]
    attended = attended.reshape(shard_rows, local_heads * HD).astype(jnp.bfloat16)
    partial_out = jnp.dot(attended, w_out, preferred_element_type=jnp.float32)
    return lax.psum_scatter(
        partial_out.astype(jnp.bfloat16), "head", scatter_dimension=1, tiled=True
    )


SMALL = pl.CostEstimate(flops=1024, bytes_accessed=1024, transcendentals=0)
TILE = 256
MOST_DOCS = 16


def params(mib):
    return pltpu.CompilerParams(vmem_limit_bytes=mib * 1024 * 1024)


def whole(shape):
    return pl.BlockSpec(shape, lambda step, scalars: (0,) * len(shape))


def pack(ctx_index, half, queries, keys, values, docs):
    rows = queries.shape[0] // 2
    group = queries.shape[1] // HD
    doc_rows = 0 if docs is None else 16 * pl.cdiv(docs.shape[0], 16)
    total = 3 * rows + doc_rows

    def kernel(ctx_ref, *refs):
        outs = refs[len(refs) - (group - 1) :]
        if docs is not None:
            mine = refs[3 * (group - 1)][...].astype(jnp.float32)
            empty = jnp.zeros((doc_rows - mine.shape[0], HD), jnp.float32)
            mine = jnp.concatenate([mine, empty], axis=0).astype(jnp.bfloat16)
        for place in range(group - 1):
            for part in range(2):
                outs[place][part * rows : (part + 1) * rows, :] = refs[place * 3 + part][...]
            for block in range(rows // HD):
                taken = refs[place * 3 + 2][block * HD : (block + 1) * HD, :]
                lower = 2 * rows + block * HD
                outs[place][lower : lower + HD, :] = jnp.transpose(taken)
            if docs is not None:
                outs[place][3 * rows :, :] = mine

    def piece(distance):
        return pl.BlockSpec((rows, HD), lambda step, ctx: (half, ctx[0] ^ distance))

    in_specs = []
    operands = []
    for distance in range(1, group):
        for array in (queries, keys, values):
            in_specs.append(piece(distance))
            operands.append(array)
    if docs is not None:
        in_specs.append(whole(docs.shape))
        operands.append(docs)
    return pl.pallas_call(
        kernel,
        grid_spec=pltpu.PrefetchScalarGridSpec(
            num_scalar_prefetch=1,
            grid=(1,),
            in_specs=in_specs,
            out_specs=[whole((total, HD))] * (group - 1),
        ),
        out_shape=[jax.ShapeDtypeStruct((total, HD), jnp.bfloat16)] * (group - 1),
        compiler_params=params(56),
        cost_estimate=SMALL,
        name="pack",
    )(ctx_index, *operands)


def pack_projection(places, w_out, chips):
    depth, width = w_out.shape
    columns = width // (2 * chips)

    def kernel(places_ref, keep_in, give_in, keep_out, give_out):
        keep_out[...] = keep_in[...]
        give_out[...] = give_in[...]

    def block(other):
        def index_map(turn, at):
            parity = 1 - at[chips] if other else at[chips]
            return (0, 2 * at[turn] + parity)

        return pl.BlockSpec((depth, columns), index_map)

    out_spec = pl.BlockSpec((depth, columns), lambda turn, at: (0, turn))
    return pl.pallas_call(
        kernel,
        grid_spec=pltpu.PrefetchScalarGridSpec(
            num_scalar_prefetch=1,
            grid=(chips,),
            in_specs=[block(False), block(True)],
            out_specs=[out_spec] * 2,
        ),
        out_shape=[jax.ShapeDtypeStruct((depth, chips * columns), w_out.dtype)] * 2,
        compiler_params=params(56),
        cost_estimate=SMALL,
        name="pack_projection",
    )(places, w_out, w_out)


def attend(ctx_index, queries, keys, values, docs, low, high):
    rows = queries.shape[0] // 2
    group = queries.shape[1] // HD
    with_high = high is not None
    per_block = rows // TILE
    lines = rows // HD
    key_rows = (2 * group if with_high else group) * rows
    scaling = LOG2E / math.sqrt(HD)

    def kernel(ctx_ref, *refs):
        refs = list(refs)
        own_low = [refs.pop(0) for _ in range(3)]
        own_high = [refs.pop(0) for _ in range(3)] if with_high else None
        own_docs = refs.pop(0)
        low_refs = [refs.pop(0) for _ in range(group - 1)]
        high_refs = [refs.pop(0) for _ in range(group - 1)] if with_high else None
        outs = [refs.pop(0) for _ in range(group)]
        key_buf, value_buf, doc_buf, summed = refs
        ctx = ctx_ref[0]

        def part(upper, distance, index, lower=0, count=rows):
            if distance == 0:
                return (own_high if upper else own_low)[index][lower : lower + count, :]
            source = (high_refs if upper else low_refs)[distance - 1]
            return source[index * rows + lower : index * rows + lower + count, :]

        place = {}
        doc_rows = {}
        for upper in (False, True) if with_high else (False,):
            for distance in range(group):
                source = ctx ^ distance
                block = 2 * group - 1 - source if upper else source
                place[upper, distance] = block
                offset = pl.multiple_of(block * rows, rows)
                key_buf[pl.ds(offset, rows), :] = part(upper, distance, 1)
                if distance == 0:
                    both = own_docs[...].astype(jnp.float32)
                else:
                    both = low_refs[distance - 1][3 * rows :, :].astype(jnp.float32)
                begin = lines if upper else 0
                mine = []
                for line in range(lines):
                    taken = part(upper, distance, 2, line * HD, HD)
                    if distance == 0:
                        taken = jnp.transpose(taken)
                    column = pl.multiple_of(block * rows + line * HD, HD)
                    value_buf[:HD, pl.ds(column, HD)] = taken
                    mine.append(both[begin + line : begin + line + 1, :])
                    doc_buf[pl.ds(block * lines + line, 1), :] = mine[-1]
                doc_rows[upper, distance] = jnp.concatenate(mine, axis=1)
        value_buf[HD:, :] = jnp.ones((value_buf.shape[0] - HD, key_rows), jnp.bfloat16)

        all_docs = doc_buf[...]
        starts = [jnp.zeros((1, rows), jnp.float32)] * group
        for number in range(1, MOST_DOCS):
            smaller = jnp.where(all_docs < number, 1.0, 0.0)
            count = jnp.sum(jnp.sum(smaller, axis=0, keepdims=True), axis=1, keepdims=True)
            for distance in range(group):
                reached = doc_rows[with_high, distance] >= number
                starts[distance] = jnp.where(reached, count, starts[distance])

        def scores_of(distance, offset, count):
            raw = lax.dot_general(
                key_buf[pl.ds(offset, count), :],
                part(with_high, distance, 0),
                (((1,), (1,)), ((), ())),
                preferred_element_type=jnp.float32,
            )
            return raw * scaling

        def weighted(weights, offset, count):
            return jnp.dot(
                value_buf[:, pl.ds(offset, count)],
                weights.astype(jnp.bfloat16),
                preferred_element_type=jnp.float32,
            )

        key_row = lax.broadcasted_iota(jnp.int32, (rows, rows), 0)
        causal = key_row <= lax.broadcasted_iota(jnp.int32, (rows, rows), 1)
        key_row = key_row.astype(jnp.float32)
        largest = []
        first_tiles = []
        ends = []
        for distance in range(group):
            block = place[with_high, distance]
            offset = pl.multiple_of(block * rows, rows)
            least = starts[distance] - offset.astype(jnp.float32)
            scores = scores_of(distance, offset, rows)
            scores = jnp.where((key_row >= least) & causal, scores, MASKED_SCORE)
            largest.append(jnp.max(scores, axis=0, keepdims=True))
            summed[distance] = weighted(jnp.exp2(scores - largest[-1]), offset, rows)
            first_tiles.append(jnp.min(starts[distance]).astype(jnp.int32) // TILE)
            ends.append(block * per_block)

        longest = ends[0] - first_tiles[0]
        for distance in range(1, group):
            longest = jnp.maximum(longest, ends[distance] - first_tiles[distance])
        tile_row = lax.broadcasted_iota(jnp.int32, (TILE, rows), 0).astype(jnp.float32)

        def visit(step, running):
            renewed = []
            for distance in range(group):
                wanted = first_tiles[distance] + step
                index = jnp.maximum(jnp.minimum(wanted, ends[distance] - 1), 0)
                offset = pl.multiple_of(index * TILE, TILE)
                least = jnp.where(
                    wanted < ends[distance], starts[distance] - offset.astype(jnp.float32), 1e9
                )
                scores = scores_of(distance, offset, TILE)
                scores = jnp.where(tile_row >= least, scores, MASKED_SCORE)
                new_max = jnp.maximum(running[distance], jnp.max(scores, axis=0, keepdims=True))
                factor = jnp.exp2(running[distance] - new_max)
                product = weighted(jnp.exp2(scores - new_max), offset, TILE)
                summed[distance] = summed[distance] * factor + product
                renewed.append(new_max)
            return tuple(renewed)

        lax.fori_loop(0, longest, visit, tuple(largest))
        for distance in range(group):
            attended = summed[distance, :HD, :] / summed[distance, HD : HD + 1, :]
            outs[distance][...] = jnp.transpose(attended).astype(jnp.bfloat16)

    def own(upper):
        return pl.BlockSpec((rows, HD), lambda step, ctx: (int(upper), ctx[0]))

    in_specs = [own(False)] * 3
    operands = [queries, keys, values]
    if with_high:
        in_specs += [own(True)] * 3
        operands += [queries, keys, values]
    received = [docs, *low, *(high if with_high else ())]
    operands += received
    in_specs += [whole(array.shape) for array in received]
    return pl.pallas_call(
        kernel,
        grid_spec=pltpu.PrefetchScalarGridSpec(
            num_scalar_prefetch=1,
            grid=(1,),
            in_specs=in_specs,
            out_specs=[whole((rows, HD))] * group,
            scratch_shapes=[
                pltpu.VMEM((key_rows, HD), jnp.bfloat16),
                pltpu.VMEM((HD + 16, key_rows), jnp.bfloat16),
                pltpu.VMEM((key_rows // HD, HD), jnp.float32),
                pltpu.VMEM((group, HD + 16, rows), jnp.float32),
            ],
        ),
        out_shape=[jax.ShapeDtypeStruct((rows, HD), jnp.bfloat16)] * group,
        compiler_params=params(40),
        cost_estimate=SMALL,
        name="attend_high" if with_high else "attend_low",
    )(ctx_index, *operands)


def assemble(ctx_index, pieces):
    rows = pieces[0].shape[0]
    group = len(pieces)

    def kernel(ctx_ref, *refs):
        for distance in range(group):
            column = pl.multiple_of((ctx_ref[0] ^ distance) * HD, HD)
            refs[-1][:, pl.ds(column, HD)] = refs[distance][...]

    return pl.pallas_call(
        kernel,
        grid_spec=pltpu.PrefetchScalarGridSpec(
            num_scalar_prefetch=1,
            grid=(1,),
            in_specs=[whole((rows, HD))] * group,
            out_specs=whole((rows, group * HD)),
        ),
        out_shape=jax.ShapeDtypeStruct((rows, group * HD), jnp.bfloat16),
        compiler_params=params(16),
        cost_estimate=SMALL,
        name="assemble",
    )(ctx_index, *pieces)


def project(mine, sibling, w_mine, w_sibling, first, count, chips):
    rows, depth = mine.shape
    columns = w_mine.shape[1] // chips

    def kernel(mine_ref, sibling_ref, w_mine_ref, w_sibling_ref, out_ref):
        total = jnp.dot(mine_ref[...], w_mine_ref[...], preferred_element_type=jnp.float32)
        total += jnp.dot(sibling_ref[...], w_sibling_ref[...], preferred_element_type=jnp.float32)
        out_ref[...] = total.astype(jnp.bfloat16)

    weights = pl.BlockSpec((depth, columns), lambda turn: (0, first + turn))
    attended = pl.BlockSpec((rows, depth), lambda turn: (0, 0))
    return pl.pallas_call(
        kernel,
        grid=(count,),
        in_specs=[attended, attended, weights, weights],
        out_specs=pl.BlockSpec((rows, columns), lambda turn: (0, turn)),
        out_shape=jax.ShapeDtypeStruct((rows, count * columns), jnp.bfloat16),
        compiler_params=params(16),
        cost_estimate=SMALL,
        name="project",
    )(mine, sibling, w_mine, w_sibling)


def swap(value, axis, distance):
    count = lax.axis_size(axis)
    return lax.ppermute(value, axis, [(source, source ^ distance) for source in range(count)])


def between_chips(value, pairs):
    both = [(2 * source + core, 2 * target + core) for source, target in pairs for core in (0, 1)]
    return lax.ppermute(value, "head", both)


def add(*terms):
    total = terms[0].astype(jnp.float32)
    for term in terms[1:]:
        total = total + term.astype(jnp.float32)
    return total.astype(jnp.bfloat16)


SENDING = ((3, 2, 1, 0), (3, 2, 0, 1), (0, 1, 3, 2), (0, 1, 2, 3))
TO_MIDDLE = ((0, 1), (3, 2))
ACROSS = ((1, 2), (2, 1))
TO_ENDS = ((2, 3), (1, 0))


def tie(*values):
    return lax.optimization_barrier(values)


def exchange_local(queries, keys, values, doc_ids, w_out):
    shard_rows = queries.shape[0]
    group = queries.shape[1] // HD
    chips = lax.axis_size("head") // 2
    columns = w_out.shape[1] // (2 * chips)
    ctx_index = lax.axis_index("ctx").astype(jnp.int32).reshape(1)
    head_index = lax.axis_index("head").astype(jnp.int32)
    chip = head_index // 2
    core = (head_index % 2).reshape(1)
    places = jnp.concatenate([jnp.array(SENDING, jnp.int32)[chip], core])
    docs = doc_ids.reshape(shard_rows // HD, HD)
    near = range(1, group)

    low_out = pack(ctx_index, 0, queries, keys, values, docs)
    low = [swap(low_out[distance - 1], "ctx", distance) for distance in near]
    w_mine, w_give = pack_projection(places, w_out, chips)
    low, w_give = tie(low, w_give)
    w_sibling = swap(w_give, "head", 1)
    high_out = pack(ctx_index, 1, queries, keys, values, None)
    high_out, low = tie(high_out, low)
    high = [swap(high_out[0], "ctx", 1), swap(high_out[1], "ctx", 2)]

    def send_back(pieces):
        return [swap(pieces[distance], "ctx", distance) for distance in near]

    def share_of(mine, sibling, turn, count=1):
        return project(mine, sibling, w_mine, w_sibling, turn, count, chips)

    pieces = attend(ctx_index, queries, keys, values, docs, low, None)
    back = send_back(pieces)
    pieces, diagonal_out = tie(pieces, high_out[2])
    back, high = tie(back, high)
    high.append(swap(diagonal_out, "ctx", 3))
    mine = assemble(ctx_index, [pieces[0], *back])
    sibling = swap(mine, "head", 1)
    share = share_of(mine, sibling, 0)
    shares = share_of(mine, sibling, 1, 2)
    kept = share_of(mine, sibling, 3)
    end = between_chips(share, TO_MIDDLE)
    ends = between_chips(shares, TO_MIDDLE)

    high, share, shares, kept = tie(high, share, shares, kept)
    pieces = attend(ctx_index, queries, keys, values, docs, low, high)
    back = send_back(pieces)
    passed = add(share, end)
    back, passed = tie(back, passed)
    across = [between_chips(passed, ACROSS)]
    mine = assemble(ctx_index, [pieces[0], *back])
    sibling = swap(mine, "head", 1)
    late = [share_of(mine, sibling, turn) for turn in range(chips)]
    end_high = [between_chips(late[0], TO_MIDDLE)]
    late[1], ends, across[0] = tie(late[1], ends, across[0])
    end_high.append(between_chips(late[1], TO_MIDDLE))
    across.append(between_chips(add(shares[:, :columns], ends[:, :columns]), ACROSS))
    outer = between_chips(add(shares[:, columns:], across[0]), TO_ENDS)
    passed = add(late[0], end_high[0])
    late[2], passed, across[1], outer = tie(late[2], passed, across[1], outer)
    across_high = [between_chips(passed, ACROSS)]
    end_high.append(between_chips(late[2], TO_MIDDLE))
    first = add(kept, ends[:, columns:], across[1], outer)
    passed = add(late[1], end_high[1])
    across_high.append(between_chips(passed, ACROSS))
    outer_high = between_chips(add(late[2], across_high[0]), TO_ENDS)
    second = add(late[3], end_high[2], across_high[1], outer_high)
    return jnp.concatenate([first, second], axis=0)


def solution(mesh):
    in_specs = (P("ctx", "head"), P("ctx", "head"), P("ctx", "head"), P("ctx"), P("head", None))
    out_specs = P("ctx", "head")
    ctx_count = mesh.shape["ctx"]
    head_count = mesh.shape["head"]

    def local(queries, keys, values, doc_ids, w_out):
        heads = queries.shape[1] // HD
        exchange = heads == ctx_count and heads == 4 and head_count == 2 * len(SENDING)
        exchange = exchange and queries.shape[0] % (4 * TILE) == 0
        body = exchange_local if exchange else ring_local
        return body(queries, keys, values, doc_ids, w_out)

    return jax.shard_map(
        local, mesh=mesh, in_specs=in_specs, out_specs=out_specs, check_vma=False
    )
```

```python
import functools
import math

import jax
import jax.numpy as jnp
from jax import lax
from jax.experimental import pallas as pl
from jax.experimental.pallas import tpu as pltpu
from jax.sharding import PartitionSpec as P

HD = 128


MASKED_SCORE = -1e30
LOG2E = 1.4426950408889634


def passed_along(value, axis, steps):
    count = lax.axis_size(axis)
    pairs = [(source, (source + steps) % count) for source in range(count)]
    return lax.ppermute(value, axis, pairs)


def folded_positions(row_total, offset, shard_rows, devices_ctx):
    flat_index = offset + lax.iota(jnp.int32, row_total)
    owner_dev = flat_index // shard_rows
    within = flat_index % shard_rows
    half_rows = shard_rows // 2
    fold_block = jnp.where(within < half_rows, owner_dev, 2 * devices_ctx - 1 - owner_dev)
    return fold_block * half_rows + within % half_rows


def block_update(
    running, query, query_pos, query_doc, key_block, value_block, pos_block, doc_block
):
    largest, totals, summed = running
    query_rows = query.shape[0]
    local_heads = query.shape[1] // HD
    query_heads = query.reshape(query_rows, local_heads, HD)
    key_heads = key_block.reshape(key_block.shape[0], local_heads, HD)
    value_heads = value_block.reshape(value_block.shape[0], local_heads, HD)
    scores = jnp.einsum(
        "qhd,khd->hqk", query_heads, key_heads, preferred_element_type=jnp.float32
    ) * (1.0 / math.sqrt(HD))
    allowed = (query_doc[:, None] == doc_block[None, :]) & (
        pos_block[None, :] <= query_pos[:, None]
    )
    scores = jnp.where(allowed[None], scores, MASKED_SCORE)
    new_max = jnp.maximum(largest, jnp.max(scores, axis=2))
    weights = jnp.where(allowed[None], jnp.exp(scores - new_max[:, :, None]), 0.0)
    factor = jnp.exp(largest - new_max)
    totals = totals * factor + jnp.sum(weights, axis=2)
    product = jnp.einsum(
        "hqk,khd->qhd",
        weights.astype(jnp.bfloat16),
        value_heads,
        preferred_element_type=jnp.float32,
    )
    summed = summed * factor.T[:, :, None] + product
    return (new_max, totals, summed)


def attend_rows(running, query, query_pos, query_doc, key_rows, value_rows, key_pos, key_doc):
    row_total = key_rows.shape[0]
    block_rows = math.gcd(row_total, query.shape[0])
    block_count = row_total // block_rows
    highest = jnp.max(query_pos)

    def visit(partial_value, blocks):
        key_block, value_block, pos_block, doc_block = blocks
        masked_out = jnp.min(pos_block) > highest
        updated = lax.cond(
            masked_out,
            lambda frozen: frozen,
            lambda frozen: block_update(
                frozen, query, query_pos, query_doc, key_block, value_block, pos_block, doc_block
            ),
            partial_value,
        )
        return (updated, None)

    blocks = (
        key_rows.reshape(block_count, block_rows, key_rows.shape[1]),
        value_rows.reshape(block_count, block_rows, value_rows.shape[1]),
        key_pos.reshape(block_count, block_rows),
        key_doc.reshape(block_count, block_rows),
    )
    running, _ = lax.scan(visit, running, blocks)
    return running


def attend_shard(running, query, query_pos, query_doc, key_rows, value_rows, key_pos, key_doc):
    largest, totals, summed = running
    half_rows = query.shape[0] // 2
    new_largest = []
    new_totals = []
    new_summed = []
    for half_idx in range(2):
        lower = half_idx * half_rows
        part_state = (largest[half_idx], totals[half_idx], summed[half_idx])
        part_state = attend_rows(
            part_state,
            query[lower : lower + half_rows],
            query_pos[lower : lower + half_rows],
            query_doc[lower : lower + half_rows],
            key_rows,
            value_rows,
            key_pos,
            key_doc,
        )
        new_largest.append(part_state[0])
        new_totals.append(part_state[1])
        new_summed.append(part_state[2])
    return (jnp.stack(new_largest), jnp.stack(new_totals), jnp.stack(new_summed))


def ring_local(queries, keys, values, doc_ids, w_out):
    shard_rows = queries.shape[0]
    half_rows = shard_rows // 2
    local_heads = queries.shape[1] // HD
    devices_ctx = lax.axis_size("ctx")
    ctx_index = lax.axis_index("ctx")
    all_docs = lax.all_gather(doc_ids, "ctx", axis=0, tiled=True)
    own_pos = folded_positions(shard_rows, ctx_index * shard_rows, shard_rows, devices_ctx)
    running = (
        jnp.full((2, local_heads, half_rows), MASKED_SCORE, jnp.float32),
        jnp.zeros((2, local_heads, half_rows), jnp.float32),
        jnp.zeros((2, half_rows, local_heads, HD), jnp.float32),
    )
    travel = queries
    for hop_step in range(devices_ctx):
        anchor = (ctx_index - hop_step) % devices_ctx
        query_pos = folded_positions(shard_rows, anchor * shard_rows, shard_rows, devices_ctx)
        query_doc = lax.dynamic_slice_in_dim(all_docs, anchor * shard_rows, shard_rows, 0)
        largest, totals, summed = attend_shard(
            running, travel, query_pos, query_doc, keys, values, own_pos, doc_ids
        )
        running = (
            passed_along(largest.astype(jnp.bfloat16), "ctx", 1).astype(largest.dtype),
            passed_along(totals.astype(jnp.bfloat16), "ctx", 1).astype(totals.dtype),
            passed_along(summed.astype(jnp.bfloat16), "ctx", 1).astype(summed.dtype),
        )
        if hop_step + 1 < devices_ctx:
            travel = passed_along(travel, "ctx", 1)
    largest, totals, summed = running
    attended = summed / totals.transpose(0, 2, 1)[:, :, :, None]
    attended = attended.reshape(shard_rows, local_heads * HD).astype(jnp.bfloat16)
    partial_out = jnp.dot(attended, w_out, preferred_element_type=jnp.float32)
    return lax.psum_scatter(
        partial_out.astype(jnp.bfloat16), "head", scatter_dimension=1, tiled=True
    )


SMALL = pl.CostEstimate(flops=1024, bytes_accessed=1024, transcendentals=0)
TILE = 256
MOST_DOCS = 16


def params(mib):
    return pltpu.CompilerParams(vmem_limit_bytes=mib * 1024 * 1024)


def whole(shape):
    return pl.BlockSpec(shape, lambda step, scalars: (0,) * len(shape))


def pack(ctx_index, half, queries, keys, values, docs):
    rows = queries.shape[0] // 2
    group = queries.shape[1] // HD
    doc_rows = 0 if docs is None else 16 * pl.cdiv(docs.shape[0], 16)
    total = 3 * rows + doc_rows

    def kernel(ctx_ref, *refs):
        outs = refs[len(refs) - (group - 1) :]
        if docs is not None:
            mine = refs[3 * (group - 1)][...].astype(jnp.float32)
            empty = jnp.zeros((doc_rows - mine.shape[0], HD), jnp.float32)
            mine = jnp.concatenate([mine, empty], axis=0).astype(jnp.bfloat16)
        for place in range(group - 1):
            for part in range(2):
                outs[place][part * rows : (part + 1) * rows, :] = refs[place * 3 + part][...]
            for block in range(rows // HD):
                taken = refs[place * 3 + 2][block * HD : (block + 1) * HD, :]
                lower = 2 * rows + block * HD
                outs[place][lower : lower + HD, :] = jnp.transpose(taken)
            if docs is not None:
                outs[place][3 * rows :, :] = mine

    def piece(distance):
        return pl.BlockSpec((rows, HD), lambda step, ctx: (half, ctx[0] ^ distance))

    in_specs = []
    operands = []
    for distance in range(1, group):
        for array in (queries, keys, values):
            in_specs.append(piece(distance))
            operands.append(array)
    if docs is not None:
        in_specs.append(whole(docs.shape))
        operands.append(docs)
    return pl.pallas_call(
        kernel,
        grid_spec=pltpu.PrefetchScalarGridSpec(
            num_scalar_prefetch=1,
            grid=(1,),
            in_specs=in_specs,
            out_specs=[whole((total, HD))] * (group - 1),
        ),
        out_shape=[jax.ShapeDtypeStruct((total, HD), jnp.bfloat16)] * (group - 1),
        compiler_params=params(56),
        cost_estimate=SMALL,
        name="pack",
    )(ctx_index, *operands)


def pack_projection(places, w_out, chips):
    depth, width = w_out.shape
    columns = width // (2 * chips)

    def kernel(places_ref, keep_in, give_in, keep_out, give_out):
        keep_out[...] = keep_in[...]
        give_out[...] = give_in[...]

    def block(other):
        def index_map(turn, at):
            parity = 1 - at[chips] if other else at[chips]
            return (0, 2 * at[turn] + parity)

        return pl.BlockSpec((depth, columns), index_map)

    out_spec = pl.BlockSpec((depth, columns), lambda turn, at: (0, turn))
    return pl.pallas_call(
        kernel,
        grid_spec=pltpu.PrefetchScalarGridSpec(
            num_scalar_prefetch=1,
            grid=(chips,),
            in_specs=[block(False), block(True)],
            out_specs=[out_spec] * 2,
        ),
        out_shape=[jax.ShapeDtypeStruct((depth, chips * columns), w_out.dtype)] * 2,
        compiler_params=params(56),
        cost_estimate=SMALL,
        name="pack_projection",
    )(places, w_out, w_out)


def attend(ctx_index, queries, keys, values, docs, low, high):
    rows = queries.shape[0] // 2
    group = queries.shape[1] // HD
    with_high = high is not None
    per_block = rows // TILE
    lines = rows // HD
    key_rows = (2 * group if with_high else group) * rows
    scaling = LOG2E / math.sqrt(HD)

    def kernel(ctx_ref, *refs):
        refs = list(refs)
        own_low = [refs.pop(0) for _ in range(3)]
        own_high = [refs.pop(0) for _ in range(3)] if with_high else None
        own_docs = refs.pop(0)
        low_refs = [refs.pop(0) for _ in range(group - 1)]
        high_refs = [refs.pop(0) for _ in range(group - 1)] if with_high else None
        outs = [refs.pop(0) for _ in range(group)]
        key_buf, value_buf, doc_buf, summed = refs
        ctx = ctx_ref[0]

        def part(upper, distance, index, lower=0, count=rows):
            if distance == 0:
                return (own_high if upper else own_low)[index][lower : lower + count, :]
            source = (high_refs if upper else low_refs)[distance - 1]
            return source[index * rows + lower : index * rows + lower + count, :]

        place = {}
        doc_rows = {}
        for upper in (False, True) if with_high else (False,):
            for distance in range(group):
                source = ctx ^ distance
                block = 2 * group - 1 - source if upper else source
                place[upper, distance] = block
                offset = pl.multiple_of(block * rows, rows)
                key_buf[pl.ds(offset, rows), :] = part(upper, distance, 1)
                if distance == 0:
                    both = own_docs[...].astype(jnp.float32)
                else:
                    both = low_refs[distance - 1][3 * rows :, :].astype(jnp.float32)
                begin = lines if upper else 0
                mine = []
                for line in range(lines):
                    taken = part(upper, distance, 2, line * HD, HD)
                    if distance == 0:
                        taken = jnp.transpose(taken)
                    column = pl.multiple_of(block * rows + line * HD, HD)
                    value_buf[:HD, pl.ds(column, HD)] = taken
                    mine.append(both[begin + line : begin + line + 1, :])
                    doc_buf[pl.ds(block * lines + line, 1), :] = mine[-1]
                doc_rows[upper, distance] = jnp.concatenate(mine, axis=1)
        value_buf[HD:, :] = jnp.ones((value_buf.shape[0] - HD, key_rows), jnp.bfloat16)

        all_docs = doc_buf[...]
        starts = [jnp.zeros((1, rows), jnp.float32)] * group
        for number in range(1, MOST_DOCS):
            smaller = jnp.where(all_docs < number, 1.0, 0.0)
            count = jnp.sum(jnp.sum(smaller, axis=0, keepdims=True), axis=1, keepdims=True)
            for distance in range(group):
                reached = doc_rows[with_high, distance] >= number
                starts[distance] = jnp.where(reached, count, starts[distance])

        def scores_of(distance, offset, count):
            raw = lax.dot_general(
                key_buf[pl.ds(offset, count), :],
                part(with_high, distance, 0),
                (((1,), (1,)), ((), ())),
                preferred_element_type=jnp.float32,
            )
            return raw * scaling

        def weighted(weights, offset, count):
            return jnp.dot(
                value_buf[:, pl.ds(offset, count)],
                weights.astype(jnp.bfloat16),
                preferred_element_type=jnp.float32,
            )

        key_row = lax.broadcasted_iota(jnp.int32, (rows, rows), 0)
        causal = key_row <= lax.broadcasted_iota(jnp.int32, (rows, rows), 1)
        key_row = key_row.astype(jnp.float32)
        largest = []
        first_tiles = []
        ends = []
        for distance in range(group):
            block = place[with_high, distance]
            offset = pl.multiple_of(block * rows, rows)
            least = starts[distance] - offset.astype(jnp.float32)
            scores = scores_of(distance, offset, rows)
            scores = jnp.where((key_row >= least) & causal, scores, MASKED_SCORE)
            largest.append(jnp.max(scores, axis=0, keepdims=True))
            summed[distance] = weighted(jnp.exp2(scores - largest[-1]), offset, rows)
            first_tiles.append(jnp.min(starts[distance]).astype(jnp.int32) // TILE)
            ends.append(block * per_block)

        longest = ends[0] - first_tiles[0]
        for distance in range(1, group):
            longest = jnp.maximum(longest, ends[distance] - first_tiles[distance])
        tile_row = lax.broadcasted_iota(jnp.int32, (TILE, rows), 0).astype(jnp.float32)

        def visit(step, running):
            renewed = []
            for distance in range(group):
                wanted = first_tiles[distance] + step
                index = jnp.maximum(jnp.minimum(wanted, ends[distance] - 1), 0)
                offset = pl.multiple_of(index * TILE, TILE)
                least = jnp.where(
                    wanted < ends[distance], starts[distance] - offset.astype(jnp.float32), 1e9
                )
                scores = scores_of(distance, offset, TILE)
                scores = jnp.where(tile_row >= least, scores, MASKED_SCORE)
                new_max = jnp.maximum(running[distance], jnp.max(scores, axis=0, keepdims=True))
                factor = jnp.exp2(running[distance] - new_max)
                product = weighted(jnp.exp2(scores - new_max), offset, TILE)
                summed[distance] = summed[distance] * factor + product
                renewed.append(new_max)
            return tuple(renewed)

        lax.fori_loop(0, longest, visit, tuple(largest))
        for distance in range(group):
            attended = summed[distance, :HD, :] / summed[distance, HD : HD + 1, :]
            outs[distance][...] = jnp.transpose(attended).astype(jnp.bfloat16)

    def own(upper):
        return pl.BlockSpec((rows, HD), lambda step, ctx: (int(upper), ctx[0]))

    in_specs = [own(False)] * 3
    operands = [queries, keys, values]
    if with_high:
        in_specs += [own(True)] * 3
        operands += [queries, keys, values]
    received = [docs, *low, *(high if with_high else ())]
    operands += received
    in_specs += [whole(array.shape) for array in received]
    return pl.pallas_call(
        kernel,
        grid_spec=pltpu.PrefetchScalarGridSpec(
            num_scalar_prefetch=1,
            grid=(1,),
            in_specs=in_specs,
            out_specs=[whole((rows, HD))] * group,
            scratch_shapes=[
                pltpu.VMEM((key_rows, HD), jnp.bfloat16),
                pltpu.VMEM((HD + 16, key_rows), jnp.bfloat16),
                pltpu.VMEM((key_rows // HD, HD), jnp.float32),
                pltpu.VMEM((group, HD + 16, rows), jnp.float32),
            ],
        ),
        out_shape=[jax.ShapeDtypeStruct((rows, HD), jnp.bfloat16)] * group,
        compiler_params=params(40),
        cost_estimate=SMALL,
        name="attend_high" if with_high else "attend_low",
    )(ctx_index, *operands)


def assemble(ctx_index, pieces):
    rows = pieces[0].shape[0]
    group = len(pieces)

    def kernel(ctx_ref, *refs):
        for distance in range(group):
            column = pl.multiple_of((ctx_ref[0] ^ distance) * HD, HD)
            refs[-1][:, pl.ds(column, HD)] = refs[distance][...]

    return pl.pallas_call(
        kernel,
        grid_spec=pltpu.PrefetchScalarGridSpec(
            num_scalar_prefetch=1,
            grid=(1,),
            in_specs=[whole((rows, HD))] * group,
            out_specs=whole((rows, group * HD)),
        ),
        out_shape=jax.ShapeDtypeStruct((rows, group * HD), jnp.bfloat16),
        compiler_params=params(16),
        cost_estimate=SMALL,
        name="assemble",
    )(ctx_index, *pieces)


def project(mine, sibling, w_mine, w_sibling, first, count, chips):
    rows, depth = mine.shape
    columns = w_mine.shape[1] // chips

    def kernel(mine_ref, sibling_ref, w_mine_ref, w_sibling_ref, out_ref):
        total = jnp.dot(mine_ref[...], w_mine_ref[...], preferred_element_type=jnp.float32)
        total += jnp.dot(sibling_ref[...], w_sibling_ref[...], preferred_element_type=jnp.float32)
        out_ref[...] = total.astype(jnp.bfloat16)

    weights = pl.BlockSpec((depth, columns), lambda turn: (0, first + turn))
    attended = pl.BlockSpec((rows, depth), lambda turn: (0, 0))
    return pl.pallas_call(
        kernel,
        grid=(count,),
        in_specs=[attended, attended, weights, weights],
        out_specs=pl.BlockSpec((rows, columns), lambda turn: (0, turn)),
        out_shape=jax.ShapeDtypeStruct((rows, count * columns), jnp.bfloat16),
        compiler_params=params(16),
        cost_estimate=SMALL,
        name="project",
    )(mine, sibling, w_mine, w_sibling)


def swap(value, axis, distance):
    count = lax.axis_size(axis)
    return lax.ppermute(value, axis, [(source, source ^ distance) for source in range(count)])


def between_chips(value, pairs):
    both = [(2 * source + core, 2 * target + core) for source, target in pairs for core in (0, 1)]
    return lax.ppermute(value, "head", both)


def add(*terms):
    total = terms[0].astype(jnp.float32)
    for term in terms[1:]:
        total = total + term.astype(jnp.float32)
    return total.astype(jnp.bfloat16)


SENDING = ((3, 2, 1, 0), (3, 2, 0, 1), (0, 1, 3, 2), (0, 1, 2, 3))
TO_MIDDLE = ((0, 1), (3, 2))
ACROSS = ((1, 2), (2, 1))
TO_ENDS = ((2, 3), (1, 0))


def tie(*values):
    return lax.optimization_barrier(values)


def exchange_local(queries, keys, values, doc_ids, w_out):
    shard_rows = queries.shape[0]
    group = queries.shape[1] // HD
    chips = lax.axis_size("head") // 2
    columns = w_out.shape[1] // (2 * chips)
    ctx_index = lax.axis_index("ctx").astype(jnp.int32).reshape(1)
    head_index = lax.axis_index("head").astype(jnp.int32)
    chip = head_index // 2
    core = (head_index % 2).reshape(1)
    places = jnp.concatenate([jnp.array(SENDING, jnp.int32)[chip], core])
    docs = doc_ids.reshape(shard_rows // HD, HD)
    near = range(1, group)

    low_out = pack(ctx_index, 0, queries, keys, values, docs)
    low_out, later = tie(low_out, (queries, keys, values))
    low = [swap(low_out[distance - 1], "ctx", distance) for distance in near]
    high_out = pack(ctx_index, 1, *later, None)
    high_out, w_out = tie(high_out, w_out)
    w_mine, w_give = pack_projection(places, w_out, chips)
    high_out, low, w_give = tie(high_out, low, w_give)
    w_sibling = swap(w_give, "head", 1)
    high = [swap(high_out[0], "ctx", 1), swap(high_out[1], "ctx", 2)]

    def send_back(pieces):
        return [swap(pieces[distance], "ctx", distance) for distance in near]

    def share_of(mine, sibling, turn, count=1):
        return project(mine, sibling, w_mine, w_sibling, turn, count, chips)

    pieces = attend(ctx_index, queries, keys, values, docs, low, None)
    pieces, diagonal_out, w_sibling = tie(pieces, high_out[2], w_sibling)
    back = send_back(pieces)
    back, high = tie(back, high)
    high.append(swap(diagonal_out, "ctx", 3))
    mine = assemble(ctx_index, [pieces[0], *back])
    sibling = swap(mine, "head", 1)
    share = share_of(mine, sibling, 0)
    shares = share_of(mine, sibling, 1, 2)
    kept = share_of(mine, sibling, 3)
    end = between_chips(share, TO_MIDDLE)
    shares, high[2] = tie(shares, high[2])
    ends = between_chips(shares, TO_MIDDLE)

    high, share, shares, kept = tie(high, share, shares, kept)
    pieces = attend(ctx_index, queries, keys, values, docs, low, high)
    back = send_back(pieces)
    passed = add(share, end)
    back, passed = tie(back, passed)
    across = between_chips(passed, ACROSS)
    mine = assemble(ctx_index, [pieces[0], *back])
    sibling = swap(mine, "head", 1)
    late = [share_of(mine, sibling, turn) for turn in range(chips)]
    end_high = [between_chips(late[0], TO_MIDDLE)]
    late[1], ends, across = tie(late[1], ends, across)
    end_high.append(between_chips(late[1], TO_MIDDLE))
    across_second = between_chips(add(shares[:, :columns], ends[:, :columns]), ACROSS)
    passed = add(late[0], end_high[0])
    late[2], passed = tie(late[2], passed)
    across_high = between_chips(passed, ACROSS)
    outer = between_chips(add(shares[:, columns:], across), TO_ENDS)
    end_high.append(between_chips(late[2], TO_MIDDLE))
    passed = add(late[1], end_high[1])
    passed, across_second = tie(passed, across_second)
    across_high_second = between_chips(passed, ACROSS)
    passed = add(late[2], across_high)
    passed, outer = tie(passed, outer)
    outer_high = between_chips(passed, TO_ENDS)
    first = add(kept, ends[:, columns:], across_second, outer)
    second = add(late[3], end_high[2], across_high_second, outer_high)
    return jnp.concatenate([first, second], axis=0)


def solution(mesh):
    in_specs = (P("ctx", "head"), P("ctx", "head"), P("ctx", "head"), P("ctx"), P("head", None))
    out_specs = P("ctx", "head")
    ctx_count = mesh.shape["ctx"]
    head_count = mesh.shape["head"]

    def local(queries, keys, values, doc_ids, w_out):
        heads = queries.shape[1] // HD
        exchange = heads == ctx_count and heads == 4 and head_count == 2 * len(SENDING)
        exchange = exchange and queries.shape[0] % (4 * TILE) == 0
        body = exchange_local if exchange else ring_local
        return body(queries, keys, values, doc_ids, w_out)

    return jax.shard_map(
        local, mesh=mesh, in_specs=in_specs, out_specs=out_specs, check_vma=False
    )
```

```python
import functools
import math

import jax
import jax.numpy as jnp
from jax import lax
from jax.experimental import pallas as pl
from jax.experimental.pallas import tpu as pltpu
from jax.sharding import PartitionSpec as P

HD = 128


MASKED_SCORE = -1e30
LOG2E = 1.4426950408889634


def passed_along(value, axis, steps):
    count = lax.axis_size(axis)
    pairs = [(source, (source + steps) % count) for source in range(count)]
    return lax.ppermute(value, axis, pairs)


def folded_positions(row_total, offset, shard_rows, devices_ctx):
    flat_index = offset + lax.iota(jnp.int32, row_total)
    owner_dev = flat_index // shard_rows
    within = flat_index % shard_rows
    half_rows = shard_rows // 2
    fold_block = jnp.where(within < half_rows, owner_dev, 2 * devices_ctx - 1 - owner_dev)
    return fold_block * half_rows + within % half_rows


def block_update(
    running, query, query_pos, query_doc, key_block, value_block, pos_block, doc_block
):
    largest, totals, summed = running
    query_rows = query.shape[0]
    local_heads = query.shape[1] // HD
    query_heads = query.reshape(query_rows, local_heads, HD)
    key_heads = key_block.reshape(key_block.shape[0], local_heads, HD)
    value_heads = value_block.reshape(value_block.shape[0], local_heads, HD)
    scores = jnp.einsum(
        "qhd,khd->hqk", query_heads, key_heads, preferred_element_type=jnp.float32
    ) * (1.0 / math.sqrt(HD))
    allowed = (query_doc[:, None] == doc_block[None, :]) & (
        pos_block[None, :] <= query_pos[:, None]
    )
    scores = jnp.where(allowed[None], scores, MASKED_SCORE)
    new_max = jnp.maximum(largest, jnp.max(scores, axis=2))
    weights = jnp.where(allowed[None], jnp.exp(scores - new_max[:, :, None]), 0.0)
    factor = jnp.exp(largest - new_max)
    totals = totals * factor + jnp.sum(weights, axis=2)
    product = jnp.einsum(
        "hqk,khd->qhd",
        weights.astype(jnp.bfloat16),
        value_heads,
        preferred_element_type=jnp.float32,
    )
    summed = summed * factor.T[:, :, None] + product
    return (new_max, totals, summed)


def attend_rows(running, query, query_pos, query_doc, key_rows, value_rows, key_pos, key_doc):
    row_total = key_rows.shape[0]
    block_rows = math.gcd(row_total, query.shape[0])
    block_count = row_total // block_rows
    highest = jnp.max(query_pos)

    def visit(partial_value, blocks):
        key_block, value_block, pos_block, doc_block = blocks
        masked_out = jnp.min(pos_block) > highest
        updated = lax.cond(
            masked_out,
            lambda frozen: frozen,
            lambda frozen: block_update(
                frozen, query, query_pos, query_doc, key_block, value_block, pos_block, doc_block
            ),
            partial_value,
        )
        return (updated, None)

    blocks = (
        key_rows.reshape(block_count, block_rows, key_rows.shape[1]),
        value_rows.reshape(block_count, block_rows, value_rows.shape[1]),
        key_pos.reshape(block_count, block_rows),
        key_doc.reshape(block_count, block_rows),
    )
    running, _ = lax.scan(visit, running, blocks)
    return running


def attend_shard(running, query, query_pos, query_doc, key_rows, value_rows, key_pos, key_doc):
    largest, totals, summed = running
    half_rows = query.shape[0] // 2
    new_largest = []
    new_totals = []
    new_summed = []
    for half_idx in range(2):
        lower = half_idx * half_rows
        part_state = (largest[half_idx], totals[half_idx], summed[half_idx])
        part_state = attend_rows(
            part_state,
            query[lower : lower + half_rows],
            query_pos[lower : lower + half_rows],
            query_doc[lower : lower + half_rows],
            key_rows,
            value_rows,
            key_pos,
            key_doc,
        )
        new_largest.append(part_state[0])
        new_totals.append(part_state[1])
        new_summed.append(part_state[2])
    return (jnp.stack(new_largest), jnp.stack(new_totals), jnp.stack(new_summed))


def ring_local(queries, keys, values, doc_ids, w_out):
    shard_rows = queries.shape[0]
    half_rows = shard_rows // 2
    local_heads = queries.shape[1] // HD
    devices_ctx = lax.axis_size("ctx")
    ctx_index = lax.axis_index("ctx")
    all_docs = lax.all_gather(doc_ids, "ctx", axis=0, tiled=True)
    own_pos = folded_positions(shard_rows, ctx_index * shard_rows, shard_rows, devices_ctx)
    running = (
        jnp.full((2, local_heads, half_rows), MASKED_SCORE, jnp.float32),
        jnp.zeros((2, local_heads, half_rows), jnp.float32),
        jnp.zeros((2, half_rows, local_heads, HD), jnp.float32),
    )
    travel = queries
    for hop_step in range(devices_ctx):
        anchor = (ctx_index - hop_step) % devices_ctx
        query_pos = folded_positions(shard_rows, anchor * shard_rows, shard_rows, devices_ctx)
        query_doc = lax.dynamic_slice_in_dim(all_docs, anchor * shard_rows, shard_rows, 0)
        largest, totals, summed = attend_shard(
            running, travel, query_pos, query_doc, keys, values, own_pos, doc_ids
        )
        running = (
            passed_along(largest.astype(jnp.bfloat16), "ctx", 1).astype(largest.dtype),
            passed_along(totals.astype(jnp.bfloat16), "ctx", 1).astype(totals.dtype),
            passed_along(summed.astype(jnp.bfloat16), "ctx", 1).astype(summed.dtype),
        )
        if hop_step + 1 < devices_ctx:
            travel = passed_along(travel, "ctx", 1)
    largest, totals, summed = running
    attended = summed / totals.transpose(0, 2, 1)[:, :, :, None]
    attended = attended.reshape(shard_rows, local_heads * HD).astype(jnp.bfloat16)
    partial_out = jnp.dot(attended, w_out, preferred_element_type=jnp.float32)
    return lax.psum_scatter(
        partial_out.astype(jnp.bfloat16), "head", scatter_dimension=1, tiled=True
    )


SMALL = pl.CostEstimate(flops=1024, bytes_accessed=1024, transcendentals=0)
TILE = 256
MOST_DOCS = 16


def params(mib):
    return pltpu.CompilerParams(vmem_limit_bytes=mib * 1024 * 1024)


def whole(shape):
    return pl.BlockSpec(shape, lambda step, scalars: (0,) * len(shape))


def pack(ctx_index, half, queries, keys, values, docs):
    rows = queries.shape[0] // 2
    group = queries.shape[1] // HD
    doc_rows = 0 if docs is None else 16 * pl.cdiv(docs.shape[0], 16)
    total = 3 * rows + doc_rows

    def kernel(ctx_ref, *refs):
        outs = refs[len(refs) - (group - 1) :]
        if docs is not None:
            mine = refs[3 * (group - 1)][...].astype(jnp.float32)
            empty = jnp.zeros((doc_rows - mine.shape[0], HD), jnp.float32)
            mine = jnp.concatenate([mine, empty], axis=0).astype(jnp.bfloat16)
        for place in range(group - 1):
            for part in range(2):
                outs[place][part * rows : (part + 1) * rows, :] = refs[place * 3 + part][...]
            for block in range(rows // HD):
                taken = refs[place * 3 + 2][block * HD : (block + 1) * HD, :]
                lower = 2 * rows + block * HD
                outs[place][lower : lower + HD, :] = jnp.transpose(taken)
            if docs is not None:
                outs[place][3 * rows :, :] = mine

    def piece(distance):
        return pl.BlockSpec((rows, HD), lambda step, ctx: (half, ctx[0] ^ distance))

    in_specs = []
    operands = []
    for distance in range(1, group):
        for array in (queries, keys, values):
            in_specs.append(piece(distance))
            operands.append(array)
    if docs is not None:
        in_specs.append(whole(docs.shape))
        operands.append(docs)
    return pl.pallas_call(
        kernel,
        grid_spec=pltpu.PrefetchScalarGridSpec(
            num_scalar_prefetch=1,
            grid=(1,),
            in_specs=in_specs,
            out_specs=[whole((total, HD))] * (group - 1),
        ),
        out_shape=[jax.ShapeDtypeStruct((total, HD), jnp.bfloat16)] * (group - 1),
        compiler_params=params(56),
        cost_estimate=SMALL,
        name="pack",
    )(ctx_index, *operands)


def pack_projection(places, w_out, chips):
    depth, width = w_out.shape
    columns = width // (2 * chips)

    def kernel(places_ref, keep_in, give_in, keep_out, give_out):
        keep_out[...] = keep_in[...]
        give_out[...] = give_in[...]

    def block(other):
        def index_map(turn, at):
            parity = 1 - at[chips] if other else at[chips]
            return (0, 2 * at[turn] + parity)

        return pl.BlockSpec((depth, columns), index_map)

    out_spec = pl.BlockSpec((depth, columns), lambda turn, at: (0, turn))
    return pl.pallas_call(
        kernel,
        grid_spec=pltpu.PrefetchScalarGridSpec(
            num_scalar_prefetch=1,
            grid=(chips,),
            in_specs=[block(False), block(True)],
            out_specs=[out_spec] * 2,
        ),
        out_shape=[jax.ShapeDtypeStruct((depth, chips * columns), w_out.dtype)] * 2,
        compiler_params=params(56),
        cost_estimate=SMALL,
        name="pack_projection",
    )(places, w_out, w_out)


def attend(ctx_index, queries, keys, values, docs, low, high):
    rows = queries.shape[0] // 2
    group = queries.shape[1] // HD
    with_high = high is not None
    per_block = rows // TILE
    lines = rows // HD
    key_rows = (2 * group if with_high else group) * rows
    scaling = LOG2E / math.sqrt(HD)

    def kernel(ctx_ref, *refs):
        refs = list(refs)
        own_low = [refs.pop(0) for _ in range(3)]
        own_high = [refs.pop(0) for _ in range(3)] if with_high else None
        own_docs = refs.pop(0)
        low_refs = [refs.pop(0) for _ in range(group - 1)]
        high_refs = [refs.pop(0) for _ in range(group - 1)] if with_high else None
        outs = [refs.pop(0) for _ in range(group)]
        key_buf, value_buf, doc_buf, summed = refs
        ctx = ctx_ref[0]

        def part(upper, distance, index, lower=0, count=rows):
            if distance == 0:
                return (own_high if upper else own_low)[index][lower : lower + count, :]
            source = (high_refs if upper else low_refs)[distance - 1]
            return source[index * rows + lower : index * rows + lower + count, :]

        place = {}
        doc_rows = {}
        for upper in (False, True) if with_high else (False,):
            for distance in range(group):
                source = ctx ^ distance
                block = 2 * group - 1 - source if upper else source
                place[upper, distance] = block
                offset = pl.multiple_of(block * rows, rows)
                key_buf[pl.ds(offset, rows), :] = part(upper, distance, 1)
                if distance == 0:
                    both = own_docs[...].astype(jnp.float32)
                else:
                    both = low_refs[distance - 1][3 * rows :, :].astype(jnp.float32)
                begin = lines if upper else 0
                mine = []
                for line in range(lines):
                    taken = part(upper, distance, 2, line * HD, HD)
                    if distance == 0:
                        taken = jnp.transpose(taken)
                    column = pl.multiple_of(block * rows + line * HD, HD)
                    value_buf[:HD, pl.ds(column, HD)] = taken
                    mine.append(both[begin + line : begin + line + 1, :])
                    doc_buf[pl.ds(block * lines + line, 1), :] = mine[-1]
                doc_rows[upper, distance] = jnp.concatenate(mine, axis=1)
        value_buf[HD:, :] = jnp.ones((value_buf.shape[0] - HD, key_rows), jnp.bfloat16)

        all_docs = doc_buf[...]
        starts = [jnp.zeros((1, rows), jnp.float32)] * group
        for number in range(1, MOST_DOCS):
            smaller = jnp.where(all_docs < number, 1.0, 0.0)
            count = jnp.sum(jnp.sum(smaller, axis=0, keepdims=True), axis=1, keepdims=True)
            for distance in range(group):
                reached = doc_rows[with_high, distance] >= number
                starts[distance] = jnp.where(reached, count, starts[distance])

        def scores_of(distance, offset, count):
            raw = lax.dot_general(
                key_buf[pl.ds(offset, count), :],
                part(with_high, distance, 0),
                (((1,), (1,)), ((), ())),
                preferred_element_type=jnp.float32,
            )
            return raw * scaling

        def weighted(weights, offset, count):
            return jnp.dot(
                value_buf[:, pl.ds(offset, count)],
                weights.astype(jnp.bfloat16),
                preferred_element_type=jnp.float32,
            )

        key_row = lax.broadcasted_iota(jnp.int32, (rows, rows), 0)
        causal = key_row <= lax.broadcasted_iota(jnp.int32, (rows, rows), 1)
        key_row = key_row.astype(jnp.float32)
        largest = []
        first_tiles = []
        ends = []
        for distance in range(group):
            block = place[with_high, distance]
            offset = pl.multiple_of(block * rows, rows)
            least = starts[distance] - offset.astype(jnp.float32)
            scores = scores_of(distance, offset, rows)
            scores = jnp.where((key_row >= least) & causal, scores, MASKED_SCORE)
            largest.append(jnp.max(scores, axis=0, keepdims=True))
            summed[distance] = weighted(jnp.exp2(scores - largest[-1]), offset, rows)
            first_tiles.append(jnp.min(starts[distance]).astype(jnp.int32) // TILE)
            ends.append(block * per_block)

        longest = ends[0] - first_tiles[0]
        for distance in range(1, group):
            longest = jnp.maximum(longest, ends[distance] - first_tiles[distance])
        tile_row = lax.broadcasted_iota(jnp.int32, (TILE, rows), 0).astype(jnp.float32)

        def visit(step, running):
            renewed = []
            for distance in range(group):
                wanted = first_tiles[distance] + step
                index = jnp.maximum(jnp.minimum(wanted, ends[distance] - 1), 0)
                offset = pl.multiple_of(index * TILE, TILE)
                least = jnp.where(
                    wanted < ends[distance], starts[distance] - offset.astype(jnp.float32), 1e9
                )
                scores = scores_of(distance, offset, TILE)
                scores = jnp.where(tile_row >= least, scores, MASKED_SCORE)
                new_max = jnp.maximum(running[distance], jnp.max(scores, axis=0, keepdims=True))
                factor = jnp.exp2(running[distance] - new_max)
                product = weighted(jnp.exp2(scores - new_max), offset, TILE)
                summed[distance] = summed[distance] * factor + product
                renewed.append(new_max)
            return tuple(renewed)

        lax.fori_loop(0, longest, visit, tuple(largest))
        for distance in range(group):
            attended = summed[distance, :HD, :] / summed[distance, HD : HD + 1, :]
            outs[distance][...] = jnp.transpose(attended).astype(jnp.bfloat16)

    def own(upper):
        return pl.BlockSpec((rows, HD), lambda step, ctx: (int(upper), ctx[0]))

    in_specs = [own(False)] * 3
    operands = [queries, keys, values]
    if with_high:
        in_specs += [own(True)] * 3
        operands += [queries, keys, values]
    received = [docs, *low, *(high if with_high else ())]
    operands += received
    in_specs += [whole(array.shape) for array in received]
    return pl.pallas_call(
        kernel,
        grid_spec=pltpu.PrefetchScalarGridSpec(
            num_scalar_prefetch=1,
            grid=(1,),
            in_specs=in_specs,
            out_specs=[whole((rows, HD))] * group,
            scratch_shapes=[
                pltpu.VMEM((key_rows, HD), jnp.bfloat16),
                pltpu.VMEM((HD + 16, key_rows), jnp.bfloat16),
                pltpu.VMEM((key_rows // HD, HD), jnp.float32),
                pltpu.VMEM((group, HD + 16, rows), jnp.float32),
            ],
        ),
        out_shape=[jax.ShapeDtypeStruct((rows, HD), jnp.bfloat16)] * group,
        compiler_params=params(40),
        cost_estimate=SMALL,
        name="attend_high" if with_high else "attend_low",
    )(ctx_index, *operands)


def assemble(ctx_index, pieces):
    rows = pieces[0].shape[0]
    group = len(pieces)

    def kernel(ctx_ref, *refs):
        for distance in range(group):
            column = pl.multiple_of((ctx_ref[0] ^ distance) * HD, HD)
            refs[-1][:, pl.ds(column, HD)] = refs[distance][...]

    return pl.pallas_call(
        kernel,
        grid_spec=pltpu.PrefetchScalarGridSpec(
            num_scalar_prefetch=1,
            grid=(1,),
            in_specs=[whole((rows, HD))] * group,
            out_specs=whole((rows, group * HD)),
        ),
        out_shape=jax.ShapeDtypeStruct((rows, group * HD), jnp.bfloat16),
        compiler_params=params(16),
        cost_estimate=SMALL,
        name="assemble",
    )(ctx_index, *pieces)


def project(mine, sibling, w_mine, w_sibling, first, count, chips):
    rows, depth = mine.shape
    columns = w_mine.shape[1] // chips

    def kernel(mine_ref, sibling_ref, w_mine_ref, w_sibling_ref, out_ref):
        total = jnp.dot(mine_ref[...], w_mine_ref[...], preferred_element_type=jnp.float32)
        total += jnp.dot(sibling_ref[...], w_sibling_ref[...], preferred_element_type=jnp.float32)
        out_ref[...] = total.astype(jnp.bfloat16)

    weights = pl.BlockSpec((depth, columns), lambda turn: (0, first + turn))
    attended = pl.BlockSpec((rows, depth), lambda turn: (0, 0))
    return pl.pallas_call(
        kernel,
        grid=(count,),
        in_specs=[attended, attended, weights, weights],
        out_specs=pl.BlockSpec((rows, columns), lambda turn: (0, turn)),
        out_shape=jax.ShapeDtypeStruct((rows, count * columns), jnp.bfloat16),
        compiler_params=params(16),
        cost_estimate=SMALL,
        name="project",
    )(mine, sibling, w_mine, w_sibling)


def swap(value, axis, distance):
    count = lax.axis_size(axis)
    return lax.ppermute(value, axis, [(source, source ^ distance) for source in range(count)])


def add(*terms):
    total = terms[0].astype(jnp.float32)
    for term in terms[1:]:
        total = total + term.astype(jnp.float32)
    return total.astype(jnp.bfloat16)


TURNS = (3, 1, 2, 0)


def tie(*values):
    return lax.optimization_barrier(values)


def exchange_local(queries, keys, values, doc_ids, w_out):
    shard_rows = queries.shape[0]
    group = queries.shape[1] // HD
    chips = lax.axis_size("head") // 2
    columns = w_out.shape[1] // (2 * chips)
    ctx_index = lax.axis_index("ctx").astype(jnp.int32).reshape(1)
    head_index = lax.axis_index("head").astype(jnp.int32)
    chip = head_index // 2
    core = (head_index % 2).reshape(1)
    places = jnp.concatenate([chip ^ jnp.array(TURNS, jnp.int32), core])
    docs = doc_ids.reshape(shard_rows // HD, HD)
    near = range(1, group)

    low_out = pack(ctx_index, 0, queries, keys, values, docs)
    low_out, later = tie(low_out, (queries, keys, values))
    low = [swap(low_out[distance - 1], "ctx", distance) for distance in near]
    high_out = pack(ctx_index, 1, *later, None)
    high_out, w_out = tie(high_out, w_out)
    w_mine, w_give = pack_projection(places, w_out, chips)
    high_out, low, w_give = tie(high_out, low, w_give)
    w_sibling = swap(w_give, "head", 1)
    high = [swap(high_out[0], "ctx", 1), swap(high_out[1], "ctx", 2)]

    def send_back(pieces):
        return [swap(pieces[distance], "ctx", distance) for distance in near]

    def share_of(mine, sibling, turn, count=1):
        return project(mine, sibling, w_mine, w_sibling, turn, count, chips)

    pieces = attend(ctx_index, queries, keys, values, docs, low, None)
    pieces, diagonal_out, w_sibling = tie(pieces, high_out[2], w_sibling)
    back = send_back(pieces)
    back, high = tie(back, high)
    high.append(swap(diagonal_out, "ctx", 3))
    mine = assemble(ctx_index, [pieces[0], *back])
    sibling = swap(mine, "head", 1)
    shares = [share_of(mine, sibling, turn) for turn in range(chips)]
    far = swap(shares[0], "head", 2)
    near_sum = swap(shares[1], "head", 2)

    high, shares = tie(high, shares)
    pieces = attend(ctx_index, queries, keys, values, docs, low, high)
    back = send_back(pieces)
    passed = add(shares[2], far)
    back, passed, near_sum = tie(back, passed, near_sum)
    across = swap(passed, "head", 4)
    mine = assemble(ctx_index, [pieces[0], *back])
    sibling = swap(mine, "head", 1)
    late = [share_of(mine, sibling, turn) for turn in range(chips)]
    far = swap(late[0], "head", 2)
    late[1], across = tie(late[1], across)
    first = add(shares[3], near_sum, across)
    near_sum = swap(late[1], "head", 2)
    across = swap(add(late[2], far), "head", 4)
    second = add(late[3], near_sum, across)
    return jnp.concatenate([first, second], axis=0)


def solution(mesh):
    in_specs = (P("ctx", "head"), P("ctx", "head"), P("ctx", "head"), P("ctx"), P("head", None))
    out_specs = P("ctx", "head")
    ctx_count = mesh.shape["ctx"]
    head_count = mesh.shape["head"]

    def local(queries, keys, values, doc_ids, w_out):
        heads = queries.shape[1] // HD
        exchange = heads == ctx_count and heads == 4 and head_count == 2 * len(TURNS)
        exchange = exchange and queries.shape[0] % (4 * TILE) == 0
        body = exchange_local if exchange else ring_local
        return body(queries, keys, values, doc_ids, w_out)

    return jax.shard_map(
        local, mesh=mesh, in_specs=in_specs, out_specs=out_specs, check_vma=False
    )
```

```python
import functools
import math

import jax
import jax.numpy as jnp
from jax import lax
from jax.experimental import pallas as pl
from jax.experimental.pallas import tpu as pltpu
from jax.sharding import PartitionSpec as P

HD = 128


MASKED_SCORE = -1e30
LOG2E = 1.4426950408889634


def passed_along(value, axis, steps):
    count = lax.axis_size(axis)
    pairs = [(source, (source + steps) % count) for source in range(count)]
    return lax.ppermute(value, axis, pairs)


def folded_positions(row_total, offset, shard_rows, devices_ctx):
    flat_index = offset + lax.iota(jnp.int32, row_total)
    owner_dev = flat_index // shard_rows
    within = flat_index % shard_rows
    half_rows = shard_rows // 2
    fold_block = jnp.where(within < half_rows, owner_dev, 2 * devices_ctx - 1 - owner_dev)
    return fold_block * half_rows + within % half_rows


def block_update(
    running, query, query_pos, query_doc, key_block, value_block, pos_block, doc_block
):
    largest, totals, summed = running
    query_rows = query.shape[0]
    local_heads = query.shape[1] // HD
    query_heads = query.reshape(query_rows, local_heads, HD)
    key_heads = key_block.reshape(key_block.shape[0], local_heads, HD)
    value_heads = value_block.reshape(value_block.shape[0], local_heads, HD)
    scores = jnp.einsum(
        "qhd,khd->hqk", query_heads, key_heads, preferred_element_type=jnp.float32
    ) * (1.0 / math.sqrt(HD))
    allowed = (query_doc[:, None] == doc_block[None, :]) & (
        pos_block[None, :] <= query_pos[:, None]
    )
    scores = jnp.where(allowed[None], scores, MASKED_SCORE)
    new_max = jnp.maximum(largest, jnp.max(scores, axis=2))
    weights = jnp.where(allowed[None], jnp.exp(scores - new_max[:, :, None]), 0.0)
    factor = jnp.exp(largest - new_max)
    totals = totals * factor + jnp.sum(weights, axis=2)
    product = jnp.einsum(
        "hqk,khd->qhd",
        weights.astype(jnp.bfloat16),
        value_heads,
        preferred_element_type=jnp.float32,
    )
    summed = summed * factor.T[:, :, None] + product
    return (new_max, totals, summed)


def attend_rows(running, query, query_pos, query_doc, key_rows, value_rows, key_pos, key_doc):
    row_total = key_rows.shape[0]
    block_rows = math.gcd(row_total, query.shape[0])
    block_count = row_total // block_rows
    highest = jnp.max(query_pos)

    def visit(partial_value, blocks):
        key_block, value_block, pos_block, doc_block = blocks
        masked_out = jnp.min(pos_block) > highest
        updated = lax.cond(
            masked_out,
            lambda frozen: frozen,
            lambda frozen: block_update(
                frozen, query, query_pos, query_doc, key_block, value_block, pos_block, doc_block
            ),
            partial_value,
        )
        return (updated, None)

    blocks = (
        key_rows.reshape(block_count, block_rows, key_rows.shape[1]),
        value_rows.reshape(block_count, block_rows, value_rows.shape[1]),
        key_pos.reshape(block_count, block_rows),
        key_doc.reshape(block_count, block_rows),
    )
    running, _ = lax.scan(visit, running, blocks)
    return running


def attend_shard(running, query, query_pos, query_doc, key_rows, value_rows, key_pos, key_doc):
    largest, totals, summed = running
    half_rows = query.shape[0] // 2
    new_largest = []
    new_totals = []
    new_summed = []
    for half_idx in range(2):
        lower = half_idx * half_rows
        part_state = (largest[half_idx], totals[half_idx], summed[half_idx])
        part_state = attend_rows(
            part_state,
            query[lower : lower + half_rows],
            query_pos[lower : lower + half_rows],
            query_doc[lower : lower + half_rows],
            key_rows,
            value_rows,
            key_pos,
            key_doc,
        )
        new_largest.append(part_state[0])
        new_totals.append(part_state[1])
        new_summed.append(part_state[2])
    return (jnp.stack(new_largest), jnp.stack(new_totals), jnp.stack(new_summed))


def ring_local(queries, keys, values, doc_ids, w_out):
    shard_rows = queries.shape[0]
    half_rows = shard_rows // 2
    local_heads = queries.shape[1] // HD
    devices_ctx = lax.axis_size("ctx")
    ctx_index = lax.axis_index("ctx")
    all_docs = lax.all_gather(doc_ids, "ctx", axis=0, tiled=True)
    own_pos = folded_positions(shard_rows, ctx_index * shard_rows, shard_rows, devices_ctx)
    running = (
        jnp.full((2, local_heads, half_rows), MASKED_SCORE, jnp.float32),
        jnp.zeros((2, local_heads, half_rows), jnp.float32),
        jnp.zeros((2, half_rows, local_heads, HD), jnp.float32),
    )
    travel = queries
    for hop_step in range(devices_ctx):
        anchor = (ctx_index - hop_step) % devices_ctx
        query_pos = folded_positions(shard_rows, anchor * shard_rows, shard_rows, devices_ctx)
        query_doc = lax.dynamic_slice_in_dim(all_docs, anchor * shard_rows, shard_rows, 0)
        largest, totals, summed = attend_shard(
            running, travel, query_pos, query_doc, keys, values, own_pos, doc_ids
        )
        running = (
            passed_along(largest.astype(jnp.bfloat16), "ctx", 1).astype(largest.dtype),
            passed_along(totals.astype(jnp.bfloat16), "ctx", 1).astype(totals.dtype),
            passed_along(summed.astype(jnp.bfloat16), "ctx", 1).astype(summed.dtype),
        )
        if hop_step + 1 < devices_ctx:
            travel = passed_along(travel, "ctx", 1)
    largest, totals, summed = running
    attended = summed / totals.transpose(0, 2, 1)[:, :, :, None]
    attended = attended.reshape(shard_rows, local_heads * HD).astype(jnp.bfloat16)
    partial_out = jnp.dot(attended, w_out, preferred_element_type=jnp.float32)
    return lax.psum_scatter(
        partial_out.astype(jnp.bfloat16), "head", scatter_dimension=1, tiled=True
    )


SMALL = pl.CostEstimate(flops=1024, bytes_accessed=1024, transcendentals=0)
TILE = 256
MOST_DOCS = 16


def params(mib):
    return pltpu.CompilerParams(vmem_limit_bytes=mib * 1024 * 1024)


def whole(shape):
    return pl.BlockSpec(shape, lambda step, scalars: (0,) * len(shape))


def pack(ctx_index, half, queries, keys, values, docs):
    rows = queries.shape[0] // 2
    group = queries.shape[1] // HD
    doc_rows = 0 if docs is None else 16 * pl.cdiv(docs.shape[0], 16)
    total = 3 * rows + doc_rows

    def kernel(ctx_ref, *refs):
        outs = refs[len(refs) - (group - 1) :]
        if docs is not None:
            mine = refs[3 * (group - 1)][...].astype(jnp.float32)
            empty = jnp.zeros((doc_rows - mine.shape[0], HD), jnp.float32)
            mine = jnp.concatenate([mine, empty], axis=0).astype(jnp.bfloat16)
        for place in range(group - 1):
            for part in range(2):
                outs[place][part * rows : (part + 1) * rows, :] = refs[place * 3 + part][...]
            for block in range(rows // HD):
                taken = refs[place * 3 + 2][block * HD : (block + 1) * HD, :]
                lower = 2 * rows + block * HD
                outs[place][lower : lower + HD, :] = jnp.transpose(taken)
            if docs is not None:
                outs[place][3 * rows :, :] = mine

    def piece(distance):
        return pl.BlockSpec((rows, HD), lambda step, ctx: (half, ctx[0] ^ distance))

    in_specs = []
    operands = []
    for distance in range(1, group):
        for array in (queries, keys, values):
            in_specs.append(piece(distance))
            operands.append(array)
    if docs is not None:
        in_specs.append(whole(docs.shape))
        operands.append(docs)
    return pl.pallas_call(
        kernel,
        grid_spec=pltpu.PrefetchScalarGridSpec(
            num_scalar_prefetch=1,
            grid=(1,),
            in_specs=in_specs,
            out_specs=[whole((total, HD))] * (group - 1),
        ),
        out_shape=[jax.ShapeDtypeStruct((total, HD), jnp.bfloat16)] * (group - 1),
        compiler_params=params(56),
        cost_estimate=SMALL,
        name="pack",
    )(ctx_index, *operands)


def pack_projection(places, w_out, chips):
    depth, width = w_out.shape
    columns = width // (2 * chips)

    def kernel(places_ref, keep_in, give_in, keep_out, give_out):
        keep_out[...] = keep_in[...]
        give_out[...] = give_in[...]

    def block(other):
        def index_map(turn, at):
            parity = 1 - at[chips] if other else at[chips]
            return (0, 2 * at[turn] + parity)

        return pl.BlockSpec((depth, columns), index_map)

    out_spec = pl.BlockSpec((depth, columns), lambda turn, at: (0, turn))
    return pl.pallas_call(
        kernel,
        grid_spec=pltpu.PrefetchScalarGridSpec(
            num_scalar_prefetch=1,
            grid=(chips,),
            in_specs=[block(False), block(True)],
            out_specs=[out_spec] * 2,
        ),
        out_shape=[jax.ShapeDtypeStruct((depth, chips * columns), w_out.dtype)] * 2,
        compiler_params=params(56),
        cost_estimate=SMALL,
        name="pack_projection",
    )(places, w_out, w_out)


def attend(ctx_index, queries, keys, values, docs, low, high):
    rows = queries.shape[0] // 2
    group = queries.shape[1] // HD
    with_high = high is not None
    per_block = rows // TILE
    lines = rows // HD
    key_rows = (2 * group if with_high else group) * rows
    key_tiles = key_rows // TILE
    scaling = LOG2E / math.sqrt(HD)

    def kernel(ctx_ref, *refs):
        refs = list(refs)
        own_low = [refs.pop(0) for _ in range(3)]
        own_high = [refs.pop(0) for _ in range(3)] if with_high else None
        own_docs = refs.pop(0)
        low_refs = [refs.pop(0) for _ in range(group - 1)]
        high_refs = [refs.pop(0) for _ in range(group - 1)] if with_high else None
        outs = [refs.pop(0) for _ in range(group)]
        key_buf, value_buf, doc_buf, query_buf, start_buf, largest_buf, summed = refs
        ctx = ctx_ref[0]

        def part(upper, distance, index, lower=0, count=rows):
            if distance == 0:
                return (own_high if upper else own_low)[index][lower : lower + count, :]
            source = (high_refs if upper else low_refs)[distance - 1]
            return source[index * rows + lower : index * rows + lower + count, :]

        place = {}
        doc_rows = {}
        for upper in (False, True) if with_high else (False,):
            for distance in range(group):
                source = ctx ^ distance
                block = 2 * group - 1 - source if upper else source
                place[upper, distance] = block
                offset = pl.multiple_of(block * rows, rows)
                key_buf[pl.ds(offset, rows), :] = part(upper, distance, 1)
                if distance == 0:
                    both = own_docs[...].astype(jnp.float32)
                else:
                    both = low_refs[distance - 1][3 * rows :, :].astype(jnp.float32)
                begin = lines if upper else 0
                mine = []
                for line in range(lines):
                    taken = part(upper, distance, 2, line * HD, HD)
                    if distance == 0:
                        taken = jnp.transpose(taken)
                    column = pl.multiple_of(block * rows + line * HD, HD)
                    value_buf[:HD, pl.ds(column, HD)] = taken
                    mine.append(both[begin + line : begin + line + 1, :])
                    doc_buf[pl.ds(block * lines + line, 1), :] = mine[-1]
                doc_rows[upper, distance] = jnp.concatenate(mine, axis=1)
        value_buf[HD:, :] = jnp.ones((value_buf.shape[0] - HD, key_rows), jnp.bfloat16)

        all_docs = doc_buf[...]
        starts = [jnp.zeros((1, rows), jnp.float32)] * group
        for number in range(1, MOST_DOCS):
            smaller = jnp.where(all_docs < number, 1.0, 0.0)
            count = jnp.sum(jnp.sum(smaller, axis=0, keepdims=True), axis=1, keepdims=True)
            for distance in range(group):
                reached = doc_rows[with_high, distance] >= number
                starts[distance] = jnp.where(reached, count, starts[distance])

        def scores_of(query, offset):
            raw = lax.dot_general(
                key_buf[pl.ds(offset, TILE), :],
                query,
                (((1,), (1,)), ((), ())),
                preferred_element_type=jnp.float32,
            )
            return raw * scaling

        def weighted(weights, offset):
            return jnp.dot(
                value_buf[:, pl.ds(offset, TILE)],
                weights.astype(jnp.bfloat16),
                preferred_element_type=jnp.float32,
            )

        key_row = lax.broadcasted_iota(jnp.int32, (TILE, TILE), 0)
        causal = key_row <= lax.broadcasted_iota(jnp.int32, (TILE, TILE), 1)
        key_row = key_row.astype(jnp.float32)
        first_tiles = []
        ends = []
        for tile in range(per_block):
            for distance in range(group):
                slot = tile * group + distance
                query = part(with_high, distance, 0, tile * TILE, TILE)
                query_buf[slot] = query
                start = starts[distance][:, tile * TILE : (tile + 1) * TILE]
                start_buf[slot, 0:1, :] = start
                end = place[with_high, distance] * per_block + tile
                offset = pl.multiple_of(end * TILE, TILE)
                least = start - offset.astype(jnp.float32)
                scores = scores_of(query, offset)
                scores = jnp.where((key_row >= least) & causal, scores, MASKED_SCORE)
                largest = jnp.max(scores, axis=0, keepdims=True)
                largest_buf[slot, 0:1, :] = largest
                summed[slot] = weighted(jnp.exp2(scores - largest), offset)
                first_tiles.append(jnp.min(start).astype(jnp.int32) // TILE)
                ends.append(end)

        counts = [end - first for end, first in zip(ends, first_tiles)]
        lanes = [
            [tile * group + (lane ^ (tile * (group - 1))) for tile in range(per_block)]
            for lane in range(group)
        ]
        longest = jnp.int32(0)
        for lane in lanes:
            longest = jnp.maximum(longest, sum(counts[slot] for slot in lane))

        def visit(step, carry):
            for lane in lanes:
                slot = jnp.int32(lane[0])
                index = first_tiles[lane[0]] + step
                before = counts[lane[0]]
                for later in lane[1:]:
                    reached = step >= before
                    slot = jnp.where(reached, later, slot)
                    index = jnp.where(reached, first_tiles[later] + step - before, index)
                    before = before + counts[later]
                offset = pl.multiple_of(jnp.minimum(index, key_tiles - 1) * TILE, TILE)
                beyond = jnp.where(step < before, -offset.astype(jnp.float32), 1e9)
                scores = scores_of(query_buf[slot], offset)
                least = start_buf[slot, 0:1, :] + beyond
                scores = jnp.where(key_row >= least, scores, MASKED_SCORE)
                largest = largest_buf[slot, 0:1, :]
                new_max = jnp.maximum(largest, jnp.max(scores, axis=0, keepdims=True))
                product = weighted(jnp.exp2(scores - new_max), offset)
                summed[slot] = summed[slot] * jnp.exp2(largest - new_max) + product
                largest_buf[slot, 0:1, :] = new_max
            return carry

        lax.fori_loop(0, longest, visit, jnp.int32(0))
        for tile in range(per_block):
            for distance in range(group):
                slot = tile * group + distance
                attended = summed[slot, :HD, :] / summed[slot, HD : HD + 1, :]
                outs[distance][tile * TILE : (tile + 1) * TILE, :] = jnp.transpose(
                    attended
                ).astype(jnp.bfloat16)

    def own(upper):
        return pl.BlockSpec((rows, HD), lambda step, ctx: (int(upper), ctx[0]))

    in_specs = [own(False)] * 3
    operands = [queries, keys, values]
    if with_high:
        in_specs += [own(True)] * 3
        operands += [queries, keys, values]
    received = [docs, *low, *(high if with_high else ())]
    operands += received
    in_specs += [whole(array.shape) for array in received]
    return pl.pallas_call(
        kernel,
        grid_spec=pltpu.PrefetchScalarGridSpec(
            num_scalar_prefetch=1,
            grid=(1,),
            in_specs=in_specs,
            out_specs=[whole((rows, HD))] * group,
            scratch_shapes=[
                pltpu.VMEM((key_rows, HD), jnp.bfloat16),
                pltpu.VMEM((HD + 16, key_rows), jnp.bfloat16),
                pltpu.VMEM((key_rows // HD, HD), jnp.float32),
                pltpu.VMEM((group * per_block, TILE, HD), jnp.bfloat16),
                pltpu.VMEM((group * per_block, 8, TILE), jnp.float32),
                pltpu.VMEM((group * per_block, 8, TILE), jnp.float32),
                pltpu.VMEM((group * per_block, HD + 16, TILE), jnp.float32),
            ],
        ),
        out_shape=[jax.ShapeDtypeStruct((rows, HD), jnp.bfloat16)] * group,
        compiler_params=params(40),
        cost_estimate=SMALL,
        name="attend_high" if with_high else "attend_low",
    )(ctx_index, *operands)


def assemble(ctx_index, pieces):
    rows = pieces[0].shape[0]
    group = len(pieces)

    def kernel(ctx_ref, *refs):
        for distance in range(group):
            column = pl.multiple_of((ctx_ref[0] ^ distance) * HD, HD)
            refs[-1][:, pl.ds(column, HD)] = refs[distance][...]

    return pl.pallas_call(
        kernel,
        grid_spec=pltpu.PrefetchScalarGridSpec(
            num_scalar_prefetch=1,
            grid=(1,),
            in_specs=[whole((rows, HD))] * group,
            out_specs=whole((rows, group * HD)),
        ),
        out_shape=jax.ShapeDtypeStruct((rows, group * HD), jnp.bfloat16),
        compiler_params=params(16),
        cost_estimate=SMALL,
        name="assemble",
    )(ctx_index, *pieces)


def project(mine, sibling, w_mine, w_sibling, first, count, chips):
    rows, depth = mine.shape
    columns = w_mine.shape[1] // chips

    def kernel(mine_ref, sibling_ref, w_mine_ref, w_sibling_ref, out_ref):
        total = jnp.dot(mine_ref[...], w_mine_ref[...], preferred_element_type=jnp.float32)
        total += jnp.dot(sibling_ref[...], w_sibling_ref[...], preferred_element_type=jnp.float32)
        out_ref[...] = total.astype(jnp.bfloat16)

    weights = pl.BlockSpec((depth, columns), lambda turn: (0, first + turn))
    attended = pl.BlockSpec((rows, depth), lambda turn: (0, 0))
    return pl.pallas_call(
        kernel,
        grid=(count,),
        in_specs=[attended, attended, weights, weights],
        out_specs=pl.BlockSpec((rows, columns), lambda turn: (0, turn)),
        out_shape=jax.ShapeDtypeStruct((rows, count * columns), jnp.bfloat16),
        compiler_params=params(16),
        cost_estimate=SMALL,
        name="project",
    )(mine, sibling, w_mine, w_sibling)


def swap(value, axis, distance):
    count = lax.axis_size(axis)
    return lax.ppermute(value, axis, [(source, source ^ distance) for source in range(count)])


def add(*terms):
    total = terms[0].astype(jnp.float32)
    for term in terms[1:]:
        total = total + term.astype(jnp.float32)
    return total.astype(jnp.bfloat16)


TURNS = (3, 1, 2, 0)


def tie(*values):
    return lax.optimization_barrier(values)


def exchange_local(queries, keys, values, doc_ids, w_out):
    shard_rows = queries.shape[0]
    group = queries.shape[1] // HD
    chips = lax.axis_size("head") // 2
    columns = w_out.shape[1] // (2 * chips)
    ctx_index = lax.axis_index("ctx").astype(jnp.int32).reshape(1)
    head_index = lax.axis_index("head").astype(jnp.int32)
    chip = head_index // 2
    core = (head_index % 2).reshape(1)
    places = jnp.concatenate([chip ^ jnp.array(TURNS, jnp.int32), core])
    docs = doc_ids.reshape(shard_rows // HD, HD)
    near = range(1, group)

    low_out = pack(ctx_index, 0, queries, keys, values, docs)
    low_out, later = tie(low_out, (queries, keys, values))
    low = [swap(low_out[distance - 1], "ctx", distance) for distance in near]
    high_out = pack(ctx_index, 1, *later, None)
    high_out, w_out = tie(high_out, w_out)
    w_mine, w_give = pack_projection(places, w_out, chips)
    high_out, low, w_give = tie(high_out, low, w_give)
    w_sibling = swap(w_give, "head", 1)
    high = [swap(high_out[0], "ctx", 1), swap(high_out[1], "ctx", 2)]

    def send_back(pieces):
        return [swap(pieces[distance], "ctx", distance) for distance in near]

    def share_of(mine, sibling, turn, count=1):
        return project(mine, sibling, w_mine, w_sibling, turn, count, chips)

    pieces = attend(ctx_index, queries, keys, values, docs, low, None)
    pieces, diagonal_out, w_sibling = tie(pieces, high_out[2], w_sibling)
    back = send_back(pieces)
    back, high = tie(back, high)
    high.append(swap(diagonal_out, "ctx", 3))
    mine = assemble(ctx_index, [pieces[0], *back])
    sibling = swap(mine, "head", 1)
    shares = [share_of(mine, sibling, turn) for turn in range(chips)]
    far = swap(shares[0], "head", 2)
    shares[1], high[2] = tie(shares[1], high[2])
    near_sum = swap(shares[1], "head", 2)

    high, shares = tie(high, shares)
    pieces = attend(ctx_index, queries, keys, values, docs, low, high)
    back = send_back(pieces)
    passed = add(shares[2], far)
    back, passed, near_sum = tie(back, passed, near_sum)
    across = swap(passed, "head", 4)
    mine = assemble(ctx_index, [pieces[0], *back])
    sibling = swap(mine, "head", 1)
    late = [share_of(mine, sibling, turn) for turn in range(chips)]
    far = swap(late[0], "head", 2)
    late[1], across = tie(late[1], across)
    first = add(shares[3], near_sum, across)
    near_sum = swap(late[1], "head", 2)
    across = swap(add(late[2], far), "head", 4)
    second = add(late[3], near_sum, across)
    return jnp.concatenate([first, second], axis=0)


def solution(mesh):
    in_specs = (P("ctx", "head"), P("ctx", "head"), P("ctx", "head"), P("ctx"), P("head", None))
    out_specs = P("ctx", "head")
    ctx_count = mesh.shape["ctx"]
    head_count = mesh.shape["head"]

    def local(queries, keys, values, doc_ids, w_out):
        heads = queries.shape[1] // HD
        exchange = heads == ctx_count and heads == 4 and head_count == 2 * len(TURNS)
        exchange = exchange and queries.shape[0] % (4 * TILE) == 0
        body = exchange_local if exchange else ring_local
        return body(queries, keys, values, doc_ids, w_out)

    return jax.shard_map(
        local, mesh=mesh, in_specs=in_specs, out_specs=out_specs, check_vma=False
    )
```

```python
import functools
import math

import jax
import jax.numpy as jnp
from jax import lax
from jax.experimental import pallas as pl
from jax.experimental.pallas import tpu as pltpu
from jax.sharding import PartitionSpec as P

HD = 128


MASKED_SCORE = -1e30
LOG2E = 1.4426950408889634


def passed_along(value, axis, steps):
    count = lax.axis_size(axis)
    pairs = [(source, (source + steps) % count) for source in range(count)]
    return lax.ppermute(value, axis, pairs)


def folded_positions(row_total, offset, shard_rows, devices_ctx):
    flat_index = offset + lax.iota(jnp.int32, row_total)
    owner_dev = flat_index // shard_rows
    within = flat_index % shard_rows
    half_rows = shard_rows // 2
    fold_block = jnp.where(within < half_rows, owner_dev, 2 * devices_ctx - 1 - owner_dev)
    return fold_block * half_rows + within % half_rows


def block_update(
    running, query, query_pos, query_doc, key_block, value_block, pos_block, doc_block
):
    largest, totals, summed = running
    query_rows = query.shape[0]
    local_heads = query.shape[1] // HD
    query_heads = query.reshape(query_rows, local_heads, HD)
    key_heads = key_block.reshape(key_block.shape[0], local_heads, HD)
    value_heads = value_block.reshape(value_block.shape[0], local_heads, HD)
    scores = jnp.einsum(
        "qhd,khd->hqk", query_heads, key_heads, preferred_element_type=jnp.float32
    ) * (1.0 / math.sqrt(HD))
    allowed = (query_doc[:, None] == doc_block[None, :]) & (
        pos_block[None, :] <= query_pos[:, None]
    )
    scores = jnp.where(allowed[None], scores, MASKED_SCORE)
    new_max = jnp.maximum(largest, jnp.max(scores, axis=2))
    weights = jnp.where(allowed[None], jnp.exp(scores - new_max[:, :, None]), 0.0)
    factor = jnp.exp(largest - new_max)
    totals = totals * factor + jnp.sum(weights, axis=2)
    product = jnp.einsum(
        "hqk,khd->qhd",
        weights.astype(jnp.bfloat16),
        value_heads,
        preferred_element_type=jnp.float32,
    )
    summed = summed * factor.T[:, :, None] + product
    return (new_max, totals, summed)


def attend_rows(running, query, query_pos, query_doc, key_rows, value_rows, key_pos, key_doc):
    row_total = key_rows.shape[0]
    block_rows = math.gcd(row_total, query.shape[0])
    block_count = row_total // block_rows
    highest = jnp.max(query_pos)

    def visit(partial_value, blocks):
        key_block, value_block, pos_block, doc_block = blocks
        masked_out = jnp.min(pos_block) > highest
        updated = lax.cond(
            masked_out,
            lambda frozen: frozen,
            lambda frozen: block_update(
                frozen, query, query_pos, query_doc, key_block, value_block, pos_block, doc_block
            ),
            partial_value,
        )
        return (updated, None)

    blocks = (
        key_rows.reshape(block_count, block_rows, key_rows.shape[1]),
        value_rows.reshape(block_count, block_rows, value_rows.shape[1]),
        key_pos.reshape(block_count, block_rows),
        key_doc.reshape(block_count, block_rows),
    )
    running, _ = lax.scan(visit, running, blocks)
    return running


def attend_shard(running, query, query_pos, query_doc, key_rows, value_rows, key_pos, key_doc):
    largest, totals, summed = running
    half_rows = query.shape[0] // 2
    new_largest = []
    new_totals = []
    new_summed = []
    for half_idx in range(2):
        lower = half_idx * half_rows
        part_state = (largest[half_idx], totals[half_idx], summed[half_idx])
        part_state = attend_rows(
            part_state,
            query[lower : lower + half_rows],
            query_pos[lower : lower + half_rows],
            query_doc[lower : lower + half_rows],
            key_rows,
            value_rows,
            key_pos,
            key_doc,
        )
        new_largest.append(part_state[0])
        new_totals.append(part_state[1])
        new_summed.append(part_state[2])
    return (jnp.stack(new_largest), jnp.stack(new_totals), jnp.stack(new_summed))


def ring_local(queries, keys, values, doc_ids, w_out):
    shard_rows = queries.shape[0]
    half_rows = shard_rows // 2
    local_heads = queries.shape[1] // HD
    devices_ctx = lax.axis_size("ctx")
    ctx_index = lax.axis_index("ctx")
    all_docs = lax.all_gather(doc_ids, "ctx", axis=0, tiled=True)
    own_pos = folded_positions(shard_rows, ctx_index * shard_rows, shard_rows, devices_ctx)
    running = (
        jnp.full((2, local_heads, half_rows), MASKED_SCORE, jnp.float32),
        jnp.zeros((2, local_heads, half_rows), jnp.float32),
        jnp.zeros((2, half_rows, local_heads, HD), jnp.float32),
    )
    travel = queries
    for hop_step in range(devices_ctx):
        anchor = (ctx_index - hop_step) % devices_ctx
        query_pos = folded_positions(shard_rows, anchor * shard_rows, shard_rows, devices_ctx)
        query_doc = lax.dynamic_slice_in_dim(all_docs, anchor * shard_rows, shard_rows, 0)
        largest, totals, summed = attend_shard(
            running, travel, query_pos, query_doc, keys, values, own_pos, doc_ids
        )
        running = (
            passed_along(largest.astype(jnp.bfloat16), "ctx", 1).astype(largest.dtype),
            passed_along(totals.astype(jnp.bfloat16), "ctx", 1).astype(totals.dtype),
            passed_along(summed.astype(jnp.bfloat16), "ctx", 1).astype(summed.dtype),
        )
        if hop_step + 1 < devices_ctx:
            travel = passed_along(travel, "ctx", 1)
    largest, totals, summed = running
    attended = summed / totals.transpose(0, 2, 1)[:, :, :, None]
    attended = attended.reshape(shard_rows, local_heads * HD).astype(jnp.bfloat16)
    partial_out = jnp.dot(attended, w_out, preferred_element_type=jnp.float32)
    return lax.psum_scatter(
        partial_out.astype(jnp.bfloat16), "head", scatter_dimension=1, tiled=True
    )


SMALL = pl.CostEstimate(flops=1024, bytes_accessed=1024, transcendentals=0)
TILE = 256
MOST_DOCS = 16


def params(mib):
    return pltpu.CompilerParams(vmem_limit_bytes=mib * 1024 * 1024)


def whole(shape):
    return pl.BlockSpec(shape, lambda step, scalars: (0,) * len(shape))


def pack(ctx_index, half, queries, keys, values, docs):
    rows = queries.shape[0] // 2
    group = queries.shape[1] // HD
    doc_rows = 0 if docs is None else 16 * pl.cdiv(docs.shape[0], 16)
    total = 3 * rows + doc_rows

    def kernel(ctx_ref, *refs):
        outs = refs[len(refs) - (group - 1) :]
        if docs is not None:
            mine = refs[3 * (group - 1)][...].astype(jnp.float32)
            empty = jnp.zeros((doc_rows - mine.shape[0], HD), jnp.float32)
            mine = jnp.concatenate([mine, empty], axis=0).astype(jnp.bfloat16)
        for place in range(group - 1):
            for part in range(2):
                outs[place][part * rows : (part + 1) * rows, :] = refs[place * 3 + part][...]
            for block in range(rows // HD):
                taken = refs[place * 3 + 2][block * HD : (block + 1) * HD, :]
                lower = 2 * rows + block * HD
                outs[place][lower : lower + HD, :] = jnp.transpose(taken)
            if docs is not None:
                outs[place][3 * rows :, :] = mine

    def piece(distance):
        return pl.BlockSpec((rows, HD), lambda step, ctx: (half, ctx[0] ^ distance))

    in_specs = []
    operands = []
    for distance in range(1, group):
        for array in (queries, keys, values):
            in_specs.append(piece(distance))
            operands.append(array)
    if docs is not None:
        in_specs.append(whole(docs.shape))
        operands.append(docs)
    return pl.pallas_call(
        kernel,
        grid_spec=pltpu.PrefetchScalarGridSpec(
            num_scalar_prefetch=1,
            grid=(1,),
            in_specs=in_specs,
            out_specs=[whole((total, HD))] * (group - 1),
        ),
        out_shape=[jax.ShapeDtypeStruct((total, HD), jnp.bfloat16)] * (group - 1),
        compiler_params=params(56),
        cost_estimate=SMALL,
        name="pack",
    )(ctx_index, *operands)


def pack_projection(places, w_out, chips):
    depth, width = w_out.shape
    columns = width // (2 * chips)

    def kernel(places_ref, keep_in, give_in, keep_out, give_out):
        keep_out[...] = keep_in[...]
        give_out[...] = give_in[...]

    def block(other):
        def index_map(turn, at):
            parity = 1 - at[chips] if other else at[chips]
            return (0, 2 * at[turn] + parity)

        return pl.BlockSpec((depth, columns), index_map)

    out_spec = pl.BlockSpec((depth, columns), lambda turn, at: (0, turn))
    return pl.pallas_call(
        kernel,
        grid_spec=pltpu.PrefetchScalarGridSpec(
            num_scalar_prefetch=1,
            grid=(chips,),
            in_specs=[block(False), block(True)],
            out_specs=[out_spec] * 2,
        ),
        out_shape=[jax.ShapeDtypeStruct((depth, chips * columns), w_out.dtype)] * 2,
        compiler_params=params(56),
        cost_estimate=SMALL,
        name="pack_projection",
    )(places, w_out, w_out)


def attend(ctx_index, queries, keys, values, docs, low, high):
    rows = queries.shape[0] // 2
    group = queries.shape[1] // HD
    with_high = high is not None
    per_block = rows // TILE
    lines = rows // HD
    key_rows = (2 * group if with_high else group) * rows
    key_tiles = key_rows // TILE
    scaling = LOG2E / math.sqrt(HD)

    def kernel(ctx_ref, *refs):
        refs = list(refs)
        own_low = [refs.pop(0) for _ in range(3)]
        own_high = [refs.pop(0) for _ in range(3)] if with_high else None
        own_docs = refs.pop(0)
        low_refs = [refs.pop(0) for _ in range(group - 1)]
        high_refs = [refs.pop(0) for _ in range(group - 1)] if with_high else None
        outs = [refs.pop(0) for _ in range(group)]
        key_buf, value_buf, doc_buf = refs[:3]
        query_buf, start_buf, largest_buf, summed = (
            refs[3 + kind * group : 3 + (kind + 1) * group] for kind in range(4)
        )
        ctx = ctx_ref[0]

        def part(upper, distance, index, lower=0, count=rows):
            if distance == 0:
                return (own_high if upper else own_low)[index][lower : lower + count, :]
            source = (high_refs if upper else low_refs)[distance - 1]
            return source[index * rows + lower : index * rows + lower + count, :]

        place = {}
        doc_rows = {}
        for upper in (False, True) if with_high else (False,):
            for distance in range(group):
                source = ctx ^ distance
                block = 2 * group - 1 - source if upper else source
                place[upper, distance] = block
                offset = pl.multiple_of(block * rows, rows)
                key_buf[pl.ds(offset, rows), :] = part(upper, distance, 1)
                if distance == 0:
                    both = own_docs[...].astype(jnp.float32)
                else:
                    both = low_refs[distance - 1][3 * rows :, :].astype(jnp.float32)
                begin = lines if upper else 0
                mine = []
                for line in range(lines):
                    taken = part(upper, distance, 2, line * HD, HD)
                    if distance == 0:
                        taken = jnp.transpose(taken)
                    column = pl.multiple_of(block * rows + line * HD, HD)
                    value_buf[:HD, pl.ds(column, HD)] = taken
                    mine.append(both[begin + line : begin + line + 1, :])
                    doc_buf[pl.ds(block * lines + line, 1), :] = mine[-1]
                doc_rows[upper, distance] = jnp.concatenate(mine, axis=1)
        value_buf[HD:, :] = jnp.ones((value_buf.shape[0] - HD, key_rows), jnp.bfloat16)

        all_docs = doc_buf[...]
        starts = [jnp.zeros((1, rows), jnp.float32)] * group
        for number in range(1, MOST_DOCS):
            smaller = jnp.where(all_docs < number, 1.0, 0.0)
            count = jnp.sum(jnp.sum(smaller, axis=0, keepdims=True), axis=1, keepdims=True)
            for distance in range(group):
                reached = doc_rows[with_high, distance] >= number
                starts[distance] = jnp.where(reached, count, starts[distance])

        def scores_of(query, offset):
            raw = lax.dot_general(
                key_buf[pl.ds(offset, TILE), :],
                query,
                (((1,), (1,)), ((), ())),
                preferred_element_type=jnp.float32,
            )
            return raw * scaling

        def weighted(weights, offset):
            return jnp.dot(
                value_buf[:, pl.ds(offset, TILE)],
                weights.astype(jnp.bfloat16),
                preferred_element_type=jnp.float32,
            )

        key_row = lax.broadcasted_iota(jnp.int32, (TILE, TILE), 0)
        causal = key_row <= lax.broadcasted_iota(jnp.int32, (TILE, TILE), 1)
        key_row = key_row.astype(jnp.float32)
        firsts = []
        counts = []
        for lane in range(group):
            for slot in range(per_block):
                distance = lane ^ (slot * (group - 1))
                query = part(with_high, distance, 0, slot * TILE, TILE)
                query_buf[lane][slot] = query
                start = starts[distance][:, slot * TILE : (slot + 1) * TILE]
                start_buf[lane][slot, 0:1, :] = start
                end = place[with_high, distance] * per_block + slot
                offset = pl.multiple_of(end * TILE, TILE)
                least = start - offset.astype(jnp.float32)
                scores = scores_of(query, offset)
                scores = jnp.where((key_row >= least) & causal, scores, MASKED_SCORE)
                largest = jnp.max(scores, axis=0, keepdims=True)
                largest_buf[lane][slot, 0:1, :] = largest
                summed[lane][slot] = weighted(jnp.exp2(scores - largest), offset)
                first = jnp.min(start).astype(jnp.int32) // TILE
                firsts.append(first)
                counts.append(end - first)

        longest = jnp.int32(0)
        for lane in range(group):
            of_lane = counts[lane * per_block : (lane + 1) * per_block]
            longest = jnp.maximum(longest, sum(of_lane))

        def visit(step, carry):
            slots = []
            offsets = []
            beyonds = []
            for lane in range(group):
                slot = jnp.int32(0)
                index = firsts[lane * per_block] + step
                before = counts[lane * per_block]
                for later in range(1, per_block):
                    reached = step >= before
                    slot = jnp.where(reached, later, slot)
                    place_later = lane * per_block + later
                    index = jnp.where(reached, firsts[place_later] + step - before, index)
                    before = before + counts[place_later]
                offset = pl.multiple_of(jnp.minimum(index, key_tiles - 1) * TILE, TILE)
                slots.append(slot)
                offsets.append(offset)
                beyonds.append(jnp.where(step < before, -offset.astype(jnp.float32), 1e9))
            each = range(group)
            scores = [scores_of(query_buf[lane][slots[lane]], offsets[lane]) for lane in each]
            old_max = [largest_buf[lane][slots[lane], 0:1, :] for lane in each]
            new_max = []
            for lane in each:
                least = start_buf[lane][slots[lane], 0:1, :] + beyonds[lane]
                scores[lane] = jnp.where(key_row >= least, scores[lane], MASKED_SCORE)
                tile_max = jnp.max(scores[lane], axis=0, keepdims=True)
                new_max.append(jnp.maximum(old_max[lane], tile_max))
            products = [
                weighted(jnp.exp2(scores[lane] - new_max[lane]), offsets[lane]) for lane in each
            ]
            for lane in each:
                factor = jnp.exp2(old_max[lane] - new_max[lane])
                summed[lane][slots[lane]] = summed[lane][slots[lane]] * factor + products[lane]
                largest_buf[lane][slots[lane], 0:1, :] = new_max[lane]
            return carry

        lax.fori_loop(0, longest, visit, jnp.int32(0))
        for lane in range(group):
            for slot in range(per_block):
                state = summed[lane]
                attended = state[slot, :HD, :] / state[slot, HD : HD + 1, :]
                out = outs[lane ^ (slot * (group - 1))]
                out[slot * TILE : (slot + 1) * TILE, :] = jnp.transpose(attended).astype(
                    jnp.bfloat16
                )

    def own(upper):
        return pl.BlockSpec((rows, HD), lambda step, ctx: (int(upper), ctx[0]))

    in_specs = [own(False)] * 3
    operands = [queries, keys, values]
    if with_high:
        in_specs += [own(True)] * 3
        operands += [queries, keys, values]
    received = [docs, *low, *(high if with_high else ())]
    operands += received
    in_specs += [whole(array.shape) for array in received]
    return pl.pallas_call(
        kernel,
        grid_spec=pltpu.PrefetchScalarGridSpec(
            num_scalar_prefetch=1,
            grid=(1,),
            in_specs=in_specs,
            out_specs=[whole((rows, HD))] * group,
            scratch_shapes=[
                pltpu.VMEM((key_rows, HD), jnp.bfloat16),
                pltpu.VMEM((HD + 16, key_rows), jnp.bfloat16),
                pltpu.VMEM((key_rows // HD, HD), jnp.float32),
                *[pltpu.VMEM((per_block, TILE, HD), jnp.bfloat16)] * group,
                *[pltpu.VMEM((per_block, 8, TILE), jnp.float32)] * (2 * group),
                *[pltpu.VMEM((per_block, HD + 16, TILE), jnp.float32)] * group,
            ],
        ),
        out_shape=[jax.ShapeDtypeStruct((rows, HD), jnp.bfloat16)] * group,
        compiler_params=params(40),
        cost_estimate=SMALL,
        name="attend_high" if with_high else "attend_low",
    )(ctx_index, *operands)


def assemble(ctx_index, pieces):
    rows = pieces[0].shape[0]
    group = len(pieces)

    def kernel(ctx_ref, *refs):
        for distance in range(group):
            column = pl.multiple_of((ctx_ref[0] ^ distance) * HD, HD)
            refs[-1][:, pl.ds(column, HD)] = refs[distance][...]

    return pl.pallas_call(
        kernel,
        grid_spec=pltpu.PrefetchScalarGridSpec(
            num_scalar_prefetch=1,
            grid=(1,),
            in_specs=[whole((rows, HD))] * group,
            out_specs=whole((rows, group * HD)),
        ),
        out_shape=jax.ShapeDtypeStruct((rows, group * HD), jnp.bfloat16),
        compiler_params=params(16),
        cost_estimate=SMALL,
        name="assemble",
    )(ctx_index, *pieces)


def project(mine, sibling, w_mine, w_sibling, first, count, chips):
    rows, depth = mine.shape
    columns = w_mine.shape[1] // chips

    def kernel(mine_ref, sibling_ref, w_mine_ref, w_sibling_ref, out_ref):
        total = jnp.dot(mine_ref[...], w_mine_ref[...], preferred_element_type=jnp.float32)
        total += jnp.dot(sibling_ref[...], w_sibling_ref[...], preferred_element_type=jnp.float32)
        out_ref[...] = total.astype(jnp.bfloat16)

    weights = pl.BlockSpec((depth, columns), lambda turn: (0, first + turn))
    attended = pl.BlockSpec((rows, depth), lambda turn: (0, 0))
    return pl.pallas_call(
        kernel,
        grid=(count,),
        in_specs=[attended, attended, weights, weights],
        out_specs=pl.BlockSpec((rows, columns), lambda turn: (0, turn)),
        out_shape=jax.ShapeDtypeStruct((rows, count * columns), jnp.bfloat16),
        compiler_params=params(16),
        cost_estimate=SMALL,
        name="project",
    )(mine, sibling, w_mine, w_sibling)


def swap(value, axis, distance):
    count = lax.axis_size(axis)
    return lax.ppermute(value, axis, [(source, source ^ distance) for source in range(count)])


def add(*terms):
    total = terms[0].astype(jnp.float32)
    for term in terms[1:]:
        total = total + term.astype(jnp.float32)
    return total.astype(jnp.bfloat16)


TURNS = (3, 1, 2, 0)


def tie(*values):
    return lax.optimization_barrier(values)


def exchange_local(queries, keys, values, doc_ids, w_out):
    shard_rows = queries.shape[0]
    group = queries.shape[1] // HD
    chips = lax.axis_size("head") // 2
    columns = w_out.shape[1] // (2 * chips)
    ctx_index = lax.axis_index("ctx").astype(jnp.int32).reshape(1)
    head_index = lax.axis_index("head").astype(jnp.int32)
    chip = head_index // 2
    core = (head_index % 2).reshape(1)
    places = jnp.concatenate([chip ^ jnp.array(TURNS, jnp.int32), core])
    docs = doc_ids.reshape(shard_rows // HD, HD)
    near = range(1, group)

    low_out = pack(ctx_index, 0, queries, keys, values, docs)
    low_out, later = tie(low_out, (queries, keys, values))
    low = [swap(low_out[distance - 1], "ctx", distance) for distance in near]
    high_out = pack(ctx_index, 1, *later, None)
    high_out, w_out = tie(high_out, w_out)
    w_mine, w_give = pack_projection(places, w_out, chips)
    high_out, low, w_give = tie(high_out, low, w_give)
    w_sibling = swap(w_give, "head", 1)
    high = [swap(high_out[0], "ctx", 1), swap(high_out[1], "ctx", 2)]

    def send_back(pieces):
        return [swap(pieces[distance], "ctx", distance) for distance in near]

    def share_of(mine, sibling, turn, count=1):
        return project(mine, sibling, w_mine, w_sibling, turn, count, chips)

    pieces = attend(ctx_index, queries, keys, values, docs, low, None)
    pieces, diagonal_out, w_sibling = tie(pieces, high_out[2], w_sibling)
    back = send_back(pieces)
    back, high = tie(back, high)
    high.append(swap(diagonal_out, "ctx", 3))
    mine = assemble(ctx_index, [pieces[0], *back])
    sibling = swap(mine, "head", 1)
    shares = [share_of(mine, sibling, turn) for turn in range(chips)]
    far = swap(shares[0], "head", 2)
    shares[1], high[2] = tie(shares[1], high[2])
    near_sum = swap(shares[1], "head", 2)

    high, shares = tie(high, shares)
    pieces = attend(ctx_index, queries, keys, values, docs, low, high)
    back = send_back(pieces)
    passed = add(shares[2], far)
    back, passed, near_sum = tie(back, passed, near_sum)
    across = swap(passed, "head", 4)
    mine = assemble(ctx_index, [pieces[0], *back])
    sibling = swap(mine, "head", 1)
    late = [share_of(mine, sibling, turn) for turn in range(chips)]
    far = swap(late[0], "head", 2)
    late[1], across = tie(late[1], across)
    first = add(shares[3], near_sum, across)
    near_sum = swap(late[1], "head", 2)
    across = swap(add(late[2], far), "head", 4)
    second = add(late[3], near_sum, across)
    return jnp.concatenate([first, second], axis=0)


def solution(mesh):
    in_specs = (P("ctx", "head"), P("ctx", "head"), P("ctx", "head"), P("ctx"), P("head", None))
    out_specs = P("ctx", "head")
    ctx_count = mesh.shape["ctx"]
    head_count = mesh.shape["head"]

    def local(queries, keys, values, doc_ids, w_out):
        heads = queries.shape[1] // HD
        exchange = heads == ctx_count and heads == 4 and head_count == 2 * len(TURNS)
        exchange = exchange and queries.shape[0] % (4 * TILE) == 0
        body = exchange_local if exchange else ring_local
        return body(queries, keys, values, doc_ids, w_out)

    return jax.shard_map(
        local, mesh=mesh, in_specs=in_specs, out_specs=out_specs, check_vma=False
    )
```

```python
import functools
import math

import jax
import jax.numpy as jnp
from jax import lax
from jax.experimental import pallas as pl
from jax.experimental.pallas import tpu as pltpu
from jax.sharding import PartitionSpec as P

HD = 128


MASKED_SCORE = -1e30
LOG2E = 1.4426950408889634


def passed_along(value, axis, steps):
    count = lax.axis_size(axis)
    pairs = [(source, (source + steps) % count) for source in range(count)]
    return lax.ppermute(value, axis, pairs)


def folded_positions(row_total, offset, shard_rows, devices_ctx):
    flat_index = offset + lax.iota(jnp.int32, row_total)
    owner_dev = flat_index // shard_rows
    within = flat_index % shard_rows
    half_rows = shard_rows // 2
    fold_block = jnp.where(within < half_rows, owner_dev, 2 * devices_ctx - 1 - owner_dev)
    return fold_block * half_rows + within % half_rows


def block_update(
    running, query, query_pos, query_doc, key_block, value_block, pos_block, doc_block
):
    largest, totals, summed = running
    query_rows = query.shape[0]
    local_heads = query.shape[1] // HD
    query_heads = query.reshape(query_rows, local_heads, HD)
    key_heads = key_block.reshape(key_block.shape[0], local_heads, HD)
    value_heads = value_block.reshape(value_block.shape[0], local_heads, HD)
    scores = jnp.einsum(
        "qhd,khd->hqk", query_heads, key_heads, preferred_element_type=jnp.float32
    ) * (1.0 / math.sqrt(HD))
    allowed = (query_doc[:, None] == doc_block[None, :]) & (
        pos_block[None, :] <= query_pos[:, None]
    )
    scores = jnp.where(allowed[None], scores, MASKED_SCORE)
    new_max = jnp.maximum(largest, jnp.max(scores, axis=2))
    weights = jnp.where(allowed[None], jnp.exp(scores - new_max[:, :, None]), 0.0)
    factor = jnp.exp(largest - new_max)
    totals = totals * factor + jnp.sum(weights, axis=2)
    product = jnp.einsum(
        "hqk,khd->qhd",
        weights.astype(jnp.bfloat16),
        value_heads,
        preferred_element_type=jnp.float32,
    )
    summed = summed * factor.T[:, :, None] + product
    return (new_max, totals, summed)


def attend_rows(running, query, query_pos, query_doc, key_rows, value_rows, key_pos, key_doc):
    row_total = key_rows.shape[0]
    block_rows = math.gcd(row_total, query.shape[0])
    block_count = row_total // block_rows
    highest = jnp.max(query_pos)

    def visit(partial_value, blocks):
        key_block, value_block, pos_block, doc_block = blocks
        masked_out = jnp.min(pos_block) > highest
        updated = lax.cond(
            masked_out,
            lambda frozen: frozen,
            lambda frozen: block_update(
                frozen, query, query_pos, query_doc, key_block, value_block, pos_block, doc_block
            ),
            partial_value,
        )
        return (updated, None)

    blocks = (
        key_rows.reshape(block_count, block_rows, key_rows.shape[1]),
        value_rows.reshape(block_count, block_rows, value_rows.shape[1]),
        key_pos.reshape(block_count, block_rows),
        key_doc.reshape(block_count, block_rows),
    )
    running, _ = lax.scan(visit, running, blocks)
    return running


def attend_shard(running, query, query_pos, query_doc, key_rows, value_rows, key_pos, key_doc):
    largest, totals, summed = running
    half_rows = query.shape[0] // 2
    new_largest = []
    new_totals = []
    new_summed = []
    for half_idx in range(2):
        lower = half_idx * half_rows
        part_state = (largest[half_idx], totals[half_idx], summed[half_idx])
        part_state = attend_rows(
            part_state,
            query[lower : lower + half_rows],
            query_pos[lower : lower + half_rows],
            query_doc[lower : lower + half_rows],
            key_rows,
            value_rows,
            key_pos,
            key_doc,
        )
        new_largest.append(part_state[0])
        new_totals.append(part_state[1])
        new_summed.append(part_state[2])
    return (jnp.stack(new_largest), jnp.stack(new_totals), jnp.stack(new_summed))


def ring_local(queries, keys, values, doc_ids, w_out):
    shard_rows = queries.shape[0]
    half_rows = shard_rows // 2
    local_heads = queries.shape[1] // HD
    devices_ctx = lax.axis_size("ctx")
    ctx_index = lax.axis_index("ctx")
    all_docs = lax.all_gather(doc_ids, "ctx", axis=0, tiled=True)
    own_pos = folded_positions(shard_rows, ctx_index * shard_rows, shard_rows, devices_ctx)
    running = (
        jnp.full((2, local_heads, half_rows), MASKED_SCORE, jnp.float32),
        jnp.zeros((2, local_heads, half_rows), jnp.float32),
        jnp.zeros((2, half_rows, local_heads, HD), jnp.float32),
    )
    travel = queries
    for hop_step in range(devices_ctx):
        anchor = (ctx_index - hop_step) % devices_ctx
        query_pos = folded_positions(shard_rows, anchor * shard_rows, shard_rows, devices_ctx)
        query_doc = lax.dynamic_slice_in_dim(all_docs, anchor * shard_rows, shard_rows, 0)
        largest, totals, summed = attend_shard(
            running, travel, query_pos, query_doc, keys, values, own_pos, doc_ids
        )
        running = (
            passed_along(largest.astype(jnp.bfloat16), "ctx", 1).astype(largest.dtype),
            passed_along(totals.astype(jnp.bfloat16), "ctx", 1).astype(totals.dtype),
            passed_along(summed.astype(jnp.bfloat16), "ctx", 1).astype(summed.dtype),
        )
        if hop_step + 1 < devices_ctx:
            travel = passed_along(travel, "ctx", 1)
    largest, totals, summed = running
    attended = summed / totals.transpose(0, 2, 1)[:, :, :, None]
    attended = attended.reshape(shard_rows, local_heads * HD).astype(jnp.bfloat16)
    partial_out = jnp.dot(attended, w_out, preferred_element_type=jnp.float32)
    return lax.psum_scatter(
        partial_out.astype(jnp.bfloat16), "head", scatter_dimension=1, tiled=True
    )


SMALL = pl.CostEstimate(flops=1024, bytes_accessed=1024, transcendentals=0)
TILE = 256
MOST_DOCS = 16


def params(mib):
    return pltpu.CompilerParams(vmem_limit_bytes=mib * 1024 * 1024)


def whole(shape):
    return pl.BlockSpec(shape, lambda step, scalars: (0,) * len(shape))


def pack(ctx_index, half, queries, keys, values, docs):
    rows = queries.shape[0] // 2
    group = queries.shape[1] // HD
    doc_rows = 0 if docs is None else 16 * pl.cdiv(docs.shape[0], 16)
    total = 3 * rows + doc_rows

    def kernel(ctx_ref, *refs):
        outs = refs[len(refs) - (group - 1) :]
        if docs is not None:
            mine = refs[3 * (group - 1)][...].astype(jnp.float32)
            empty = jnp.zeros((doc_rows - mine.shape[0], HD), jnp.float32)
            mine = jnp.concatenate([mine, empty], axis=0).astype(jnp.bfloat16)
        for place in range(group - 1):
            for part in range(2):
                outs[place][part * rows : (part + 1) * rows, :] = refs[place * 3 + part][...]
            for block in range(rows // HD):
                taken = refs[place * 3 + 2][block * HD : (block + 1) * HD, :]
                lower = 2 * rows + block * HD
                outs[place][lower : lower + HD, :] = jnp.transpose(taken)
            if docs is not None:
                outs[place][3 * rows :, :] = mine

    def piece(distance):
        return pl.BlockSpec((rows, HD), lambda step, ctx: (half, ctx[0] ^ distance))

    in_specs = []
    operands = []
    for distance in range(1, group):
        for array in (queries, keys, values):
            in_specs.append(piece(distance))
            operands.append(array)
    if docs is not None:
        in_specs.append(whole(docs.shape))
        operands.append(docs)
    return pl.pallas_call(
        kernel,
        grid_spec=pltpu.PrefetchScalarGridSpec(
            num_scalar_prefetch=1,
            grid=(1,),
            in_specs=in_specs,
            out_specs=[whole((total, HD))] * (group - 1),
        ),
        out_shape=[jax.ShapeDtypeStruct((total, HD), jnp.bfloat16)] * (group - 1),
        compiler_params=params(56),
        cost_estimate=SMALL,
        name="pack",
    )(ctx_index, *operands)


def attend(ctx_index, queries, keys, values, docs, low, high):
    rows = queries.shape[0] // 2
    group = queries.shape[1] // HD
    with_high = high is not None
    per_block = rows // TILE
    lines = rows // HD
    key_rows = (2 * group if with_high else group) * rows
    key_tiles = key_rows // TILE
    scaling = LOG2E / math.sqrt(HD)

    def kernel(ctx_ref, *refs):
        refs = list(refs)
        own_low = [refs.pop(0) for _ in range(3)]
        own_high = [refs.pop(0) for _ in range(3)] if with_high else None
        own_docs = refs.pop(0)
        low_refs = [refs.pop(0) for _ in range(group - 1)]
        high_refs = [refs.pop(0) for _ in range(group - 1)] if with_high else None
        outs = [refs.pop(0) for _ in range(group)]
        key_buf, value_buf, doc_buf = refs[:3]
        query_buf, start_buf, largest_buf, summed = (
            refs[3 + kind * group : 3 + (kind + 1) * group] for kind in range(4)
        )
        ctx = ctx_ref[0]

        def part(upper, distance, index, lower=0, count=rows):
            if distance == 0:
                return (own_high if upper else own_low)[index][lower : lower + count, :]
            source = (high_refs if upper else low_refs)[distance - 1]
            return source[index * rows + lower : index * rows + lower + count, :]

        place = {}
        doc_rows = {}
        for upper in (False, True) if with_high else (False,):
            for distance in range(group):
                source = ctx ^ distance
                block = 2 * group - 1 - source if upper else source
                place[upper, distance] = block
                offset = pl.multiple_of(block * rows, rows)
                key_buf[pl.ds(offset, rows), :] = part(upper, distance, 1)
                if distance == 0:
                    both = own_docs[...].astype(jnp.float32)
                else:
                    both = low_refs[distance - 1][3 * rows :, :].astype(jnp.float32)
                begin = lines if upper else 0
                mine = []
                for line in range(lines):
                    taken = part(upper, distance, 2, line * HD, HD)
                    if distance == 0:
                        taken = jnp.transpose(taken)
                    column = pl.multiple_of(block * rows + line * HD, HD)
                    value_buf[:HD, pl.ds(column, HD)] = taken
                    mine.append(both[begin + line : begin + line + 1, :])
                    doc_buf[pl.ds(block * lines + line, 1), :] = mine[-1]
                doc_rows[upper, distance] = jnp.concatenate(mine, axis=1)
        value_buf[HD:, :] = jnp.ones((value_buf.shape[0] - HD, key_rows), jnp.bfloat16)

        all_docs = doc_buf[...]
        starts = [jnp.zeros((1, rows), jnp.float32)] * group
        for number in range(1, MOST_DOCS):
            smaller = jnp.where(all_docs < number, 1.0, 0.0)
            count = jnp.sum(jnp.sum(smaller, axis=0, keepdims=True), axis=1, keepdims=True)
            for distance in range(group):
                reached = doc_rows[with_high, distance] >= number
                starts[distance] = jnp.where(reached, count, starts[distance])

        def scores_of(query, offset):
            raw = lax.dot_general(
                key_buf[pl.ds(offset, TILE), :],
                query,
                (((1,), (1,)), ((), ())),
                preferred_element_type=jnp.float32,
            )
            return raw * scaling

        def weighted(weights, offset):
            return jnp.dot(
                value_buf[:, pl.ds(offset, TILE)],
                weights.astype(jnp.bfloat16),
                preferred_element_type=jnp.float32,
            )

        key_row = lax.broadcasted_iota(jnp.int32, (TILE, TILE), 0)
        causal = key_row <= lax.broadcasted_iota(jnp.int32, (TILE, TILE), 1)
        key_row = key_row.astype(jnp.float32)
        firsts = []
        counts = []
        for lane in range(group):
            for slot in range(per_block):
                distance = lane ^ (slot * (group - 1))
                query = part(with_high, distance, 0, slot * TILE, TILE)
                query_buf[lane][slot] = query
                start = starts[distance][:, slot * TILE : (slot + 1) * TILE]
                start_buf[lane][slot, 0:1, :] = start
                end = place[with_high, distance] * per_block + slot
                offset = pl.multiple_of(end * TILE, TILE)
                least = start - offset.astype(jnp.float32)
                scores = scores_of(query, offset)
                scores = jnp.where((key_row >= least) & causal, scores, MASKED_SCORE)
                largest = jnp.max(scores, axis=0, keepdims=True)
                largest_buf[lane][slot, 0:1, :] = largest
                summed[lane][slot] = weighted(jnp.exp2(scores - largest), offset)
                first = jnp.min(start).astype(jnp.int32) // TILE
                firsts.append(first)
                counts.append(end - first)

        longest = jnp.int32(0)
        for lane in range(group):
            of_lane = counts[lane * per_block : (lane + 1) * per_block]
            longest = jnp.maximum(longest, sum(of_lane))

        def visit(step, carry):
            slots = []
            offsets = []
            beyonds = []
            for lane in range(group):
                slot = jnp.int32(0)
                index = firsts[lane * per_block] + step
                before = counts[lane * per_block]
                for later in range(1, per_block):
                    reached = step >= before
                    slot = jnp.where(reached, later, slot)
                    place_later = lane * per_block + later
                    index = jnp.where(reached, firsts[place_later] + step - before, index)
                    before = before + counts[place_later]
                offset = pl.multiple_of(jnp.minimum(index, key_tiles - 1) * TILE, TILE)
                slots.append(slot)
                offsets.append(offset)
                beyonds.append(jnp.where(step < before, -offset.astype(jnp.float32), 1e9))
            each = range(group)
            scores = [scores_of(query_buf[lane][slots[lane]], offsets[lane]) for lane in each]
            old_max = [largest_buf[lane][slots[lane], 0:1, :] for lane in each]
            new_max = []
            for lane in each:
                least = start_buf[lane][slots[lane], 0:1, :] + beyonds[lane]
                scores[lane] = jnp.where(key_row >= least, scores[lane], MASKED_SCORE)
                tile_max = jnp.max(scores[lane], axis=0, keepdims=True)
                new_max.append(jnp.maximum(old_max[lane], tile_max))
            products = [
                weighted(jnp.exp2(scores[lane] - new_max[lane]), offsets[lane]) for lane in each
            ]
            for lane in each:
                factor = jnp.exp2(old_max[lane] - new_max[lane])
                summed[lane][slots[lane]] = summed[lane][slots[lane]] * factor + products[lane]
                largest_buf[lane][slots[lane], 0:1, :] = new_max[lane]
            return carry

        lax.fori_loop(0, longest, visit, jnp.int32(0))
        for lane in range(group):
            for slot in range(per_block):
                state = summed[lane]
                attended = state[slot, :HD, :] / state[slot, HD : HD + 1, :]
                out = outs[lane ^ (slot * (group - 1))]
                out[slot * TILE : (slot + 1) * TILE, :] = jnp.transpose(attended).astype(
                    jnp.bfloat16
                )

    def own(upper):
        return pl.BlockSpec((rows, HD), lambda step, ctx: (int(upper), ctx[0]))

    in_specs = [own(False)] * 3
    operands = [queries, keys, values]
    if with_high:
        in_specs += [own(True)] * 3
        operands += [queries, keys, values]
    received = [docs, *low, *(high if with_high else ())]
    operands += received
    in_specs += [whole(array.shape) for array in received]
    return pl.pallas_call(
        kernel,
        grid_spec=pltpu.PrefetchScalarGridSpec(
            num_scalar_prefetch=1,
            grid=(1,),
            in_specs=in_specs,
            out_specs=[whole((rows, HD))] * group,
            scratch_shapes=[
                pltpu.VMEM((key_rows, HD), jnp.bfloat16),
                pltpu.VMEM((HD + 16, key_rows), jnp.bfloat16),
                pltpu.VMEM((key_rows // HD, HD), jnp.float32),
                *[pltpu.VMEM((per_block, TILE, HD), jnp.bfloat16)] * group,
                *[pltpu.VMEM((per_block, 8, TILE), jnp.float32)] * (2 * group),
                *[pltpu.VMEM((per_block, HD + 16, TILE), jnp.float32)] * group,
            ],
        ),
        out_shape=[jax.ShapeDtypeStruct((rows, HD), jnp.bfloat16)] * group,
        compiler_params=params(40),
        cost_estimate=SMALL,
        name="attend_high" if with_high else "attend_low",
    )(ctx_index, *operands)


def assemble(ctx_index, pieces):
    rows = pieces[0].shape[0]
    group = len(pieces)

    def kernel(ctx_ref, *refs):
        for distance in range(group):
            column = pl.multiple_of((ctx_ref[0] ^ distance) * HD, HD)
            refs[-1][:, pl.ds(column, HD)] = refs[distance][...]

    return pl.pallas_call(
        kernel,
        grid_spec=pltpu.PrefetchScalarGridSpec(
            num_scalar_prefetch=1,
            grid=(1,),
            in_specs=[whole((rows, HD))] * group,
            out_specs=whole((rows, group * HD)),
        ),
        out_shape=jax.ShapeDtypeStruct((rows, group * HD), jnp.bfloat16),
        compiler_params=params(16),
        cost_estimate=SMALL,
        name="assemble",
    )(ctx_index, *pieces)


def project(places, turn, mine, sibling, w_mine, w_sibling):
    rows, depth = mine.shape
    columns = w_mine.shape[1] // (2 * len(TURNS))

    def kernel(places_ref, mine_ref, sibling_ref, w_mine_ref, w_sibling_ref, out_ref):
        total = jnp.dot(mine_ref[...], w_mine_ref[...], preferred_element_type=jnp.float32)
        total += jnp.dot(sibling_ref[...], w_sibling_ref[...], preferred_element_type=jnp.float32)
        out_ref[...] = total.astype(jnp.bfloat16)

    weights = pl.BlockSpec((depth, columns), lambda step, at: (0, at[turn]))
    return pl.pallas_call(
        kernel,
        grid_spec=pltpu.PrefetchScalarGridSpec(
            num_scalar_prefetch=1,
            grid=(1,),
            in_specs=[whole((rows, depth)), whole((rows, depth)), weights, weights],
            out_specs=whole((rows, columns)),
        ),
        out_shape=jax.ShapeDtypeStruct((rows, columns), jnp.bfloat16),
        compiler_params=params(16),
        cost_estimate=SMALL,
        name="project",
    )(places, mine, sibling, w_mine, w_sibling)


def swap(value, axis, distance):
    count = lax.axis_size(axis)
    return lax.ppermute(value, axis, [(source, source ^ distance) for source in range(count)])


def add(*terms):
    total = terms[0].astype(jnp.float32)
    for term in terms[1:]:
        total = total + term.astype(jnp.float32)
    return total.astype(jnp.bfloat16)


TURNS = (3, 1, 2, 0)


def tie(*values):
    return lax.optimization_barrier(values)


def exchange_local(queries, keys, values, doc_ids, w_out):
    shard_rows = queries.shape[0]
    group = queries.shape[1] // HD
    ctx_index = lax.axis_index("ctx").astype(jnp.int32).reshape(1)
    head_index = lax.axis_index("head").astype(jnp.int32)
    places = head_index ^ (2 * jnp.array(TURNS, jnp.int32))
    docs = doc_ids.reshape(shard_rows // HD, HD)
    near = range(1, group)

    w_sibling = swap(w_out, "head", 1)
    low_out = pack(ctx_index, 0, queries, keys, values, docs)
    low_out, later = tie(low_out, (queries, keys, values))
    low = [swap(low_out[distance - 1], "ctx", distance) for distance in near]
    high_out = pack(ctx_index, 1, *later, None)
    high_out, low = tie(high_out, low)
    high = [swap(high_out[0], "ctx", 1), swap(high_out[1], "ctx", 2)]

    def send_back(pieces):
        return [swap(pieces[distance], "ctx", distance) for distance in near]

    def share_of(mine, sibling, turn):
        return project(places, turn, mine, sibling, w_out, w_sibling)

    pieces = attend(ctx_index, queries, keys, values, docs, low, None)
    pieces, diagonal_out, w_sibling = tie(pieces, high_out[2], w_sibling)
    back = send_back(pieces)
    back, high = tie(back, high)
    high.append(swap(diagonal_out, "ctx", 3))
    mine = assemble(ctx_index, [pieces[0], *back])
    sibling = swap(mine, "head", 1)
    shares = [share_of(mine, sibling, turn) for turn in range(len(TURNS))]
    far = swap(shares[0], "head", 2)
    shares[1], high[2] = tie(shares[1], high[2])
    near_sum = swap(shares[1], "head", 2)

    passed = add(shares[2], far)
    high, shares, passed = tie(high, shares, passed)
    across = swap(passed, "head", 4)
    pieces = attend(ctx_index, queries, keys, values, docs, low, high)
    back = send_back(pieces)
    mine = assemble(ctx_index, [pieces[0], *back])
    mine, across, near_sum = tie(mine, across, near_sum)
    first = add(shares[3], near_sum, across)
    sibling = swap(mine, "head", 1)
    late = [share_of(mine, sibling, turn) for turn in range(len(TURNS))]
    far = swap(late[0], "head", 2)
    near_sum = swap(late[1], "head", 2)
    across = swap(add(late[2], far), "head", 4)
    second = add(late[3], near_sum, across)
    return jnp.concatenate([first, second], axis=0)


def solution(mesh):
    in_specs = (P("ctx", "head"), P("ctx", "head"), P("ctx", "head"), P("ctx"), P("head", None))
    out_specs = P("ctx", "head")
    ctx_count = mesh.shape["ctx"]
    head_count = mesh.shape["head"]

    def local(queries, keys, values, doc_ids, w_out):
        heads = queries.shape[1] // HD
        exchange = heads == ctx_count and heads == 4 and head_count == 2 * len(TURNS)
        exchange = exchange and queries.shape[0] % (4 * TILE) == 0
        body = exchange_local if exchange else ring_local
        return body(queries, keys, values, doc_ids, w_out)

    return jax.shard_map(
        local, mesh=mesh, in_specs=in_specs, out_specs=out_specs, check_vma=False
    )
```

```python
import functools
import math

import jax
import jax.numpy as jnp
from jax import lax
from jax.experimental import pallas as pl
from jax.experimental.pallas import tpu as pltpu
from jax.sharding import PartitionSpec as P

HD = 128


MASKED_SCORE = -1e30
LOG2E = 1.4426950408889634


def passed_along(value, axis, steps):
    count = lax.axis_size(axis)
    pairs = [(source, (source + steps) % count) for source in range(count)]
    return lax.ppermute(value, axis, pairs)


def folded_positions(row_total, offset, shard_rows, devices_ctx):
    flat_index = offset + lax.iota(jnp.int32, row_total)
    owner_dev = flat_index // shard_rows
    within = flat_index % shard_rows
    half_rows = shard_rows // 2
    fold_block = jnp.where(within < half_rows, owner_dev, 2 * devices_ctx - 1 - owner_dev)
    return fold_block * half_rows + within % half_rows


def block_update(
    running, query, query_pos, query_doc, key_block, value_block, pos_block, doc_block
):
    largest, totals, summed = running
    query_rows = query.shape[0]
    local_heads = query.shape[1] // HD
    query_heads = query.reshape(query_rows, local_heads, HD)
    key_heads = key_block.reshape(key_block.shape[0], local_heads, HD)
    value_heads = value_block.reshape(value_block.shape[0], local_heads, HD)
    scores = jnp.einsum(
        "qhd,khd->hqk", query_heads, key_heads, preferred_element_type=jnp.float32
    ) * (1.0 / math.sqrt(HD))
    allowed = (query_doc[:, None] == doc_block[None, :]) & (
        pos_block[None, :] <= query_pos[:, None]
    )
    scores = jnp.where(allowed[None], scores, MASKED_SCORE)
    new_max = jnp.maximum(largest, jnp.max(scores, axis=2))
    weights = jnp.where(allowed[None], jnp.exp(scores - new_max[:, :, None]), 0.0)
    factor = jnp.exp(largest - new_max)
    totals = totals * factor + jnp.sum(weights, axis=2)
    product = jnp.einsum(
        "hqk,khd->qhd",
        weights.astype(jnp.bfloat16),
        value_heads,
        preferred_element_type=jnp.float32,
    )
    summed = summed * factor.T[:, :, None] + product
    return (new_max, totals, summed)


def attend_rows(running, query, query_pos, query_doc, key_rows, value_rows, key_pos, key_doc):
    row_total = key_rows.shape[0]
    block_rows = math.gcd(row_total, query.shape[0])
    block_count = row_total // block_rows
    highest = jnp.max(query_pos)

    def visit(partial_value, blocks):
        key_block, value_block, pos_block, doc_block = blocks
        masked_out = jnp.min(pos_block) > highest
        updated = lax.cond(
            masked_out,
            lambda frozen: frozen,
            lambda frozen: block_update(
                frozen, query, query_pos, query_doc, key_block, value_block, pos_block, doc_block
            ),
            partial_value,
        )
        return (updated, None)

    blocks = (
        key_rows.reshape(block_count, block_rows, key_rows.shape[1]),
        value_rows.reshape(block_count, block_rows, value_rows.shape[1]),
        key_pos.reshape(block_count, block_rows),
        key_doc.reshape(block_count, block_rows),
    )
    running, _ = lax.scan(visit, running, blocks)
    return running


def attend_shard(running, query, query_pos, query_doc, key_rows, value_rows, key_pos, key_doc):
    largest, totals, summed = running
    half_rows = query.shape[0] // 2
    new_largest = []
    new_totals = []
    new_summed = []
    for half_idx in range(2):
        lower = half_idx * half_rows
        part_state = (largest[half_idx], totals[half_idx], summed[half_idx])
        part_state = attend_rows(
            part_state,
            query[lower : lower + half_rows],
            query_pos[lower : lower + half_rows],
            query_doc[lower : lower + half_rows],
            key_rows,
            value_rows,
            key_pos,
            key_doc,
        )
        new_largest.append(part_state[0])
        new_totals.append(part_state[1])
        new_summed.append(part_state[2])
    return (jnp.stack(new_largest), jnp.stack(new_totals), jnp.stack(new_summed))


def ring_local(queries, keys, values, doc_ids, w_out):
    shard_rows = queries.shape[0]
    half_rows = shard_rows // 2
    local_heads = queries.shape[1] // HD
    devices_ctx = lax.axis_size("ctx")
    ctx_index = lax.axis_index("ctx")
    all_docs = lax.all_gather(doc_ids, "ctx", axis=0, tiled=True)
    own_pos = folded_positions(shard_rows, ctx_index * shard_rows, shard_rows, devices_ctx)
    running = (
        jnp.full((2, local_heads, half_rows), MASKED_SCORE, jnp.float32),
        jnp.zeros((2, local_heads, half_rows), jnp.float32),
        jnp.zeros((2, half_rows, local_heads, HD), jnp.float32),
    )
    travel = queries
    for hop_step in range(devices_ctx):
        anchor = (ctx_index - hop_step) % devices_ctx
        query_pos = folded_positions(shard_rows, anchor * shard_rows, shard_rows, devices_ctx)
        query_doc = lax.dynamic_slice_in_dim(all_docs, anchor * shard_rows, shard_rows, 0)
        largest, totals, summed = attend_shard(
            running, travel, query_pos, query_doc, keys, values, own_pos, doc_ids
        )
        running = (
            passed_along(largest.astype(jnp.bfloat16), "ctx", 1).astype(largest.dtype),
            passed_along(totals.astype(jnp.bfloat16), "ctx", 1).astype(totals.dtype),
            passed_along(summed.astype(jnp.bfloat16), "ctx", 1).astype(summed.dtype),
        )
        if hop_step + 1 < devices_ctx:
            travel = passed_along(travel, "ctx", 1)
    largest, totals, summed = running
    attended = summed / totals.transpose(0, 2, 1)[:, :, :, None]
    attended = attended.reshape(shard_rows, local_heads * HD).astype(jnp.bfloat16)
    partial_out = jnp.dot(attended, w_out, preferred_element_type=jnp.float32)
    return lax.psum_scatter(
        partial_out.astype(jnp.bfloat16), "head", scatter_dimension=1, tiled=True
    )


SMALL = pl.CostEstimate(flops=1024, bytes_accessed=1024, transcendentals=0)
TILE = 256
MOST_DOCS = 16


def params(mib):
    return pltpu.CompilerParams(vmem_limit_bytes=mib * 1024 * 1024)


def whole(shape):
    return pl.BlockSpec(shape, lambda step, scalars: (0,) * len(shape))


def pack(ctx_index, half, queries, keys, values, docs):
    rows = queries.shape[0] // 2
    group = queries.shape[1] // HD
    doc_rows = 0 if docs is None else 16 * pl.cdiv(docs.shape[0], 16)
    total = 3 * rows + doc_rows

    def kernel(ctx_ref, *refs):
        outs = refs[len(refs) - (group - 1) :]
        if docs is not None:
            mine = refs[3 * (group - 1)][...].astype(jnp.float32)
            empty = jnp.zeros((doc_rows - mine.shape[0], HD), jnp.float32)
            mine = jnp.concatenate([mine, empty], axis=0).astype(jnp.bfloat16)
        for place in range(group - 1):
            for part in range(2):
                outs[place][part * rows : (part + 1) * rows, :] = refs[place * 3 + part][...]
            for block in range(rows // HD):
                taken = refs[place * 3 + 2][block * HD : (block + 1) * HD, :]
                lower = 2 * rows + block * HD
                outs[place][lower : lower + HD, :] = jnp.transpose(taken)
            if docs is not None:
                outs[place][3 * rows :, :] = mine

    def piece(distance):
        return pl.BlockSpec((rows, HD), lambda step, ctx: (half, ctx[0] ^ distance))

    in_specs = []
    operands = []
    for distance in range(1, group):
        for array in (queries, keys, values):
            in_specs.append(piece(distance))
            operands.append(array)
    if docs is not None:
        in_specs.append(whole(docs.shape))
        operands.append(docs)
    return pl.pallas_call(
        kernel,
        grid_spec=pltpu.PrefetchScalarGridSpec(
            num_scalar_prefetch=1,
            grid=(1,),
            in_specs=in_specs,
            out_specs=[whole((total, HD))] * (group - 1),
        ),
        out_shape=[jax.ShapeDtypeStruct((total, HD), jnp.bfloat16)] * (group - 1),
        compiler_params=params(56),
        cost_estimate=SMALL,
        name="pack",
    )(ctx_index, *operands)


def pack_projection(places, w_mine, w_sibling):
    depth, width = w_mine.shape
    turns = len(TURNS)
    columns = width // (2 * turns)

    def kernel(places_ref, mine_in, sibling_in, mine_out, sibling_out):
        mine_out[...] = mine_in[...]
        sibling_out[...] = sibling_in[...]

    in_spec = pl.BlockSpec((depth, columns), lambda turn, at: (0, at[turn]))
    out_spec = pl.BlockSpec((depth, columns), lambda turn, at: (0, turn))
    return pl.pallas_call(
        kernel,
        grid_spec=pltpu.PrefetchScalarGridSpec(
            num_scalar_prefetch=1,
            grid=(turns,),
            in_specs=[in_spec] * 2,
            out_specs=[out_spec] * 2,
        ),
        out_shape=[jax.ShapeDtypeStruct((depth, turns * columns), w_mine.dtype)] * 2,
        compiler_params=params(56),
        cost_estimate=SMALL,
        name="pack_projection",
    )(places, w_mine, w_sibling)


def attend(ctx_index, queries, keys, values, docs, low, high):
    rows = queries.shape[0] // 2
    group = queries.shape[1] // HD
    with_high = high is not None
    per_block = rows // TILE
    lines = rows // HD
    key_rows = (2 * group if with_high else group) * rows
    key_tiles = key_rows // TILE
    scaling = LOG2E / math.sqrt(HD)

    def kernel(ctx_ref, *refs):
        refs = list(refs)
        own_low = [refs.pop(0) for _ in range(3)]
        own_high = [refs.pop(0) for _ in range(3)] if with_high else None
        own_docs = refs.pop(0)
        low_refs = [refs.pop(0) for _ in range(group - 1)]
        high_refs = [refs.pop(0) for _ in range(group - 1)] if with_high else None
        outs = [refs.pop(0) for _ in range(group)]
        key_buf, value_buf, doc_buf = refs[:3]
        query_buf, start_buf, largest_buf, summed = (
            refs[3 + kind * group : 3 + (kind + 1) * group] for kind in range(4)
        )
        ctx = ctx_ref[0]

        def part(upper, distance, index, lower=0, count=rows):
            if distance == 0:
                return (own_high if upper else own_low)[index][lower : lower + count, :]
            source = (high_refs if upper else low_refs)[distance - 1]
            return source[index * rows + lower : index * rows + lower + count, :]

        place = {}
        doc_rows = {}
        for upper in (False, True) if with_high else (False,):
            for distance in range(group):
                source = ctx ^ distance
                block = 2 * group - 1 - source if upper else source
                place[upper, distance] = block
                offset = pl.multiple_of(block * rows, rows)
                key_buf[pl.ds(offset, rows), :] = part(upper, distance, 1)
                if distance == 0:
                    both = own_docs[...].astype(jnp.float32)
                else:
                    both = low_refs[distance - 1][3 * rows :, :].astype(jnp.float32)
                begin = lines if upper else 0
                mine = []
                for line in range(lines):
                    taken = part(upper, distance, 2, line * HD, HD)
                    if distance == 0:
                        taken = jnp.transpose(taken)
                    column = pl.multiple_of(block * rows + line * HD, HD)
                    value_buf[:HD, pl.ds(column, HD)] = taken
                    mine.append(both[begin + line : begin + line + 1, :])
                    doc_buf[pl.ds(block * lines + line, 1), :] = mine[-1]
                doc_rows[upper, distance] = jnp.concatenate(mine, axis=1)
        value_buf[HD:, :] = jnp.ones((value_buf.shape[0] - HD, key_rows), jnp.bfloat16)

        all_docs = doc_buf[...]
        starts = [jnp.zeros((1, rows), jnp.float32)] * group
        for number in range(1, MOST_DOCS):
            smaller = jnp.where(all_docs < number, 1.0, 0.0)
            count = jnp.sum(jnp.sum(smaller, axis=0, keepdims=True), axis=1, keepdims=True)
            for distance in range(group):
                reached = doc_rows[with_high, distance] >= number
                starts[distance] = jnp.where(reached, count, starts[distance])

        def scores_of(query, offset):
            raw = lax.dot_general(
                key_buf[pl.ds(offset, TILE), :],
                query,
                (((1,), (1,)), ((), ())),
                preferred_element_type=jnp.float32,
            )
            return raw * scaling

        def weighted(weights, offset):
            return jnp.dot(
                value_buf[:, pl.ds(offset, TILE)],
                weights.astype(jnp.bfloat16),
                preferred_element_type=jnp.float32,
            )

        key_row = lax.broadcasted_iota(jnp.int32, (TILE, TILE), 0)
        causal = key_row <= lax.broadcasted_iota(jnp.int32, (TILE, TILE), 1)
        key_row = key_row.astype(jnp.float32)
        firsts = []
        counts = []
        for lane in range(group):
            for slot in range(per_block):
                distance = lane ^ (slot * (group - 1))
                query = part(with_high, distance, 0, slot * TILE, TILE)
                query_buf[lane][slot] = query
                start = starts[distance][:, slot * TILE : (slot + 1) * TILE]
                start_buf[lane][slot, 0:1, :] = start
                end = place[with_high, distance] * per_block + slot
                offset = pl.multiple_of(end * TILE, TILE)
                least = start - offset.astype(jnp.float32)
                scores = scores_of(query, offset)
                scores = jnp.where((key_row >= least) & causal, scores, MASKED_SCORE)
                largest = jnp.max(scores, axis=0, keepdims=True)
                largest_buf[lane][slot, 0:1, :] = largest
                summed[lane][slot] = weighted(jnp.exp2(scores - largest), offset)
                first = jnp.min(start).astype(jnp.int32) // TILE
                firsts.append(first)
                counts.append(end - first)

        longest = jnp.int32(0)
        for lane in range(group):
            of_lane = counts[lane * per_block : (lane + 1) * per_block]
            longest = jnp.maximum(longest, sum(of_lane))

        def visit(step, carry):
            slots = []
            offsets = []
            beyonds = []
            for lane in range(group):
                slot = jnp.int32(0)
                index = firsts[lane * per_block] + step
                before = counts[lane * per_block]
                for later in range(1, per_block):
                    reached = step >= before
                    slot = jnp.where(reached, later, slot)
                    place_later = lane * per_block + later
                    index = jnp.where(reached, firsts[place_later] + step - before, index)
                    before = before + counts[place_later]
                offset = pl.multiple_of(jnp.minimum(index, key_tiles - 1) * TILE, TILE)
                slots.append(slot)
                offsets.append(offset)
                beyonds.append(jnp.where(step < before, -offset.astype(jnp.float32), 1e9))
            each = range(group)
            scores = [scores_of(query_buf[lane][slots[lane]], offsets[lane]) for lane in each]
            old_max = [largest_buf[lane][slots[lane], 0:1, :] for lane in each]
            new_max = []
            for lane in each:
                least = start_buf[lane][slots[lane], 0:1, :] + beyonds[lane]
                scores[lane] = jnp.where(key_row >= least, scores[lane], MASKED_SCORE)
                tile_max = jnp.max(scores[lane], axis=0, keepdims=True)
                new_max.append(jnp.maximum(old_max[lane], tile_max))
            products = [
                weighted(jnp.exp2(scores[lane] - new_max[lane]), offsets[lane]) for lane in each
            ]
            for lane in each:
                factor = jnp.exp2(old_max[lane] - new_max[lane])
                summed[lane][slots[lane]] = summed[lane][slots[lane]] * factor + products[lane]
                largest_buf[lane][slots[lane], 0:1, :] = new_max[lane]
            return carry

        lax.fori_loop(0, longest, visit, jnp.int32(0))
        for lane in range(group):
            for slot in range(per_block):
                state = summed[lane]
                attended = state[slot, :HD, :] / state[slot, HD : HD + 1, :]
                out = outs[lane ^ (slot * (group - 1))]
                out[slot * TILE : (slot + 1) * TILE, :] = jnp.transpose(attended).astype(
                    jnp.bfloat16
                )

    def own(upper):
        return pl.BlockSpec((rows, HD), lambda step, ctx: (int(upper), ctx[0]))

    in_specs = [own(False)] * 3
    operands = [queries, keys, values]
    if with_high:
        in_specs += [own(True)] * 3
        operands += [queries, keys, values]
    received = [docs, *low, *(high if with_high else ())]
    operands += received
    in_specs += [whole(array.shape) for array in received]
    return pl.pallas_call(
        kernel,
        grid_spec=pltpu.PrefetchScalarGridSpec(
            num_scalar_prefetch=1,
            grid=(1,),
            in_specs=in_specs,
            out_specs=[whole((rows, HD))] * group,
            scratch_shapes=[
                pltpu.VMEM((key_rows, HD), jnp.bfloat16),
                pltpu.VMEM((HD + 16, key_rows), jnp.bfloat16),
                pltpu.VMEM((key_rows // HD, HD), jnp.float32),
                *[pltpu.VMEM((per_block, TILE, HD), jnp.bfloat16)] * group,
                *[pltpu.VMEM((per_block, 8, TILE), jnp.float32)] * (2 * group),
                *[pltpu.VMEM((per_block, HD + 16, TILE), jnp.float32)] * group,
            ],
        ),
        out_shape=[jax.ShapeDtypeStruct((rows, HD), jnp.bfloat16)] * group,
        compiler_params=params(40),
        cost_estimate=SMALL,
        name="attend_high" if with_high else "attend_low",
    )(ctx_index, *operands)


def assemble(ctx_index, pieces):
    rows = pieces[0].shape[0]
    group = len(pieces)

    def kernel(ctx_ref, *refs):
        for distance in range(group):
            column = pl.multiple_of((ctx_ref[0] ^ distance) * HD, HD)
            refs[-1][:, pl.ds(column, HD)] = refs[distance][...]

    return pl.pallas_call(
        kernel,
        grid_spec=pltpu.PrefetchScalarGridSpec(
            num_scalar_prefetch=1,
            grid=(1,),
            in_specs=[whole((rows, HD))] * group,
            out_specs=whole((rows, group * HD)),
        ),
        out_shape=jax.ShapeDtypeStruct((rows, group * HD), jnp.bfloat16),
        compiler_params=params(16),
        cost_estimate=SMALL,
        name="assemble",
    )(ctx_index, *pieces)


def project(turn, mine, sibling, w_mine, w_sibling):
    rows, depth = mine.shape
    columns = w_mine.shape[1] // len(TURNS)

    def kernel(mine_ref, sibling_ref, w_mine_ref, w_sibling_ref, out_ref):
        total = jnp.dot(mine_ref[...], w_mine_ref[...], preferred_element_type=jnp.float32)
        total += jnp.dot(sibling_ref[...], w_sibling_ref[...], preferred_element_type=jnp.float32)
        out_ref[...] = total.astype(jnp.bfloat16)

    weights = pl.BlockSpec((depth, columns), lambda step: (0, turn))
    attended = pl.BlockSpec((rows, depth), lambda step: (0, 0))
    return pl.pallas_call(
        kernel,
        grid=(1,),
        in_specs=[attended, attended, weights, weights],
        out_specs=pl.BlockSpec((rows, columns), lambda step: (0, 0)),
        out_shape=jax.ShapeDtypeStruct((rows, columns), jnp.bfloat16),
        compiler_params=params(16),
        cost_estimate=SMALL,
        name="project",
    )(mine, sibling, w_mine, w_sibling)


def swap(value, axis, distance):
    count = lax.axis_size(axis)
    return lax.ppermute(value, axis, [(source, source ^ distance) for source in range(count)])


def add(*terms):
    total = terms[0].astype(jnp.float32)
    for term in terms[1:]:
        total = total + term.astype(jnp.float32)
    return total.astype(jnp.bfloat16)


TURNS = (3, 1, 2, 0)


def tie(*values):
    return lax.optimization_barrier(values)


def exchange_local(queries, keys, values, doc_ids, w_out):
    shard_rows = queries.shape[0]
    group = queries.shape[1] // HD
    ctx_index = lax.axis_index("ctx").astype(jnp.int32).reshape(1)
    head_index = lax.axis_index("head").astype(jnp.int32)
    places = head_index ^ (2 * jnp.array(TURNS, jnp.int32))
    docs = doc_ids.reshape(shard_rows // HD, HD)
    near = range(1, group)

    w_sibling = swap(w_out, "head", 1)
    low_out = pack(ctx_index, 0, queries, keys, values, docs)
    low_out, later = tie(low_out, (queries, keys, values))
    low = [swap(low_out[distance - 1], "ctx", distance) for distance in near]
    high_out = pack(ctx_index, 1, *later, None)
    w_packed = pack_projection(places, w_out, w_sibling)
    high_out, low, w_packed = tie(high_out, low, w_packed)
    high = [swap(high_out[0], "ctx", 1), swap(high_out[1], "ctx", 2)]

    def send_back(pieces):
        return [swap(pieces[distance], "ctx", distance) for distance in near]

    def share_of(mine, sibling, turn):
        return project(turn, mine, sibling, *w_packed)

    pieces = attend(ctx_index, queries, keys, values, docs, low, None)
    pieces, diagonal_out = tie(pieces, high_out[2])
    back = send_back(pieces)
    back, high = tie(back, high)
    high.append(swap(diagonal_out, "ctx", 3))
    mine = assemble(ctx_index, [pieces[0], *back])
    sibling = swap(mine, "head", 1)
    shares = [share_of(mine, sibling, turn) for turn in range(len(TURNS))]
    far = swap(shares[0], "head", 2)
    shares[1], high[2] = tie(shares[1], high[2])
    near_sum = swap(shares[1], "head", 2)

    passed = add(shares[2], far)
    high, shares, passed = tie(high, shares, passed)
    across = swap(passed, "head", 4)
    pieces = attend(ctx_index, queries, keys, values, docs, low, high)
    back = send_back(pieces)
    mine = assemble(ctx_index, [pieces[0], *back])
    mine, across, near_sum = tie(mine, across, near_sum)
    first = add(shares[3], near_sum, across)
    sibling = swap(mine, "head", 1)
    late = [share_of(mine, sibling, turn) for turn in range(len(TURNS))]
    far = swap(late[0], "head", 2)
    near_sum = swap(late[1], "head", 2)
    across = swap(add(late[2], far), "head", 4)
    second = add(late[3], near_sum, across)
    return jnp.concatenate([first, second], axis=0)


def solution(mesh):
    in_specs = (P("ctx", "head"), P("ctx", "head"), P("ctx", "head"), P("ctx"), P("head", None))
    out_specs = P("ctx", "head")
    ctx_count = mesh.shape["ctx"]
    head_count = mesh.shape["head"]

    def local(queries, keys, values, doc_ids, w_out):
        heads = queries.shape[1] // HD
        exchange = heads == ctx_count and heads == 4 and head_count == 2 * len(TURNS)
        exchange = exchange and queries.shape[0] % (4 * TILE) == 0
        body = exchange_local if exchange else ring_local
        return body(queries, keys, values, doc_ids, w_out)

    return jax.shard_map(
        local, mesh=mesh, in_specs=in_specs, out_specs=out_specs, check_vma=False
    )
```

```python
import functools
import math

import jax
import jax.numpy as jnp
from jax import lax
from jax.experimental import pallas as pl
from jax.experimental.pallas import tpu as pltpu
from jax.sharding import PartitionSpec as P

HD = 128


MASKED_SCORE = -1e30
LOG2E = 1.4426950408889634


def passed_along(value, axis, steps):
    count = lax.axis_size(axis)
    pairs = [(source, (source + steps) % count) for source in range(count)]
    return lax.ppermute(value, axis, pairs)


def folded_positions(row_total, offset, shard_rows, devices_ctx):
    flat_index = offset + lax.iota(jnp.int32, row_total)
    owner_dev = flat_index // shard_rows
    within = flat_index % shard_rows
    half_rows = shard_rows // 2
    fold_block = jnp.where(within < half_rows, owner_dev, 2 * devices_ctx - 1 - owner_dev)
    return fold_block * half_rows + within % half_rows


def block_update(
    running, query, query_pos, query_doc, key_block, value_block, pos_block, doc_block
):
    largest, totals, summed = running
    query_rows = query.shape[0]
    local_heads = query.shape[1] // HD
    query_heads = query.reshape(query_rows, local_heads, HD)
    key_heads = key_block.reshape(key_block.shape[0], local_heads, HD)
    value_heads = value_block.reshape(value_block.shape[0], local_heads, HD)
    scores = jnp.einsum(
        "qhd,khd->hqk", query_heads, key_heads, preferred_element_type=jnp.float32
    ) * (1.0 / math.sqrt(HD))
    allowed = (query_doc[:, None] == doc_block[None, :]) & (
        pos_block[None, :] <= query_pos[:, None]
    )
    scores = jnp.where(allowed[None], scores, MASKED_SCORE)
    new_max = jnp.maximum(largest, jnp.max(scores, axis=2))
    weights = jnp.where(allowed[None], jnp.exp(scores - new_max[:, :, None]), 0.0)
    factor = jnp.exp(largest - new_max)
    totals = totals * factor + jnp.sum(weights, axis=2)
    product = jnp.einsum(
        "hqk,khd->qhd",
        weights.astype(jnp.bfloat16),
        value_heads,
        preferred_element_type=jnp.float32,
    )
    summed = summed * factor.T[:, :, None] + product
    return (new_max, totals, summed)


def attend_rows(running, query, query_pos, query_doc, key_rows, value_rows, key_pos, key_doc):
    row_total = key_rows.shape[0]
    block_rows = math.gcd(row_total, query.shape[0])
    block_count = row_total // block_rows
    highest = jnp.max(query_pos)

    def visit(partial_value, blocks):
        key_block, value_block, pos_block, doc_block = blocks
        masked_out = jnp.min(pos_block) > highest
        updated = lax.cond(
            masked_out,
            lambda frozen: frozen,
            lambda frozen: block_update(
                frozen, query, query_pos, query_doc, key_block, value_block, pos_block, doc_block
            ),
            partial_value,
        )
        return (updated, None)

    blocks = (
        key_rows.reshape(block_count, block_rows, key_rows.shape[1]),
        value_rows.reshape(block_count, block_rows, value_rows.shape[1]),
        key_pos.reshape(block_count, block_rows),
        key_doc.reshape(block_count, block_rows),
    )
    running, _ = lax.scan(visit, running, blocks)
    return running


def attend_shard(running, query, query_pos, query_doc, key_rows, value_rows, key_pos, key_doc):
    largest, totals, summed = running
    half_rows = query.shape[0] // 2
    new_largest = []
    new_totals = []
    new_summed = []
    for half_idx in range(2):
        lower = half_idx * half_rows
        part_state = (largest[half_idx], totals[half_idx], summed[half_idx])
        part_state = attend_rows(
            part_state,
            query[lower : lower + half_rows],
            query_pos[lower : lower + half_rows],
            query_doc[lower : lower + half_rows],
            key_rows,
            value_rows,
            key_pos,
            key_doc,
        )
        new_largest.append(part_state[0])
        new_totals.append(part_state[1])
        new_summed.append(part_state[2])
    return (jnp.stack(new_largest), jnp.stack(new_totals), jnp.stack(new_summed))


def ring_local(queries, keys, values, doc_ids, w_out):
    shard_rows = queries.shape[0]
    half_rows = shard_rows // 2
    local_heads = queries.shape[1] // HD
    devices_ctx = lax.axis_size("ctx")
    ctx_index = lax.axis_index("ctx")
    all_docs = lax.all_gather(doc_ids, "ctx", axis=0, tiled=True)
    own_pos = folded_positions(shard_rows, ctx_index * shard_rows, shard_rows, devices_ctx)
    running = (
        jnp.full((2, local_heads, half_rows), MASKED_SCORE, jnp.float32),
        jnp.zeros((2, local_heads, half_rows), jnp.float32),
        jnp.zeros((2, half_rows, local_heads, HD), jnp.float32),
    )
    travel = queries
    for hop_step in range(devices_ctx):
        anchor = (ctx_index - hop_step) % devices_ctx
        query_pos = folded_positions(shard_rows, anchor * shard_rows, shard_rows, devices_ctx)
        query_doc = lax.dynamic_slice_in_dim(all_docs, anchor * shard_rows, shard_rows, 0)
        largest, totals, summed = attend_shard(
            running, travel, query_pos, query_doc, keys, values, own_pos, doc_ids
        )
        running = (
            passed_along(largest.astype(jnp.bfloat16), "ctx", 1).astype(largest.dtype),
            passed_along(totals.astype(jnp.bfloat16), "ctx", 1).astype(totals.dtype),
            passed_along(summed.astype(jnp.bfloat16), "ctx", 1).astype(summed.dtype),
        )
        if hop_step + 1 < devices_ctx:
            travel = passed_along(travel, "ctx", 1)
    largest, totals, summed = running
    attended = summed / totals.transpose(0, 2, 1)[:, :, :, None]
    attended = attended.reshape(shard_rows, local_heads * HD).astype(jnp.bfloat16)
    partial_out = jnp.dot(attended, w_out, preferred_element_type=jnp.float32)
    return lax.psum_scatter(
        partial_out.astype(jnp.bfloat16), "head", scatter_dimension=1, tiled=True
    )


SMALL = pl.CostEstimate(flops=1024, bytes_accessed=1024, transcendentals=0)
TILE = 256
MOST_DOCS = 16


def params(mib):
    return pltpu.CompilerParams(vmem_limit_bytes=mib * 1024 * 1024)


def whole(shape):
    return pl.BlockSpec(shape, lambda step, scalars: (0,) * len(shape))


def pack(ctx_index, distance, half, queries, keys, values, docs):
    rows = queries.shape[0] // 2
    doc_rows = 0 if docs is None else 16 * pl.cdiv(docs.shape[0], 16)
    total = 3 * rows + doc_rows

    def kernel(ctx_ref, *refs):
        out = refs[-1]
        for part in range(2):
            out[part * rows : (part + 1) * rows, :] = refs[part][...]
        for block in range(rows // HD):
            taken = refs[2][block * HD : (block + 1) * HD, :]
            lower = 2 * rows + block * HD
            out[lower : lower + HD, :] = jnp.transpose(taken)
        if docs is not None:
            mine = refs[3][...].astype(jnp.float32)
            empty = jnp.zeros((doc_rows - mine.shape[0], HD), jnp.float32)
            out[3 * rows :, :] = jnp.concatenate([mine, empty], axis=0).astype(jnp.bfloat16)

    piece = pl.BlockSpec((rows, HD), lambda step, ctx: (half, ctx[0] ^ distance))
    in_specs = [piece] * 3
    operands = [queries, keys, values]
    if docs is not None:
        in_specs.append(whole(docs.shape))
        operands.append(docs)
    return pl.pallas_call(
        kernel,
        grid_spec=pltpu.PrefetchScalarGridSpec(
            num_scalar_prefetch=1,
            grid=(1,),
            in_specs=in_specs,
            out_specs=whole((total, HD)),
        ),
        out_shape=jax.ShapeDtypeStruct((total, HD), jnp.bfloat16),
        compiler_params=params(56),
        cost_estimate=SMALL,
        name="pack",
    )(ctx_index, *operands)


def pack_projection(places, w_mine, w_sibling):
    depth, width = w_mine.shape
    turns = len(TURNS)
    columns = width // (2 * turns)

    def kernel(places_ref, mine_in, sibling_in, mine_out, sibling_out):
        mine_out[...] = mine_in[...]
        sibling_out[...] = sibling_in[...]

    in_spec = pl.BlockSpec((depth, columns), lambda turn, at: (0, at[turn]))
    out_spec = pl.BlockSpec((depth, columns), lambda turn, at: (0, turn))
    return pl.pallas_call(
        kernel,
        grid_spec=pltpu.PrefetchScalarGridSpec(
            num_scalar_prefetch=1,
            grid=(turns,),
            in_specs=[in_spec] * 2,
            out_specs=[out_spec] * 2,
        ),
        out_shape=[jax.ShapeDtypeStruct((depth, turns * columns), w_mine.dtype)] * 2,
        compiler_params=params(56),
        cost_estimate=SMALL,
        name="pack_projection",
    )(places, w_mine, w_sibling)


def attend(ctx_index, queries, keys, values, docs, low, high):
    rows = queries.shape[0] // 2
    group = queries.shape[1] // HD
    with_high = high is not None
    per_block = rows // TILE
    lines = rows // HD
    key_rows = (2 * group if with_high else group) * rows
    key_tiles = key_rows // TILE
    scaling = LOG2E / math.sqrt(HD)

    def kernel(ctx_ref, *refs):
        refs = list(refs)
        own_low = [refs.pop(0) for _ in range(3)]
        own_high = [refs.pop(0) for _ in range(3)] if with_high else None
        own_docs = refs.pop(0)
        low_refs = [refs.pop(0) for _ in range(group - 1)]
        high_refs = [refs.pop(0) for _ in range(group - 1)] if with_high else None
        outs = [refs.pop(0) for _ in range(group)]
        key_buf, value_buf, doc_buf = refs[:3]
        query_buf, start_buf, largest_buf, summed = (
            refs[3 + kind * group : 3 + (kind + 1) * group] for kind in range(4)
        )
        ctx = ctx_ref[0]

        def part(upper, distance, index, lower=0, count=rows):
            if distance == 0:
                return (own_high if upper else own_low)[index][lower : lower + count, :]
            source = (high_refs if upper else low_refs)[distance - 1]
            return source[index * rows + lower : index * rows + lower + count, :]

        place = {}
        doc_rows = {}
        for upper in (False, True) if with_high else (False,):
            for distance in range(group):
                source = ctx ^ distance
                block = 2 * group - 1 - source if upper else source
                place[upper, distance] = block
                offset = pl.multiple_of(block * rows, rows)
                key_buf[pl.ds(offset, rows), :] = part(upper, distance, 1)
                if distance == 0:
                    both = own_docs[...].astype(jnp.float32)
                else:
                    both = low_refs[distance - 1][3 * rows :, :].astype(jnp.float32)
                begin = lines if upper else 0
                mine = []
                for line in range(lines):
                    taken = part(upper, distance, 2, line * HD, HD)
                    if distance == 0:
                        taken = jnp.transpose(taken)
                    column = pl.multiple_of(block * rows + line * HD, HD)
                    value_buf[:HD, pl.ds(column, HD)] = taken
                    mine.append(both[begin + line : begin + line + 1, :])
                    doc_buf[pl.ds(block * lines + line, 1), :] = mine[-1]
                doc_rows[upper, distance] = jnp.concatenate(mine, axis=1)
        value_buf[HD:, :] = jnp.ones((value_buf.shape[0] - HD, key_rows), jnp.bfloat16)

        all_docs = doc_buf[...]
        starts = [jnp.zeros((1, rows), jnp.float32)] * group
        for number in range(1, MOST_DOCS):
            smaller = jnp.where(all_docs < number, 1.0, 0.0)
            count = jnp.sum(jnp.sum(smaller, axis=0, keepdims=True), axis=1, keepdims=True)
            for distance in range(group):
                reached = doc_rows[with_high, distance] >= number
                starts[distance] = jnp.where(reached, count, starts[distance])

        def scores_of(query, offset):
            raw = lax.dot_general(
                key_buf[pl.ds(offset, TILE), :],
                query,
                (((1,), (1,)), ((), ())),
                preferred_element_type=jnp.float32,
            )
            return raw * scaling

        def weighted(weights, offset):
            return jnp.dot(
                value_buf[:, pl.ds(offset, TILE)],
                weights.astype(jnp.bfloat16),
                preferred_element_type=jnp.float32,
            )

        key_row = lax.broadcasted_iota(jnp.int32, (TILE, TILE), 0)
        causal = key_row <= lax.broadcasted_iota(jnp.int32, (TILE, TILE), 1)
        key_row = key_row.astype(jnp.float32)
        firsts = []
        counts = []
        for lane in range(group):
            for slot in range(per_block):
                distance = lane ^ (slot * (group - 1))
                query = part(with_high, distance, 0, slot * TILE, TILE)
                query_buf[lane][slot] = query
                start = starts[distance][:, slot * TILE : (slot + 1) * TILE]
                start_buf[lane][slot, 0:1, :] = start
                end = place[with_high, distance] * per_block + slot
                offset = pl.multiple_of(end * TILE, TILE)
                least = start - offset.astype(jnp.float32)
                scores = scores_of(query, offset)
                scores = jnp.where((key_row >= least) & causal, scores, MASKED_SCORE)
                largest = jnp.max(scores, axis=0, keepdims=True)
                largest_buf[lane][slot, 0:1, :] = largest
                summed[lane][slot] = weighted(jnp.exp2(scores - largest), offset)
                first = jnp.min(start).astype(jnp.int32) // TILE
                firsts.append(first)
                counts.append(end - first)

        longest = jnp.int32(0)
        for lane in range(group):
            of_lane = counts[lane * per_block : (lane + 1) * per_block]
            longest = jnp.maximum(longest, sum(of_lane))

        def visit(step, carry):
            slots = []
            offsets = []
            beyonds = []
            for lane in range(group):
                slot = jnp.int32(0)
                index = firsts[lane * per_block] + step
                before = counts[lane * per_block]
                for later in range(1, per_block):
                    reached = step >= before
                    slot = jnp.where(reached, later, slot)
                    place_later = lane * per_block + later
                    index = jnp.where(reached, firsts[place_later] + step - before, index)
                    before = before + counts[place_later]
                offset = pl.multiple_of(jnp.minimum(index, key_tiles - 1) * TILE, TILE)
                slots.append(slot)
                offsets.append(offset)
                beyonds.append(jnp.where(step < before, -offset.astype(jnp.float32), 1e9))
            each = range(group)
            scores = [scores_of(query_buf[lane][slots[lane]], offsets[lane]) for lane in each]
            old_max = [largest_buf[lane][slots[lane], 0:1, :] for lane in each]
            new_max = []
            for lane in each:
                least = start_buf[lane][slots[lane], 0:1, :] + beyonds[lane]
                scores[lane] = jnp.where(key_row >= least, scores[lane], MASKED_SCORE)
                tile_max = jnp.max(scores[lane], axis=0, keepdims=True)
                new_max.append(jnp.maximum(old_max[lane], tile_max))
            products = [
                weighted(jnp.exp2(scores[lane] - new_max[lane]), offsets[lane]) for lane in each
            ]
            for lane in each:
                factor = jnp.exp2(old_max[lane] - new_max[lane])
                summed[lane][slots[lane]] = summed[lane][slots[lane]] * factor + products[lane]
                largest_buf[lane][slots[lane], 0:1, :] = new_max[lane]
            return carry

        lax.fori_loop(0, longest, visit, jnp.int32(0))
        for lane in range(group):
            for slot in range(per_block):
                state = summed[lane]
                attended = state[slot, :HD, :] / state[slot, HD : HD + 1, :]
                out = outs[lane ^ (slot * (group - 1))]
                out[slot * TILE : (slot + 1) * TILE, :] = jnp.transpose(attended).astype(
                    jnp.bfloat16
                )

    def own(upper):
        return pl.BlockSpec((rows, HD), lambda step, ctx: (int(upper), ctx[0]))

    in_specs = [own(False)] * 3
    operands = [queries, keys, values]
    if with_high:
        in_specs += [own(True)] * 3
        operands += [queries, keys, values]
    received = [docs, *low, *(high if with_high else ())]
    operands += received
    in_specs += [whole(array.shape) for array in received]
    return pl.pallas_call(
        kernel,
        grid_spec=pltpu.PrefetchScalarGridSpec(
            num_scalar_prefetch=1,
            grid=(1,),
            in_specs=in_specs,
            out_specs=[whole((rows, HD))] * group,
            scratch_shapes=[
                pltpu.VMEM((key_rows, HD), jnp.bfloat16),
                pltpu.VMEM((HD + 16, key_rows), jnp.bfloat16),
                pltpu.VMEM((key_rows // HD, HD), jnp.float32),
                *[pltpu.VMEM((per_block, TILE, HD), jnp.bfloat16)] * group,
                *[pltpu.VMEM((per_block, 8, TILE), jnp.float32)] * (2 * group),
                *[pltpu.VMEM((per_block, HD + 16, TILE), jnp.float32)] * group,
            ],
        ),
        out_shape=[jax.ShapeDtypeStruct((rows, HD), jnp.bfloat16)] * group,
        compiler_params=params(40),
        cost_estimate=SMALL,
        name="attend_high" if with_high else "attend_low",
    )(ctx_index, *operands)


def assemble(ctx_index, pieces, parts):
    rows = pieces[0].shape[0]
    group = len(pieces)
    part_rows = rows // parts

    def kernel(ctx_ref, *refs):
        for part in range(parts):
            for distance in range(group):
                column = pl.multiple_of((ctx_ref[0] ^ distance) * HD, HD)
                taken = refs[distance][part * part_rows : (part + 1) * part_rows, :]
                refs[group + part][:, pl.ds(column, HD)] = taken

    return pl.pallas_call(
        kernel,
        grid_spec=pltpu.PrefetchScalarGridSpec(
            num_scalar_prefetch=1,
            grid=(1,),
            in_specs=[whole((rows, HD))] * group,
            out_specs=[whole((part_rows, group * HD))] * parts,
        ),
        out_shape=[jax.ShapeDtypeStruct((part_rows, group * HD), jnp.bfloat16)] * parts,
        compiler_params=params(16),
        cost_estimate=SMALL,
        name="assemble",
    )(ctx_index, *pieces)


def project(turn, mine, sibling, w_mine, w_sibling):
    parts = len(mine)
    rows, depth = mine[0].shape
    columns = w_mine.shape[1] // len(TURNS)

    def kernel(*refs):
        w_mine_ref, w_sibling_ref, out_ref = refs[2 * parts :]
        for part in range(parts):
            total = jnp.dot(refs[part][...], w_mine_ref[...], preferred_element_type=jnp.float32)
            total += jnp.dot(
                refs[parts + part][...], w_sibling_ref[...], preferred_element_type=jnp.float32
            )
            out_ref[part * rows : (part + 1) * rows, :] = total.astype(jnp.bfloat16)

    weights = pl.BlockSpec((depth, columns), lambda step: (0, turn))
    attended = pl.BlockSpec((rows, depth), lambda step: (0, 0))
    return pl.pallas_call(
        kernel,
        grid=(1,),
        in_specs=[attended] * (2 * parts) + [weights] * 2,
        out_specs=pl.BlockSpec((parts * rows, columns), lambda step: (0, 0)),
        out_shape=jax.ShapeDtypeStruct((parts * rows, columns), jnp.bfloat16),
        compiler_params=params(16),
        cost_estimate=SMALL,
        name="project",
    )(*mine, *sibling, w_mine, w_sibling)


def finish(half, terms, result):
    rows, columns = terms[0].shape

    def kernel(*refs):
        total = refs[0][...].astype(jnp.float32)
        for ref in refs[1 : len(terms)]:
            total += ref[...].astype(jnp.float32)
        refs[-1][...] = total.astype(jnp.bfloat16)

    in_specs = [pl.BlockSpec((rows, columns), lambda step: (0, 0))] * len(terms)
    operands = list(terms)
    aliases = {}
    if result is not None:
        in_specs.append(pl.BlockSpec(memory_space=pl.ANY))
        operands.append(result)
        aliases = {len(terms): 0}
    return pl.pallas_call(
        kernel,
        grid=(1,),
        in_specs=in_specs,
        out_specs=pl.BlockSpec((rows, columns), lambda step: (half, 0)),
        out_shape=jax.ShapeDtypeStruct((2 * rows, columns), jnp.bfloat16),
        input_output_aliases=aliases,
        compiler_params=params(16),
        cost_estimate=SMALL,
        name="finish",
    )(*operands)


def swap(value, axis, distance):
    count = lax.axis_size(axis)
    return lax.ppermute(value, axis, [(source, source ^ distance) for source in range(count)])


def add(*terms):
    total = terms[0].astype(jnp.float32)
    for term in terms[1:]:
        total = total + term.astype(jnp.float32)
    return total.astype(jnp.bfloat16)


TURNS = (3, 1, 2, 0)


def tie(*values):
    return lax.optimization_barrier(values)


def exchange_local(queries, keys, values, doc_ids, w_out):
    shard_rows = queries.shape[0]
    group = queries.shape[1] // HD
    ctx_index = lax.axis_index("ctx").astype(jnp.int32).reshape(1)
    head_index = lax.axis_index("head").astype(jnp.int32)
    places = head_index ^ (2 * jnp.array(TURNS, jnp.int32))
    docs = doc_ids.reshape(shard_rows // HD, HD)
    near = range(1, group)

    w_sibling = swap(w_out, "head", 1)

    def exchange(half, distance, arrays):
        packed = pack(ctx_index, distance, half, *arrays, None if half else docs)
        return packed, swap(packed, "ctx", distance)

    low = {}
    arrays = (queries, keys, values)
    for distance in (3, 1, 2):
        packed, low[distance] = exchange(0, distance, arrays)
        packed, arrays = tie(packed, arrays)
    high_out = {}
    high = {}
    for distance in (1, 2):
        high_out[distance], high[distance] = exchange(1, distance, arrays)
    low = [low[distance] for distance in near]
    diagonal_out = pack(ctx_index, 3, 1, *arrays, None)
    w_packed = pack_projection(places, w_out, w_sibling)
    low, w_packed, diagonal_out = tie(low, w_packed, diagonal_out)

    def send_back(pieces):
        return [swap(pieces[distance], "ctx", distance) for distance in near]

    def shares_of(mine, sibling):
        return [project(turn, mine, sibling, *w_packed) for turn in range(len(TURNS))]

    pieces = attend(ctx_index, queries, keys, values, docs, low, None)
    pieces, diagonal_out = tie(pieces, diagonal_out)
    back = send_back(pieces)
    back, high = tie(back, high)
    high = [high[1], high[2], swap(diagonal_out, "ctx", 3)]
    mine = assemble(ctx_index, [pieces[0], *back], 1)
    shares = shares_of(mine, [swap(mine[0], "head", 1)])
    far = swap(shares[0], "head", 2)
    near_sum = swap(shares[1], "head", 2)

    high, shares = tie(high, shares)
    pieces = attend(ctx_index, queries, keys, values, docs, low, high)
    back = send_back(pieces)
    pieces, passed = tie(pieces, add(shares[2], far))
    across = swap(passed, "head", 4)
    back, near_sum = tie(back, near_sum)
    mine = assemble(ctx_index, [pieces[0], *back], 2)
    late = shares_of(mine, [swap(part, "head", 1) for part in mine])
    late[0], across = tie(late[0], across)
    result = finish(0, [shares[3], near_sum, across], None)
    far = swap(late[0], "head", 2)
    near_sum = swap(late[1], "head", 2)
    across = swap(add(late[2], far), "head", 4)
    return finish(1, [late[3], near_sum, across], result)


def solution(mesh):
    in_specs = (P("ctx", "head"), P("ctx", "head"), P("ctx", "head"), P("ctx"), P("head", None))
    out_specs = P("ctx", "head")
    ctx_count = mesh.shape["ctx"]
    head_count = mesh.shape["head"]

    def local(queries, keys, values, doc_ids, w_out):
        heads = queries.shape[1] // HD
        exchange = heads == ctx_count and heads == 4 and head_count == 2 * len(TURNS)
        exchange = exchange and queries.shape[0] % (4 * TILE) == 0
        body = exchange_local if exchange else ring_local
        return body(queries, keys, values, doc_ids, w_out)

    return jax.shard_map(
        local, mesh=mesh, in_specs=in_specs, out_specs=out_specs, check_vma=False
    )
```

```python
import functools
import math

import jax
import jax.numpy as jnp
from jax import lax
from jax.experimental import pallas as pl
from jax.experimental.pallas import tpu as pltpu
from jax.sharding import PartitionSpec as P

HD = 128


MASKED_SCORE = -1e30
LOG2E = 1.4426950408889634


def passed_along(value, axis, steps):
    count = lax.axis_size(axis)
    pairs = [(source, (source + steps) % count) for source in range(count)]
    return lax.ppermute(value, axis, pairs)


def folded_positions(row_total, offset, shard_rows, devices_ctx):
    flat_index = offset + lax.iota(jnp.int32, row_total)
    owner_dev = flat_index // shard_rows
    within = flat_index % shard_rows
    half_rows = shard_rows // 2
    fold_block = jnp.where(within < half_rows, owner_dev, 2 * devices_ctx - 1 - owner_dev)
    return fold_block * half_rows + within % half_rows


def block_update(
    running, query, query_pos, query_doc, key_block, value_block, pos_block, doc_block
):
    largest, totals, summed = running
    query_rows = query.shape[0]
    local_heads = query.shape[1] // HD
    query_heads = query.reshape(query_rows, local_heads, HD)
    key_heads = key_block.reshape(key_block.shape[0], local_heads, HD)
    value_heads = value_block.reshape(value_block.shape[0], local_heads, HD)
    scores = jnp.einsum(
        "qhd,khd->hqk", query_heads, key_heads, preferred_element_type=jnp.float32
    ) * (1.0 / math.sqrt(HD))
    allowed = (query_doc[:, None] == doc_block[None, :]) & (
        pos_block[None, :] <= query_pos[:, None]
    )
    scores = jnp.where(allowed[None], scores, MASKED_SCORE)
    new_max = jnp.maximum(largest, jnp.max(scores, axis=2))
    weights = jnp.where(allowed[None], jnp.exp(scores - new_max[:, :, None]), 0.0)
    factor = jnp.exp(largest - new_max)
    totals = totals * factor + jnp.sum(weights, axis=2)
    product = jnp.einsum(
        "hqk,khd->qhd",
        weights.astype(jnp.bfloat16),
        value_heads,
        preferred_element_type=jnp.float32,
    )
    summed = summed * factor.T[:, :, None] + product
    return (new_max, totals, summed)


def attend_rows(running, query, query_pos, query_doc, key_rows, value_rows, key_pos, key_doc):
    row_total = key_rows.shape[0]
    block_rows = math.gcd(row_total, query.shape[0])
    block_count = row_total // block_rows
    highest = jnp.max(query_pos)

    def visit(partial_value, blocks):
        key_block, value_block, pos_block, doc_block = blocks
        masked_out = jnp.min(pos_block) > highest
        updated = lax.cond(
            masked_out,
            lambda frozen: frozen,
            lambda frozen: block_update(
                frozen, query, query_pos, query_doc, key_block, value_block, pos_block, doc_block
            ),
            partial_value,
        )
        return (updated, None)

    blocks = (
        key_rows.reshape(block_count, block_rows, key_rows.shape[1]),
        value_rows.reshape(block_count, block_rows, value_rows.shape[1]),
        key_pos.reshape(block_count, block_rows),
        key_doc.reshape(block_count, block_rows),
    )
    running, _ = lax.scan(visit, running, blocks)
    return running


def attend_shard(running, query, query_pos, query_doc, key_rows, value_rows, key_pos, key_doc):
    largest, totals, summed = running
    half_rows = query.shape[0] // 2
    new_largest = []
    new_totals = []
    new_summed = []
    for half_idx in range(2):
        lower = half_idx * half_rows
        part_state = (largest[half_idx], totals[half_idx], summed[half_idx])
        part_state = attend_rows(
            part_state,
            query[lower : lower + half_rows],
            query_pos[lower : lower + half_rows],
            query_doc[lower : lower + half_rows],
            key_rows,
            value_rows,
            key_pos,
            key_doc,
        )
        new_largest.append(part_state[0])
        new_totals.append(part_state[1])
        new_summed.append(part_state[2])
    return (jnp.stack(new_largest), jnp.stack(new_totals), jnp.stack(new_summed))


def ring_local(queries, keys, values, doc_ids, w_out):
    shard_rows = queries.shape[0]
    half_rows = shard_rows // 2
    local_heads = queries.shape[1] // HD
    devices_ctx = lax.axis_size("ctx")
    ctx_index = lax.axis_index("ctx")
    all_docs = lax.all_gather(doc_ids, "ctx", axis=0, tiled=True)
    own_pos = folded_positions(shard_rows, ctx_index * shard_rows, shard_rows, devices_ctx)
    running = (
        jnp.full((2, local_heads, half_rows), MASKED_SCORE, jnp.float32),
        jnp.zeros((2, local_heads, half_rows), jnp.float32),
        jnp.zeros((2, half_rows, local_heads, HD), jnp.float32),
    )
    travel = queries
    for hop_step in range(devices_ctx):
        anchor = (ctx_index - hop_step) % devices_ctx
        query_pos = folded_positions(shard_rows, anchor * shard_rows, shard_rows, devices_ctx)
        query_doc = lax.dynamic_slice_in_dim(all_docs, anchor * shard_rows, shard_rows, 0)
        largest, totals, summed = attend_shard(
            running, travel, query_pos, query_doc, keys, values, own_pos, doc_ids
        )
        running = (
            passed_along(largest.astype(jnp.bfloat16), "ctx", 1).astype(largest.dtype),
            passed_along(totals.astype(jnp.bfloat16), "ctx", 1).astype(totals.dtype),
            passed_along(summed.astype(jnp.bfloat16), "ctx", 1).astype(summed.dtype),
        )
        if hop_step + 1 < devices_ctx:
            travel = passed_along(travel, "ctx", 1)
    largest, totals, summed = running
    attended = summed / totals.transpose(0, 2, 1)[:, :, :, None]
    attended = attended.reshape(shard_rows, local_heads * HD).astype(jnp.bfloat16)
    partial_out = jnp.dot(attended, w_out, preferred_element_type=jnp.float32)
    return lax.psum_scatter(
        partial_out.astype(jnp.bfloat16), "head", scatter_dimension=1, tiled=True
    )


SMALL = pl.CostEstimate(flops=1024, bytes_accessed=1024, transcendentals=0)
TILE = 256
MOST_DOCS = 16


def params(mib):
    return pltpu.CompilerParams(vmem_limit_bytes=mib * 1024 * 1024)


def whole(shape):
    return pl.BlockSpec(shape, lambda step, scalars: (0,) * len(shape))


def pack(ctx_index, half, queries, keys, values, docs):
    rows = queries.shape[0] // 2
    group = queries.shape[1] // HD
    doc_rows = 0 if docs is None else 16 * pl.cdiv(docs.shape[0], 16)
    total = 3 * rows + doc_rows

    def kernel(ctx_ref, *refs):
        outs = refs[len(refs) - (group - 1) :]
        if docs is not None:
            mine = refs[3 * (group - 1)][...].astype(jnp.float32)
            empty = jnp.zeros((doc_rows - mine.shape[0], HD), jnp.float32)
            mine = jnp.concatenate([mine, empty], axis=0).astype(jnp.bfloat16)
        for place in range(group - 1):
            for part in range(2):
                outs[place][part * rows : (part + 1) * rows, :] = refs[place * 3 + part][...]
            for block in range(rows // HD):
                taken = refs[place * 3 + 2][block * HD : (block + 1) * HD, :]
                lower = 2 * rows + block * HD
                outs[place][lower : lower + HD, :] = jnp.transpose(taken)
            if docs is not None:
                outs[place][3 * rows :, :] = mine

    def piece(distance):
        return pl.BlockSpec((rows, HD), lambda step, ctx: (half, ctx[0] ^ distance))

    in_specs = []
    operands = []
    for distance in range(1, group):
        for array in (queries, keys, values):
            in_specs.append(piece(distance))
            operands.append(array)
    if docs is not None:
        in_specs.append(whole(docs.shape))
        operands.append(docs)
    return pl.pallas_call(
        kernel,
        grid_spec=pltpu.PrefetchScalarGridSpec(
            num_scalar_prefetch=1,
            grid=(1,),
            in_specs=in_specs,
            out_specs=[whole((total, HD))] * (group - 1),
        ),
        out_shape=[jax.ShapeDtypeStruct((total, HD), jnp.bfloat16)] * (group - 1),
        compiler_params=params(56),
        cost_estimate=SMALL,
        name="pack",
    )(ctx_index, *operands)


def pack_projection(places, w_mine, w_sibling):
    depth, width = w_mine.shape
    turns = len(TURNS)
    columns = width // (2 * turns)

    def kernel(places_ref, mine_in, sibling_in, mine_out, sibling_out):
        mine_out[...] = mine_in[...]
        sibling_out[...] = sibling_in[...]

    in_spec = pl.BlockSpec((depth, columns), lambda turn, at: (0, at[turn]))
    out_spec = pl.BlockSpec((depth, columns), lambda turn, at: (0, turn))
    return pl.pallas_call(
        kernel,
        grid_spec=pltpu.PrefetchScalarGridSpec(
            num_scalar_prefetch=1,
            grid=(turns,),
            in_specs=[in_spec] * 2,
            out_specs=[out_spec] * 2,
        ),
        out_shape=[jax.ShapeDtypeStruct((depth, turns * columns), w_mine.dtype)] * 2,
        compiler_params=params(56),
        cost_estimate=SMALL,
        name="pack_projection",
    )(places, w_mine, w_sibling)


def attend(ctx_index, queries, keys, values, docs, low, high):
    rows = queries.shape[0] // 2
    group = queries.shape[1] // HD
    with_high = high is not None
    per_block = rows // TILE
    lines = rows // HD
    key_rows = (2 * group if with_high else group) * rows
    key_tiles = key_rows // TILE
    scaling = LOG2E / math.sqrt(HD)

    def kernel(ctx_ref, *refs):
        refs = list(refs)
        own_low = [refs.pop(0) for _ in range(3)]
        own_high = [refs.pop(0) for _ in range(3)] if with_high else None
        own_docs = refs.pop(0)
        low_refs = [refs.pop(0) for _ in range(group - 1)]
        high_refs = [refs.pop(0) for _ in range(group - 1)] if with_high else None
        outs = [refs.pop(0) for _ in range(group)]
        key_buf, value_buf, doc_buf = refs[:3]
        query_buf, start_buf, largest_buf, summed = (
            refs[3 + kind * group : 3 + (kind + 1) * group] for kind in range(4)
        )
        ctx = ctx_ref[0]

        def part(upper, distance, index, lower=0, count=rows):
            if distance == 0:
                return (own_high if upper else own_low)[index][lower : lower + count, :]
            source = (high_refs if upper else low_refs)[distance - 1]
            return source[index * rows + lower : index * rows + lower + count, :]

        place = {}
        doc_rows = {}
        for upper in (False, True) if with_high else (False,):
            for distance in range(group):
                source = ctx ^ distance
                block = 2 * group - 1 - source if upper else source
                place[upper, distance] = block
                offset = pl.multiple_of(block * rows, rows)
                key_buf[pl.ds(offset, rows), :] = part(upper, distance, 1)
                if distance == 0:
                    both = own_docs[...].astype(jnp.float32)
                else:
                    both = low_refs[distance - 1][3 * rows :, :].astype(jnp.float32)
                begin = lines if upper else 0
                mine = []
                for line in range(lines):
                    taken = part(upper, distance, 2, line * HD, HD)
                    if distance == 0:
                        taken = jnp.transpose(taken)
                    column = pl.multiple_of(block * rows + line * HD, HD)
                    value_buf[:HD, pl.ds(column, HD)] = taken
                    mine.append(both[begin + line : begin + line + 1, :])
                    doc_buf[pl.ds(block * lines + line, 1), :] = mine[-1]
                doc_rows[upper, distance] = jnp.concatenate(mine, axis=1)
        value_buf[HD:, :] = jnp.ones((value_buf.shape[0] - HD, key_rows), jnp.bfloat16)

        all_docs = doc_buf[...]
        starts = [jnp.zeros((1, rows), jnp.float32)] * group
        for number in range(1, MOST_DOCS):
            smaller = jnp.where(all_docs < number, 1.0, 0.0)
            count = jnp.sum(jnp.sum(smaller, axis=0, keepdims=True), axis=1, keepdims=True)
            for distance in range(group):
                reached = doc_rows[with_high, distance] >= number
                starts[distance] = jnp.where(reached, count, starts[distance])

        def scores_of(query, offset):
            raw = lax.dot_general(
                key_buf[pl.ds(offset, TILE), :],
                query,
                (((1,), (1,)), ((), ())),
                preferred_element_type=jnp.float32,
            )
            return raw * scaling

        def weighted(weights, offset):
            return jnp.dot(
                value_buf[:, pl.ds(offset, TILE)],
                weights.astype(jnp.bfloat16),
                preferred_element_type=jnp.float32,
            )

        key_row = lax.broadcasted_iota(jnp.int32, (TILE, TILE), 0)
        causal = key_row <= lax.broadcasted_iota(jnp.int32, (TILE, TILE), 1)
        key_row = key_row.astype(jnp.float32)
        firsts = []
        counts = []
        for lane in range(group):
            for slot in range(per_block):
                distance = lane ^ (slot * (group - 1))
                query = part(with_high, distance, 0, slot * TILE, TILE)
                query_buf[lane][slot] = query
                start = starts[distance][:, slot * TILE : (slot + 1) * TILE]
                start_buf[lane][slot, 0:1, :] = start
                end = place[with_high, distance] * per_block + slot
                offset = pl.multiple_of(end * TILE, TILE)
                least = start - offset.astype(jnp.float32)
                scores = scores_of(query, offset)
                scores = jnp.where((key_row >= least) & causal, scores, MASKED_SCORE)
                largest = jnp.max(scores, axis=0, keepdims=True)
                largest_buf[lane][slot, 0:1, :] = largest
                summed[lane][slot] = weighted(jnp.exp2(scores - largest), offset)
                first = jnp.min(start).astype(jnp.int32) // TILE
                firsts.append(first)
                counts.append(end - first)

        longest = jnp.int32(0)
        for lane in range(group):
            of_lane = counts[lane * per_block : (lane + 1) * per_block]
            longest = jnp.maximum(longest, sum(of_lane))

        def visit(step, carry):
            slots = []
            offsets = []
            beyonds = []
            for lane in range(group):
                slot = jnp.int32(0)
                index = firsts[lane * per_block] + step
                before = counts[lane * per_block]
                for later in range(1, per_block):
                    reached = step >= before
                    slot = jnp.where(reached, later, slot)
                    place_later = lane * per_block + later
                    index = jnp.where(reached, firsts[place_later] + step - before, index)
                    before = before + counts[place_later]
                offset = pl.multiple_of(jnp.minimum(index, key_tiles - 1) * TILE, TILE)
                slots.append(slot)
                offsets.append(offset)
                beyonds.append(jnp.where(step < before, -offset.astype(jnp.float32), 1e9))
            each = range(group)
            scores = [scores_of(query_buf[lane][slots[lane]], offsets[lane]) for lane in each]
            old_max = [largest_buf[lane][slots[lane], 0:1, :] for lane in each]
            new_max = []
            for lane in each:
                least = start_buf[lane][slots[lane], 0:1, :] + beyonds[lane]
                scores[lane] = jnp.where(key_row >= least, scores[lane], MASKED_SCORE)
                tile_max = jnp.max(scores[lane], axis=0, keepdims=True)
                new_max.append(jnp.maximum(old_max[lane], tile_max))
            products = [
                weighted(jnp.exp2(scores[lane] - new_max[lane]), offsets[lane]) for lane in each
            ]
            for lane in each:
                factor = jnp.exp2(old_max[lane] - new_max[lane])
                summed[lane][slots[lane]] = summed[lane][slots[lane]] * factor + products[lane]
                largest_buf[lane][slots[lane], 0:1, :] = new_max[lane]
            return carry

        lax.fori_loop(0, longest, visit, jnp.int32(0))
        for lane in range(group):
            for slot in range(per_block):
                state = summed[lane]
                attended = state[slot, :HD, :] / state[slot, HD : HD + 1, :]
                out = outs[lane ^ (slot * (group - 1))]
                out[slot * TILE : (slot + 1) * TILE, :] = jnp.transpose(attended).astype(
                    jnp.bfloat16
                )

    def own(upper):
        return pl.BlockSpec((rows, HD), lambda step, ctx: (int(upper), ctx[0]))

    in_specs = [own(False)] * 3
    operands = [queries, keys, values]
    if with_high:
        in_specs += [own(True)] * 3
        operands += [queries, keys, values]
    received = [docs, *low, *(high if with_high else ())]
    operands += received
    in_specs += [whole(array.shape) for array in received]
    return pl.pallas_call(
        kernel,
        grid_spec=pltpu.PrefetchScalarGridSpec(
            num_scalar_prefetch=1,
            grid=(1,),
            in_specs=in_specs,
            out_specs=[whole((rows, HD))] * group,
            scratch_shapes=[
                pltpu.VMEM((key_rows, HD), jnp.bfloat16),
                pltpu.VMEM((HD + 16, key_rows), jnp.bfloat16),
                pltpu.VMEM((key_rows // HD, HD), jnp.float32),
                *[pltpu.VMEM((per_block, TILE, HD), jnp.bfloat16)] * group,
                *[pltpu.VMEM((per_block, 8, TILE), jnp.float32)] * (2 * group),
                *[pltpu.VMEM((per_block, HD + 16, TILE), jnp.float32)] * group,
            ],
        ),
        out_shape=[jax.ShapeDtypeStruct((rows, HD), jnp.bfloat16)] * group,
        compiler_params=params(40),
        cost_estimate=SMALL,
        name="attend_high" if with_high else "attend_low",
    )(ctx_index, *operands)


def assemble(ctx_index, pieces, parts):
    rows = pieces[0].shape[0]
    group = len(pieces)
    part_rows = rows // parts

    def kernel(ctx_ref, *refs):
        for part in range(parts):
            for distance in range(group):
                column = pl.multiple_of((ctx_ref[0] ^ distance) * HD, HD)
                taken = refs[distance][part * part_rows : (part + 1) * part_rows, :]
                refs[group + part][:, pl.ds(column, HD)] = taken

    return pl.pallas_call(
        kernel,
        grid_spec=pltpu.PrefetchScalarGridSpec(
            num_scalar_prefetch=1,
            grid=(1,),
            in_specs=[whole((rows, HD))] * group,
            out_specs=[whole((part_rows, group * HD))] * parts,
        ),
        out_shape=[jax.ShapeDtypeStruct((part_rows, group * HD), jnp.bfloat16)] * parts,
        compiler_params=params(16),
        cost_estimate=SMALL,
        name="assemble",
    )(ctx_index, *pieces)


def project(turn, mine, sibling, w_mine, w_sibling):
    parts = len(mine)
    rows, depth = mine[0].shape
    columns = w_mine.shape[1] // len(TURNS)

    def kernel(*refs):
        w_mine_ref, w_sibling_ref = refs[2 * parts : 2 * parts + 2]
        for part in range(parts):
            total = jnp.dot(refs[part][...], w_mine_ref[...], preferred_element_type=jnp.float32)
            total += jnp.dot(
                refs[parts + part][...], w_sibling_ref[...], preferred_element_type=jnp.float32
            )
            refs[2 * parts + 2 + part][...] = total.astype(jnp.bfloat16)

    weights = pl.BlockSpec((depth, columns), lambda step: (0, turn))
    attended = pl.BlockSpec((rows, depth), lambda step: (0, 0))
    return pl.pallas_call(
        kernel,
        grid=(1,),
        in_specs=[attended] * (2 * parts) + [weights] * 2,
        out_specs=[pl.BlockSpec((rows, columns), lambda step: (0, 0))] * parts,
        out_shape=[jax.ShapeDtypeStruct((rows, columns), jnp.bfloat16)] * parts,
        compiler_params=params(16),
        cost_estimate=SMALL,
        name="project",
    )(*mine, *sibling, w_mine, w_sibling)


def finish(half, terms, result):
    parts = len(terms[0])
    rows, columns = terms[0][0].shape
    flat = [part for term in terms for part in term]

    def kernel(*refs):
        for part in range(parts):
            total = refs[part][...].astype(jnp.float32)
            for term in range(1, len(terms)):
                total += refs[term * parts + part][...].astype(jnp.float32)
            refs[-1][part * rows : (part + 1) * rows, :] = total.astype(jnp.bfloat16)

    in_specs = [pl.BlockSpec((rows, columns), lambda step: (0, 0))] * len(flat)
    operands = list(flat)
    aliases = {}
    if result is not None:
        in_specs.append(pl.BlockSpec(memory_space=pl.ANY))
        operands.append(result)
        aliases = {len(flat): 0}
    return pl.pallas_call(
        kernel,
        grid=(1,),
        in_specs=in_specs,
        out_specs=pl.BlockSpec((parts * rows, columns), lambda step: (half, 0)),
        out_shape=jax.ShapeDtypeStruct((2 * parts * rows, columns), jnp.bfloat16),
        input_output_aliases=aliases,
        compiler_params=params(16),
        cost_estimate=SMALL,
        name="finish",
    )(*operands)


def swap(value, axis, distance):
    count = lax.axis_size(axis)
    return lax.ppermute(value, axis, [(source, source ^ distance) for source in range(count)])


def add(*terms):
    total = terms[0].astype(jnp.float32)
    for term in terms[1:]:
        total = total + term.astype(jnp.float32)
    return total.astype(jnp.bfloat16)


TURNS = (3, 1, 2, 0)


def tie(*values):
    return lax.optimization_barrier(values)


def exchange_local(queries, keys, values, doc_ids, w_out):
    shard_rows = queries.shape[0]
    group = queries.shape[1] // HD
    ctx_index = lax.axis_index("ctx").astype(jnp.int32).reshape(1)
    head_index = lax.axis_index("head").astype(jnp.int32)
    places = head_index ^ (2 * jnp.array(TURNS, jnp.int32))
    docs = doc_ids.reshape(shard_rows // HD, HD)
    near = range(1, group)

    w_sibling = swap(w_out, "head", 1)
    low_out = pack(ctx_index, 0, queries, keys, values, docs)
    low_out, later = tie(low_out, (queries, keys, values))
    low = [swap(low_out[distance - 1], "ctx", distance) for distance in near]
    high_out = pack(ctx_index, 1, *later, None)
    high = [swap(high_out[distance - 1], "ctx", distance) for distance in near[:-1]]
    w_packed = pack_projection(places, w_out, w_sibling)
    low, w_packed = tie(low, w_packed)

    def send_back(pieces):
        return [swap(pieces[distance], "ctx", distance) for distance in near]

    def shares_of(mine):
        sibling = [swap(part, "head", 1) for part in mine]
        return [project(turn, mine, sibling, *w_packed) for turn in range(len(TURNS))]

    def to_next(parts, distance):
        return [swap(part, "head", 2 * distance) for part in parts]

    pieces = attend(ctx_index, queries, keys, values, docs, low, None)
    pieces, diagonal_out = tie(pieces, high_out[-1])
    back = send_back(pieces)
    back, high = tie(back, high)
    high = [*high, swap(diagonal_out, "ctx", near[-1])]
    shares = shares_of(assemble(ctx_index, [pieces[0], *back], 1))
    far = to_next(shares[0], 1)
    near_sum = to_next(shares[1], 1)

    passed = [add(*both) for both in zip(shares[2], far)]
    high, shares, passed = tie(high, shares, passed)
    across = to_next(passed, 2)
    pieces = attend(ctx_index, queries, keys, values, docs, low, high)
    back = send_back(pieces)
    back, near_sum = tie(back, near_sum)
    late = shares_of(assemble(ctx_index, [pieces[0], *back], 2))
    late[0], across = tie(late[0], across)
    result = finish(0, [shares[3], near_sum, across], None)
    far = to_next(late[0], 1)
    near_sum = to_next(late[1], 1)
    across = to_next([add(*both) for both in zip(late[2], far)], 2)
    return finish(1, [late[3], near_sum, across], result)


def solution(mesh):
    in_specs = (P("ctx", "head"), P("ctx", "head"), P("ctx", "head"), P("ctx"), P("head", None))
    out_specs = P("ctx", "head")
    ctx_count = mesh.shape["ctx"]
    head_count = mesh.shape["head"]

    def local(queries, keys, values, doc_ids, w_out):
        heads = queries.shape[1] // HD
        exchange = heads == ctx_count and heads == 4 and head_count == 2 * len(TURNS)
        exchange = exchange and queries.shape[0] % (4 * TILE) == 0
        body = exchange_local if exchange else ring_local
        return body(queries, keys, values, doc_ids, w_out)

    return jax.shard_map(
        local, mesh=mesh, in_specs=in_specs, out_specs=out_specs, check_vma=False
    )
```

```python
import functools
import math

import jax
import jax.numpy as jnp
from jax import lax
from jax.experimental import pallas as pl
from jax.experimental.pallas import tpu as pltpu
from jax.sharding import PartitionSpec as P

HD = 128


MASKED_SCORE = -1e30
LOG2E = 1.4426950408889634


def passed_along(value, axis, steps):
    count = lax.axis_size(axis)
    pairs = [(source, (source + steps) % count) for source in range(count)]
    return lax.ppermute(value, axis, pairs)


def folded_positions(row_total, offset, shard_rows, devices_ctx):
    flat_index = offset + lax.iota(jnp.int32, row_total)
    owner_dev = flat_index // shard_rows
    within = flat_index % shard_rows
    half_rows = shard_rows // 2
    fold_block = jnp.where(within < half_rows, owner_dev, 2 * devices_ctx - 1 - owner_dev)
    return fold_block * half_rows + within % half_rows


def block_update(
    running, query, query_pos, query_doc, key_block, value_block, pos_block, doc_block
):
    largest, totals, summed = running
    query_rows = query.shape[0]
    local_heads = query.shape[1] // HD
    query_heads = query.reshape(query_rows, local_heads, HD)
    key_heads = key_block.reshape(key_block.shape[0], local_heads, HD)
    value_heads = value_block.reshape(value_block.shape[0], local_heads, HD)
    scores = jnp.einsum(
        "qhd,khd->hqk", query_heads, key_heads, preferred_element_type=jnp.float32
    ) * (1.0 / math.sqrt(HD))
    allowed = (query_doc[:, None] == doc_block[None, :]) & (
        pos_block[None, :] <= query_pos[:, None]
    )
    scores = jnp.where(allowed[None], scores, MASKED_SCORE)
    new_max = jnp.maximum(largest, jnp.max(scores, axis=2))
    weights = jnp.where(allowed[None], jnp.exp(scores - new_max[:, :, None]), 0.0)
    factor = jnp.exp(largest - new_max)
    totals = totals * factor + jnp.sum(weights, axis=2)
    product = jnp.einsum(
        "hqk,khd->qhd",
        weights.astype(jnp.bfloat16),
        value_heads,
        preferred_element_type=jnp.float32,
    )
    summed = summed * factor.T[:, :, None] + product
    return (new_max, totals, summed)


def attend_rows(running, query, query_pos, query_doc, key_rows, value_rows, key_pos, key_doc):
    row_total = key_rows.shape[0]
    block_rows = math.gcd(row_total, query.shape[0])
    block_count = row_total // block_rows
    highest = jnp.max(query_pos)

    def visit(partial_value, blocks):
        key_block, value_block, pos_block, doc_block = blocks
        masked_out = jnp.min(pos_block) > highest
        updated = lax.cond(
            masked_out,
            lambda frozen: frozen,
            lambda frozen: block_update(
                frozen, query, query_pos, query_doc, key_block, value_block, pos_block, doc_block
            ),
            partial_value,
        )
        return (updated, None)

    blocks = (
        key_rows.reshape(block_count, block_rows, key_rows.shape[1]),
        value_rows.reshape(block_count, block_rows, value_rows.shape[1]),
        key_pos.reshape(block_count, block_rows),
        key_doc.reshape(block_count, block_rows),
    )
    running, _ = lax.scan(visit, running, blocks)
    return running


def attend_shard(running, query, query_pos, query_doc, key_rows, value_rows, key_pos, key_doc):
    largest, totals, summed = running
    half_rows = query.shape[0] // 2
    new_largest = []
    new_totals = []
    new_summed = []
    for half_idx in range(2):
        lower = half_idx * half_rows
        part_state = (largest[half_idx], totals[half_idx], summed[half_idx])
        part_state = attend_rows(
            part_state,
            query[lower : lower + half_rows],
            query_pos[lower : lower + half_rows],
            query_doc[lower : lower + half_rows],
            key_rows,
            value_rows,
            key_pos,
            key_doc,
        )
        new_largest.append(part_state[0])
        new_totals.append(part_state[1])
        new_summed.append(part_state[2])
    return (jnp.stack(new_largest), jnp.stack(new_totals), jnp.stack(new_summed))


def ring_local(queries, keys, values, doc_ids, w_out):
    shard_rows = queries.shape[0]
    half_rows = shard_rows // 2
    local_heads = queries.shape[1] // HD
    devices_ctx = lax.axis_size("ctx")
    ctx_index = lax.axis_index("ctx")
    all_docs = lax.all_gather(doc_ids, "ctx", axis=0, tiled=True)
    own_pos = folded_positions(shard_rows, ctx_index * shard_rows, shard_rows, devices_ctx)
    running = (
        jnp.full((2, local_heads, half_rows), MASKED_SCORE, jnp.float32),
        jnp.zeros((2, local_heads, half_rows), jnp.float32),
        jnp.zeros((2, half_rows, local_heads, HD), jnp.float32),
    )
    travel = queries
    for hop_step in range(devices_ctx):
        anchor = (ctx_index - hop_step) % devices_ctx
        query_pos = folded_positions(shard_rows, anchor * shard_rows, shard_rows, devices_ctx)
        query_doc = lax.dynamic_slice_in_dim(all_docs, anchor * shard_rows, shard_rows, 0)
        largest, totals, summed = attend_shard(
            running, travel, query_pos, query_doc, keys, values, own_pos, doc_ids
        )
        running = (
            passed_along(largest.astype(jnp.bfloat16), "ctx", 1).astype(largest.dtype),
            passed_along(totals.astype(jnp.bfloat16), "ctx", 1).astype(totals.dtype),
            passed_along(summed.astype(jnp.bfloat16), "ctx", 1).astype(summed.dtype),
        )
        if hop_step + 1 < devices_ctx:
            travel = passed_along(travel, "ctx", 1)
    largest, totals, summed = running
    attended = summed / totals.transpose(0, 2, 1)[:, :, :, None]
    attended = attended.reshape(shard_rows, local_heads * HD).astype(jnp.bfloat16)
    partial_out = jnp.dot(attended, w_out, preferred_element_type=jnp.float32)
    return lax.psum_scatter(
        partial_out.astype(jnp.bfloat16), "head", scatter_dimension=1, tiled=True
    )


SMALL = pl.CostEstimate(flops=1024, bytes_accessed=1024, transcendentals=0)
TILE = 256
MOST_DOCS = 16


def params(mib):
    return pltpu.CompilerParams(vmem_limit_bytes=mib * 1024 * 1024)


def whole(shape):
    return pl.BlockSpec(shape, lambda step, scalars: (0,) * len(shape))


def pack(ctx_index, half, queries, keys, values, docs):
    rows = queries.shape[0] // 2
    group = queries.shape[1] // HD
    doc_rows = 0 if docs is None else 16 * pl.cdiv(docs.shape[0], 16)
    total = 3 * rows + doc_rows

    def kernel(ctx_ref, *refs):
        outs = refs[len(refs) - (group - 1) :]
        if docs is not None:
            mine = refs[3 * (group - 1)][...].astype(jnp.float32)
            empty = jnp.zeros((doc_rows - mine.shape[0], HD), jnp.float32)
            mine = jnp.concatenate([mine, empty], axis=0).astype(jnp.bfloat16)
        for place in range(group - 1):
            for part in range(2):
                outs[place][part * rows : (part + 1) * rows, :] = refs[place * 3 + part][...]
            for block in range(rows // HD):
                taken = refs[place * 3 + 2][block * HD : (block + 1) * HD, :]
                lower = 2 * rows + block * HD
                outs[place][lower : lower + HD, :] = jnp.transpose(taken)
            if docs is not None:
                outs[place][3 * rows :, :] = mine

    def piece(distance):
        return pl.BlockSpec((rows, HD), lambda step, ctx: (half, ctx[0] ^ distance))

    in_specs = []
    operands = []
    for distance in range(1, group):
        for array in (queries, keys, values):
            in_specs.append(piece(distance))
            operands.append(array)
    if docs is not None:
        in_specs.append(whole(docs.shape))
        operands.append(docs)
    return pl.pallas_call(
        kernel,
        grid_spec=pltpu.PrefetchScalarGridSpec(
            num_scalar_prefetch=1,
            grid=(1,),
            in_specs=in_specs,
            out_specs=[whole((total, HD))] * (group - 1),
        ),
        out_shape=[jax.ShapeDtypeStruct((total, HD), jnp.bfloat16)] * (group - 1),
        compiler_params=params(56),
        cost_estimate=SMALL,
        name="pack",
    )(ctx_index, *operands)


def pack_projection(places, w_mine, w_sibling):
    depth, width = w_mine.shape
    turns = len(TURNS)
    columns = width // (2 * turns)

    def kernel(places_ref, mine_in, sibling_in, mine_out, sibling_out):
        mine_out[...] = mine_in[...]
        sibling_out[...] = sibling_in[...]

    in_spec = pl.BlockSpec((depth, columns), lambda turn, at: (0, at[turn]))
    out_spec = pl.BlockSpec((depth, columns), lambda turn, at: (0, turn))
    return pl.pallas_call(
        kernel,
        grid_spec=pltpu.PrefetchScalarGridSpec(
            num_scalar_prefetch=1,
            grid=(turns,),
            in_specs=[in_spec] * 2,
            out_specs=[out_spec] * 2,
        ),
        out_shape=[jax.ShapeDtypeStruct((depth, turns * columns), w_mine.dtype)] * 2,
        compiler_params=params(56),
        cost_estimate=SMALL,
        name="pack_projection",
    )(places, w_mine, w_sibling)


def attend(ctx_index, queries, keys, values, docs, low, high):
    rows = queries.shape[0] // 2
    group = queries.shape[1] // HD
    with_high = high is not None
    per_block = rows // TILE
    lines = rows // HD
    key_rows = (2 * group if with_high else group) * rows
    key_tiles = key_rows // TILE
    scaling = LOG2E / math.sqrt(HD)

    def kernel(ctx_ref, *refs):
        refs = list(refs)
        own_low = [refs.pop(0) for _ in range(3)]
        own_high = [refs.pop(0) for _ in range(3)] if with_high else None
        own_docs = refs.pop(0)
        low_refs = [refs.pop(0) for _ in range(group - 1)]
        high_refs = [refs.pop(0) for _ in range(group - 1)] if with_high else None
        outs = [refs.pop(0) for _ in range(group)]
        key_buf, value_buf, doc_buf = refs[:3]
        query_buf, start_buf, largest_buf, summed = (
            refs[3 + kind * group : 3 + (kind + 1) * group] for kind in range(4)
        )
        ctx = ctx_ref[0]

        def part(upper, distance, index, lower=0, count=rows):
            if distance == 0:
                return (own_high if upper else own_low)[index][lower : lower + count, :]
            source = (high_refs if upper else low_refs)[distance - 1]
            return source[index * rows + lower : index * rows + lower + count, :]

        place = {}
        doc_rows = {}
        for upper in (False, True) if with_high else (False,):
            for distance in range(group):
                source = ctx ^ distance
                block = 2 * group - 1 - source if upper else source
                place[upper, distance] = block
                offset = pl.multiple_of(block * rows, rows)
                key_buf[pl.ds(offset, rows), :] = part(upper, distance, 1)
                if distance == 0:
                    both = own_docs[...].astype(jnp.float32)
                else:
                    both = low_refs[distance - 1][3 * rows :, :].astype(jnp.float32)
                begin = lines if upper else 0
                mine = []
                for line in range(lines):
                    taken = part(upper, distance, 2, line * HD, HD)
                    if distance == 0:
                        taken = jnp.transpose(taken)
                    column = pl.multiple_of(block * rows + line * HD, HD)
                    value_buf[:HD, pl.ds(column, HD)] = taken
                    mine.append(both[begin + line : begin + line + 1, :])
                    doc_buf[pl.ds(block * lines + line, 1), :] = mine[-1]
                doc_rows[upper, distance] = jnp.concatenate(mine, axis=1)
        value_buf[HD:, :] = jnp.ones((value_buf.shape[0] - HD, key_rows), jnp.bfloat16)

        all_docs = doc_buf[...]
        starts = [jnp.zeros((1, rows), jnp.float32)] * group
        for number in range(1, MOST_DOCS):
            smaller = jnp.where(all_docs < number, 1.0, 0.0)
            count = jnp.sum(jnp.sum(smaller, axis=0, keepdims=True), axis=1, keepdims=True)
            for distance in range(group):
                reached = doc_rows[with_high, distance] >= number
                starts[distance] = jnp.where(reached, count, starts[distance])

        def scores_of(query, offset):
            raw = lax.dot_general(
                key_buf[pl.ds(offset, TILE), :],
                query,
                (((1,), (1,)), ((), ())),
                preferred_element_type=jnp.float32,
            )
            return raw * scaling

        def weighted(weights, offset):
            return jnp.dot(
                value_buf[:, pl.ds(offset, TILE)],
                weights.astype(jnp.bfloat16),
                preferred_element_type=jnp.float32,
            )

        key_row = lax.broadcasted_iota(jnp.int32, (TILE, TILE), 0)
        causal = key_row <= lax.broadcasted_iota(jnp.int32, (TILE, TILE), 1)
        key_row = key_row.astype(jnp.float32)
        firsts = []
        counts = []
        for lane in range(group):
            for slot in range(per_block):
                distance = lane ^ (slot * (group - 1))
                query = part(with_high, distance, 0, slot * TILE, TILE)
                query_buf[lane][slot] = query
                start = starts[distance][:, slot * TILE : (slot + 1) * TILE]
                start_buf[lane][slot, 0:1, :] = start
                end = place[with_high, distance] * per_block + slot
                offset = pl.multiple_of(end * TILE, TILE)
                least = start - offset.astype(jnp.float32)
                scores = scores_of(query, offset)
                scores = jnp.where((key_row >= least) & causal, scores, MASKED_SCORE)
                largest = jnp.max(scores, axis=0, keepdims=True)
                largest_buf[lane][slot, 0:1, :] = largest
                summed[lane][slot] = weighted(jnp.exp2(scores - largest), offset)
                first = start[0, 0].astype(jnp.int32) // TILE
                firsts.append(first)
                counts.append(end - first)

        longest = jnp.int32(0)
        for lane in range(group):
            of_lane = counts[lane * per_block : (lane + 1) * per_block]
            longest = jnp.maximum(longest, sum(of_lane))

        def visit(step, carry):
            slots = []
            offsets = []
            beyonds = []
            for lane in range(group):
                slot = jnp.int32(0)
                index = firsts[lane * per_block] + step
                before = counts[lane * per_block]
                for later in range(1, per_block):
                    reached = step >= before
                    slot = jnp.where(reached, later, slot)
                    place_later = lane * per_block + later
                    index = jnp.where(reached, firsts[place_later] + step - before, index)
                    before = before + counts[place_later]
                offset = pl.multiple_of(jnp.minimum(index, key_tiles - 1) * TILE, TILE)
                slots.append(slot)
                offsets.append(offset)
                beyonds.append(jnp.where(step < before, -offset.astype(jnp.float32), 1e9))
            each = range(group)
            scores = [scores_of(query_buf[lane][slots[lane]], offsets[lane]) for lane in each]
            old_max = [largest_buf[lane][slots[lane], 0:1, :] for lane in each]
            new_max = []
            for lane in each:
                least = start_buf[lane][slots[lane], 0:1, :] + beyonds[lane]
                scores[lane] = jnp.where(key_row >= least, scores[lane], MASKED_SCORE)
                tile_max = jnp.max(scores[lane], axis=0, keepdims=True)
                new_max.append(jnp.maximum(old_max[lane], tile_max))
            products = [
                weighted(jnp.exp2(scores[lane] - new_max[lane]), offsets[lane]) for lane in each
            ]
            for lane in each:
                factor = jnp.exp2(old_max[lane] - new_max[lane])
                summed[lane][slots[lane]] = summed[lane][slots[lane]] * factor + products[lane]
                largest_buf[lane][slots[lane], 0:1, :] = new_max[lane]
            return carry

        lax.fori_loop(0, longest, visit, jnp.int32(0))
        for lane in range(group):
            for slot in range(per_block):
                state = summed[lane]
                attended = state[slot, :HD, :] * (1.0 / state[slot, HD : HD + 1, :])
                out = outs[lane ^ (slot * (group - 1))]
                out[slot * TILE : (slot + 1) * TILE, :] = jnp.transpose(
                    attended.astype(jnp.bfloat16)
                )

    def own(upper):
        return pl.BlockSpec((rows, HD), lambda step, ctx: (int(upper), ctx[0]))

    in_specs = [own(False)] * 3
    operands = [queries, keys, values]
    if with_high:
        in_specs += [own(True)] * 3
        operands += [queries, keys, values]
    received = [docs, *low, *(high if with_high else ())]
    operands += received
    in_specs += [whole(array.shape) for array in received]
    return pl.pallas_call(
        kernel,
        grid_spec=pltpu.PrefetchScalarGridSpec(
            num_scalar_prefetch=1,
            grid=(1,),
            in_specs=in_specs,
            out_specs=[whole((rows, HD))] * group,
            scratch_shapes=[
                pltpu.VMEM((key_rows, HD), jnp.bfloat16),
                pltpu.VMEM((HD + 16, key_rows), jnp.bfloat16),
                pltpu.VMEM((key_rows // HD, HD), jnp.float32),
                *[pltpu.VMEM((per_block, TILE, HD), jnp.bfloat16)] * group,
                *[pltpu.VMEM((per_block, 8, TILE), jnp.float32)] * (2 * group),
                *[pltpu.VMEM((per_block, HD + 16, TILE), jnp.float32)] * group,
            ],
        ),
        out_shape=[jax.ShapeDtypeStruct((rows, HD), jnp.bfloat16)] * group,
        compiler_params=params(40),
        cost_estimate=SMALL,
        name="attend_high" if with_high else "attend_low",
    )(ctx_index, *operands)


def assemble(ctx_index, pieces, parts):
    rows = pieces[0].shape[0]
    group = len(pieces)
    part_rows = rows // parts

    def kernel(ctx_ref, *refs):
        for part in range(parts):
            for distance in range(group):
                column = pl.multiple_of((ctx_ref[0] ^ distance) * HD, HD)
                taken = refs[distance][part * part_rows : (part + 1) * part_rows, :]
                refs[group + part][:, pl.ds(column, HD)] = taken

    return pl.pallas_call(
        kernel,
        grid_spec=pltpu.PrefetchScalarGridSpec(
            num_scalar_prefetch=1,
            grid=(1,),
            in_specs=[whole((rows, HD))] * group,
            out_specs=[whole((part_rows, group * HD))] * parts,
        ),
        out_shape=[jax.ShapeDtypeStruct((part_rows, group * HD), jnp.bfloat16)] * parts,
        compiler_params=params(16),
        cost_estimate=SMALL,
        name="assemble",
    )(ctx_index, *pieces)


def project(turn, mine, sibling, w_mine, w_sibling):
    parts = len(mine)
    rows, depth = mine[0].shape
    columns = w_mine.shape[1] // len(TURNS)

    def kernel(*refs):
        w_mine_ref, w_sibling_ref = refs[2 * parts : 2 * parts + 2]
        for part in range(parts):
            total = jnp.dot(refs[part][...], w_mine_ref[...], preferred_element_type=jnp.float32)
            total += jnp.dot(
                refs[parts + part][...], w_sibling_ref[...], preferred_element_type=jnp.float32
            )
            refs[2 * parts + 2 + part][...] = total.astype(jnp.bfloat16)

    weights = pl.BlockSpec((depth, columns), lambda step: (0, turn))
    attended = pl.BlockSpec((rows, depth), lambda step: (0, 0))
    return pl.pallas_call(
        kernel,
        grid=(1,),
        in_specs=[attended] * (2 * parts) + [weights] * 2,
        out_specs=[pl.BlockSpec((rows, columns), lambda step: (0, 0))] * parts,
        out_shape=[jax.ShapeDtypeStruct((rows, columns), jnp.bfloat16)] * parts,
        compiler_params=params(16),
        cost_estimate=SMALL,
        name="project",
    )(*mine, *sibling, w_mine, w_sibling)


def finish(half, terms, result):
    parts = len(terms[0])
    rows, columns = terms[0][0].shape
    flat = [part for term in terms for part in term]

    def kernel(*refs):
        for part in range(parts):
            total = refs[part][...].astype(jnp.float32)
            for term in range(1, len(terms)):
                total += refs[term * parts + part][...].astype(jnp.float32)
            refs[-1][part * rows : (part + 1) * rows, :] = total.astype(jnp.bfloat16)

    in_specs = [pl.BlockSpec((rows, columns), lambda step: (0, 0))] * len(flat)
    operands = list(flat)
    aliases = {}
    if result is not None:
        in_specs.append(pl.BlockSpec(memory_space=pl.ANY))
        operands.append(result)
        aliases = {len(flat): 0}
    return pl.pallas_call(
        kernel,
        grid=(1,),
        in_specs=in_specs,
        out_specs=pl.BlockSpec((parts * rows, columns), lambda step: (half, 0)),
        out_shape=jax.ShapeDtypeStruct((2 * parts * rows, columns), jnp.bfloat16),
        input_output_aliases=aliases,
        compiler_params=params(16),
        cost_estimate=SMALL,
        name="finish",
    )(*operands)


def swap(value, axis, distance):
    count = lax.axis_size(axis)
    return lax.ppermute(value, axis, [(source, source ^ distance) for source in range(count)])


def add(*terms):
    total = terms[0].astype(jnp.float32)
    for term in terms[1:]:
        total = total + term.astype(jnp.float32)
    return total.astype(jnp.bfloat16)


TURNS = (3, 1, 2, 0)


def tie(*values):
    return lax.optimization_barrier(values)


def exchange_local(queries, keys, values, doc_ids, w_out):
    shard_rows = queries.shape[0]
    group = queries.shape[1] // HD
    ctx_index = lax.axis_index("ctx").astype(jnp.int32).reshape(1)
    head_index = lax.axis_index("head").astype(jnp.int32)
    places = head_index ^ (2 * jnp.array(TURNS, jnp.int32))
    docs = doc_ids.reshape(shard_rows // HD, HD)
    near = range(1, group)

    w_sibling = swap(w_out, "head", 1)
    low_out = pack(ctx_index, 0, queries, keys, values, docs)
    low_out, later = tie(low_out, (queries, keys, values))
    low = [swap(low_out[distance - 1], "ctx", distance) for distance in near]
    high_out = pack(ctx_index, 1, *later, None)
    high = [swap(high_out[distance - 1], "ctx", distance) for distance in near[:-1]]
    w_packed = pack_projection(places, w_out, w_sibling)
    low, w_packed = tie(low, w_packed)

    def send_back(pieces):
        return [swap(pieces[distance], "ctx", distance) for distance in near]

    def shares_of(mine):
        sibling = [swap(part, "head", 1) for part in mine]
        return [project(turn, mine, sibling, *w_packed) for turn in range(len(TURNS))]

    def to_next(parts, distance):
        return [swap(part, "head", 2 * distance) for part in parts]

    pieces = attend(ctx_index, queries, keys, values, docs, low, None)
    pieces, diagonal_out = tie(pieces, high_out[-1])
    back = send_back(pieces)
    back, high = tie(back, high)
    high = [*high, swap(diagonal_out, "ctx", near[-1])]
    shares = shares_of(assemble(ctx_index, [pieces[0], *back], 1))
    far = to_next(shares[0], 1)
    near_sum = to_next(shares[1], 1)

    passed = [add(*both) for both in zip(shares[2], far)]
    high, shares, passed = tie(high, shares, passed)
    across = to_next(passed, 2)
    pieces = attend(ctx_index, queries, keys, values, docs, low, high)
    back = send_back(pieces)
    late = shares_of(assemble(ctx_index, [pieces[0], *back], 2))
    late[0], near_sum, across = tie(late[0], near_sum, across)
    result = finish(0, [shares[3], near_sum, across], None)
    far = to_next(late[0], 1)
    passed = [add(*both) for both in zip(late[2], far)]
    across = to_next(passed, 2)
    late[1], passed = tie(late[1], passed)
    near_sum = to_next(late[1], 1)
    return finish(1, [late[3], near_sum, across], result)


def solution(mesh):
    in_specs = (P("ctx", "head"), P("ctx", "head"), P("ctx", "head"), P("ctx"), P("head", None))
    out_specs = P("ctx", "head")
    ctx_count = mesh.shape["ctx"]
    head_count = mesh.shape["head"]

    def local(queries, keys, values, doc_ids, w_out):
        heads = queries.shape[1] // HD
        exchange = heads == ctx_count and heads == 4 and head_count == 2 * len(TURNS)
        exchange = exchange and queries.shape[0] % (4 * TILE) == 0
        body = exchange_local if exchange else ring_local
        return body(queries, keys, values, doc_ids, w_out)

    return jax.shard_map(
        local, mesh=mesh, in_specs=in_specs, out_specs=out_specs, check_vma=False
    )
```

```python
import functools
import math

import jax
import jax.numpy as jnp
from jax import lax
from jax.experimental import pallas as pl
from jax.experimental.pallas import tpu as pltpu
from jax.sharding import PartitionSpec as P

HD = 128


MASKED_SCORE = -1e30
LOG2E = 1.4426950408889634


def passed_along(value, axis, steps):
    count = lax.axis_size(axis)
    pairs = [(source, (source + steps) % count) for source in range(count)]
    return lax.ppermute(value, axis, pairs)


def folded_positions(row_total, offset, shard_rows, devices_ctx):
    flat_index = offset + lax.iota(jnp.int32, row_total)
    owner_dev = flat_index // shard_rows
    within = flat_index % shard_rows
    half_rows = shard_rows // 2
    fold_block = jnp.where(within < half_rows, owner_dev, 2 * devices_ctx - 1 - owner_dev)
    return fold_block * half_rows + within % half_rows


def block_update(
    running, query, query_pos, query_doc, key_block, value_block, pos_block, doc_block
):
    largest, totals, summed = running
    query_rows = query.shape[0]
    local_heads = query.shape[1] // HD
    query_heads = query.reshape(query_rows, local_heads, HD)
    key_heads = key_block.reshape(key_block.shape[0], local_heads, HD)
    value_heads = value_block.reshape(value_block.shape[0], local_heads, HD)
    scores = jnp.einsum(
        "qhd,khd->hqk", query_heads, key_heads, preferred_element_type=jnp.float32
    ) * (1.0 / math.sqrt(HD))
    allowed = (query_doc[:, None] == doc_block[None, :]) & (
        pos_block[None, :] <= query_pos[:, None]
    )
    scores = jnp.where(allowed[None], scores, MASKED_SCORE)
    new_max = jnp.maximum(largest, jnp.max(scores, axis=2))
    weights = jnp.where(allowed[None], jnp.exp(scores - new_max[:, :, None]), 0.0)
    factor = jnp.exp(largest - new_max)
    totals = totals * factor + jnp.sum(weights, axis=2)
    product = jnp.einsum(
        "hqk,khd->qhd",
        weights.astype(jnp.bfloat16),
        value_heads,
        preferred_element_type=jnp.float32,
    )
    summed = summed * factor.T[:, :, None] + product
    return (new_max, totals, summed)


def attend_rows(running, query, query_pos, query_doc, key_rows, value_rows, key_pos, key_doc):
    row_total = key_rows.shape[0]
    block_rows = math.gcd(row_total, query.shape[0])
    block_count = row_total // block_rows
    highest = jnp.max(query_pos)

    def visit(partial_value, blocks):
        key_block, value_block, pos_block, doc_block = blocks
        masked_out = jnp.min(pos_block) > highest
        updated = lax.cond(
            masked_out,
            lambda frozen: frozen,
            lambda frozen: block_update(
                frozen, query, query_pos, query_doc, key_block, value_block, pos_block, doc_block
            ),
            partial_value,
        )
        return (updated, None)

    blocks = (
        key_rows.reshape(block_count, block_rows, key_rows.shape[1]),
        value_rows.reshape(block_count, block_rows, value_rows.shape[1]),
        key_pos.reshape(block_count, block_rows),
        key_doc.reshape(block_count, block_rows),
    )
    running, _ = lax.scan(visit, running, blocks)
    return running


def attend_shard(running, query, query_pos, query_doc, key_rows, value_rows, key_pos, key_doc):
    largest, totals, summed = running
    half_rows = query.shape[0] // 2
    new_largest = []
    new_totals = []
    new_summed = []
    for half_idx in range(2):
        lower = half_idx * half_rows
        part_state = (largest[half_idx], totals[half_idx], summed[half_idx])
        part_state = attend_rows(
            part_state,
            query[lower : lower + half_rows],
            query_pos[lower : lower + half_rows],
            query_doc[lower : lower + half_rows],
            key_rows,
            value_rows,
            key_pos,
            key_doc,
        )
        new_largest.append(part_state[0])
        new_totals.append(part_state[1])
        new_summed.append(part_state[2])
    return (jnp.stack(new_largest), jnp.stack(new_totals), jnp.stack(new_summed))


def ring_local(queries, keys, values, doc_ids, w_out):
    shard_rows = queries.shape[0]
    half_rows = shard_rows // 2
    local_heads = queries.shape[1] // HD
    devices_ctx = lax.axis_size("ctx")
    ctx_index = lax.axis_index("ctx")
    all_docs = lax.all_gather(doc_ids, "ctx", axis=0, tiled=True)
    own_pos = folded_positions(shard_rows, ctx_index * shard_rows, shard_rows, devices_ctx)
    running = (
        jnp.full((2, local_heads, half_rows), MASKED_SCORE, jnp.float32),
        jnp.zeros((2, local_heads, half_rows), jnp.float32),
        jnp.zeros((2, half_rows, local_heads, HD), jnp.float32),
    )
    travel = queries
    for hop_step in range(devices_ctx):
        anchor = (ctx_index - hop_step) % devices_ctx
        query_pos = folded_positions(shard_rows, anchor * shard_rows, shard_rows, devices_ctx)
        query_doc = lax.dynamic_slice_in_dim(all_docs, anchor * shard_rows, shard_rows, 0)
        largest, totals, summed = attend_shard(
            running, travel, query_pos, query_doc, keys, values, own_pos, doc_ids
        )
        running = (
            passed_along(largest.astype(jnp.bfloat16), "ctx", 1).astype(largest.dtype),
            passed_along(totals.astype(jnp.bfloat16), "ctx", 1).astype(totals.dtype),
            passed_along(summed.astype(jnp.bfloat16), "ctx", 1).astype(summed.dtype),
        )
        if hop_step + 1 < devices_ctx:
            travel = passed_along(travel, "ctx", 1)
    largest, totals, summed = running
    attended = summed / totals.transpose(0, 2, 1)[:, :, :, None]
    attended = attended.reshape(shard_rows, local_heads * HD).astype(jnp.bfloat16)
    partial_out = jnp.dot(attended, w_out, preferred_element_type=jnp.float32)
    return lax.psum_scatter(
        partial_out.astype(jnp.bfloat16), "head", scatter_dimension=1, tiled=True
    )


SMALL = pl.CostEstimate(flops=1024, bytes_accessed=1024, transcendentals=0)
TILE = 256
MOST_DOCS = 16


def params(mib):
    return pltpu.CompilerParams(vmem_limit_bytes=mib * 1024 * 1024)


def whole(shape):
    return pl.BlockSpec(shape, lambda step, scalars: (0,) * len(shape))


def pack(ctx_index, half, queries, keys, values, docs):
    rows = queries.shape[0] // 2
    group = queries.shape[1] // HD
    doc_rows = 0 if docs is None else 16 * pl.cdiv(docs.shape[0], 16)
    total = 3 * rows + doc_rows

    def kernel(ctx_ref, *refs):
        outs = refs[len(refs) - (group - 1) :]
        if docs is not None:
            mine = refs[3 * (group - 1)][...].astype(jnp.float32)
            empty = jnp.zeros((doc_rows - mine.shape[0], HD), jnp.float32)
            mine = jnp.concatenate([mine, empty], axis=0).astype(jnp.bfloat16)
        for place in range(group - 1):
            for part in range(2):
                outs[place][part * rows : (part + 1) * rows, :] = refs[place * 3 + part][...]
            for block in range(rows // HD):
                taken = refs[place * 3 + 2][block * HD : (block + 1) * HD, :]
                lower = 2 * rows + block * HD
                outs[place][lower : lower + HD, :] = jnp.transpose(taken)
            if docs is not None:
                outs[place][3 * rows :, :] = mine

    def piece(distance):
        return pl.BlockSpec((rows, HD), lambda step, ctx: (half, ctx[0] ^ distance))

    in_specs = []
    operands = []
    for distance in range(1, group):
        for array in (queries, keys, values):
            in_specs.append(piece(distance))
            operands.append(array)
    if docs is not None:
        in_specs.append(whole(docs.shape))
        operands.append(docs)
    return pl.pallas_call(
        kernel,
        grid_spec=pltpu.PrefetchScalarGridSpec(
            num_scalar_prefetch=1,
            grid=(1,),
            in_specs=in_specs,
            out_specs=[whole((total, HD))] * (group - 1),
        ),
        out_shape=[jax.ShapeDtypeStruct((total, HD), jnp.bfloat16)] * (group - 1),
        compiler_params=params(56),
        cost_estimate=SMALL,
        name="pack",
    )(ctx_index, *operands)


def pack_projection(places, w_mine, w_sibling):
    depth, width = w_mine.shape
    turns = len(TURNS)
    columns = width // (2 * turns)

    def kernel(places_ref, mine_in, sibling_in, mine_out, sibling_out):
        mine_out[...] = mine_in[...]
        sibling_out[...] = sibling_in[...]

    in_spec = pl.BlockSpec((depth, columns), lambda turn, at: (0, at[turn]))
    out_spec = pl.BlockSpec((depth, columns), lambda turn, at: (0, turn))
    return pl.pallas_call(
        kernel,
        grid_spec=pltpu.PrefetchScalarGridSpec(
            num_scalar_prefetch=1,
            grid=(turns,),
            in_specs=[in_spec] * 2,
            out_specs=[out_spec] * 2,
        ),
        out_shape=[jax.ShapeDtypeStruct((depth, turns * columns), w_mine.dtype)] * 2,
        compiler_params=params(56),
        cost_estimate=SMALL,
        name="pack_projection",
    )(places, w_mine, w_sibling)


def attend(ctx_index, queries, keys, values, docs, low, high):
    rows = queries.shape[0] // 2
    group = queries.shape[1] // HD
    with_high = high is not None
    per_block = rows // TILE
    lines = rows // HD
    key_rows = (2 * group if with_high else group) * rows
    key_tiles = key_rows // TILE
    scaling = LOG2E / math.sqrt(HD)

    def kernel(ctx_ref, *refs):
        refs = list(refs)
        own_low = [refs.pop(0) for _ in range(3)]
        own_high = [refs.pop(0) for _ in range(3)] if with_high else None
        own_docs = refs.pop(0)
        low_refs = [refs.pop(0) for _ in range(group - 1)]
        high_refs = [refs.pop(0) for _ in range(group - 1)] if with_high else None
        outs = [refs.pop(0) for _ in range(group)]
        key_buf, value_buf, doc_buf = refs[:3]
        query_buf, start_buf, largest_buf, summed = (
            refs[3 + kind * group : 3 + (kind + 1) * group] for kind in range(4)
        )
        ctx = ctx_ref[0]

        def part(upper, distance, index, lower=0, count=rows):
            if distance == 0:
                return (own_high if upper else own_low)[index][lower : lower + count, :]
            source = (high_refs if upper else low_refs)[distance - 1]
            return source[index * rows + lower : index * rows + lower + count, :]

        place = {}
        doc_rows = {}
        for upper in (False, True) if with_high else (False,):
            for distance in range(group):
                source = ctx ^ distance
                block = 2 * group - 1 - source if upper else source
                place[upper, distance] = block
                offset = pl.multiple_of(block * rows, rows)
                key_buf[pl.ds(offset, rows), :] = part(upper, distance, 1)
                if distance == 0:
                    both = own_docs[...].astype(jnp.float32)
                else:
                    both = low_refs[distance - 1][3 * rows :, :].astype(jnp.float32)
                begin = lines if upper else 0
                mine = []
                for line in range(lines):
                    taken = part(upper, distance, 2, line * HD, HD)
                    if distance == 0:
                        taken = jnp.transpose(taken)
                    column = pl.multiple_of(block * rows + line * HD, HD)
                    value_buf[:HD, pl.ds(column, HD)] = taken
                    mine.append(both[begin + line : begin + line + 1, :])
                    doc_buf[pl.ds(block * lines + line, 1), :] = mine[-1]
                doc_rows[upper, distance] = jnp.concatenate(mine, axis=1)
        value_buf[HD:, :] = jnp.ones((value_buf.shape[0] - HD, key_rows), jnp.bfloat16)

        all_docs = doc_buf[...]
        starts = [jnp.zeros((1, rows), jnp.float32)] * group
        for number in range(1, MOST_DOCS):
            smaller = jnp.where(all_docs < number, 1.0, 0.0)
            count = jnp.sum(jnp.sum(smaller, axis=0, keepdims=True), axis=1, keepdims=True)
            for distance in range(group):
                reached = doc_rows[with_high, distance] >= number
                starts[distance] = jnp.where(reached, count, starts[distance])

        def scores_of(query, offset):
            raw = lax.dot_general(
                key_buf[pl.ds(offset, TILE), :],
                query,
                (((1,), (1,)), ((), ())),
                preferred_element_type=jnp.float32,
            )
            return raw * scaling

        def weighted(weights, offset):
            return jnp.dot(
                value_buf[:, pl.ds(offset, TILE)],
                weights.astype(jnp.bfloat16),
                preferred_element_type=jnp.float32,
            )

        key_row = lax.broadcasted_iota(jnp.int32, (TILE, TILE), 0)
        causal = key_row <= lax.broadcasted_iota(jnp.int32, (TILE, TILE), 1)
        key_row = key_row.astype(jnp.float32)
        firsts = []
        counts = []
        for lane in range(group):
            for slot in range(per_block):
                distance = lane ^ (slot * (group - 1))
                query = part(with_high, distance, 0, slot * TILE, TILE)
                query_buf[lane][slot] = query
                start = starts[distance][:, slot * TILE : (slot + 1) * TILE]
                start_buf[lane][slot, 0:1, :] = start
                end = place[with_high, distance] * per_block + slot
                offset = pl.multiple_of(end * TILE, TILE)
                least = start - offset.astype(jnp.float32)
                scores = scores_of(query, offset)
                scores = jnp.where((key_row >= least) & causal, scores, MASKED_SCORE)
                largest = jnp.max(scores, axis=0, keepdims=True)
                largest_buf[lane][slot, 0:1, :] = largest
                summed[lane][slot] = weighted(jnp.exp2(scores - largest), offset)
                first = start[0, 0].astype(jnp.int32) // TILE
                firsts.append(first)
                counts.append(end - first)

        longest = jnp.int32(0)
        for lane in range(group):
            of_lane = counts[lane * per_block : (lane + 1) * per_block]
            longest = jnp.maximum(longest, sum(of_lane))

        def visit(step, carry):
            slots = []
            offsets = []
            beyonds = []
            for lane in range(group):
                slot = jnp.int32(0)
                index = firsts[lane * per_block] + step
                before = counts[lane * per_block]
                for later in range(1, per_block):
                    reached = step >= before
                    slot = jnp.where(reached, later, slot)
                    place_later = lane * per_block + later
                    index = jnp.where(reached, firsts[place_later] + step - before, index)
                    before = before + counts[place_later]
                offset = pl.multiple_of(jnp.minimum(index, key_tiles - 1) * TILE, TILE)
                slots.append(slot)
                offsets.append(offset)
                beyonds.append(jnp.where(step < before, -offset.astype(jnp.float32), 1e9))
            each = range(group)
            scores = [scores_of(query_buf[lane][slots[lane]], offsets[lane]) for lane in each]
            old_max = [largest_buf[lane][slots[lane], 0:1, :] for lane in each]
            new_max = []
            for lane in each:
                least = start_buf[lane][slots[lane], 0:1, :] + beyonds[lane]
                scores[lane] = jnp.where(key_row >= least, scores[lane], MASKED_SCORE)
                tile_max = jnp.max(scores[lane], axis=0, keepdims=True)
                new_max.append(jnp.maximum(old_max[lane], tile_max))
            products = [
                weighted(jnp.exp2(scores[lane] - new_max[lane]), offsets[lane]) for lane in each
            ]
            for lane in each:
                factor = jnp.exp2(old_max[lane] - new_max[lane])
                summed[lane][slots[lane]] = summed[lane][slots[lane]] * factor + products[lane]
                largest_buf[lane][slots[lane], 0:1, :] = new_max[lane]
            return carry

        lax.fori_loop(0, longest, visit, jnp.int32(0))
        for lane in range(group):
            for slot in range(per_block):
                state = summed[lane]
                attended = state[slot, :HD, :] * (1.0 / state[slot, HD : HD + 1, :])
                out = outs[lane ^ (slot * (group - 1))]
                out[slot * TILE : (slot + 1) * TILE, :] = jnp.transpose(
                    attended.astype(jnp.bfloat16)
                )

    def own(upper):
        return pl.BlockSpec((rows, HD), lambda step, ctx: (int(upper), ctx[0]))

    in_specs = [own(False)] * 3
    operands = [queries, keys, values]
    if with_high:
        in_specs += [own(True)] * 3
        operands += [queries, keys, values]
    received = [docs, *low, *(high if with_high else ())]
    operands += received
    in_specs += [whole(array.shape) for array in received]
    return pl.pallas_call(
        kernel,
        grid_spec=pltpu.PrefetchScalarGridSpec(
            num_scalar_prefetch=1,
            grid=(1,),
            in_specs=in_specs,
            out_specs=[whole((rows, HD))] * group,
            scratch_shapes=[
                pltpu.VMEM((key_rows, HD), jnp.bfloat16),
                pltpu.VMEM((HD + 16, key_rows), jnp.bfloat16),
                pltpu.VMEM((key_rows // HD, HD), jnp.float32),
                *[pltpu.VMEM((per_block, TILE, HD), jnp.bfloat16)] * group,
                *[pltpu.VMEM((per_block, 8, TILE), jnp.float32)] * (2 * group),
                *[pltpu.VMEM((per_block, HD + 16, TILE), jnp.float32)] * group,
            ],
        ),
        out_shape=[jax.ShapeDtypeStruct((rows, HD), jnp.bfloat16)] * group,
        compiler_params=params(40),
        cost_estimate=SMALL,
        name="attend_high" if with_high else "attend_low",
    )(ctx_index, *operands)


def assemble(ctx_index, pieces, cuts):
    rows = pieces[0].shape[0]
    group = len(pieces)
    spans = list(zip(cuts[:-1], cuts[1:]))

    def kernel(ctx_ref, *refs):
        for part, (lower, upper) in enumerate(spans):
            for distance in range(group):
                column = pl.multiple_of((ctx_ref[0] ^ distance) * HD, HD)
                refs[group + part][:, pl.ds(column, HD)] = refs[distance][lower:upper, :]

    shapes = [(upper - lower, group * HD) for lower, upper in spans]
    return pl.pallas_call(
        kernel,
        grid_spec=pltpu.PrefetchScalarGridSpec(
            num_scalar_prefetch=1,
            grid=(1,),
            in_specs=[whole((rows, HD))] * group,
            out_specs=[whole(shape) for shape in shapes],
        ),
        out_shape=[jax.ShapeDtypeStruct(shape, jnp.bfloat16) for shape in shapes],
        compiler_params=params(16),
        cost_estimate=SMALL,
        name="assemble",
    )(ctx_index, *pieces)


def plain(shape):
    return pl.BlockSpec(shape, lambda step: (0,) * len(shape))


def stacked(refs):
    values = [ref[...] for ref in refs]
    return values[0] if len(values) == 1 else jnp.concatenate(values, axis=0)


def project(wanted, mine, sibling, w_mine, w_sibling):
    parts = len(mine)
    depth = mine[0].shape[1]
    columns = w_mine.shape[1] // len(TURNS)
    turns = sorted({turn for output in wanted for turn, _, _ in output})

    def kernel(*refs):
        own_rows = stacked(refs[:parts])
        other_rows = stacked(refs[parts : 2 * parts])
        weights = refs[2 * parts : 2 * parts + 2 * len(turns)]
        outs = refs[2 * parts + 2 * len(turns) :]
        for out, output in zip(outs, wanted):
            place = 0
            for turn, lower, upper in output:
                at = turns.index(turn)
                total = jnp.dot(
                    own_rows[lower:upper, :], weights[at][...], preferred_element_type=jnp.float32
                )
                total += jnp.dot(
                    other_rows[lower:upper, :],
                    weights[len(turns) + at][...],
                    preferred_element_type=jnp.float32,
                )
                out[place : place + upper - lower, :] = total.astype(jnp.bfloat16)
                place += upper - lower

    def columns_of(turn):
        return pl.BlockSpec((depth, columns), lambda step: (0, turn))

    shapes = [(sum(upper - lower for _, lower, upper in output), columns) for output in wanted]
    return pl.pallas_call(
        kernel,
        grid=(1,),
        in_specs=[plain(part.shape) for part in (*mine, *sibling)]
        + [columns_of(turn) for turn in turns] * 2,
        out_specs=[plain(shape) for shape in shapes],
        out_shape=[jax.ShapeDtypeStruct(shape, jnp.bfloat16) for shape in shapes],
        compiler_params=params(24),
        cost_estimate=SMALL,
        name="project",
    )(*mine, *sibling, *([w_mine] * len(turns)), *([w_sibling] * len(turns)))


def finish(half, rows, terms, result):
    flat = [array for term in terms for array, _ in term]
    columns = flat[0].shape[1]

    def kernel(*refs):
        refs = list(refs)
        total = None
        for term in terms:
            values = [refs.pop(0)[first:, :].astype(jnp.float32) for _, first in term]
            value = values[0] if len(values) == 1 else jnp.concatenate(values, axis=0)
            total = value if total is None else total + value
        refs[-1][...] = total.astype(jnp.bfloat16)

    in_specs = [plain(array.shape) for array in flat]
    operands = list(flat)
    aliases = {}
    if result is not None:
        in_specs.append(pl.BlockSpec(memory_space=pl.ANY))
        operands.append(result)
        aliases = {len(flat): 0}
    return pl.pallas_call(
        kernel,
        grid=(1,),
        in_specs=in_specs,
        out_specs=pl.BlockSpec((rows, columns), lambda step: (half, 0)),
        out_shape=jax.ShapeDtypeStruct((2 * rows, columns), jnp.bfloat16),
        input_output_aliases=aliases,
        compiler_params=params(16),
        cost_estimate=SMALL,
        name="finish",
    )(*operands)


def swap(value, axis, distance):
    count = lax.axis_size(axis)
    return lax.ppermute(value, axis, [(source, source ^ distance) for source in range(count)])


def add(*terms):
    total = terms[0].astype(jnp.float32)
    for term in terms[1:]:
        total = total + term.astype(jnp.float32)
    return total.astype(jnp.bfloat16)


TURNS = (3, 1, 2, 0)


def tie(*values):
    return lax.optimization_barrier(values)


def exchange_local(queries, keys, values, doc_ids, w_out):
    shard_rows = queries.shape[0]
    group = queries.shape[1] // HD
    ctx_index = lax.axis_index("ctx").astype(jnp.int32).reshape(1)
    head_index = lax.axis_index("head").astype(jnp.int32)
    places = head_index ^ (2 * jnp.array(TURNS, jnp.int32))
    docs = doc_ids.reshape(shard_rows // HD, HD)
    near = range(1, group)

    w_sibling = swap(w_out, "head", 1)
    low_out = pack(ctx_index, 0, queries, keys, values, docs)
    low_out, later = tie(low_out, (queries, keys, values))
    low = [swap(low_out[distance - 1], "ctx", distance) for distance in near]
    high_out = pack(ctx_index, 1, *later, None)
    high = [swap(high_out[distance - 1], "ctx", distance) for distance in near[:-1]]
    w_packed = pack_projection(places, w_out, w_sibling)
    low, w_packed = tie(low, w_packed)

    def send_back(pieces):
        return [swap(pieces[distance], "ctx", distance) for distance in near]

    rows = shard_rows // 2
    cut = rows * 21 // 32 // 16 * 16
    middle = rows // 2

    def projected(mine, sibling, *wanted):
        return list(project(wanted, mine, sibling, *w_packed))

    def to_next(part, distance):
        return swap(part, "head", 2 * distance)

    pieces = attend(ctx_index, queries, keys, values, docs, low, None)
    pieces, diagonal_out = tie(pieces, high_out[-1])
    back = send_back(pieces)
    back, high = tie(back, high)
    high = [*high, swap(diagonal_out, "ctx", near[-1])]
    mine = assemble(ctx_index, [pieces[0], *back], (0, rows))
    sibling = [swap(part, "head", 1) for part in mine]
    (share,) = projected(mine, sibling, [(0, 0, cut)])
    far = to_next(share, 1)
    (behind,) = projected(mine, sibling, [(0, cut, rows), (1, 0, rows)])
    shares = projected(mine, sibling, [(2, 0, cut)], [(2, cut, rows)])
    (kept,) = projected(mine, sibling, [(3, 0, rows)])

    passed = add(shares[0], far)
    high, passed, _, shares[1], kept = tie(high, passed, behind, shares[1], kept)
    behind = to_next(behind, 1)
    across = to_next(passed, 2)
    pieces = attend(ctx_index, queries, keys, values, docs, low, high)
    back = send_back(pieces)
    mine = assemble(ctx_index, [pieces[0], *back], (0, cut, rows))
    mine, across = tie(mine, across)
    sibling = [swap(part, "head", 1) for part in mine]
    late = projected(mine, sibling, [(0, 0, cut)], [(0, cut, rows)])
    late, behind = tie(late, behind)
    far = [to_next(part, 1) for part in late]
    across = [across, to_next(add(shares[1], behind[: rows - cut]), 2)]
    late = projected(mine, sibling, [(2, 0, cut)], [(2, cut, rows)])
    passed = [add(*both) for both in zip(late, far)]
    passed[0], across[1] = tie(passed[0], across[1])
    terms = [[(kept, 0)], [(behind, rows - cut)], [(part, 0) for part in across]]
    result = finish(0, rows, terms, None)
    across = [to_next(part, 2) for part in passed]
    late = projected(mine, sibling, [(1, 0, middle)], [(1, middle, rows)])
    late, passed = tie(late, passed)
    near_sum = [to_next(part, 1) for part in late]
    (kept,) = projected(mine, sibling, [(3, 0, rows)])
    terms = [[(kept, 0)], [(part, 0) for part in near_sum], [(part, 0) for part in across]]
    return finish(1, rows, terms, result)


def solution(mesh):
    in_specs = (P("ctx", "head"), P("ctx", "head"), P("ctx", "head"), P("ctx"), P("head", None))
    out_specs = P("ctx", "head")
    ctx_count = mesh.shape["ctx"]
    head_count = mesh.shape["head"]

    def local(queries, keys, values, doc_ids, w_out):
        heads = queries.shape[1] // HD
        exchange = heads == ctx_count and heads == 4 and head_count == 2 * len(TURNS)
        exchange = exchange and queries.shape[0] % (4 * TILE) == 0
        body = exchange_local if exchange else ring_local
        return body(queries, keys, values, doc_ids, w_out)

    return jax.shard_map(
        local, mesh=mesh, in_specs=in_specs, out_specs=out_specs, check_vma=False
    )
```

```python
import functools
import math

import jax
import jax.numpy as jnp
from jax import lax
from jax.experimental import pallas as pl
from jax.experimental.pallas import tpu as pltpu
from jax.sharding import PartitionSpec as P

HD = 128


MASKED_SCORE = -1e30
LOG2E = 1.4426950408889634


def passed_along(value, axis, steps):
    count = lax.axis_size(axis)
    pairs = [(source, (source + steps) % count) for source in range(count)]
    return lax.ppermute(value, axis, pairs)


def folded_positions(row_total, offset, shard_rows, devices_ctx):
    flat_index = offset + lax.iota(jnp.int32, row_total)
    owner_dev = flat_index // shard_rows
    within = flat_index % shard_rows
    half_rows = shard_rows // 2
    fold_block = jnp.where(within < half_rows, owner_dev, 2 * devices_ctx - 1 - owner_dev)
    return fold_block * half_rows + within % half_rows


def block_update(
    running, query, query_pos, query_doc, key_block, value_block, pos_block, doc_block
):
    largest, totals, summed = running
    query_rows = query.shape[0]
    local_heads = query.shape[1] // HD
    query_heads = query.reshape(query_rows, local_heads, HD)
    key_heads = key_block.reshape(key_block.shape[0], local_heads, HD)
    value_heads = value_block.reshape(value_block.shape[0], local_heads, HD)
    scores = jnp.einsum(
        "qhd,khd->hqk", query_heads, key_heads, preferred_element_type=jnp.float32
    ) * (1.0 / math.sqrt(HD))
    allowed = (query_doc[:, None] == doc_block[None, :]) & (
        pos_block[None, :] <= query_pos[:, None]
    )
    scores = jnp.where(allowed[None], scores, MASKED_SCORE)
    new_max = jnp.maximum(largest, jnp.max(scores, axis=2))
    weights = jnp.where(allowed[None], jnp.exp(scores - new_max[:, :, None]), 0.0)
    factor = jnp.exp(largest - new_max)
    totals = totals * factor + jnp.sum(weights, axis=2)
    product = jnp.einsum(
        "hqk,khd->qhd",
        weights.astype(jnp.bfloat16),
        value_heads,
        preferred_element_type=jnp.float32,
    )
    summed = summed * factor.T[:, :, None] + product
    return (new_max, totals, summed)


def attend_rows(running, query, query_pos, query_doc, key_rows, value_rows, key_pos, key_doc):
    row_total = key_rows.shape[0]
    block_rows = math.gcd(row_total, query.shape[0])
    block_count = row_total // block_rows
    highest = jnp.max(query_pos)

    def visit(partial_value, blocks):
        key_block, value_block, pos_block, doc_block = blocks
        masked_out = jnp.min(pos_block) > highest
        updated = lax.cond(
            masked_out,
            lambda frozen: frozen,
            lambda frozen: block_update(
                frozen, query, query_pos, query_doc, key_block, value_block, pos_block, doc_block
            ),
            partial_value,
        )
        return (updated, None)

    blocks = (
        key_rows.reshape(block_count, block_rows, key_rows.shape[1]),
        value_rows.reshape(block_count, block_rows, value_rows.shape[1]),
        key_pos.reshape(block_count, block_rows),
        key_doc.reshape(block_count, block_rows),
    )
    running, _ = lax.scan(visit, running, blocks)
    return running


def attend_shard(running, query, query_pos, query_doc, key_rows, value_rows, key_pos, key_doc):
    largest, totals, summed = running
    half_rows = query.shape[0] // 2
    new_largest = []
    new_totals = []
    new_summed = []
    for half_idx in range(2):
        lower = half_idx * half_rows
        part_state = (largest[half_idx], totals[half_idx], summed[half_idx])
        part_state = attend_rows(
            part_state,
            query[lower : lower + half_rows],
            query_pos[lower : lower + half_rows],
            query_doc[lower : lower + half_rows],
            key_rows,
            value_rows,
            key_pos,
            key_doc,
        )
        new_largest.append(part_state[0])
        new_totals.append(part_state[1])
        new_summed.append(part_state[2])
    return (jnp.stack(new_largest), jnp.stack(new_totals), jnp.stack(new_summed))


def ring_local(queries, keys, values, doc_ids, w_out):
    shard_rows = queries.shape[0]
    half_rows = shard_rows // 2
    local_heads = queries.shape[1] // HD
    devices_ctx = lax.axis_size("ctx")
    ctx_index = lax.axis_index("ctx")
    all_docs = lax.all_gather(doc_ids, "ctx", axis=0, tiled=True)
    own_pos = folded_positions(shard_rows, ctx_index * shard_rows, shard_rows, devices_ctx)
    running = (
        jnp.full((2, local_heads, half_rows), MASKED_SCORE, jnp.float32),
        jnp.zeros((2, local_heads, half_rows), jnp.float32),
        jnp.zeros((2, half_rows, local_heads, HD), jnp.float32),
    )
    travel = queries
    for hop_step in range(devices_ctx):
        anchor = (ctx_index - hop_step) % devices_ctx
        query_pos = folded_positions(shard_rows, anchor * shard_rows, shard_rows, devices_ctx)
        query_doc = lax.dynamic_slice_in_dim(all_docs, anchor * shard_rows, shard_rows, 0)
        largest, totals, summed = attend_shard(
            running, travel, query_pos, query_doc, keys, values, own_pos, doc_ids
        )
        running = (
            passed_along(largest.astype(jnp.bfloat16), "ctx", 1).astype(largest.dtype),
            passed_along(totals.astype(jnp.bfloat16), "ctx", 1).astype(totals.dtype),
            passed_along(summed.astype(jnp.bfloat16), "ctx", 1).astype(summed.dtype),
        )
        if hop_step + 1 < devices_ctx:
            travel = passed_along(travel, "ctx", 1)
    largest, totals, summed = running
    attended = summed / totals.transpose(0, 2, 1)[:, :, :, None]
    attended = attended.reshape(shard_rows, local_heads * HD).astype(jnp.bfloat16)
    partial_out = jnp.dot(attended, w_out, preferred_element_type=jnp.float32)
    return lax.psum_scatter(
        partial_out.astype(jnp.bfloat16), "head", scatter_dimension=1, tiled=True
    )


SMALL = pl.CostEstimate(flops=1024, bytes_accessed=1024, transcendentals=0)
TILE = 256
MOST_DOCS = 16


def params(mib):
    return pltpu.CompilerParams(vmem_limit_bytes=mib * 1024 * 1024)


def whole(shape):
    return pl.BlockSpec(shape, lambda step, scalars: (0,) * len(shape))


def pack(ctx_index, half, queries, keys, values, docs):
    rows = queries.shape[0] // 2
    group = queries.shape[1] // HD
    doc_rows = 0 if docs is None else 16 * pl.cdiv(docs.shape[0], 16)
    total = 3 * rows + doc_rows

    def kernel(ctx_ref, *refs):
        outs = refs[len(refs) - (group - 1) :]
        if docs is not None:
            mine = refs[3 * (group - 1)][...].astype(jnp.float32)
            empty = jnp.zeros((doc_rows - mine.shape[0], HD), jnp.float32)
            mine = jnp.concatenate([mine, empty], axis=0).astype(jnp.bfloat16)
        for place in range(group - 1):
            for part in range(2):
                outs[place][part * rows : (part + 1) * rows, :] = refs[place * 3 + part][...]
            for block in range(rows // HD):
                taken = refs[place * 3 + 2][block * HD : (block + 1) * HD, :]
                lower = 2 * rows + block * HD
                outs[place][lower : lower + HD, :] = jnp.transpose(taken)
            if docs is not None:
                outs[place][3 * rows :, :] = mine

    def piece(distance):
        return pl.BlockSpec((rows, HD), lambda step, ctx: (half, ctx[0] ^ distance))

    in_specs = []
    operands = []
    for distance in range(1, group):
        for array in (queries, keys, values):
            in_specs.append(piece(distance))
            operands.append(array)
    if docs is not None:
        in_specs.append(whole(docs.shape))
        operands.append(docs)
    return pl.pallas_call(
        kernel,
        grid_spec=pltpu.PrefetchScalarGridSpec(
            num_scalar_prefetch=1,
            grid=(1,),
            in_specs=in_specs,
            out_specs=[whole((total, HD))] * (group - 1),
        ),
        out_shape=[jax.ShapeDtypeStruct((total, HD), jnp.bfloat16)] * (group - 1),
        compiler_params=params(56),
        cost_estimate=SMALL,
        name="pack",
    )(ctx_index, *operands)


def pack_projection(places, w_mine, w_sibling):
    depth, width = w_mine.shape
    turns = len(TURNS)
    columns = width // (2 * turns)

    def kernel(places_ref, mine_in, sibling_in, mine_out, sibling_out):
        mine_out[...] = mine_in[...]
        sibling_out[...] = sibling_in[...]

    in_spec = pl.BlockSpec((depth, columns), lambda turn, at: (0, at[turn]))
    out_spec = pl.BlockSpec((depth, columns), lambda turn, at: (0, turn))
    return pl.pallas_call(
        kernel,
        grid_spec=pltpu.PrefetchScalarGridSpec(
            num_scalar_prefetch=1,
            grid=(turns,),
            in_specs=[in_spec] * 2,
            out_specs=[out_spec] * 2,
        ),
        out_shape=[jax.ShapeDtypeStruct((depth, turns * columns), w_mine.dtype)] * 2,
        compiler_params=params(56),
        cost_estimate=SMALL,
        name="pack_projection",
    )(places, w_mine, w_sibling)


def attend(ctx_index, queries, keys, values, docs, low, high):
    rows = queries.shape[0] // 2
    group = queries.shape[1] // HD
    with_high = high is not None
    per_block = rows // TILE
    lines = rows // HD
    key_rows = (2 * group if with_high else group) * rows
    key_tiles = key_rows // TILE
    scaling = LOG2E / math.sqrt(HD)

    def kernel(ctx_ref, *refs):
        refs = list(refs)
        own_low = [refs.pop(0) for _ in range(3)]
        own_high = [refs.pop(0) for _ in range(3)] if with_high else None
        own_docs = refs.pop(0)
        low_refs = [refs.pop(0) for _ in range(group - 1)]
        high_refs = [refs.pop(0) for _ in range(group - 1)] if with_high else None
        outs = [refs.pop(0) for _ in range(group)]
        key_buf, value_buf, doc_buf = refs[:3]
        query_buf, start_buf, largest_buf, summed = (
            refs[3 + kind * group : 3 + (kind + 1) * group] for kind in range(4)
        )
        ctx = ctx_ref[0]

        def part(upper, distance, index, lower=0, count=rows):
            if distance == 0:
                return (own_high if upper else own_low)[index][lower : lower + count, :]
            source = (high_refs if upper else low_refs)[distance - 1]
            return source[index * rows + lower : index * rows + lower + count, :]

        place = {}
        doc_rows = {}
        for upper in (False, True) if with_high else (False,):
            for distance in range(group):
                source = ctx ^ distance
                block = 2 * group - 1 - source if upper else source
                place[upper, distance] = block
                offset = pl.multiple_of(block * rows, rows)
                key_buf[pl.ds(offset, rows), :] = part(upper, distance, 1)
                if distance == 0:
                    both = own_docs[...].astype(jnp.float32)
                else:
                    both = low_refs[distance - 1][3 * rows :, :].astype(jnp.float32)
                begin = lines if upper else 0
                mine = []
                for line in range(lines):
                    taken = part(upper, distance, 2, line * HD, HD)
                    if distance == 0:
                        taken = jnp.transpose(taken)
                    column = pl.multiple_of(block * rows + line * HD, HD)
                    value_buf[:HD, pl.ds(column, HD)] = taken
                    mine.append(both[begin + line : begin + line + 1, :])
                    doc_buf[pl.ds(block * lines + line, 1), :] = mine[-1]
                doc_rows[upper, distance] = jnp.concatenate(mine, axis=1)
        value_buf[HD:, :] = jnp.ones((value_buf.shape[0] - HD, key_rows), jnp.bfloat16)

        all_docs = doc_buf[...]
        starts = [jnp.zeros((1, rows), jnp.float32)] * group
        for number in range(1, MOST_DOCS):
            smaller = jnp.where(all_docs < number, 1.0, 0.0)
            count = jnp.sum(jnp.sum(smaller, axis=0, keepdims=True), axis=1, keepdims=True)
            for distance in range(group):
                reached = doc_rows[with_high, distance] >= number
                starts[distance] = jnp.where(reached, count, starts[distance])

        def scores_of(query, offset):
            raw = lax.dot_general(
                key_buf[pl.ds(offset, TILE), :],
                query,
                (((1,), (1,)), ((), ())),
                preferred_element_type=jnp.float32,
            )
            return raw * scaling

        def weighted(weights, offset):
            return jnp.dot(
                value_buf[:, pl.ds(offset, TILE)],
                weights.astype(jnp.bfloat16),
                preferred_element_type=jnp.float32,
            )

        key_row = lax.broadcasted_iota(jnp.int32, (TILE, TILE), 0)
        causal = key_row <= lax.broadcasted_iota(jnp.int32, (TILE, TILE), 1)
        key_row = key_row.astype(jnp.float32)
        firsts = []
        counts = []
        for lane in range(group):
            for slot in range(per_block):
                distance = lane ^ (slot * (group - 1))
                query = part(with_high, distance, 0, slot * TILE, TILE)
                query_buf[lane][slot] = query
                start = starts[distance][:, slot * TILE : (slot + 1) * TILE]
                start_buf[lane][slot, 0:1, :] = start
                end = place[with_high, distance] * per_block + slot
                offset = pl.multiple_of(end * TILE, TILE)
                least = start - offset.astype(jnp.float32)
                scores = scores_of(query, offset)
                scores = jnp.where((key_row >= least) & causal, scores, MASKED_SCORE)
                largest = jnp.max(scores, axis=0, keepdims=True)
                largest_buf[lane][slot, 0:1, :] = largest
                summed[lane][slot] = weighted(jnp.exp2(scores - largest), offset)
                first = start[0, 0].astype(jnp.int32) // TILE
                firsts.append(first)
                counts.append(end - first)

        longest = jnp.int32(0)
        for lane in range(group):
            of_lane = counts[lane * per_block : (lane + 1) * per_block]
            longest = jnp.maximum(longest, sum(of_lane))

        def visit(step, carry):
            slots = []
            offsets = []
            beyonds = []
            for lane in range(group):
                slot = jnp.int32(0)
                index = firsts[lane * per_block] + step
                before = counts[lane * per_block]
                for later in range(1, per_block):
                    reached = step >= before
                    slot = jnp.where(reached, later, slot)
                    place_later = lane * per_block + later
                    index = jnp.where(reached, firsts[place_later] + step - before, index)
                    before = before + counts[place_later]
                offset = pl.multiple_of(jnp.minimum(index, key_tiles - 1) * TILE, TILE)
                slots.append(slot)
                offsets.append(offset)
                beyonds.append(jnp.where(step < before, -offset.astype(jnp.float32), 1e9))
            each = range(group)
            scores = [scores_of(query_buf[lane][slots[lane]], offsets[lane]) for lane in each]
            old_max = [largest_buf[lane][slots[lane], 0:1, :] for lane in each]
            new_max = []
            for lane in each:
                least = start_buf[lane][slots[lane], 0:1, :] + beyonds[lane]
                scores[lane] = jnp.where(key_row >= least, scores[lane], MASKED_SCORE)
                tile_max = jnp.max(scores[lane], axis=0, keepdims=True)
                new_max.append(jnp.maximum(old_max[lane], tile_max))
            products = [
                weighted(jnp.exp2(scores[lane] - new_max[lane]), offsets[lane]) for lane in each
            ]
            for lane in each:
                factor = jnp.exp2(old_max[lane] - new_max[lane])
                summed[lane][slots[lane]] = summed[lane][slots[lane]] * factor + products[lane]
                largest_buf[lane][slots[lane], 0:1, :] = new_max[lane]
            return carry

        lax.fori_loop(0, longest, visit, jnp.int32(0))
        for lane in range(group):
            for slot in range(per_block):
                state = summed[lane]
                attended = state[slot, :HD, :] * (1.0 / state[slot, HD : HD + 1, :])
                out = outs[lane ^ (slot * (group - 1))]
                out[slot * TILE : (slot + 1) * TILE, :] = jnp.transpose(
                    attended.astype(jnp.bfloat16)
                )

    def own(upper):
        return pl.BlockSpec((rows, HD), lambda step, ctx: (int(upper), ctx[0]))

    in_specs = [own(False)] * 3
    operands = [queries, keys, values]
    if with_high:
        in_specs += [own(True)] * 3
        operands += [queries, keys, values]
    received = [docs, *low, *(high if with_high else ())]
    operands += received
    in_specs += [whole(array.shape) for array in received]
    return pl.pallas_call(
        kernel,
        grid_spec=pltpu.PrefetchScalarGridSpec(
            num_scalar_prefetch=1,
            grid=(1,),
            in_specs=in_specs,
            out_specs=[whole((rows, HD))] * group,
            scratch_shapes=[
                pltpu.VMEM((key_rows, HD), jnp.bfloat16),
                pltpu.VMEM((HD + 16, key_rows), jnp.bfloat16),
                pltpu.VMEM((key_rows // HD, HD), jnp.float32),
                *[pltpu.VMEM((per_block, TILE, HD), jnp.bfloat16)] * group,
                *[pltpu.VMEM((per_block, 8, TILE), jnp.float32)] * (2 * group),
                *[pltpu.VMEM((per_block, HD + 16, TILE), jnp.float32)] * group,
            ],
        ),
        out_shape=[jax.ShapeDtypeStruct((rows, HD), jnp.bfloat16)] * group,
        compiler_params=params(40),
        cost_estimate=SMALL,
        name="attend_high" if with_high else "attend_low",
    )(ctx_index, *operands)


def assemble(ctx_index, pieces, cuts):
    rows = pieces[0].shape[0]
    group = len(pieces)
    spans = list(zip(cuts[:-1], cuts[1:]))

    def kernel(ctx_ref, *refs):
        for part, (lower, upper) in enumerate(spans):
            for distance in range(group):
                column = pl.multiple_of((ctx_ref[0] ^ distance) * HD, HD)
                refs[group + part][:, pl.ds(column, HD)] = refs[distance][lower:upper, :]

    shapes = [(upper - lower, group * HD) for lower, upper in spans]
    return pl.pallas_call(
        kernel,
        grid_spec=pltpu.PrefetchScalarGridSpec(
            num_scalar_prefetch=1,
            grid=(1,),
            in_specs=[whole((rows, HD))] * group,
            out_specs=[whole(shape) for shape in shapes],
        ),
        out_shape=[jax.ShapeDtypeStruct(shape, jnp.bfloat16) for shape in shapes],
        compiler_params=params(16),
        cost_estimate=SMALL,
        name="assemble",
    )(ctx_index, *pieces)


def plain(shape):
    return pl.BlockSpec(shape, lambda step: (0,) * len(shape))


def stacked(refs):
    values = [ref[...] for ref in refs]
    return values[0] if len(values) == 1 else jnp.concatenate(values, axis=0)


def project(wanted, mine, sibling, w_mine, w_sibling):
    parts = len(mine)
    depth = mine[0].shape[1]
    columns = w_mine.shape[1] // len(TURNS)
    turns = sorted({turn for output in wanted for turn, _, _ in output})

    def kernel(*refs):
        own_rows = stacked(refs[:parts])
        other_rows = stacked(refs[parts : 2 * parts])
        weights = refs[2 * parts : 2 * parts + 2 * len(turns)]
        outs = refs[2 * parts + 2 * len(turns) :]
        for out, output in zip(outs, wanted):
            place = 0
            for turn, lower, upper in output:
                at = turns.index(turn)
                total = jnp.dot(
                    own_rows[lower:upper, :], weights[at][...], preferred_element_type=jnp.float32
                )
                total += jnp.dot(
                    other_rows[lower:upper, :],
                    weights[len(turns) + at][...],
                    preferred_element_type=jnp.float32,
                )
                out[place : place + upper - lower, :] = total.astype(jnp.bfloat16)
                place += upper - lower

    def columns_of(turn):
        return pl.BlockSpec((depth, columns), lambda step: (0, turn))

    shapes = [(sum(upper - lower for _, lower, upper in output), columns) for output in wanted]
    return pl.pallas_call(
        kernel,
        grid=(1,),
        in_specs=[plain(part.shape) for part in (*mine, *sibling)]
        + [columns_of(turn) for turn in turns] * 2,
        out_specs=[plain(shape) for shape in shapes],
        out_shape=[jax.ShapeDtypeStruct(shape, jnp.bfloat16) for shape in shapes],
        compiler_params=params(24),
        cost_estimate=SMALL,
        name="project",
    )(*mine, *sibling, *([w_mine] * len(turns)), *([w_sibling] * len(turns)))


def finish(half, rows, terms, result):
    flat = [array for term in terms for array, _ in term]
    columns = flat[0].shape[1]

    def kernel(*refs):
        refs = list(refs)
        total = None
        for term in terms:
            values = [refs.pop(0)[first:, :].astype(jnp.float32) for _, first in term]
            value = values[0] if len(values) == 1 else jnp.concatenate(values, axis=0)
            total = value if total is None else total + value
        refs[-1][...] = total.astype(jnp.bfloat16)

    in_specs = [plain(array.shape) for array in flat]
    operands = list(flat)
    aliases = {}
    if result is not None:
        in_specs.append(pl.BlockSpec(memory_space=pl.ANY))
        operands.append(result)
        aliases = {len(flat): 0}
    return pl.pallas_call(
        kernel,
        grid=(1,),
        in_specs=in_specs,
        out_specs=pl.BlockSpec((rows, columns), lambda step: (half, 0)),
        out_shape=jax.ShapeDtypeStruct((2 * rows, columns), jnp.bfloat16),
        input_output_aliases=aliases,
        compiler_params=params(16),
        cost_estimate=SMALL,
        name="finish",
    )(*operands)


def swap(value, axis, distance):
    count = lax.axis_size(axis)
    return lax.ppermute(value, axis, [(source, source ^ distance) for source in range(count)])


def add(*terms):
    total = terms[0].astype(jnp.float32)
    for term in terms[1:]:
        total = total + term.astype(jnp.float32)
    return total.astype(jnp.bfloat16)


TURNS = (3, 1, 2, 0)


def tie(*values):
    return lax.optimization_barrier(values)


def exchange_local(queries, keys, values, doc_ids, w_out):
    shard_rows = queries.shape[0]
    group = queries.shape[1] // HD
    ctx_index = lax.axis_index("ctx").astype(jnp.int32).reshape(1)
    head_index = lax.axis_index("head").astype(jnp.int32)
    places = head_index ^ (2 * jnp.array(TURNS, jnp.int32))
    docs = doc_ids.reshape(shard_rows // HD, HD)
    near = range(1, group)

    w_sibling = swap(w_out, "head", 1)
    low_out = pack(ctx_index, 0, queries, keys, values, docs)
    low_out, later = tie(low_out, (queries, keys, values))
    low = [swap(low_out[distance - 1], "ctx", distance) for distance in near]
    high_out = pack(ctx_index, 1, *later, None)
    high = [swap(high_out[distance - 1], "ctx", distance) for distance in near[:-1]]
    w_packed = pack_projection(places, w_out, w_sibling)
    low, w_packed = tie(low, w_packed)

    def send_back(pieces):
        return [swap(pieces[distance], "ctx", distance) for distance in near]

    rows = shard_rows // 2
    cuts = (0, rows // 2, rows)

    def projected(mine, sibling, *wanted):
        return list(project(wanted, mine, sibling, *w_packed))

    def to_next(part, distance):
        return swap(part, "head", 2 * distance)

    pieces = attend(ctx_index, queries, keys, values, docs, low, None)
    pieces, diagonal_out = tie(pieces, high_out[-1])
    back = send_back(pieces)
    back, high = tie(back, high)
    high = [*high, swap(diagonal_out, "ctx", near[-1])]
    mine = assemble(ctx_index, [pieces[0], *back], (0, rows))
    sibling = [swap(part, "head", 1) for part in mine]
    shares = [projected(mine, sibling, [(turn, 0, rows)])[0] for turn in range(len(TURNS))]
    far = to_next(shares[0], 1)
    passed = add(shares[2], far)
    shares, passed = tie(shares, passed)
    across = to_next(passed, 2)
    near_sum = to_next(shares[1], 1)

    high, kept, passed = tie(high, shares[3], passed)
    pieces = attend(ctx_index, queries, keys, values, docs, low, high)
    back = send_back(pieces)
    mine = assemble(ctx_index, [pieces[0], *back], cuts)
    sibling = [swap(part, "head", 1) for part in mine]
    late = [projected(mine, sibling, [(turn, 0, rows)])[0] for turn in (0, 2, 3)]
    late[0], near_sum, across = tie(late[0], near_sum, across)
    result = finish(0, rows, [[(kept, 0)], [(near_sum, 0)], [(across, 0)]], None)
    far = to_next(late[0], 1)
    passed = add(late[1], far)
    across = to_next(passed, 2)
    last = projected(mine, sibling, *[[(1, *span)] for span in zip(cuts[:-1], cuts[1:])])
    last, passed = tie(last, passed)
    near_sum = [to_next(part, 1) for part in last]
    terms = [[(late[2], 0)], [(part, 0) for part in near_sum], [(across, 0)]]
    return finish(1, rows, terms, result)


def solution(mesh):
    in_specs = (P("ctx", "head"), P("ctx", "head"), P("ctx", "head"), P("ctx"), P("head", None))
    out_specs = P("ctx", "head")
    ctx_count = mesh.shape["ctx"]
    head_count = mesh.shape["head"]

    def local(queries, keys, values, doc_ids, w_out):
        heads = queries.shape[1] // HD
        exchange = heads == ctx_count and heads == 4 and head_count == 2 * len(TURNS)
        exchange = exchange and queries.shape[0] % (4 * TILE) == 0
        body = exchange_local if exchange else ring_local
        return body(queries, keys, values, doc_ids, w_out)

    return jax.shard_map(
        local, mesh=mesh, in_specs=in_specs, out_specs=out_specs, check_vma=False
    )
```

```python
import functools
import math

import jax
import jax.numpy as jnp
from jax import lax
from jax.experimental import pallas as pl
from jax.experimental.pallas import tpu as pltpu
from jax.sharding import PartitionSpec as P

HD = 128


MASKED_SCORE = -1e30
LOG2E = 1.4426950408889634


def passed_along(value, axis, steps):
    count = lax.axis_size(axis)
    pairs = [(source, (source + steps) % count) for source in range(count)]
    return lax.ppermute(value, axis, pairs)


def folded_positions(row_total, offset, shard_rows, devices_ctx):
    flat_index = offset + lax.iota(jnp.int32, row_total)
    owner_dev = flat_index // shard_rows
    within = flat_index % shard_rows
    half_rows = shard_rows // 2
    fold_block = jnp.where(within < half_rows, owner_dev, 2 * devices_ctx - 1 - owner_dev)
    return fold_block * half_rows + within % half_rows


def block_update(
    running, query, query_pos, query_doc, key_block, value_block, pos_block, doc_block
):
    largest, totals, summed = running
    query_rows = query.shape[0]
    local_heads = query.shape[1] // HD
    query_heads = query.reshape(query_rows, local_heads, HD)
    key_heads = key_block.reshape(key_block.shape[0], local_heads, HD)
    value_heads = value_block.reshape(value_block.shape[0], local_heads, HD)
    scores = jnp.einsum(
        "qhd,khd->hqk", query_heads, key_heads, preferred_element_type=jnp.float32
    ) * (1.0 / math.sqrt(HD))
    allowed = (query_doc[:, None] == doc_block[None, :]) & (
        pos_block[None, :] <= query_pos[:, None]
    )
    scores = jnp.where(allowed[None], scores, MASKED_SCORE)
    new_max = jnp.maximum(largest, jnp.max(scores, axis=2))
    weights = jnp.where(allowed[None], jnp.exp(scores - new_max[:, :, None]), 0.0)
    factor = jnp.exp(largest - new_max)
    totals = totals * factor + jnp.sum(weights, axis=2)
    product = jnp.einsum(
        "hqk,khd->qhd",
        weights.astype(jnp.bfloat16),
        value_heads,
        preferred_element_type=jnp.float32,
    )
    summed = summed * factor.T[:, :, None] + product
    return (new_max, totals, summed)


def attend_rows(running, query, query_pos, query_doc, key_rows, value_rows, key_pos, key_doc):
    row_total = key_rows.shape[0]
    block_rows = math.gcd(row_total, query.shape[0])
    block_count = row_total // block_rows
    highest = jnp.max(query_pos)

    def visit(partial_value, blocks):
        key_block, value_block, pos_block, doc_block = blocks
        masked_out = jnp.min(pos_block) > highest
        updated = lax.cond(
            masked_out,
            lambda frozen: frozen,
            lambda frozen: block_update(
                frozen, query, query_pos, query_doc, key_block, value_block, pos_block, doc_block
            ),
            partial_value,
        )
        return (updated, None)

    blocks = (
        key_rows.reshape(block_count, block_rows, key_rows.shape[1]),
        value_rows.reshape(block_count, block_rows, value_rows.shape[1]),
        key_pos.reshape(block_count, block_rows),
        key_doc.reshape(block_count, block_rows),
    )
    running, _ = lax.scan(visit, running, blocks)
    return running


def attend_shard(running, query, query_pos, query_doc, key_rows, value_rows, key_pos, key_doc):
    largest, totals, summed = running
    half_rows = query.shape[0] // 2
    new_largest = []
    new_totals = []
    new_summed = []
    for half_idx in range(2):
        lower = half_idx * half_rows
        part_state = (largest[half_idx], totals[half_idx], summed[half_idx])
        part_state = attend_rows(
            part_state,
            query[lower : lower + half_rows],
            query_pos[lower : lower + half_rows],
            query_doc[lower : lower + half_rows],
            key_rows,
            value_rows,
            key_pos,
            key_doc,
        )
        new_largest.append(part_state[0])
        new_totals.append(part_state[1])
        new_summed.append(part_state[2])
    return (jnp.stack(new_largest), jnp.stack(new_totals), jnp.stack(new_summed))


def ring_local(queries, keys, values, doc_ids, w_out):
    shard_rows = queries.shape[0]
    half_rows = shard_rows // 2
    local_heads = queries.shape[1] // HD
    devices_ctx = lax.axis_size("ctx")
    ctx_index = lax.axis_index("ctx")
    all_docs = lax.all_gather(doc_ids, "ctx", axis=0, tiled=True)
    own_pos = folded_positions(shard_rows, ctx_index * shard_rows, shard_rows, devices_ctx)
    running = (
        jnp.full((2, local_heads, half_rows), MASKED_SCORE, jnp.float32),
        jnp.zeros((2, local_heads, half_rows), jnp.float32),
        jnp.zeros((2, half_rows, local_heads, HD), jnp.float32),
    )
    travel = queries
    for hop_step in range(devices_ctx):
        anchor = (ctx_index - hop_step) % devices_ctx
        query_pos = folded_positions(shard_rows, anchor * shard_rows, shard_rows, devices_ctx)
        query_doc = lax.dynamic_slice_in_dim(all_docs, anchor * shard_rows, shard_rows, 0)
        largest, totals, summed = attend_shard(
            running, travel, query_pos, query_doc, keys, values, own_pos, doc_ids
        )
        running = (
            passed_along(largest.astype(jnp.bfloat16), "ctx", 1).astype(largest.dtype),
            passed_along(totals.astype(jnp.bfloat16), "ctx", 1).astype(totals.dtype),
            passed_along(summed.astype(jnp.bfloat16), "ctx", 1).astype(summed.dtype),
        )
        if hop_step + 1 < devices_ctx:
            travel = passed_along(travel, "ctx", 1)
    largest, totals, summed = running
    attended = summed / totals.transpose(0, 2, 1)[:, :, :, None]
    attended = attended.reshape(shard_rows, local_heads * HD).astype(jnp.bfloat16)
    partial_out = jnp.dot(attended, w_out, preferred_element_type=jnp.float32)
    return lax.psum_scatter(
        partial_out.astype(jnp.bfloat16), "head", scatter_dimension=1, tiled=True
    )


SMALL = pl.CostEstimate(flops=1024, bytes_accessed=1024, transcendentals=0)
TILE = 256
MOST_DOCS = 16


def params(mib):
    return pltpu.CompilerParams(vmem_limit_bytes=mib * 1024 * 1024)


def whole(shape):
    return pl.BlockSpec(shape, lambda step, scalars: (0,) * len(shape))


def pack(ctx_index, half, queries, keys, values, docs):
    rows = queries.shape[0] // 2
    group = queries.shape[1] // HD
    doc_rows = 0 if docs is None else 16 * pl.cdiv(docs.shape[0], 16)
    total = 3 * rows + doc_rows

    def kernel(ctx_ref, *refs):
        outs = refs[len(refs) - (group - 1) :]
        if docs is not None:
            mine = refs[3 * (group - 1)][...].astype(jnp.float32)
            empty = jnp.zeros((doc_rows - mine.shape[0], HD), jnp.float32)
            mine = jnp.concatenate([mine, empty], axis=0).astype(jnp.bfloat16)
        for place in range(group - 1):
            for part in range(2):
                outs[place][part * rows : (part + 1) * rows, :] = refs[place * 3 + part][...]
            for block in range(rows // HD):
                taken = refs[place * 3 + 2][block * HD : (block + 1) * HD, :]
                lower = 2 * rows + block * HD
                outs[place][lower : lower + HD, :] = jnp.transpose(taken)
            if docs is not None:
                outs[place][3 * rows :, :] = mine

    def piece(distance):
        return pl.BlockSpec((rows, HD), lambda step, ctx: (half, ctx[0] ^ distance))

    in_specs = []
    operands = []
    for distance in range(1, group):
        for array in (queries, keys, values):
            in_specs.append(piece(distance))
            operands.append(array)
    if docs is not None:
        in_specs.append(whole(docs.shape))
        operands.append(docs)
    return pl.pallas_call(
        kernel,
        grid_spec=pltpu.PrefetchScalarGridSpec(
            num_scalar_prefetch=1,
            grid=(1,),
            in_specs=in_specs,
            out_specs=[whole((total, HD))] * (group - 1),
        ),
        out_shape=[jax.ShapeDtypeStruct((total, HD), jnp.bfloat16)] * (group - 1),
        compiler_params=params(56),
        cost_estimate=SMALL,
        name="pack",
    )(ctx_index, *operands)


def pack_projection(places, w_mine, w_sibling):
    depth, width = w_mine.shape
    turns = len(TURNS)
    columns = width // (2 * turns)

    def kernel(places_ref, mine_in, sibling_in, mine_out, sibling_out):
        mine_out[...] = mine_in[...]
        sibling_out[...] = sibling_in[...]

    in_spec = pl.BlockSpec((depth, columns), lambda turn, at: (0, at[turn]))
    out_spec = pl.BlockSpec((depth, columns), lambda turn, at: (0, turn))
    return pl.pallas_call(
        kernel,
        grid_spec=pltpu.PrefetchScalarGridSpec(
            num_scalar_prefetch=1,
            grid=(turns,),
            in_specs=[in_spec] * 2,
            out_specs=[out_spec] * 2,
        ),
        out_shape=[jax.ShapeDtypeStruct((depth, turns * columns), w_mine.dtype)] * 2,
        compiler_params=params(56),
        cost_estimate=SMALL,
        name="pack_projection",
    )(places, w_mine, w_sibling)


def attend(ctx_index, queries, keys, values, docs, low, high, tiles):
    rows = queries.shape[0] // 2
    group = queries.shape[1] // HD
    with_high = high is not None
    per_block = rows // TILE
    slots_each = len(tiles)
    lines = rows // HD
    key_rows = (2 * group if with_high else group) * rows
    key_tiles = key_rows // TILE
    scaling = LOG2E / math.sqrt(HD)

    def kernel(ctx_ref, *refs):
        refs = list(refs)
        own_low = [refs.pop(0) for _ in range(3)]
        own_high = [refs.pop(0) for _ in range(3)] if with_high else None
        own_docs = refs.pop(0)
        low_refs = [refs.pop(0) for _ in range(group - 1)]
        high_refs = [refs.pop(0) for _ in range(group - 1)] if with_high else None
        outs = [refs.pop(0) for _ in range(group)]
        key_buf, value_buf, doc_buf = refs[:3]
        query_buf, start_buf, largest_buf, summed = (
            refs[3 + kind * group : 3 + (kind + 1) * group] for kind in range(4)
        )
        ctx = ctx_ref[0]

        def part(upper, distance, index, lower=0, count=rows):
            if distance == 0:
                return (own_high if upper else own_low)[index][lower : lower + count, :]
            source = (high_refs if upper else low_refs)[distance - 1]
            return source[index * rows + lower : index * rows + lower + count, :]

        place = {}
        doc_rows = {}
        for upper in (False, True) if with_high else (False,):
            for distance in range(group):
                source = ctx ^ distance
                block = 2 * group - 1 - source if upper else source
                place[upper, distance] = block
                offset = pl.multiple_of(block * rows, rows)
                key_buf[pl.ds(offset, rows), :] = part(upper, distance, 1)
                if distance == 0:
                    both = own_docs[...].astype(jnp.float32)
                else:
                    both = low_refs[distance - 1][3 * rows :, :].astype(jnp.float32)
                begin = lines if upper else 0
                mine = []
                for line in range(lines):
                    taken = part(upper, distance, 2, line * HD, HD)
                    if distance == 0:
                        taken = jnp.transpose(taken)
                    column = pl.multiple_of(block * rows + line * HD, HD)
                    value_buf[:HD, pl.ds(column, HD)] = taken
                    mine.append(both[begin + line : begin + line + 1, :])
                    doc_buf[pl.ds(block * lines + line, 1), :] = mine[-1]
                doc_rows[upper, distance] = jnp.concatenate(mine, axis=1)
        value_buf[HD:, :] = jnp.ones((value_buf.shape[0] - HD, key_rows), jnp.bfloat16)

        all_docs = doc_buf[...]
        starts = [jnp.zeros((1, rows), jnp.float32)] * group
        for number in range(1, MOST_DOCS):
            smaller = jnp.where(all_docs < number, 1.0, 0.0)
            count = jnp.sum(jnp.sum(smaller, axis=0, keepdims=True), axis=1, keepdims=True)
            for distance in range(group):
                reached = doc_rows[with_high, distance] >= number
                starts[distance] = jnp.where(reached, count, starts[distance])

        def scores_of(query, offset):
            raw = lax.dot_general(
                key_buf[pl.ds(offset, TILE), :],
                query,
                (((1,), (1,)), ((), ())),
                preferred_element_type=jnp.float32,
            )
            return raw * scaling

        def weighted(weights, offset):
            return jnp.dot(
                value_buf[:, pl.ds(offset, TILE)],
                weights.astype(jnp.bfloat16),
                preferred_element_type=jnp.float32,
            )

        key_row = lax.broadcasted_iota(jnp.int32, (TILE, TILE), 0)
        causal = key_row <= lax.broadcasted_iota(jnp.int32, (TILE, TILE), 1)
        key_row = key_row.astype(jnp.float32)
        firsts = []
        counts = []
        for lane in range(group):
            for slot, tile in enumerate(tiles):
                distance = lane ^ (slot * (group - 1))
                query = part(with_high, distance, 0, tile * TILE, TILE)
                query_buf[lane][slot] = query
                start = starts[distance][:, tile * TILE : (tile + 1) * TILE]
                start_buf[lane][slot, 0:1, :] = start
                end = place[with_high, distance] * per_block + tile
                offset = pl.multiple_of(end * TILE, TILE)
                least = start - offset.astype(jnp.float32)
                scores = scores_of(query, offset)
                scores = jnp.where((key_row >= least) & causal, scores, MASKED_SCORE)
                largest = jnp.max(scores, axis=0, keepdims=True)
                largest_buf[lane][slot, 0:1, :] = largest
                summed[lane][slot] = weighted(jnp.exp2(scores - largest), offset)
                first = start[0, 0].astype(jnp.int32) // TILE
                firsts.append(first)
                counts.append(end - first)

        longest = jnp.int32(0)
        for lane in range(group):
            of_lane = counts[lane * slots_each : (lane + 1) * slots_each]
            longest = jnp.maximum(longest, sum(of_lane))

        def visit(step, carry):
            slots = []
            offsets = []
            beyonds = []
            for lane in range(group):
                slot = jnp.int32(0)
                index = firsts[lane * slots_each] + step
                before = counts[lane * slots_each]
                for later in range(1, slots_each):
                    reached = step >= before
                    slot = jnp.where(reached, later, slot)
                    place_later = lane * slots_each + later
                    index = jnp.where(reached, firsts[place_later] + step - before, index)
                    before = before + counts[place_later]
                offset = pl.multiple_of(jnp.minimum(index, key_tiles - 1) * TILE, TILE)
                slots.append(slot)
                offsets.append(offset)
                beyonds.append(jnp.where(step < before, -offset.astype(jnp.float32), 1e9))
            each = range(group)
            scores = [scores_of(query_buf[lane][slots[lane]], offsets[lane]) for lane in each]
            old_max = [largest_buf[lane][slots[lane], 0:1, :] for lane in each]
            new_max = []
            for lane in each:
                least = start_buf[lane][slots[lane], 0:1, :] + beyonds[lane]
                scores[lane] = jnp.where(key_row >= least, scores[lane], MASKED_SCORE)
                tile_max = jnp.max(scores[lane], axis=0, keepdims=True)
                new_max.append(jnp.maximum(old_max[lane], tile_max))
            products = [
                weighted(jnp.exp2(scores[lane] - new_max[lane]), offsets[lane]) for lane in each
            ]
            for lane in each:
                factor = jnp.exp2(old_max[lane] - new_max[lane])
                summed[lane][slots[lane]] = summed[lane][slots[lane]] * factor + products[lane]
                largest_buf[lane][slots[lane], 0:1, :] = new_max[lane]
            return carry

        lax.fori_loop(0, longest, visit, jnp.int32(0))
        for lane in range(group):
            for slot in range(slots_each):
                state = summed[lane]
                attended = state[slot, :HD, :] * (1.0 / state[slot, HD : HD + 1, :])
                out = outs[lane ^ (slot * (group - 1))]
                out[slot * TILE : (slot + 1) * TILE, :] = jnp.transpose(
                    attended.astype(jnp.bfloat16)
                )

    def own(upper):
        return pl.BlockSpec((rows, HD), lambda step, ctx: (int(upper), ctx[0]))

    in_specs = [own(False)] * 3
    operands = [queries, keys, values]
    if with_high:
        in_specs += [own(True)] * 3
        operands += [queries, keys, values]
    received = [docs, *low, *(high if with_high else ())]
    operands += received
    in_specs += [whole(array.shape) for array in received]
    return pl.pallas_call(
        kernel,
        grid_spec=pltpu.PrefetchScalarGridSpec(
            num_scalar_prefetch=1,
            grid=(1,),
            in_specs=in_specs,
            out_specs=[whole((slots_each * TILE, HD))] * group,
            scratch_shapes=[
                pltpu.VMEM((key_rows, HD), jnp.bfloat16),
                pltpu.VMEM((HD + 16, key_rows), jnp.bfloat16),
                pltpu.VMEM((key_rows // HD, HD), jnp.float32),
                *[pltpu.VMEM((slots_each, TILE, HD), jnp.bfloat16)] * group,
                *[pltpu.VMEM((slots_each, 8, TILE), jnp.float32)] * (2 * group),
                *[pltpu.VMEM((slots_each, HD + 16, TILE), jnp.float32)] * group,
            ],
        ),
        out_shape=[jax.ShapeDtypeStruct((slots_each * TILE, HD), jnp.bfloat16)] * group,
        compiler_params=params(40),
        cost_estimate=SMALL,
        name="attend_high" if with_high else "attend_low",
    )(ctx_index, *operands)


def assemble(ctx_index, pieces, cuts):
    rows = pieces[0].shape[0]
    group = len(pieces)
    spans = list(zip(cuts[:-1], cuts[1:]))

    def kernel(ctx_ref, *refs):
        for part, (lower, upper) in enumerate(spans):
            for distance in range(group):
                column = pl.multiple_of((ctx_ref[0] ^ distance) * HD, HD)
                refs[group + part][:, pl.ds(column, HD)] = refs[distance][lower:upper, :]

    shapes = [(upper - lower, group * HD) for lower, upper in spans]
    return pl.pallas_call(
        kernel,
        grid_spec=pltpu.PrefetchScalarGridSpec(
            num_scalar_prefetch=1,
            grid=(1,),
            in_specs=[whole((rows, HD))] * group,
            out_specs=[whole(shape) for shape in shapes],
        ),
        out_shape=[jax.ShapeDtypeStruct(shape, jnp.bfloat16) for shape in shapes],
        compiler_params=params(16),
        cost_estimate=SMALL,
        name="assemble",
    )(ctx_index, *pieces)


def plain(shape):
    return pl.BlockSpec(shape, lambda step: (0,) * len(shape))


def stacked(refs):
    values = [ref[...] for ref in refs]
    return values[0] if len(values) == 1 else jnp.concatenate(values, axis=0)


def project(wanted, mine, sibling, w_mine, w_sibling):
    parts = len(mine)
    depth = mine[0].shape[1]
    columns = w_mine.shape[1] // len(TURNS)
    turns = sorted({turn for output in wanted for turn, _, _ in output})

    def kernel(*refs):
        own_rows = stacked(refs[:parts])
        other_rows = stacked(refs[parts : 2 * parts])
        weights = refs[2 * parts : 2 * parts + 2 * len(turns)]
        outs = refs[2 * parts + 2 * len(turns) :]
        for out, output in zip(outs, wanted):
            place = 0
            for turn, lower, upper in output:
                at = turns.index(turn)
                total = jnp.dot(
                    own_rows[lower:upper, :], weights[at][...], preferred_element_type=jnp.float32
                )
                total += jnp.dot(
                    other_rows[lower:upper, :],
                    weights[len(turns) + at][...],
                    preferred_element_type=jnp.float32,
                )
                out[place : place + upper - lower, :] = total.astype(jnp.bfloat16)
                place += upper - lower

    def columns_of(turn):
        return pl.BlockSpec((depth, columns), lambda step: (0, turn))

    shapes = [(sum(upper - lower for _, lower, upper in output), columns) for output in wanted]
    return pl.pallas_call(
        kernel,
        grid=(1,),
        in_specs=[plain(part.shape) for part in (*mine, *sibling)]
        + [columns_of(turn) for turn in turns] * 2,
        out_specs=[plain(shape) for shape in shapes],
        out_shape=[jax.ShapeDtypeStruct(shape, jnp.bfloat16) for shape in shapes],
        compiler_params=params(24),
        cost_estimate=SMALL,
        name="project",
    )(*mine, *sibling, *([w_mine] * len(turns)), *([w_sibling] * len(turns)))


def finish(half, rows, terms, result):
    flat = [array for term in terms for array, _ in term]
    columns = flat[0].shape[1]

    def kernel(*refs):
        refs = list(refs)
        total = None
        for term in terms:
            values = [refs.pop(0)[first:, :].astype(jnp.float32) for _, first in term]
            value = values[0] if len(values) == 1 else jnp.concatenate(values, axis=0)
            total = value if total is None else total + value
        refs[-1][...] = total.astype(jnp.bfloat16)

    in_specs = [plain(array.shape) for array in flat]
    operands = list(flat)
    aliases = {}
    if result is not None:
        in_specs.append(pl.BlockSpec(memory_space=pl.ANY))
        operands.append(result)
        aliases = {len(flat): 0}
    return pl.pallas_call(
        kernel,
        grid=(1,),
        in_specs=in_specs,
        out_specs=pl.BlockSpec((rows, columns), lambda step: (half, 0)),
        out_shape=jax.ShapeDtypeStruct((2 * rows, columns), jnp.bfloat16),
        input_output_aliases=aliases,
        compiler_params=params(16),
        cost_estimate=SMALL,
        name="finish",
    )(*operands)


def swap(value, axis, distance):
    count = lax.axis_size(axis)
    return lax.ppermute(value, axis, [(source, source ^ distance) for source in range(count)])


def add(*terms):
    total = terms[0].astype(jnp.float32)
    for term in terms[1:]:
        total = total + term.astype(jnp.float32)
    return total.astype(jnp.bfloat16)


TURNS = (3, 1, 2, 0)


def tie(*values):
    return lax.optimization_barrier(values)


def exchange_local(queries, keys, values, doc_ids, w_out):
    shard_rows = queries.shape[0]
    group = queries.shape[1] // HD
    ctx_index = lax.axis_index("ctx").astype(jnp.int32).reshape(1)
    head_index = lax.axis_index("head").astype(jnp.int32)
    places = head_index ^ (2 * jnp.array(TURNS, jnp.int32))
    docs = doc_ids.reshape(shard_rows // HD, HD)
    near = range(1, group)

    w_sibling = swap(w_out, "head", 1)
    low_out = pack(ctx_index, 0, queries, keys, values, docs)
    low_out, later = tie(low_out, (queries, keys, values))
    low = [swap(low_out[distance - 1], "ctx", distance) for distance in near]
    high_out = pack(ctx_index, 1, *later, None)
    high = [swap(high_out[distance - 1], "ctx", distance) for distance in near[:-1]]
    w_packed = pack_projection(places, w_out, w_sibling)
    low, w_packed = tie(low, w_packed)

    def send_back(pieces):
        return [swap(pieces[distance], "ctx", distance) for distance in near]

    rows = shard_rows // 2

    def projected(mine, sibling, *wanted):
        return list(project(wanted, mine, sibling, *w_packed))

    def to_next(part, distance):
        return swap(part, "head", 2 * distance)

    tiles = tuple(range(rows // TILE))
    pieces = attend(ctx_index, queries, keys, values, docs, low, None, tiles)
    pieces, diagonal_out = tie(pieces, high_out[-1])
    back = send_back(pieces)
    back, high = tie(back, high)
    high = [*high, swap(diagonal_out, "ctx", near[-1])]
    mine = assemble(ctx_index, [pieces[0], *back], (0, rows))
    sibling = [swap(part, "head", 1) for part in mine]
    shares = [projected(mine, sibling, [(turn, 0, rows)])[0] for turn in range(len(TURNS))]
    far = to_next(shares[0], 1)
    near_sum = to_next(shares[1], 1)
    passed = add(shares[2], far)
    high, shares = tie(high, shares)

    mine = []
    for tile in tiles:
        pieces = attend(ctx_index, queries, keys, values, docs, low, high, (tile,))
        back = send_back(pieces)
        if tile == 0:
            pieces, passed = tie(pieces, passed)
            across = to_next(passed, 2)
            high, passed = tie(high, passed)
        mine += assemble(ctx_index, [pieces[0], *back], (0, TILE))
    far = []
    sibling = []
    for part in mine:
        sibling.append(swap(part, "head", 1))
        (share,) = projected([part], [sibling[-1]], [(0, 0, TILE)])
        if far:
            share, near_sum, across = tie(share, near_sum, across)
        far.append(to_next(share, 1))
    result = finish(0, rows, [[(shares[3], 0)], [(near_sum, 0)], [(across, 0)]], None)
    spans = [(tile * TILE, (tile + 1) * TILE) for tile in tiles]
    late = projected(mine, sibling, *[[(2, *span)] for span in spans])
    passed = [add(*both) for both in zip(late, far)]
    across = [to_next(part, 2) for part in passed]
    late = projected(mine, sibling, *[[(1, *span)] for span in spans])
    late, passed = tie(late, passed)
    near_sum = [to_next(part, 1) for part in late]
    (kept,) = projected(mine, sibling, [(3, 0, rows)])
    terms = [[(kept, 0)], [(part, 0) for part in near_sum], [(part, 0) for part in across]]
    return finish(1, rows, terms, result)


def solution(mesh):
    in_specs = (P("ctx", "head"), P("ctx", "head"), P("ctx", "head"), P("ctx"), P("head", None))
    out_specs = P("ctx", "head")
    ctx_count = mesh.shape["ctx"]
    head_count = mesh.shape["head"]

    def local(queries, keys, values, doc_ids, w_out):
        heads = queries.shape[1] // HD
        exchange = heads == ctx_count and heads == 4 and head_count == 2 * len(TURNS)
        exchange = exchange and queries.shape[0] % (4 * TILE) == 0
        body = exchange_local if exchange else ring_local
        return body(queries, keys, values, doc_ids, w_out)

    return jax.shard_map(
        local, mesh=mesh, in_specs=in_specs, out_specs=out_specs, check_vma=False
    )
```

```python
import functools
import math

import jax
import jax.numpy as jnp
from jax import lax
from jax.experimental import pallas as pl
from jax.experimental.pallas import tpu as pltpu
from jax.sharding import PartitionSpec as P

HD = 128


MASKED_SCORE = -1e30
LOG2E = 1.4426950408889634


def passed_along(value, axis, steps):
    count = lax.axis_size(axis)
    pairs = [(source, (source + steps) % count) for source in range(count)]
    return lax.ppermute(value, axis, pairs)


def folded_positions(row_total, offset, shard_rows, devices_ctx):
    flat_index = offset + lax.iota(jnp.int32, row_total)
    owner_dev = flat_index // shard_rows
    within = flat_index % shard_rows
    half_rows = shard_rows // 2
    fold_block = jnp.where(within < half_rows, owner_dev, 2 * devices_ctx - 1 - owner_dev)
    return fold_block * half_rows + within % half_rows


def block_update(
    running, query, query_pos, query_doc, key_block, value_block, pos_block, doc_block
):
    largest, totals, summed = running
    query_rows = query.shape[0]
    local_heads = query.shape[1] // HD
    query_heads = query.reshape(query_rows, local_heads, HD)
    key_heads = key_block.reshape(key_block.shape[0], local_heads, HD)
    value_heads = value_block.reshape(value_block.shape[0], local_heads, HD)
    scores = jnp.einsum(
        "qhd,khd->hqk", query_heads, key_heads, preferred_element_type=jnp.float32
    ) * (1.0 / math.sqrt(HD))
    allowed = (query_doc[:, None] == doc_block[None, :]) & (
        pos_block[None, :] <= query_pos[:, None]
    )
    scores = jnp.where(allowed[None], scores, MASKED_SCORE)
    new_max = jnp.maximum(largest, jnp.max(scores, axis=2))
    weights = jnp.where(allowed[None], jnp.exp(scores - new_max[:, :, None]), 0.0)
    factor = jnp.exp(largest - new_max)
    totals = totals * factor + jnp.sum(weights, axis=2)
    product = jnp.einsum(
        "hqk,khd->qhd",
        weights.astype(jnp.bfloat16),
        value_heads,
        preferred_element_type=jnp.float32,
    )
    summed = summed * factor.T[:, :, None] + product
    return (new_max, totals, summed)


def attend_rows(running, query, query_pos, query_doc, key_rows, value_rows, key_pos, key_doc):
    row_total = key_rows.shape[0]
    block_rows = math.gcd(row_total, query.shape[0])
    block_count = row_total // block_rows
    highest = jnp.max(query_pos)

    def visit(partial_value, blocks):
        key_block, value_block, pos_block, doc_block = blocks
        masked_out = jnp.min(pos_block) > highest
        updated = lax.cond(
            masked_out,
            lambda frozen: frozen,
            lambda frozen: block_update(
                frozen, query, query_pos, query_doc, key_block, value_block, pos_block, doc_block
            ),
            partial_value,
        )
        return (updated, None)

    blocks = (
        key_rows.reshape(block_count, block_rows, key_rows.shape[1]),
        value_rows.reshape(block_count, block_rows, value_rows.shape[1]),
        key_pos.reshape(block_count, block_rows),
        key_doc.reshape(block_count, block_rows),
    )
    running, _ = lax.scan(visit, running, blocks)
    return running


def attend_shard(running, query, query_pos, query_doc, key_rows, value_rows, key_pos, key_doc):
    largest, totals, summed = running
    half_rows = query.shape[0] // 2
    new_largest = []
    new_totals = []
    new_summed = []
    for half_idx in range(2):
        lower = half_idx * half_rows
        part_state = (largest[half_idx], totals[half_idx], summed[half_idx])
        part_state = attend_rows(
            part_state,
            query[lower : lower + half_rows],
            query_pos[lower : lower + half_rows],
            query_doc[lower : lower + half_rows],
            key_rows,
            value_rows,
            key_pos,
            key_doc,
        )
        new_largest.append(part_state[0])
        new_totals.append(part_state[1])
        new_summed.append(part_state[2])
    return (jnp.stack(new_largest), jnp.stack(new_totals), jnp.stack(new_summed))


def ring_local(queries, keys, values, doc_ids, w_out):
    shard_rows = queries.shape[0]
    half_rows = shard_rows // 2
    local_heads = queries.shape[1] // HD
    devices_ctx = lax.axis_size("ctx")
    ctx_index = lax.axis_index("ctx")
    all_docs = lax.all_gather(doc_ids, "ctx", axis=0, tiled=True)
    own_pos = folded_positions(shard_rows, ctx_index * shard_rows, shard_rows, devices_ctx)
    running = (
        jnp.full((2, local_heads, half_rows), MASKED_SCORE, jnp.float32),
        jnp.zeros((2, local_heads, half_rows), jnp.float32),
        jnp.zeros((2, half_rows, local_heads, HD), jnp.float32),
    )
    travel = queries
    for hop_step in range(devices_ctx):
        anchor = (ctx_index - hop_step) % devices_ctx
        query_pos = folded_positions(shard_rows, anchor * shard_rows, shard_rows, devices_ctx)
        query_doc = lax.dynamic_slice_in_dim(all_docs, anchor * shard_rows, shard_rows, 0)
        largest, totals, summed = attend_shard(
            running, travel, query_pos, query_doc, keys, values, own_pos, doc_ids
        )
        running = (
            passed_along(largest.astype(jnp.bfloat16), "ctx", 1).astype(largest.dtype),
            passed_along(totals.astype(jnp.bfloat16), "ctx", 1).astype(totals.dtype),
            passed_along(summed.astype(jnp.bfloat16), "ctx", 1).astype(summed.dtype),
        )
        if hop_step + 1 < devices_ctx:
            travel = passed_along(travel, "ctx", 1)
    largest, totals, summed = running
    attended = summed / totals.transpose(0, 2, 1)[:, :, :, None]
    attended = attended.reshape(shard_rows, local_heads * HD).astype(jnp.bfloat16)
    partial_out = jnp.dot(attended, w_out, preferred_element_type=jnp.float32)
    return lax.psum_scatter(
        partial_out.astype(jnp.bfloat16), "head", scatter_dimension=1, tiled=True
    )


SMALL = pl.CostEstimate(flops=1024, bytes_accessed=1024, transcendentals=0)
TILE = 256
MOST_DOCS = 16


def params(mib):
    return pltpu.CompilerParams(vmem_limit_bytes=mib * 1024 * 1024)


def whole(shape):
    return pl.BlockSpec(shape, lambda step, scalars: (0,) * len(shape))


def pack(ctx_index, half, queries, keys, values, docs):
    rows = queries.shape[0] // 2
    group = queries.shape[1] // HD
    doc_rows = 0 if docs is None else 16 * pl.cdiv(docs.shape[0], 16)
    total = 3 * rows + doc_rows

    def kernel(ctx_ref, *refs):
        outs = refs[len(refs) - (group - 1) :]
        if docs is not None:
            mine = refs[3 * (group - 1)][...].astype(jnp.float32)
            empty = jnp.zeros((doc_rows - mine.shape[0], HD), jnp.float32)
            mine = jnp.concatenate([mine, empty], axis=0).astype(jnp.bfloat16)
        for place in range(group - 1):
            for part in range(2):
                outs[place][part * rows : (part + 1) * rows, :] = refs[place * 3 + part][...]
            for block in range(rows // HD):
                taken = refs[place * 3 + 2][block * HD : (block + 1) * HD, :]
                lower = 2 * rows + block * HD
                outs[place][lower : lower + HD, :] = jnp.transpose(taken)
            if docs is not None:
                outs[place][3 * rows :, :] = mine

    def piece(distance):
        return pl.BlockSpec((rows, HD), lambda step, ctx: (half, ctx[0] ^ distance))

    in_specs = []
    operands = []
    for distance in range(1, group):
        for array in (queries, keys, values):
            in_specs.append(piece(distance))
            operands.append(array)
    if docs is not None:
        in_specs.append(whole(docs.shape))
        operands.append(docs)
    return pl.pallas_call(
        kernel,
        grid_spec=pltpu.PrefetchScalarGridSpec(
            num_scalar_prefetch=1,
            grid=(1,),
            in_specs=in_specs,
            out_specs=[whole((total, HD))] * (group - 1),
        ),
        out_shape=[jax.ShapeDtypeStruct((total, HD), jnp.bfloat16)] * (group - 1),
        compiler_params=params(56),
        cost_estimate=SMALL,
        name="pack",
    )(ctx_index, *operands)


def pack_projection(places, w_mine, w_sibling):
    depth, width = w_mine.shape
    turns = len(TURNS)
    columns = width // (2 * turns)

    def kernel(places_ref, mine_in, sibling_in, mine_out, sibling_out):
        mine_out[...] = mine_in[...]
        sibling_out[...] = sibling_in[...]

    in_spec = pl.BlockSpec((depth, columns), lambda turn, at: (0, at[turn]))
    out_spec = pl.BlockSpec((depth, columns), lambda turn, at: (0, turn))
    return pl.pallas_call(
        kernel,
        grid_spec=pltpu.PrefetchScalarGridSpec(
            num_scalar_prefetch=1,
            grid=(turns,),
            in_specs=[in_spec] * 2,
            out_specs=[out_spec] * 2,
        ),
        out_shape=[jax.ShapeDtypeStruct((depth, turns * columns), w_mine.dtype)] * 2,
        compiler_params=params(56),
        cost_estimate=SMALL,
        name="pack_projection",
    )(places, w_mine, w_sibling)


def attend(ctx_index, queries, keys, values, docs, low, high):
    rows = queries.shape[0] // 2
    group = queries.shape[1] // HD
    with_high = high is not None
    per_block = rows // TILE
    lines = rows // HD
    key_rows = (2 * group if with_high else group) * rows
    key_tiles = key_rows // TILE
    scaling = LOG2E / math.sqrt(HD)

    def kernel(ctx_ref, *refs):
        refs = list(refs)
        own_low = [refs.pop(0) for _ in range(3)]
        own_high = [refs.pop(0) for _ in range(3)] if with_high else None
        own_docs = refs.pop(0)
        low_refs = [refs.pop(0) for _ in range(group - 1)]
        high_refs = [refs.pop(0) for _ in range(group - 1)] if with_high else None
        outs = [refs.pop(0) for _ in range(group)]
        key_buf, value_buf, doc_buf = refs[:3]
        query_buf, start_buf, largest_buf, summed = (
            refs[3 + kind * group : 3 + (kind + 1) * group] for kind in range(4)
        )
        ctx = ctx_ref[0]

        def part(upper, distance, index, lower=0, count=rows):
            if distance == 0:
                return (own_high if upper else own_low)[index][lower : lower + count, :]
            source = (high_refs if upper else low_refs)[distance - 1]
            return source[index * rows + lower : index * rows + lower + count, :]

        place = {}
        doc_rows = {}
        for upper in (False, True) if with_high else (False,):
            for distance in range(group):
                source = ctx ^ distance
                block = 2 * group - 1 - source if upper else source
                place[upper, distance] = block
                offset = pl.multiple_of(block * rows, rows)
                key_buf[pl.ds(offset, rows), :] = part(upper, distance, 1)
                if distance == 0:
                    both = own_docs[...].astype(jnp.float32)
                else:
                    both = low_refs[distance - 1][3 * rows :, :].astype(jnp.float32)
                begin = lines if upper else 0
                mine = []
                for line in range(lines):
                    taken = part(upper, distance, 2, line * HD, HD)
                    if distance == 0:
                        taken = jnp.transpose(taken)
                    column = pl.multiple_of(block * rows + line * HD, HD)
                    value_buf[:HD, pl.ds(column, HD)] = taken
                    mine.append(both[begin + line : begin + line + 1, :])
                    doc_buf[pl.ds(block * lines + line, 1), :] = mine[-1]
                doc_rows[upper, distance] = jnp.concatenate(mine, axis=1)
        value_buf[HD:, :] = jnp.ones((value_buf.shape[0] - HD, key_rows), jnp.bfloat16)

        all_docs = doc_buf[...]
        starts = [jnp.zeros((1, rows), jnp.float32)] * group
        for number in range(1, MOST_DOCS):
            smaller = jnp.where(all_docs < number, 1.0, 0.0)
            count = jnp.sum(jnp.sum(smaller, axis=0, keepdims=True), axis=1, keepdims=True)
            for distance in range(group):
                reached = doc_rows[with_high, distance] >= number
                starts[distance] = jnp.where(reached, count, starts[distance])

        def scores_of(query, offset):
            raw = lax.dot_general(
                key_buf[pl.ds(offset, TILE), :],
                query,
                (((1,), (1,)), ((), ())),
                preferred_element_type=jnp.float32,
            )
            return raw * scaling

        def weighted(weights, offset):
            return jnp.dot(
                value_buf[:, pl.ds(offset, TILE)],
                weights.astype(jnp.bfloat16),
                preferred_element_type=jnp.float32,
            )

        key_row = lax.broadcasted_iota(jnp.int32, (TILE, TILE), 0)
        causal = key_row <= lax.broadcasted_iota(jnp.int32, (TILE, TILE), 1)
        key_row = key_row.astype(jnp.float32)
        firsts = []
        counts = []
        for lane in range(group):
            for slot in range(per_block):
                distance = lane ^ (slot * (group - 1))
                query = part(with_high, distance, 0, slot * TILE, TILE)
                query_buf[lane][slot] = query
                start = starts[distance][:, slot * TILE : (slot + 1) * TILE]
                start_buf[lane][slot, 0:1, :] = start
                end = place[with_high, distance] * per_block + slot
                offset = pl.multiple_of(end * TILE, TILE)
                least = start - offset.astype(jnp.float32)
                scores = scores_of(query, offset)
                scores = jnp.where((key_row >= least) & causal, scores, MASKED_SCORE)
                largest = jnp.max(scores, axis=0, keepdims=True)
                largest_buf[lane][slot, 0:1, :] = largest
                summed[lane][slot] = weighted(jnp.exp2(scores - largest), offset)
                first = start[0, 0].astype(jnp.int32) // TILE
                firsts.append(first)
                counts.append(end - first)

        longest = jnp.int32(0)
        for lane in range(group):
            of_lane = counts[lane * per_block : (lane + 1) * per_block]
            longest = jnp.maximum(longest, sum(of_lane))

        def visit(step, carry):
            slots = []
            offsets = []
            beyonds = []
            for lane in range(group):
                slot = jnp.int32(0)
                index = firsts[lane * per_block] + step
                before = counts[lane * per_block]
                for later in range(1, per_block):
                    reached = step >= before
                    slot = jnp.where(reached, later, slot)
                    place_later = lane * per_block + later
                    index = jnp.where(reached, firsts[place_later] + step - before, index)
                    before = before + counts[place_later]
                offset = pl.multiple_of(jnp.minimum(index, key_tiles - 1) * TILE, TILE)
                slots.append(slot)
                offsets.append(offset)
                beyonds.append(jnp.where(step < before, -offset.astype(jnp.float32), 1e9))
            each = range(group)
            scores = [scores_of(query_buf[lane][slots[lane]], offsets[lane]) for lane in each]
            old_max = [largest_buf[lane][slots[lane], 0:1, :] for lane in each]
            new_max = []
            for lane in each:
                least = start_buf[lane][slots[lane], 0:1, :] + beyonds[lane]
                scores[lane] = jnp.where(key_row >= least, scores[lane], MASKED_SCORE)
                tile_max = jnp.max(scores[lane], axis=0, keepdims=True)
                new_max.append(jnp.maximum(old_max[lane], tile_max))
            products = [
                weighted(jnp.exp2(scores[lane] - new_max[lane]), offsets[lane]) for lane in each
            ]
            for lane in each:
                factor = jnp.exp2(old_max[lane] - new_max[lane])
                summed[lane][slots[lane]] = summed[lane][slots[lane]] * factor + products[lane]
                largest_buf[lane][slots[lane], 0:1, :] = new_max[lane]
            return carry

        lax.fori_loop(0, longest, visit, jnp.int32(0))
        for lane in range(group):
            for slot in range(per_block):
                state = summed[lane]
                attended = state[slot, :HD, :] * (1.0 / state[slot, HD : HD + 1, :])
                out = outs[lane ^ (slot * (group - 1))]
                out[slot * TILE : (slot + 1) * TILE, :] = jnp.transpose(
                    attended.astype(jnp.bfloat16)
                )

    def own(upper):
        return pl.BlockSpec((rows, HD), lambda step, ctx: (int(upper), ctx[0]))

    in_specs = [own(False)] * 3
    operands = [queries, keys, values]
    if with_high:
        in_specs += [own(True)] * 3
        operands += [queries, keys, values]
    received = [docs, *low, *(high if with_high else ())]
    operands += received
    in_specs += [whole(array.shape) for array in received]
    return pl.pallas_call(
        kernel,
        grid_spec=pltpu.PrefetchScalarGridSpec(
            num_scalar_prefetch=1,
            grid=(1,),
            in_specs=in_specs,
            out_specs=[whole((rows, HD))] * group,
            scratch_shapes=[
                pltpu.VMEM((key_rows, HD), jnp.bfloat16),
                pltpu.VMEM((HD + 16, key_rows), jnp.bfloat16),
                pltpu.VMEM((key_rows // HD, HD), jnp.float32),
                *[pltpu.VMEM((per_block, TILE, HD), jnp.bfloat16)] * group,
                *[pltpu.VMEM((per_block, 8, TILE), jnp.float32)] * (2 * group),
                *[pltpu.VMEM((per_block, HD + 16, TILE), jnp.float32)] * group,
            ],
        ),
        out_shape=[jax.ShapeDtypeStruct((rows, HD), jnp.bfloat16)] * group,
        compiler_params=params(40),
        cost_estimate=SMALL,
        name="attend_high" if with_high else "attend_low",
    )(ctx_index, *operands)


def assemble(ctx_index, pieces, cuts):
    rows = pieces[0].shape[0]
    group = len(pieces)
    spans = list(zip(cuts[:-1], cuts[1:]))

    def kernel(ctx_ref, *refs):
        for part, (lower, upper) in enumerate(spans):
            for distance in range(group):
                column = pl.multiple_of((ctx_ref[0] ^ distance) * HD, HD)
                refs[group + part][:, pl.ds(column, HD)] = refs[distance][lower:upper, :]

    shapes = [(upper - lower, group * HD) for lower, upper in spans]
    return pl.pallas_call(
        kernel,
        grid_spec=pltpu.PrefetchScalarGridSpec(
            num_scalar_prefetch=1,
            grid=(1,),
            in_specs=[whole((rows, HD))] * group,
            out_specs=[whole(shape) for shape in shapes],
        ),
        out_shape=[jax.ShapeDtypeStruct(shape, jnp.bfloat16) for shape in shapes],
        compiler_params=params(16),
        cost_estimate=SMALL,
        name="assemble",
    )(ctx_index, *pieces)


def plain(shape):
    return pl.BlockSpec(shape, lambda step: (0,) * len(shape))


def stacked(refs):
    values = [ref[...] for ref in refs]
    return values[0] if len(values) == 1 else jnp.concatenate(values, axis=0)


def project(wanted, mine, sibling, w_mine, w_sibling):
    parts = len(mine)
    depth = mine[0].shape[1]
    columns = w_mine.shape[1] // len(TURNS)
    turns = sorted({turn for output in wanted for turn, _, _ in output})

    def kernel(*refs):
        own_rows = stacked(refs[:parts])
        other_rows = stacked(refs[parts : 2 * parts])
        weights = refs[2 * parts : 2 * parts + 2 * len(turns)]
        outs = refs[2 * parts + 2 * len(turns) :]
        for out, output in zip(outs, wanted):
            place = 0
            for turn, lower, upper in output:
                at = turns.index(turn)
                total = jnp.dot(
                    own_rows[lower:upper, :], weights[at][...], preferred_element_type=jnp.float32
                )
                total += jnp.dot(
                    other_rows[lower:upper, :],
                    weights[len(turns) + at][...],
                    preferred_element_type=jnp.float32,
                )
                out[place : place + upper - lower, :] = total.astype(jnp.bfloat16)
                place += upper - lower

    def columns_of(turn):
        return pl.BlockSpec((depth, columns), lambda step: (0, turn))

    shapes = [(sum(upper - lower for _, lower, upper in output), columns) for output in wanted]
    return pl.pallas_call(
        kernel,
        grid=(1,),
        in_specs=[plain(part.shape) for part in (*mine, *sibling)]
        + [columns_of(turn) for turn in turns] * 2,
        out_specs=[plain(shape) for shape in shapes],
        out_shape=[jax.ShapeDtypeStruct(shape, jnp.bfloat16) for shape in shapes],
        compiler_params=params(24),
        cost_estimate=SMALL,
        name="project",
    )(*mine, *sibling, *([w_mine] * len(turns)), *([w_sibling] * len(turns)))


def finish(half, rows, terms, result):
    flat = [array for term in terms for array, _ in term]
    columns = flat[0].shape[1]

    def kernel(*refs):
        refs = list(refs)
        total = None
        for term in terms:
            values = [refs.pop(0)[first:, :].astype(jnp.float32) for _, first in term]
            value = values[0] if len(values) == 1 else jnp.concatenate(values, axis=0)
            total = value if total is None else total + value
        refs[-1][...] = total.astype(jnp.bfloat16)

    in_specs = [plain(array.shape) for array in flat]
    operands = list(flat)
    aliases = {}
    if result is not None:
        in_specs.append(pl.BlockSpec(memory_space=pl.ANY))
        operands.append(result)
        aliases = {len(flat): 0}
    return pl.pallas_call(
        kernel,
        grid=(1,),
        in_specs=in_specs,
        out_specs=pl.BlockSpec((rows, columns), lambda step: (half, 0)),
        out_shape=jax.ShapeDtypeStruct((2 * rows, columns), jnp.bfloat16),
        input_output_aliases=aliases,
        compiler_params=params(16),
        cost_estimate=SMALL,
        name="finish",
    )(*operands)


def swap(value, axis, distance):
    count = lax.axis_size(axis)
    return lax.ppermute(value, axis, [(source, source ^ distance) for source in range(count)])


def add(*terms):
    total = terms[0].astype(jnp.float32)
    for term in terms[1:]:
        total = total + term.astype(jnp.float32)
    return total.astype(jnp.bfloat16)


TURNS = (3, 1, 2, 0)


def tie(*values):
    return lax.optimization_barrier(values)


def exchange_local(queries, keys, values, doc_ids, w_out):
    shard_rows = queries.shape[0]
    group = queries.shape[1] // HD
    ctx_index = lax.axis_index("ctx").astype(jnp.int32).reshape(1)
    head_index = lax.axis_index("head").astype(jnp.int32)
    places = head_index ^ (2 * jnp.array(TURNS, jnp.int32))
    docs = doc_ids.reshape(shard_rows // HD, HD)
    near = range(1, group)

    w_sibling = swap(w_out, "head", 1)
    low_out = pack(ctx_index, 0, queries, keys, values, docs)
    low_out, later = tie(low_out, (queries, keys, values))
    low = [swap(low_out[distance - 1], "ctx", distance) for distance in near]
    high_out = pack(ctx_index, 1, *later, None)
    high = [swap(high_out[distance - 1], "ctx", distance) for distance in near[:-1]]
    w_packed = pack_projection(places, w_out, w_sibling)
    low, w_packed = tie(low, w_packed)

    def send_back(pieces):
        return [swap(pieces[distance], "ctx", distance) for distance in near]

    rows = shard_rows // 2
    cuts = (0, rows // 2, rows)

    def projected(mine, sibling, *wanted):
        return list(project(wanted, mine, sibling, *w_packed))

    def to_next(part, distance):
        return swap(part, "head", 2 * distance)

    pieces = attend(ctx_index, queries, keys, values, docs, low, None)
    pieces, diagonal_out = tie(pieces, high_out[-1])
    back = send_back(pieces)
    back, high = tie(back, high)
    high = [*high, swap(diagonal_out, "ctx", near[-1])]
    mine = assemble(ctx_index, [pieces[0], *back], (0, rows))
    sibling = [swap(part, "head", 1) for part in mine]
    shares = [projected(mine, sibling, [(turn, 0, rows)])[0] for turn in range(len(TURNS))]
    far = to_next(shares[0], 1)
    near_sum = to_next(shares[1], 1)
    passed = add(shares[2], far)

    high, shares, passed = tie(high, shares, passed)
    across = to_next(passed, 2)
    pieces = attend(ctx_index, queries, keys, values, docs, low, high)
    back = send_back(pieces)
    mine = assemble(ctx_index, [pieces[0], *back], cuts)
    sibling = [swap(part, "head", 1) for part in mine]
    late = [projected(mine, sibling, [(turn, 0, rows)])[0] for turn in (0, 2, 3)]
    late[0], near_sum, across = tie(late[0], near_sum, across)
    result = finish(0, rows, [[(shares[3], 0)], [(near_sum, 0)], [(across, 0)]], None)
    far = to_next(late[0], 1)
    passed = add(late[1], far)
    across = to_next(passed, 2)
    last = projected(mine, sibling, *[[(1, *span)] for span in zip(cuts[:-1], cuts[1:])])
    last, passed = tie(last, passed)
    near_sum = [to_next(part, 1) for part in last]
    terms = [[(late[2], 0)], [(part, 0) for part in near_sum], [(across, 0)]]
    return finish(1, rows, terms, result)


def solution(mesh):
    in_specs = (P("ctx", "head"), P("ctx", "head"), P("ctx", "head"), P("ctx"), P("head", None))
    out_specs = P("ctx", "head")
    ctx_count = mesh.shape["ctx"]
    head_count = mesh.shape["head"]

    def local(queries, keys, values, doc_ids, w_out):
        heads = queries.shape[1] // HD
        exchange = heads == ctx_count and heads == 4 and head_count == 2 * len(TURNS)
        exchange = exchange and queries.shape[0] % (4 * TILE) == 0
        body = exchange_local if exchange else ring_local
        return body(queries, keys, values, doc_ids, w_out)

    return jax.shard_map(
        local, mesh=mesh, in_specs=in_specs, out_specs=out_specs, check_vma=False
    )
```

```python
import functools
import math

import jax
import jax.numpy as jnp
from jax import lax
from jax.experimental import pallas as pl
from jax.experimental.pallas import tpu as pltpu
from jax.sharding import PartitionSpec as P

HD = 128


MASKED_SCORE = -1e30
LOG2E = 1.4426950408889634


def passed_along(value, axis, steps):
    count = lax.axis_size(axis)
    pairs = [(source, (source + steps) % count) for source in range(count)]
    return lax.ppermute(value, axis, pairs)


def folded_positions(row_total, offset, shard_rows, devices_ctx):
    flat_index = offset + lax.iota(jnp.int32, row_total)
    owner_dev = flat_index // shard_rows
    within = flat_index % shard_rows
    half_rows = shard_rows // 2
    fold_block = jnp.where(within < half_rows, owner_dev, 2 * devices_ctx - 1 - owner_dev)
    return fold_block * half_rows + within % half_rows


def block_update(
    running, query, query_pos, query_doc, key_block, value_block, pos_block, doc_block
):
    largest, totals, summed = running
    query_rows = query.shape[0]
    local_heads = query.shape[1] // HD
    query_heads = query.reshape(query_rows, local_heads, HD)
    key_heads = key_block.reshape(key_block.shape[0], local_heads, HD)
    value_heads = value_block.reshape(value_block.shape[0], local_heads, HD)
    scores = jnp.einsum(
        "qhd,khd->hqk", query_heads, key_heads, preferred_element_type=jnp.float32
    ) * (1.0 / math.sqrt(HD))
    allowed = (query_doc[:, None] == doc_block[None, :]) & (
        pos_block[None, :] <= query_pos[:, None]
    )
    scores = jnp.where(allowed[None], scores, MASKED_SCORE)
    new_max = jnp.maximum(largest, jnp.max(scores, axis=2))
    weights = jnp.where(allowed[None], jnp.exp(scores - new_max[:, :, None]), 0.0)
    factor = jnp.exp(largest - new_max)
    totals = totals * factor + jnp.sum(weights, axis=2)
    product = jnp.einsum(
        "hqk,khd->qhd",
        weights.astype(jnp.bfloat16),
        value_heads,
        preferred_element_type=jnp.float32,
    )
    summed = summed * factor.T[:, :, None] + product
    return (new_max, totals, summed)


def attend_rows(running, query, query_pos, query_doc, key_rows, value_rows, key_pos, key_doc):
    row_total = key_rows.shape[0]
    block_rows = math.gcd(row_total, query.shape[0])
    block_count = row_total // block_rows
    highest = jnp.max(query_pos)

    def visit(partial_value, blocks):
        key_block, value_block, pos_block, doc_block = blocks
        masked_out = jnp.min(pos_block) > highest
        updated = lax.cond(
            masked_out,
            lambda frozen: frozen,
            lambda frozen: block_update(
                frozen, query, query_pos, query_doc, key_block, value_block, pos_block, doc_block
            ),
            partial_value,
        )
        return (updated, None)

    blocks = (
        key_rows.reshape(block_count, block_rows, key_rows.shape[1]),
        value_rows.reshape(block_count, block_rows, value_rows.shape[1]),
        key_pos.reshape(block_count, block_rows),
        key_doc.reshape(block_count, block_rows),
    )
    running, _ = lax.scan(visit, running, blocks)
    return running


def attend_shard(running, query, query_pos, query_doc, key_rows, value_rows, key_pos, key_doc):
    largest, totals, summed = running
    half_rows = query.shape[0] // 2
    new_largest = []
    new_totals = []
    new_summed = []
    for half_idx in range(2):
        lower = half_idx * half_rows
        part_state = (largest[half_idx], totals[half_idx], summed[half_idx])
        part_state = attend_rows(
            part_state,
            query[lower : lower + half_rows],
            query_pos[lower : lower + half_rows],
            query_doc[lower : lower + half_rows],
            key_rows,
            value_rows,
            key_pos,
            key_doc,
        )
        new_largest.append(part_state[0])
        new_totals.append(part_state[1])
        new_summed.append(part_state[2])
    return (jnp.stack(new_largest), jnp.stack(new_totals), jnp.stack(new_summed))


def ring_local(queries, keys, values, doc_ids, w_out):
    shard_rows = queries.shape[0]
    half_rows = shard_rows // 2
    local_heads = queries.shape[1] // HD
    devices_ctx = lax.axis_size("ctx")
    ctx_index = lax.axis_index("ctx")
    all_docs = lax.all_gather(doc_ids, "ctx", axis=0, tiled=True)
    own_pos = folded_positions(shard_rows, ctx_index * shard_rows, shard_rows, devices_ctx)
    running = (
        jnp.full((2, local_heads, half_rows), MASKED_SCORE, jnp.float32),
        jnp.zeros((2, local_heads, half_rows), jnp.float32),
        jnp.zeros((2, half_rows, local_heads, HD), jnp.float32),
    )
    travel = queries
    for hop_step in range(devices_ctx):
        anchor = (ctx_index - hop_step) % devices_ctx
        query_pos = folded_positions(shard_rows, anchor * shard_rows, shard_rows, devices_ctx)
        query_doc = lax.dynamic_slice_in_dim(all_docs, anchor * shard_rows, shard_rows, 0)
        largest, totals, summed = attend_shard(
            running, travel, query_pos, query_doc, keys, values, own_pos, doc_ids
        )
        running = (
            passed_along(largest.astype(jnp.bfloat16), "ctx", 1).astype(largest.dtype),
            passed_along(totals.astype(jnp.bfloat16), "ctx", 1).astype(totals.dtype),
            passed_along(summed.astype(jnp.bfloat16), "ctx", 1).astype(summed.dtype),
        )
        if hop_step + 1 < devices_ctx:
            travel = passed_along(travel, "ctx", 1)
    largest, totals, summed = running
    attended = summed / totals.transpose(0, 2, 1)[:, :, :, None]
    attended = attended.reshape(shard_rows, local_heads * HD).astype(jnp.bfloat16)
    partial_out = jnp.dot(attended, w_out, preferred_element_type=jnp.float32)
    return lax.psum_scatter(
        partial_out.astype(jnp.bfloat16), "head", scatter_dimension=1, tiled=True
    )


SMALL = pl.CostEstimate(flops=1024, bytes_accessed=1024, transcendentals=0)
TILE = 256
MOST_DOCS = 16


def params(mib):
    return pltpu.CompilerParams(vmem_limit_bytes=mib * 1024 * 1024)


def whole(shape):
    return pl.BlockSpec(shape, lambda step, scalars: (0,) * len(shape))


def pack(ctx_index, half, queries, keys, values, docs):
    rows = queries.shape[0] // 2
    group = queries.shape[1] // HD
    doc_rows = 0 if docs is None else 16 * pl.cdiv(docs.shape[0], 16)
    total = 3 * rows + doc_rows

    def kernel(ctx_ref, *refs):
        outs = refs[len(refs) - (group - 1) :]
        if docs is not None:
            mine = refs[3 * (group - 1)][...].astype(jnp.float32)
            empty = jnp.zeros((doc_rows - mine.shape[0], HD), jnp.float32)
            mine = jnp.concatenate([mine, empty], axis=0).astype(jnp.bfloat16)
        for place in range(group - 1):
            for part in range(2):
                outs[place][part * rows : (part + 1) * rows, :] = refs[place * 3 + part][...]
            for block in range(rows // HD):
                taken = refs[place * 3 + 2][block * HD : (block + 1) * HD, :]
                lower = 2 * rows + block * HD
                outs[place][lower : lower + HD, :] = jnp.transpose(taken)
            if docs is not None:
                outs[place][3 * rows :, :] = mine

    def piece(distance):
        return pl.BlockSpec((rows, HD), lambda step, ctx: (half, ctx[0] ^ distance))

    in_specs = []
    operands = []
    for distance in range(1, group):
        for array in (queries, keys, values):
            in_specs.append(piece(distance))
            operands.append(array)
    if docs is not None:
        in_specs.append(whole(docs.shape))
        operands.append(docs)
    return pl.pallas_call(
        kernel,
        grid_spec=pltpu.PrefetchScalarGridSpec(
            num_scalar_prefetch=1,
            grid=(1,),
            in_specs=in_specs,
            out_specs=[whole((total, HD))] * (group - 1),
        ),
        out_shape=[jax.ShapeDtypeStruct((total, HD), jnp.bfloat16)] * (group - 1),
        compiler_params=params(56),
        cost_estimate=SMALL,
        name="pack",
    )(ctx_index, *operands)


def pack_projection(places, w_mine, w_sibling):
    depth, width = w_mine.shape
    turns = len(TURNS)
    columns = width // (2 * turns)

    def kernel(places_ref, mine_in, sibling_in, mine_out, sibling_out):
        mine_out[...] = mine_in[...]
        sibling_out[...] = sibling_in[...]

    in_spec = pl.BlockSpec((depth, columns), lambda turn, at: (0, at[turn]))
    out_spec = pl.BlockSpec((depth, columns), lambda turn, at: (0, turn))
    return pl.pallas_call(
        kernel,
        grid_spec=pltpu.PrefetchScalarGridSpec(
            num_scalar_prefetch=1,
            grid=(turns,),
            in_specs=[in_spec] * 2,
            out_specs=[out_spec] * 2,
        ),
        out_shape=[jax.ShapeDtypeStruct((depth, turns * columns), w_mine.dtype)] * 2,
        compiler_params=params(56),
        cost_estimate=SMALL,
        name="pack_projection",
    )(places, w_mine, w_sibling)


def attend(ctx_index, queries, keys, values, docs, low, high):
    rows = queries.shape[0] // 2
    group = queries.shape[1] // HD
    with_high = high is not None
    per_block = rows // TILE
    lines = rows // HD
    key_rows = (2 * group if with_high else group) * rows
    key_tiles = key_rows // TILE
    scaling = LOG2E / math.sqrt(HD)

    def kernel(ctx_ref, *refs):
        refs = list(refs)
        own_low = [refs.pop(0) for _ in range(3)]
        own_high = [refs.pop(0) for _ in range(3)] if with_high else None
        own_docs = refs.pop(0)
        low_refs = [refs.pop(0) for _ in range(group - 1)]
        high_refs = [refs.pop(0) for _ in range(group - 1)] if with_high else None
        outs = [refs.pop(0) for _ in range(group)]
        key_buf, value_buf, doc_buf = refs[:3]
        query_buf, start_buf, largest_buf, summed = (
            refs[3 + kind * group : 3 + (kind + 1) * group] for kind in range(4)
        )
        ctx = ctx_ref[0]

        def part(upper, distance, index, lower=0, count=rows):
            if distance == 0:
                return (own_high if upper else own_low)[index][lower : lower + count, :]
            source = (high_refs if upper else low_refs)[distance - 1]
            return source[index * rows + lower : index * rows + lower + count, :]

        place = {}
        doc_rows = {}
        for upper in (False, True) if with_high else (False,):
            for distance in range(group):
                source = ctx ^ distance
                block = 2 * group - 1 - source if upper else source
                place[upper, distance] = block
                offset = pl.multiple_of(block * rows, rows)
                key_buf[pl.ds(offset, rows), :] = part(upper, distance, 1)
                if distance == 0:
                    both = own_docs[...].astype(jnp.float32)
                else:
                    both = low_refs[distance - 1][3 * rows :, :].astype(jnp.float32)
                begin = lines if upper else 0
                mine = []
                for line in range(lines):
                    taken = part(upper, distance, 2, line * HD, HD)
                    if distance == 0:
                        taken = jnp.transpose(taken)
                    column = pl.multiple_of(block * rows + line * HD, HD)
                    value_buf[:HD, pl.ds(column, HD)] = taken
                    mine.append(both[begin + line : begin + line + 1, :])
                    doc_buf[pl.ds(block * lines + line, 1), :] = mine[-1]
                doc_rows[upper, distance] = jnp.concatenate(mine, axis=1)
        value_buf[HD:, :] = jnp.ones((value_buf.shape[0] - HD, key_rows), jnp.bfloat16)

        all_docs = doc_buf[...]
        starts = [jnp.zeros((1, rows), jnp.float32)] * group
        for number in range(1, MOST_DOCS):
            smaller = jnp.where(all_docs < number, 1.0, 0.0)
            count = jnp.sum(jnp.sum(smaller, axis=0, keepdims=True), axis=1, keepdims=True)
            for distance in range(group):
                reached = doc_rows[with_high, distance] >= number
                starts[distance] = jnp.where(reached, count, starts[distance])

        def scores_of(query, offset):
            raw = lax.dot_general(
                key_buf[pl.ds(offset, TILE), :],
                query,
                (((1,), (1,)), ((), ())),
                preferred_element_type=jnp.float32,
            )
            return raw * scaling

        def weighted(weights, offset):
            return jnp.dot(
                value_buf[:, pl.ds(offset, TILE)],
                weights.astype(jnp.bfloat16),
                preferred_element_type=jnp.float32,
            )

        key_row = lax.broadcasted_iota(jnp.int32, (TILE, TILE), 0)
        causal = key_row <= lax.broadcasted_iota(jnp.int32, (TILE, TILE), 1)
        key_row = key_row.astype(jnp.float32)
        firsts = []
        counts = []
        for lane in range(group):
            for slot in range(per_block):
                distance = lane ^ (slot * (group - 1))
                query = part(with_high, distance, 0, slot * TILE, TILE)
                query_buf[lane][slot] = query
                start = starts[distance][:, slot * TILE : (slot + 1) * TILE]
                start_buf[lane][slot, 0:1, :] = start
                end = place[with_high, distance] * per_block + slot
                offset = pl.multiple_of(end * TILE, TILE)
                least = start - offset.astype(jnp.float32)
                scores = scores_of(query, offset)
                scores = jnp.where((key_row >= least) & causal, scores, MASKED_SCORE)
                largest = jnp.max(scores, axis=0, keepdims=True)
                largest_buf[lane][slot, 0:1, :] = largest
                summed[lane][slot] = weighted(jnp.exp2(scores - largest), offset)
                first = start[0, 0].astype(jnp.int32) // TILE
                firsts.append(first)
                counts.append(end - first)

        longest = jnp.int32(0)
        for lane in range(group):
            of_lane = counts[lane * per_block : (lane + 1) * per_block]
            longest = jnp.maximum(longest, sum(of_lane))

        def visit(step, carry):
            slots = []
            offsets = []
            beyonds = []
            for lane in range(group):
                slot = jnp.int32(0)
                index = firsts[lane * per_block] + step
                before = counts[lane * per_block]
                for later in range(1, per_block):
                    reached = step >= before
                    slot = jnp.where(reached, later, slot)
                    place_later = lane * per_block + later
                    index = jnp.where(reached, firsts[place_later] + step - before, index)
                    before = before + counts[place_later]
                offset = pl.multiple_of(jnp.minimum(index, key_tiles - 1) * TILE, TILE)
                slots.append(slot)
                offsets.append(offset)
                beyonds.append(jnp.where(step < before, -offset.astype(jnp.float32), 1e9))
            each = range(group)
            scores = [scores_of(query_buf[lane][slots[lane]], offsets[lane]) for lane in each]
            old_max = [largest_buf[lane][slots[lane], 0:1, :] for lane in each]
            new_max = []
            for lane in each:
                least = start_buf[lane][slots[lane], 0:1, :] + beyonds[lane]
                scores[lane] = jnp.where(key_row >= least, scores[lane], MASKED_SCORE)
                tile_max = jnp.max(scores[lane], axis=0, keepdims=True)
                new_max.append(jnp.maximum(old_max[lane], tile_max))
            products = [
                weighted(jnp.exp2(scores[lane] - new_max[lane]), offsets[lane]) for lane in each
            ]
            for lane in each:
                factor = jnp.exp2(old_max[lane] - new_max[lane])
                summed[lane][slots[lane]] = summed[lane][slots[lane]] * factor + products[lane]
                largest_buf[lane][slots[lane], 0:1, :] = new_max[lane]
            return carry

        lax.fori_loop(0, longest, visit, jnp.int32(0))
        for lane in range(group):
            for slot in range(per_block):
                state = summed[lane]
                attended = state[slot, :HD, :] * (1.0 / state[slot, HD : HD + 1, :])
                out = outs[lane ^ (slot * (group - 1))]
                out[slot * TILE : (slot + 1) * TILE, :] = jnp.transpose(
                    attended.astype(jnp.bfloat16)
                )

    def own(upper):
        return pl.BlockSpec((rows, HD), lambda step, ctx: (int(upper), ctx[0]))

    in_specs = [own(False)] * 3
    operands = [queries, keys, values]
    if with_high:
        in_specs += [own(True)] * 3
        operands += [queries, keys, values]
    received = [docs, *low, *(high if with_high else ())]
    operands += received
    in_specs += [whole(array.shape) for array in received]
    return pl.pallas_call(
        kernel,
        grid_spec=pltpu.PrefetchScalarGridSpec(
            num_scalar_prefetch=1,
            grid=(1,),
            in_specs=in_specs,
            out_specs=[whole((rows, HD))] * group,
            scratch_shapes=[
                pltpu.VMEM((key_rows, HD), jnp.bfloat16),
                pltpu.VMEM((HD + 16, key_rows), jnp.bfloat16),
                pltpu.VMEM((key_rows // HD, HD), jnp.float32),
                *[pltpu.VMEM((per_block, TILE, HD), jnp.bfloat16)] * group,
                *[pltpu.VMEM((per_block, 8, TILE), jnp.float32)] * (2 * group),
                *[pltpu.VMEM((per_block, HD + 16, TILE), jnp.float32)] * group,
            ],
        ),
        out_shape=[jax.ShapeDtypeStruct((rows, HD), jnp.bfloat16)] * group,
        compiler_params=params(40),
        cost_estimate=SMALL,
        name="attend_high" if with_high else "attend_low",
    )(ctx_index, *operands)


def assemble(ctx_index, pieces, cuts):
    rows = pieces[0].shape[0]
    group = len(pieces)
    spans = list(zip(cuts[:-1], cuts[1:]))

    def kernel(ctx_ref, *refs):
        for part, (lower, upper) in enumerate(spans):
            for distance in range(group):
                column = pl.multiple_of((ctx_ref[0] ^ distance) * HD, HD)
                refs[group + part][:, pl.ds(column, HD)] = refs[distance][lower:upper, :]

    shapes = [(upper - lower, group * HD) for lower, upper in spans]
    return pl.pallas_call(
        kernel,
        grid_spec=pltpu.PrefetchScalarGridSpec(
            num_scalar_prefetch=1,
            grid=(1,),
            in_specs=[whole((rows, HD))] * group,
            out_specs=[whole(shape) for shape in shapes],
        ),
        out_shape=[jax.ShapeDtypeStruct(shape, jnp.bfloat16) for shape in shapes],
        compiler_params=params(16),
        cost_estimate=SMALL,
        name="assemble",
    )(ctx_index, *pieces)


def plain(shape):
    return pl.BlockSpec(shape, lambda step: (0,) * len(shape))


def stacked(refs):
    values = [ref[...] for ref in refs]
    return values[0] if len(values) == 1 else jnp.concatenate(values, axis=0)


def project(wanted, mine, sibling, w_mine, w_sibling):
    parts = len(mine)
    depth = mine[0].shape[1]
    columns = w_mine.shape[1] // len(TURNS)
    turns = sorted({turn for output in wanted for turn, _, _ in output})

    def kernel(*refs):
        own_rows = stacked(refs[:parts])
        other_rows = stacked(refs[parts : 2 * parts])
        weights = refs[2 * parts : 2 * parts + 2 * len(turns)]
        outs = refs[2 * parts + 2 * len(turns) :]
        for out, output in zip(outs, wanted):
            place = 0
            for turn, lower, upper in output:
                at = turns.index(turn)
                total = jnp.dot(
                    own_rows[lower:upper, :], weights[at][...], preferred_element_type=jnp.float32
                )
                total += jnp.dot(
                    other_rows[lower:upper, :],
                    weights[len(turns) + at][...],
                    preferred_element_type=jnp.float32,
                )
                out[place : place + upper - lower, :] = total.astype(jnp.bfloat16)
                place += upper - lower

    def columns_of(turn):
        return pl.BlockSpec((depth, columns), lambda step: (0, turn))

    shapes = [(sum(upper - lower for _, lower, upper in output), columns) for output in wanted]
    return pl.pallas_call(
        kernel,
        grid=(1,),
        in_specs=[plain(part.shape) for part in (*mine, *sibling)]
        + [columns_of(turn) for turn in turns] * 2,
        out_specs=[plain(shape) for shape in shapes],
        out_shape=[jax.ShapeDtypeStruct(shape, jnp.bfloat16) for shape in shapes],
        compiler_params=params(24),
        cost_estimate=SMALL,
        name="project",
    )(*mine, *sibling, *([w_mine] * len(turns)), *([w_sibling] * len(turns)))


def finish(half, rows, terms, result):
    flat = [array for term in terms for array, _ in term]
    columns = flat[0].shape[1]

    def kernel(*refs):
        refs = list(refs)
        total = None
        for term in terms:
            values = [refs.pop(0)[first:, :].astype(jnp.float32) for _, first in term]
            value = values[0] if len(values) == 1 else jnp.concatenate(values, axis=0)
            total = value if total is None else total + value
        refs[-1][...] = total.astype(jnp.bfloat16)

    in_specs = [plain(array.shape) for array in flat]
    operands = list(flat)
    aliases = {}
    if result is not None:
        in_specs.append(pl.BlockSpec(memory_space=pl.ANY))
        operands.append(result)
        aliases = {len(flat): 0}
    return pl.pallas_call(
        kernel,
        grid=(1,),
        in_specs=in_specs,
        out_specs=pl.BlockSpec((rows, columns), lambda step: (half, 0)),
        out_shape=jax.ShapeDtypeStruct((2 * rows, columns), jnp.bfloat16),
        input_output_aliases=aliases,
        compiler_params=params(16),
        cost_estimate=SMALL,
        name="finish",
    )(*operands)


def swap(value, axis, distance):
    count = lax.axis_size(axis)
    return lax.ppermute(value, axis, [(source, source ^ distance) for source in range(count)])


def add(*terms):
    total = terms[0].astype(jnp.float32)
    for term in terms[1:]:
        total = total + term.astype(jnp.float32)
    return total.astype(jnp.bfloat16)


TURNS = (3, 1, 2, 0)


def tie(*values):
    return lax.optimization_barrier(values)


def exchange_local(queries, keys, values, doc_ids, w_out):
    shard_rows = queries.shape[0]
    group = queries.shape[1] // HD
    ctx_index = lax.axis_index("ctx").astype(jnp.int32).reshape(1)
    head_index = lax.axis_index("head").astype(jnp.int32)
    places = head_index ^ (2 * jnp.array(TURNS, jnp.int32))
    docs = doc_ids.reshape(shard_rows // HD, HD)
    near = range(1, group)

    w_sibling = swap(w_out, "head", 1)
    low_out = pack(ctx_index, 0, queries, keys, values, docs)
    low_out, later = tie(low_out, (queries, keys, values))
    low = [swap(low_out[distance - 1], "ctx", distance) for distance in near]
    high_out = pack(ctx_index, 1, *later, None)
    high = [swap(high_out[distance - 1], "ctx", distance) for distance in near[:-1]]
    w_packed = pack_projection(places, w_out, w_sibling)
    low, w_packed = tie(low, w_packed)

    def send_back(pieces):
        return [swap(pieces[distance], "ctx", distance) for distance in near]

    rows = shard_rows // 2
    cut = rows * 23 // 32 // 16 * 16
    third = rows * 11 // 32 // 16 * 16
    middle = rows // 2

    def projected(mine, sibling, *wanted):
        return list(project(wanted, mine, sibling, *w_packed))

    def to_next(part, distance):
        return swap(part, "head", 2 * distance)

    pieces = attend(ctx_index, queries, keys, values, docs, low, None)
    pieces, diagonal_out = tie(pieces, high_out[-1])
    back = send_back(pieces)
    back, high = tie(back, high)
    high = [*high, swap(diagonal_out, "ctx", near[-1])]
    mine = assemble(ctx_index, [pieces[0], *back], (0, rows))
    sibling = [swap(part, "head", 1) for part in mine]
    (share,) = projected(mine, sibling, [(0, 0, cut)])
    far = to_next(share, 1)
    (behind,) = projected(mine, sibling, [(0, cut, rows), (1, 0, rows)])
    shares = projected(mine, sibling, [(2, 0, cut)], [(2, cut, rows)])
    (kept,) = projected(mine, sibling, [(3, 0, rows)])

    passed = add(shares[0], far)
    high, passed, _, shares[1], kept = tie(high, passed, behind, shares[1], kept)
    behind = to_next(behind, 1)
    across = to_next(passed, 2)
    pieces = attend(ctx_index, queries, keys, values, docs, low, high)
    back = send_back(pieces)
    mine = assemble(ctx_index, [pieces[0], *back], (0, third, 2 * third, rows))
    sibling = [swap(part, "head", 1) for part in mine]
    late = [projected(mine, sibling, [(turn, 0, rows)])[0] for turn in (0, 2, 3)]
    late[0], behind, across = tie(late[0], behind, across)
    far = to_next(late[0], 1)
    across = [across, to_next(add(shares[1], behind[: rows - cut]), 2)]
    passed = add(late[1], far)
    passed, across[1] = tie(passed, across[1])
    terms = [[(kept, 0)], [(behind, rows - cut)], [(part, 0) for part in across]]
    result = finish(0, rows, terms, None)
    across = to_next(passed, 2)
    last = projected(mine, sibling, [(1, 0, middle)], [(1, middle, rows)])
    last, passed = tie(last, passed)
    near_sum = [to_next(part, 1) for part in last]
    terms = [[(late[2], 0)], [(part, 0) for part in near_sum], [(across, 0)]]
    return finish(1, rows, terms, result)


def solution(mesh):
    in_specs = (P("ctx", "head"), P("ctx", "head"), P("ctx", "head"), P("ctx"), P("head", None))
    out_specs = P("ctx", "head")
    ctx_count = mesh.shape["ctx"]
    head_count = mesh.shape["head"]

    def local(queries, keys, values, doc_ids, w_out):
        heads = queries.shape[1] // HD
        exchange = heads == ctx_count and heads == 4 and head_count == 2 * len(TURNS)
        exchange = exchange and queries.shape[0] % (4 * TILE) == 0
        body = exchange_local if exchange else ring_local
        return body(queries, keys, values, doc_ids, w_out)

    return jax.shard_map(
        local, mesh=mesh, in_specs=in_specs, out_specs=out_specs, check_vma=False
    )
```

```python
import functools
import math

import jax
import jax.numpy as jnp
from jax import lax
from jax.experimental import pallas as pl
from jax.experimental.pallas import tpu as pltpu
from jax.sharding import PartitionSpec as P

HD = 128


MASKED_SCORE = -1e30
LOG2E = 1.4426950408889634


def passed_along(value, axis, steps):
    count = lax.axis_size(axis)
    pairs = [(source, (source + steps) % count) for source in range(count)]
    return lax.ppermute(value, axis, pairs)


def folded_positions(row_total, offset, shard_rows, devices_ctx):
    flat_index = offset + lax.iota(jnp.int32, row_total)
    owner_dev = flat_index // shard_rows
    within = flat_index % shard_rows
    half_rows = shard_rows // 2
    fold_block = jnp.where(within < half_rows, owner_dev, 2 * devices_ctx - 1 - owner_dev)
    return fold_block * half_rows + within % half_rows


def block_update(
    running, query, query_pos, query_doc, key_block, value_block, pos_block, doc_block
):
    largest, totals, summed = running
    query_rows = query.shape[0]
    local_heads = query.shape[1] // HD
    query_heads = query.reshape(query_rows, local_heads, HD)
    key_heads = key_block.reshape(key_block.shape[0], local_heads, HD)
    value_heads = value_block.reshape(value_block.shape[0], local_heads, HD)
    scores = jnp.einsum(
        "qhd,khd->hqk", query_heads, key_heads, preferred_element_type=jnp.float32
    ) * (1.0 / math.sqrt(HD))
    allowed = (query_doc[:, None] == doc_block[None, :]) & (
        pos_block[None, :] <= query_pos[:, None]
    )
    scores = jnp.where(allowed[None], scores, MASKED_SCORE)
    new_max = jnp.maximum(largest, jnp.max(scores, axis=2))
    weights = jnp.where(allowed[None], jnp.exp(scores - new_max[:, :, None]), 0.0)
    factor = jnp.exp(largest - new_max)
    totals = totals * factor + jnp.sum(weights, axis=2)
    product = jnp.einsum(
        "hqk,khd->qhd",
        weights.astype(jnp.bfloat16),
        value_heads,
        preferred_element_type=jnp.float32,
    )
    summed = summed * factor.T[:, :, None] + product
    return (new_max, totals, summed)


def attend_rows(running, query, query_pos, query_doc, key_rows, value_rows, key_pos, key_doc):
    row_total = key_rows.shape[0]
    block_rows = math.gcd(row_total, query.shape[0])
    block_count = row_total // block_rows
    highest = jnp.max(query_pos)

    def visit(partial_value, blocks):
        key_block, value_block, pos_block, doc_block = blocks
        masked_out = jnp.min(pos_block) > highest
        updated = lax.cond(
            masked_out,
            lambda frozen: frozen,
            lambda frozen: block_update(
                frozen, query, query_pos, query_doc, key_block, value_block, pos_block, doc_block
            ),
            partial_value,
        )
        return (updated, None)

    blocks = (
        key_rows.reshape(block_count, block_rows, key_rows.shape[1]),
        value_rows.reshape(block_count, block_rows, value_rows.shape[1]),
        key_pos.reshape(block_count, block_rows),
        key_doc.reshape(block_count, block_rows),
    )
    running, _ = lax.scan(visit, running, blocks)
    return running


def attend_shard(running, query, query_pos, query_doc, key_rows, value_rows, key_pos, key_doc):
    largest, totals, summed = running
    half_rows = query.shape[0] // 2
    new_largest = []
    new_totals = []
    new_summed = []
    for half_idx in range(2):
        lower = half_idx * half_rows
        part_state = (largest[half_idx], totals[half_idx], summed[half_idx])
        part_state = attend_rows(
            part_state,
            query[lower : lower + half_rows],
            query_pos[lower : lower + half_rows],
            query_doc[lower : lower + half_rows],
            key_rows,
            value_rows,
            key_pos,
            key_doc,
        )
        new_largest.append(part_state[0])
        new_totals.append(part_state[1])
        new_summed.append(part_state[2])
    return (jnp.stack(new_largest), jnp.stack(new_totals), jnp.stack(new_summed))


def ring_local(queries, keys, values, doc_ids, w_out):
    shard_rows = queries.shape[0]
    half_rows = shard_rows // 2
    local_heads = queries.shape[1] // HD
    devices_ctx = lax.axis_size("ctx")
    ctx_index = lax.axis_index("ctx")
    all_docs = lax.all_gather(doc_ids, "ctx", axis=0, tiled=True)
    own_pos = folded_positions(shard_rows, ctx_index * shard_rows, shard_rows, devices_ctx)
    running = (
        jnp.full((2, local_heads, half_rows), MASKED_SCORE, jnp.float32),
        jnp.zeros((2, local_heads, half_rows), jnp.float32),
        jnp.zeros((2, half_rows, local_heads, HD), jnp.float32),
    )
    travel = queries
    for hop_step in range(devices_ctx):
        anchor = (ctx_index - hop_step) % devices_ctx
        query_pos = folded_positions(shard_rows, anchor * shard_rows, shard_rows, devices_ctx)
        query_doc = lax.dynamic_slice_in_dim(all_docs, anchor * shard_rows, shard_rows, 0)
        largest, totals, summed = attend_shard(
            running, travel, query_pos, query_doc, keys, values, own_pos, doc_ids
        )
        running = (
            passed_along(largest.astype(jnp.bfloat16), "ctx", 1).astype(largest.dtype),
            passed_along(totals.astype(jnp.bfloat16), "ctx", 1).astype(totals.dtype),
            passed_along(summed.astype(jnp.bfloat16), "ctx", 1).astype(summed.dtype),
        )
        if hop_step + 1 < devices_ctx:
            travel = passed_along(travel, "ctx", 1)
    largest, totals, summed = running
    attended = summed / totals.transpose(0, 2, 1)[:, :, :, None]
    attended = attended.reshape(shard_rows, local_heads * HD).astype(jnp.bfloat16)
    partial_out = jnp.dot(attended, w_out, preferred_element_type=jnp.float32)
    return lax.psum_scatter(
        partial_out.astype(jnp.bfloat16), "head", scatter_dimension=1, tiled=True
    )


SMALL = pl.CostEstimate(flops=1024, bytes_accessed=1024, transcendentals=0)
TILE = 256
MOST_DOCS = 16


def params(mib):
    return pltpu.CompilerParams(vmem_limit_bytes=mib * 1024 * 1024)


def whole(shape):
    return pl.BlockSpec(shape, lambda step, scalars: (0,) * len(shape))


def pack(ctx_index, half, queries, keys, values, docs):
    rows = queries.shape[0] // 2
    group = queries.shape[1] // HD
    doc_rows = 0 if docs is None else 16 * pl.cdiv(docs.shape[0], 16)
    total = 3 * rows + doc_rows

    def kernel(ctx_ref, *refs):
        outs = refs[len(refs) - (group - 1) :]
        if docs is not None:
            mine = refs[3 * (group - 1)][...].astype(jnp.float32)
            empty = jnp.zeros((doc_rows - mine.shape[0], HD), jnp.float32)
            mine = jnp.concatenate([mine, empty], axis=0).astype(jnp.bfloat16)
        for place in range(group - 1):
            for part in range(2):
                outs[place][part * rows : (part + 1) * rows, :] = refs[place * 3 + part][...]
            for block in range(rows // HD):
                taken = refs[place * 3 + 2][block * HD : (block + 1) * HD, :]
                lower = 2 * rows + block * HD
                outs[place][lower : lower + HD, :] = jnp.transpose(taken)
            if docs is not None:
                outs[place][3 * rows :, :] = mine

    def piece(distance):
        return pl.BlockSpec((rows, HD), lambda step, ctx: (half, ctx[0] ^ distance))

    in_specs = []
    operands = []
    for distance in range(1, group):
        for array in (queries, keys, values):
            in_specs.append(piece(distance))
            operands.append(array)
    if docs is not None:
        in_specs.append(whole(docs.shape))
        operands.append(docs)
    return pl.pallas_call(
        kernel,
        grid_spec=pltpu.PrefetchScalarGridSpec(
            num_scalar_prefetch=1,
            grid=(1,),
            in_specs=in_specs,
            out_specs=[whole((total, HD))] * (group - 1),
        ),
        out_shape=[jax.ShapeDtypeStruct((total, HD), jnp.bfloat16)] * (group - 1),
        compiler_params=params(56),
        cost_estimate=SMALL,
        name="pack",
    )(ctx_index, *operands)


def pack_projection(places, w_mine, w_sibling):
    depth, width = w_mine.shape
    turns = len(TURNS)
    columns = width // (2 * turns)

    def kernel(places_ref, mine_in, sibling_in, mine_out, sibling_out):
        mine_out[...] = mine_in[...]
        sibling_out[...] = sibling_in[...]

    in_spec = pl.BlockSpec((depth, columns), lambda turn, at: (0, at[turn]))
    out_spec = pl.BlockSpec((depth, columns), lambda turn, at: (0, turn))
    return pl.pallas_call(
        kernel,
        grid_spec=pltpu.PrefetchScalarGridSpec(
            num_scalar_prefetch=1,
            grid=(turns,),
            in_specs=[in_spec] * 2,
            out_specs=[out_spec] * 2,
        ),
        out_shape=[jax.ShapeDtypeStruct((depth, turns * columns), w_mine.dtype)] * 2,
        compiler_params=params(56),
        cost_estimate=SMALL,
        name="pack_projection",
    )(places, w_mine, w_sibling)


def attend(ctx_index, queries, keys, values, docs, low, high):
    rows = queries.shape[0] // 2
    group = queries.shape[1] // HD
    with_high = high is not None
    per_block = rows // TILE
    lines = rows // HD
    key_rows = (2 * group if with_high else group) * rows
    key_tiles = key_rows // TILE
    scaling = LOG2E / math.sqrt(HD)

    def kernel(ctx_ref, *refs):
        refs = list(refs)
        own_low = [refs.pop(0) for _ in range(3)]
        own_high = [refs.pop(0) for _ in range(3)] if with_high else None
        own_docs = refs.pop(0)
        low_refs = [refs.pop(0) for _ in range(group - 1)]
        high_refs = [refs.pop(0) for _ in range(group - 1)] if with_high else None
        outs = [refs.pop(0) for _ in range(group)]
        key_buf, value_buf, doc_buf = refs[:3]
        query_buf, start_buf, largest_buf, summed = (
            refs[3 + kind * group : 3 + (kind + 1) * group] for kind in range(4)
        )
        ctx = ctx_ref[0]

        def part(upper, distance, index, lower=0, count=rows):
            if distance == 0:
                return (own_high if upper else own_low)[index][lower : lower + count, :]
            source = (high_refs if upper else low_refs)[distance - 1]
            return source[index * rows + lower : index * rows + lower + count, :]

        place = {}
        doc_rows = {}
        for upper in (False, True) if with_high else (False,):
            for distance in range(group):
                source = ctx ^ distance
                block = 2 * group - 1 - source if upper else source
                place[upper, distance] = block
                offset = pl.multiple_of(block * rows, rows)
                key_buf[pl.ds(offset, rows), :] = part(upper, distance, 1)
                if distance == 0:
                    both = own_docs[...].astype(jnp.float32)
                else:
                    both = low_refs[distance - 1][3 * rows :, :].astype(jnp.float32)
                begin = lines if upper else 0
                mine = []
                for line in range(lines):
                    taken = part(upper, distance, 2, line * HD, HD)
                    if distance == 0:
                        taken = jnp.transpose(taken)
                    column = pl.multiple_of(block * rows + line * HD, HD)
                    value_buf[:HD, pl.ds(column, HD)] = taken
                    mine.append(both[begin + line : begin + line + 1, :])
                    doc_buf[pl.ds(block * lines + line, 1), :] = mine[-1]
                doc_rows[upper, distance] = jnp.concatenate(mine, axis=1)
        value_buf[HD:, :] = jnp.ones((value_buf.shape[0] - HD, key_rows), jnp.bfloat16)

        all_docs = doc_buf[...]
        starts = [jnp.zeros((1, rows), jnp.float32)] * group
        for number in range(1, MOST_DOCS):
            smaller = jnp.where(all_docs < number, 1.0, 0.0)
            count = jnp.sum(jnp.sum(smaller, axis=0, keepdims=True), axis=1, keepdims=True)
            for distance in range(group):
                reached = doc_rows[with_high, distance] >= number
                starts[distance] = jnp.where(reached, count, starts[distance])

        def scores_of(query, offset):
            raw = lax.dot_general(
                key_buf[pl.ds(offset, TILE), :],
                query,
                (((1,), (1,)), ((), ())),
                preferred_element_type=jnp.float32,
            )
            return raw * scaling

        def weighted(weights, offset):
            return jnp.dot(
                value_buf[:, pl.ds(offset, TILE)],
                weights.astype(jnp.bfloat16),
                preferred_element_type=jnp.float32,
            )

        key_row = lax.broadcasted_iota(jnp.int32, (TILE, TILE), 0)
        causal = key_row <= lax.broadcasted_iota(jnp.int32, (TILE, TILE), 1)
        key_row = key_row.astype(jnp.float32)
        firsts = []
        counts = []
        for lane in range(group):
            for slot in range(per_block):
                distance = lane ^ (slot * (group - 1))
                query = part(with_high, distance, 0, slot * TILE, TILE)
                query_buf[lane][slot] = query
                start = starts[distance][:, slot * TILE : (slot + 1) * TILE]
                start_buf[lane][slot, 0:1, :] = start
                end = place[with_high, distance] * per_block + slot
                offset = pl.multiple_of(end * TILE, TILE)
                least = start - offset.astype(jnp.float32)
                scores = scores_of(query, offset)
                scores = jnp.where((key_row >= least) & causal, scores, MASKED_SCORE)
                largest = jnp.max(scores, axis=0, keepdims=True)
                largest_buf[lane][slot, 0:1, :] = largest
                summed[lane][slot] = weighted(jnp.exp2(scores - largest), offset)
                first = start[0, 0].astype(jnp.int32) // TILE
                firsts.append(first)
                counts.append(end - first)

        longest = jnp.int32(0)
        for lane in range(group):
            of_lane = counts[lane * per_block : (lane + 1) * per_block]
            longest = jnp.maximum(longest, sum(of_lane))

        def visit(step, carry):
            slots = []
            offsets = []
            beyonds = []
            for lane in range(group):
                slot = jnp.int32(0)
                index = firsts[lane * per_block] + step
                before = counts[lane * per_block]
                for later in range(1, per_block):
                    reached = step >= before
                    slot = jnp.where(reached, later, slot)
                    place_later = lane * per_block + later
                    index = jnp.where(reached, firsts[place_later] + step - before, index)
                    before = before + counts[place_later]
                offset = pl.multiple_of(jnp.minimum(index, key_tiles - 1) * TILE, TILE)
                slots.append(slot)
                offsets.append(offset)
                beyonds.append(jnp.where(step < before, -offset.astype(jnp.float32), 1e9))
            each = range(group)
            scores = [scores_of(query_buf[lane][slots[lane]], offsets[lane]) for lane in each]
            old_max = [largest_buf[lane][slots[lane], 0:1, :] for lane in each]
            new_max = []
            for lane in each:
                least = start_buf[lane][slots[lane], 0:1, :] + beyonds[lane]
                scores[lane] = jnp.where(key_row >= least, scores[lane], MASKED_SCORE)
                tile_max = jnp.max(scores[lane], axis=0, keepdims=True)
                new_max.append(jnp.maximum(old_max[lane], tile_max))
            products = [
                weighted(jnp.exp2(scores[lane] - new_max[lane]), offsets[lane]) for lane in each
            ]
            for lane in each:
                factor = jnp.exp2(old_max[lane] - new_max[lane])
                summed[lane][slots[lane]] = summed[lane][slots[lane]] * factor + products[lane]
                largest_buf[lane][slots[lane], 0:1, :] = new_max[lane]
            return carry

        lax.fori_loop(0, longest, visit, jnp.int32(0))
        for lane in range(group):
            for slot in range(per_block):
                state = summed[lane]
                attended = state[slot, :HD, :] * (1.0 / state[slot, HD : HD + 1, :])
                out = outs[lane ^ (slot * (group - 1))]
                out[slot * TILE : (slot + 1) * TILE, :] = jnp.transpose(
                    attended.astype(jnp.bfloat16)
                )

    def own(upper):
        return pl.BlockSpec((rows, HD), lambda step, ctx: (int(upper), ctx[0]))

    in_specs = [own(False)] * 3
    operands = [queries, keys, values]
    if with_high:
        in_specs += [own(True)] * 3
        operands += [queries, keys, values]
    received = [docs, *low, *(high if with_high else ())]
    operands += received
    in_specs += [whole(array.shape) for array in received]
    return pl.pallas_call(
        kernel,
        grid_spec=pltpu.PrefetchScalarGridSpec(
            num_scalar_prefetch=1,
            grid=(1,),
            in_specs=in_specs,
            out_specs=[whole((rows, HD))] * group,
            scratch_shapes=[
                pltpu.VMEM((key_rows, HD), jnp.bfloat16),
                pltpu.VMEM((HD + 16, key_rows), jnp.bfloat16),
                pltpu.VMEM((key_rows // HD, HD), jnp.float32),
                *[pltpu.VMEM((per_block, TILE, HD), jnp.bfloat16)] * group,
                *[pltpu.VMEM((per_block, 8, TILE), jnp.float32)] * (2 * group),
                *[pltpu.VMEM((per_block, HD + 16, TILE), jnp.float32)] * group,
            ],
        ),
        out_shape=[jax.ShapeDtypeStruct((rows, HD), jnp.bfloat16)] * group,
        compiler_params=params(40),
        cost_estimate=SMALL,
        name="attend_high" if with_high else "attend_low",
    )(ctx_index, *operands)


def assemble(ctx_index, pieces, cuts):
    rows = pieces[0].shape[0]
    group = len(pieces)
    spans = list(zip(cuts[:-1], cuts[1:]))

    def kernel(ctx_ref, *refs):
        for part, (lower, upper) in enumerate(spans):
            for distance in range(group):
                column = pl.multiple_of((ctx_ref[0] ^ distance) * HD, HD)
                refs[group + part][:, pl.ds(column, HD)] = refs[distance][lower:upper, :]

    shapes = [(upper - lower, group * HD) for lower, upper in spans]
    return pl.pallas_call(
        kernel,
        grid_spec=pltpu.PrefetchScalarGridSpec(
            num_scalar_prefetch=1,
            grid=(1,),
            in_specs=[whole((rows, HD))] * group,
            out_specs=[whole(shape) for shape in shapes],
        ),
        out_shape=[jax.ShapeDtypeStruct(shape, jnp.bfloat16) for shape in shapes],
        compiler_params=params(16),
        cost_estimate=SMALL,
        name="assemble",
    )(ctx_index, *pieces)


def plain(shape):
    return pl.BlockSpec(shape, lambda step: (0,) * len(shape))


def stacked(refs):
    values = [ref[...] for ref in refs]
    return values[0] if len(values) == 1 else jnp.concatenate(values, axis=0)


def project(wanted, mine, sibling, w_mine, w_sibling):
    parts = len(mine)
    depth = mine[0].shape[1]
    columns = w_mine.shape[1] // len(TURNS)
    turns = sorted({turn for output in wanted for turn, _, _ in output})

    def kernel(*refs):
        own_rows = stacked(refs[:parts])
        other_rows = stacked(refs[parts : 2 * parts])
        weights = refs[2 * parts : 2 * parts + 2 * len(turns)]
        outs = refs[2 * parts + 2 * len(turns) :]
        for out, output in zip(outs, wanted):
            place = 0
            for turn, lower, upper in output:
                at = turns.index(turn)
                total = jnp.dot(
                    own_rows[lower:upper, :], weights[at][...], preferred_element_type=jnp.float32
                )
                total += jnp.dot(
                    other_rows[lower:upper, :],
                    weights[len(turns) + at][...],
                    preferred_element_type=jnp.float32,
                )
                out[place : place + upper - lower, :] = total.astype(jnp.bfloat16)
                place += upper - lower

    def columns_of(turn):
        return pl.BlockSpec((depth, columns), lambda step: (0, turn))

    shapes = [(sum(upper - lower for _, lower, upper in output), columns) for output in wanted]
    return pl.pallas_call(
        kernel,
        grid=(1,),
        in_specs=[plain(part.shape) for part in (*mine, *sibling)]
        + [columns_of(turn) for turn in turns] * 2,
        out_specs=[plain(shape) for shape in shapes],
        out_shape=[jax.ShapeDtypeStruct(shape, jnp.bfloat16) for shape in shapes],
        compiler_params=params(24),
        cost_estimate=SMALL,
        name="project",
    )(*mine, *sibling, *([w_mine] * len(turns)), *([w_sibling] * len(turns)))


def finish(half, rows, terms, result):
    flat = [array for term in terms for array, _ in term]
    columns = flat[0].shape[1]

    def kernel(*refs):
        refs = list(refs)
        total = None
        for term in terms:
            values = [refs.pop(0)[first:, :].astype(jnp.float32) for _, first in term]
            value = values[0] if len(values) == 1 else jnp.concatenate(values, axis=0)
            total = value if total is None else total + value
        refs[-1][...] = total.astype(jnp.bfloat16)

    in_specs = [plain(array.shape) for array in flat]
    operands = list(flat)
    aliases = {}
    if result is not None:
        in_specs.append(pl.BlockSpec(memory_space=pl.ANY))
        operands.append(result)
        aliases = {len(flat): 0}
    return pl.pallas_call(
        kernel,
        grid=(1,),
        in_specs=in_specs,
        out_specs=pl.BlockSpec((rows, columns), lambda step: (half, 0)),
        out_shape=jax.ShapeDtypeStruct((2 * rows, columns), jnp.bfloat16),
        input_output_aliases=aliases,
        compiler_params=params(16),
        cost_estimate=SMALL,
        name="finish",
    )(*operands)


def swap(value, axis, distance):
    count = lax.axis_size(axis)
    return lax.ppermute(value, axis, [(source, source ^ distance) for source in range(count)])


def add(*terms):
    total = terms[0].astype(jnp.float32)
    for term in terms[1:]:
        total = total + term.astype(jnp.float32)
    return total.astype(jnp.bfloat16)


TURNS = (3, 1, 2, 0)


def tie(*values):
    return lax.optimization_barrier(values)


def exchange_local(queries, keys, values, doc_ids, w_out):
    shard_rows = queries.shape[0]
    group = queries.shape[1] // HD
    ctx_index = lax.axis_index("ctx").astype(jnp.int32).reshape(1)
    head_index = lax.axis_index("head").astype(jnp.int32)
    places = head_index ^ (2 * jnp.array(TURNS, jnp.int32))
    docs = doc_ids.reshape(shard_rows // HD, HD)
    near = range(1, group)

    w_sibling = swap(w_out, "head", 1)
    low_out = pack(ctx_index, 0, queries, keys, values, docs)
    low_out, later = tie(low_out, (queries, keys, values))
    low = [swap(low_out[distance - 1], "ctx", distance) for distance in near]
    high_out = pack(ctx_index, 1, *later, None)
    high = [swap(high_out[distance - 1], "ctx", distance) for distance in near[:-1]]
    w_packed = pack_projection(places, w_out, w_sibling)
    low, w_packed = tie(low, w_packed)

    def send_back(pieces):
        return [swap(pieces[distance], "ctx", distance) for distance in near]

    rows = shard_rows // 2
    cuts = (0, rows // 2, rows)

    def projected(mine, sibling, *wanted):
        return list(project(wanted, mine, sibling, *w_packed))

    def to_next(part, distance):
        return swap(part, "head", 2 * distance)

    pieces = attend(ctx_index, queries, keys, values, docs, low, None)
    pieces, diagonal_out = tie(pieces, high_out[-1])
    back = send_back(pieces)
    back, high = tie(back, high)
    high = [*high, swap(diagonal_out, "ctx", near[-1])]
    mine = assemble(ctx_index, [pieces[0], *back], (0, rows))
    sibling = [swap(part, "head", 1) for part in mine]
    shares = [projected(mine, sibling, [(turn, 0, rows)])[0] for turn in range(len(TURNS))]
    far = to_next(shares[0], 1)
    near_sum = to_next(shares[1], 1)
    passed = add(shares[2], far)

    high, shares, passed = tie(high, shares, passed)
    across = to_next(passed, 2)
    pieces = attend(ctx_index, queries, keys, values, docs, low, high)
    back = send_back(pieces)
    mine = assemble(ctx_index, [pieces[0], *back], cuts)
    sibling = [swap(part, "head", 1) for part in mine]
    halves = list(zip(cuts[:-1], cuts[1:]))
    late = projected(mine, sibling, *[[(0, *span)] for span in halves])
    late, near_sum, across = tie(late, near_sum, across)
    result = finish(0, rows, [[(shares[3], 0)], [(near_sum, 0)], [(across, 0)]], None)
    far = [to_next(part, 1) for part in late]
    late = projected(mine, sibling, *[[(2, *span)] for span in halves])
    passed = [add(*both) for both in zip(late, far)]
    across = [to_next(part, 2) for part in passed]
    third = rows * 11 // 32 // 16 * 16
    thirds = ((0, third), (third, 2 * third), (2 * third, rows))
    last = projected(mine, sibling, *[[(1, *span)] for span in thirds])
    last, passed = tie(last, passed)
    near_sum = [to_next(part, 1) for part in last]
    (kept,) = projected(mine, sibling, [(3, 0, rows)])
    terms = [[(kept, 0)], [(part, 0) for part in near_sum], [(part, 0) for part in across]]
    return finish(1, rows, terms, result)


def solution(mesh):
    in_specs = (P("ctx", "head"), P("ctx", "head"), P("ctx", "head"), P("ctx"), P("head", None))
    out_specs = P("ctx", "head")
    ctx_count = mesh.shape["ctx"]
    head_count = mesh.shape["head"]

    def local(queries, keys, values, doc_ids, w_out):
        heads = queries.shape[1] // HD
        exchange = heads == ctx_count and heads == 4 and head_count == 2 * len(TURNS)
        exchange = exchange and queries.shape[0] % (4 * TILE) == 0
        body = exchange_local if exchange else ring_local
        return body(queries, keys, values, doc_ids, w_out)

    return jax.shard_map(
        local, mesh=mesh, in_specs=in_specs, out_specs=out_specs, check_vma=False
    )
```

```python
import functools
import math

import jax
import jax.numpy as jnp
from jax import lax
from jax.experimental import pallas as pl
from jax.experimental.pallas import tpu as pltpu
from jax.sharding import PartitionSpec as P

HD = 128


MASKED_SCORE = -1e30
LOG2E = 1.4426950408889634


def passed_along(value, axis, steps):
    count = lax.axis_size(axis)
    pairs = [(source, (source + steps) % count) for source in range(count)]
    return lax.ppermute(value, axis, pairs)


def folded_positions(row_total, offset, shard_rows, devices_ctx):
    flat_index = offset + lax.iota(jnp.int32, row_total)
    owner_dev = flat_index // shard_rows
    within = flat_index % shard_rows
    half_rows = shard_rows // 2
    fold_block = jnp.where(within < half_rows, owner_dev, 2 * devices_ctx - 1 - owner_dev)
    return fold_block * half_rows + within % half_rows


def block_update(
    running, query, query_pos, query_doc, key_block, value_block, pos_block, doc_block
):
    largest, totals, summed = running
    query_rows = query.shape[0]
    local_heads = query.shape[1] // HD
    query_heads = query.reshape(query_rows, local_heads, HD)
    key_heads = key_block.reshape(key_block.shape[0], local_heads, HD)
    value_heads = value_block.reshape(value_block.shape[0], local_heads, HD)
    scores = jnp.einsum(
        "qhd,khd->hqk", query_heads, key_heads, preferred_element_type=jnp.float32
    ) * (1.0 / math.sqrt(HD))
    allowed = (query_doc[:, None] == doc_block[None, :]) & (
        pos_block[None, :] <= query_pos[:, None]
    )
    scores = jnp.where(allowed[None], scores, MASKED_SCORE)
    new_max = jnp.maximum(largest, jnp.max(scores, axis=2))
    weights = jnp.where(allowed[None], jnp.exp(scores - new_max[:, :, None]), 0.0)
    factor = jnp.exp(largest - new_max)
    totals = totals * factor + jnp.sum(weights, axis=2)
    product = jnp.einsum(
        "hqk,khd->qhd",
        weights.astype(jnp.bfloat16),
        value_heads,
        preferred_element_type=jnp.float32,
    )
    summed = summed * factor.T[:, :, None] + product
    return (new_max, totals, summed)


def attend_rows(running, query, query_pos, query_doc, key_rows, value_rows, key_pos, key_doc):
    row_total = key_rows.shape[0]
    block_rows = math.gcd(row_total, query.shape[0])
    block_count = row_total // block_rows
    highest = jnp.max(query_pos)

    def visit(partial_value, blocks):
        key_block, value_block, pos_block, doc_block = blocks
        masked_out = jnp.min(pos_block) > highest
        updated = lax.cond(
            masked_out,
            lambda frozen: frozen,
            lambda frozen: block_update(
                frozen, query, query_pos, query_doc, key_block, value_block, pos_block, doc_block
            ),
            partial_value,
        )
        return (updated, None)

    blocks = (
        key_rows.reshape(block_count, block_rows, key_rows.shape[1]),
        value_rows.reshape(block_count, block_rows, value_rows.shape[1]),
        key_pos.reshape(block_count, block_rows),
        key_doc.reshape(block_count, block_rows),
    )
    running, _ = lax.scan(visit, running, blocks)
    return running


def attend_shard(running, query, query_pos, query_doc, key_rows, value_rows, key_pos, key_doc):
    largest, totals, summed = running
    half_rows = query.shape[0] // 2
    new_largest = []
    new_totals = []
    new_summed = []
    for half_idx in range(2):
        lower = half_idx * half_rows
        part_state = (largest[half_idx], totals[half_idx], summed[half_idx])
        part_state = attend_rows(
            part_state,
            query[lower : lower + half_rows],
            query_pos[lower : lower + half_rows],
            query_doc[lower : lower + half_rows],
            key_rows,
            value_rows,
            key_pos,
            key_doc,
        )
        new_largest.append(part_state[0])
        new_totals.append(part_state[1])
        new_summed.append(part_state[2])
    return (jnp.stack(new_largest), jnp.stack(new_totals), jnp.stack(new_summed))


def ring_local(queries, keys, values, doc_ids, w_out):
    shard_rows = queries.shape[0]
    half_rows = shard_rows // 2
    local_heads = queries.shape[1] // HD
    devices_ctx = lax.axis_size("ctx")
    ctx_index = lax.axis_index("ctx")
    all_docs = lax.all_gather(doc_ids, "ctx", axis=0, tiled=True)
    own_pos = folded_positions(shard_rows, ctx_index * shard_rows, shard_rows, devices_ctx)
    running = (
        jnp.full((2, local_heads, half_rows), MASKED_SCORE, jnp.float32),
        jnp.zeros((2, local_heads, half_rows), jnp.float32),
        jnp.zeros((2, half_rows, local_heads, HD), jnp.float32),
    )
    travel = queries
    for hop_step in range(devices_ctx):
        anchor = (ctx_index - hop_step) % devices_ctx
        query_pos = folded_positions(shard_rows, anchor * shard_rows, shard_rows, devices_ctx)
        query_doc = lax.dynamic_slice_in_dim(all_docs, anchor * shard_rows, shard_rows, 0)
        largest, totals, summed = attend_shard(
            running, travel, query_pos, query_doc, keys, values, own_pos, doc_ids
        )
        running = (
            passed_along(largest.astype(jnp.bfloat16), "ctx", 1).astype(largest.dtype),
            passed_along(totals.astype(jnp.bfloat16), "ctx", 1).astype(totals.dtype),
            passed_along(summed.astype(jnp.bfloat16), "ctx", 1).astype(summed.dtype),
        )
        if hop_step + 1 < devices_ctx:
            travel = passed_along(travel, "ctx", 1)
    largest, totals, summed = running
    attended = summed / totals.transpose(0, 2, 1)[:, :, :, None]
    attended = attended.reshape(shard_rows, local_heads * HD).astype(jnp.bfloat16)
    partial_out = jnp.dot(attended, w_out, preferred_element_type=jnp.float32)
    return lax.psum_scatter(
        partial_out.astype(jnp.bfloat16), "head", scatter_dimension=1, tiled=True
    )


SMALL = pl.CostEstimate(flops=1024, bytes_accessed=1024, transcendentals=0)
TILE = 256
MOST_DOCS = 16


def params(mib):
    return pltpu.CompilerParams(vmem_limit_bytes=mib * 1024 * 1024)


def whole(shape):
    return pl.BlockSpec(shape, lambda step, scalars: (0,) * len(shape))


def pack(ctx_index, half, queries, keys, values, docs):
    rows = queries.shape[0] // 2
    group = queries.shape[1] // HD
    doc_rows = 0 if docs is None else 16 * pl.cdiv(docs.shape[0], 16)
    total = 3 * rows + doc_rows
    others = range(group - 1)

    def kernel(ctx_ref, query_ref, key_ref, value_ref, *refs):
        refs = list(refs)
        docs_ref = None if docs is None else refs.pop(0)
        outs = [refs.pop(0) for _ in others]
        taken, turned, taken_sem, direct_sem, turned_sem = refs
        taking = []
        direct = []
        for place in others:
            column = pl.multiple_of((ctx_ref[0] ^ (place + 1)) * HD, HD)
            piece = (pl.ds(half * rows, rows), pl.ds(column, HD))
            taking.append(
                pltpu.make_async_copy(value_ref.at[piece], taken.at[place], taken_sem.at[place])
            )
            taking[-1].start()
            for part, ref in enumerate((query_ref, key_ref)):
                target = outs[place].at[pl.ds(part * rows, rows), :]
                direct.append(
                    pltpu.make_async_copy(ref.at[piece], target, direct_sem.at[place, part])
                )
                direct[-1].start()
        if docs is not None:
            mine = docs_ref[...].astype(jnp.float32)
            empty = jnp.zeros((doc_rows - mine.shape[0], HD), jnp.float32)
            mine = jnp.concatenate([mine, empty], axis=0).astype(jnp.bfloat16)
        giving = []
        for place in others:
            taking[place].wait()
            for block in range(rows // HD):
                span = slice(block * HD, (block + 1) * HD)
                turned[place, span, :] = jnp.transpose(taken[place, span, :])
            if docs is not None:
                turned[place, rows:, :] = mine
            target = outs[place].at[pl.ds(2 * rows, rows + doc_rows), :]
            giving.append(
                pltpu.make_async_copy(turned.at[place], target, turned_sem.at[place])
            )
            giving[-1].start()
        for copy in (*direct, *giving):
            copy.wait()

    anywhere = pl.BlockSpec(memory_space=pl.ANY)
    return pl.pallas_call(
        kernel,
        grid_spec=pltpu.PrefetchScalarGridSpec(
            num_scalar_prefetch=1,
            grid=(1,),
            in_specs=[anywhere] * 3 + ([] if docs is None else [whole(docs.shape)]),
            out_specs=[anywhere] * (group - 1),
            scratch_shapes=[
                pltpu.VMEM((group - 1, rows, HD), jnp.bfloat16),
                pltpu.VMEM((group - 1, rows + doc_rows, HD), jnp.bfloat16),
                pltpu.SemaphoreType.DMA((group - 1,)),
                pltpu.SemaphoreType.DMA((group - 1, 2)),
                pltpu.SemaphoreType.DMA((group - 1,)),
            ],
        ),
        out_shape=[jax.ShapeDtypeStruct((total, HD), jnp.bfloat16)] * (group - 1),
        compiler_params=params(56),
        cost_estimate=SMALL,
        name="pack",
    )(ctx_index, queries, keys, values, *(() if docs is None else (docs,)))


def pack_projection(places, w_mine, w_sibling):
    depth, width = w_mine.shape
    turns = len(TURNS)
    columns = width // (2 * turns)

    def kernel(places_ref, mine_in, sibling_in, mine_out, sibling_out):
        mine_out[...] = mine_in[...]
        sibling_out[...] = sibling_in[...]

    in_spec = pl.BlockSpec((depth, columns), lambda turn, at: (0, at[turn]))
    out_spec = pl.BlockSpec((depth, columns), lambda turn, at: (0, turn))
    return pl.pallas_call(
        kernel,
        grid_spec=pltpu.PrefetchScalarGridSpec(
            num_scalar_prefetch=1,
            grid=(turns,),
            in_specs=[in_spec] * 2,
            out_specs=[out_spec] * 2,
        ),
        out_shape=[jax.ShapeDtypeStruct((depth, turns * columns), w_mine.dtype)] * 2,
        compiler_params=params(56),
        cost_estimate=SMALL,
        name="pack_projection",
    )(places, w_mine, w_sibling)


def attend(ctx_index, queries, keys, values, docs, low, high):
    rows = queries.shape[0] // 2
    group = queries.shape[1] // HD
    with_high = high is not None
    per_block = rows // TILE
    lines = rows // HD
    key_rows = (2 * group if with_high else group) * rows
    key_tiles = key_rows // TILE
    scaling = LOG2E / math.sqrt(HD)

    def kernel(ctx_ref, *refs):
        refs = list(refs)
        own_low = [refs.pop(0) for _ in range(3)]
        own_high = [refs.pop(0) for _ in range(3)] if with_high else None
        own_docs = refs.pop(0)
        low_refs = [refs.pop(0) for _ in range(group - 1)]
        high_refs = [refs.pop(0) for _ in range(group - 1)] if with_high else None
        outs = [refs.pop(0) for _ in range(group)]
        key_buf, value_buf, doc_buf = refs[:3]
        query_buf, start_buf, largest_buf, summed = (
            refs[3 + kind * group : 3 + (kind + 1) * group] for kind in range(4)
        )
        ctx = ctx_ref[0]

        def part(upper, distance, index, lower=0, count=rows):
            if distance == 0:
                return (own_high if upper else own_low)[index][lower : lower + count, :]
            source = (high_refs if upper else low_refs)[distance - 1]
            return source[index * rows + lower : index * rows + lower + count, :]

        place = {}
        doc_rows = {}
        for upper in (False, True) if with_high else (False,):
            for distance in range(group):
                source = ctx ^ distance
                block = 2 * group - 1 - source if upper else source
                place[upper, distance] = block
                offset = pl.multiple_of(block * rows, rows)
                key_buf[pl.ds(offset, rows), :] = part(upper, distance, 1)
                if distance == 0:
                    both = own_docs[...].astype(jnp.float32)
                else:
                    both = low_refs[distance - 1][3 * rows :, :].astype(jnp.float32)
                begin = lines if upper else 0
                mine = []
                for line in range(lines):
                    taken = part(upper, distance, 2, line * HD, HD)
                    if distance == 0:
                        taken = jnp.transpose(taken)
                    column = pl.multiple_of(block * rows + line * HD, HD)
                    value_buf[:HD, pl.ds(column, HD)] = taken
                    mine.append(both[begin + line : begin + line + 1, :])
                    doc_buf[pl.ds(block * lines + line, 1), :] = mine[-1]
                doc_rows[upper, distance] = jnp.concatenate(mine, axis=1)
        value_buf[HD:, :] = jnp.ones((value_buf.shape[0] - HD, key_rows), jnp.bfloat16)

        all_docs = doc_buf[...]
        starts = [jnp.zeros((1, rows), jnp.float32)] * group
        for number in range(1, MOST_DOCS):
            smaller = jnp.where(all_docs < number, 1.0, 0.0)
            count = jnp.sum(jnp.sum(smaller, axis=0, keepdims=True), axis=1, keepdims=True)
            for distance in range(group):
                reached = doc_rows[with_high, distance] >= number
                starts[distance] = jnp.where(reached, count, starts[distance])

        def scores_of(query, offset):
            raw = lax.dot_general(
                key_buf[pl.ds(offset, TILE), :],
                query,
                (((1,), (1,)), ((), ())),
                preferred_element_type=jnp.float32,
            )
            return raw * scaling

        def weighted(weights, offset):
            return jnp.dot(
                value_buf[:, pl.ds(offset, TILE)],
                weights.astype(jnp.bfloat16),
                preferred_element_type=jnp.float32,
            )

        key_row = lax.broadcasted_iota(jnp.int32, (TILE, TILE), 0)
        causal = key_row <= lax.broadcasted_iota(jnp.int32, (TILE, TILE), 1)
        key_row = key_row.astype(jnp.float32)
        firsts = []
        counts = []
        for lane in range(group):
            for slot in range(per_block):
                distance = lane ^ (slot * (group - 1))
                query = part(with_high, distance, 0, slot * TILE, TILE)
                query_buf[lane][slot] = query
                start = starts[distance][:, slot * TILE : (slot + 1) * TILE]
                start_buf[lane][slot, 0:1, :] = start
                end = place[with_high, distance] * per_block + slot
                offset = pl.multiple_of(end * TILE, TILE)
                least = start - offset.astype(jnp.float32)
                scores = scores_of(query, offset)
                scores = jnp.where((key_row >= least) & causal, scores, MASKED_SCORE)
                largest = jnp.max(scores, axis=0, keepdims=True)
                largest_buf[lane][slot, 0:1, :] = largest
                summed[lane][slot] = weighted(jnp.exp2(scores - largest), offset)
                first = start[0, 0].astype(jnp.int32) // TILE
                firsts.append(first)
                counts.append(end - first)

        longest = jnp.int32(0)
        for lane in range(group):
            of_lane = counts[lane * per_block : (lane + 1) * per_block]
            longest = jnp.maximum(longest, sum(of_lane))

        def visit(step, carry):
            slots = []
            offsets = []
            beyonds = []
            for lane in range(group):
                slot = jnp.int32(0)
                index = firsts[lane * per_block] + step
                before = counts[lane * per_block]
                for later in range(1, per_block):
                    reached = step >= before
                    slot = jnp.where(reached, later, slot)
                    place_later = lane * per_block + later
                    index = jnp.where(reached, firsts[place_later] + step - before, index)
                    before = before + counts[place_later]
                offset = pl.multiple_of(jnp.minimum(index, key_tiles - 1) * TILE, TILE)
                slots.append(slot)
                offsets.append(offset)
                beyonds.append(jnp.where(step < before, -offset.astype(jnp.float32), 1e9))
            each = range(group)
            scores = [scores_of(query_buf[lane][slots[lane]], offsets[lane]) for lane in each]
            old_max = [largest_buf[lane][slots[lane], 0:1, :] for lane in each]
            new_max = []
            for lane in each:
                least = start_buf[lane][slots[lane], 0:1, :] + beyonds[lane]
                scores[lane] = jnp.where(key_row >= least, scores[lane], MASKED_SCORE)
                tile_max = jnp.max(scores[lane], axis=0, keepdims=True)
                new_max.append(jnp.maximum(old_max[lane], tile_max))
            products = [
                weighted(jnp.exp2(scores[lane] - new_max[lane]), offsets[lane]) for lane in each
            ]
            for lane in each:
                factor = jnp.exp2(old_max[lane] - new_max[lane])
                summed[lane][slots[lane]] = summed[lane][slots[lane]] * factor + products[lane]
                largest_buf[lane][slots[lane], 0:1, :] = new_max[lane]
            return carry

        lax.fori_loop(0, longest, visit, jnp.int32(0))
        for lane in range(group):
            for slot in range(per_block):
                state = summed[lane]
                attended = state[slot, :HD, :] * (1.0 / state[slot, HD : HD + 1, :])
                out = outs[lane ^ (slot * (group - 1))]
                out[slot * TILE : (slot + 1) * TILE, :] = jnp.transpose(
                    attended.astype(jnp.bfloat16)
                )

    def own(upper):
        return pl.BlockSpec((rows, HD), lambda step, ctx: (int(upper), ctx[0]))

    in_specs = [own(False)] * 3
    operands = [queries, keys, values]
    if with_high:
        in_specs += [own(True)] * 3
        operands += [queries, keys, values]
    received = [docs, *low, *(high if with_high else ())]
    operands += received
    in_specs += [whole(array.shape) for array in received]
    return pl.pallas_call(
        kernel,
        grid_spec=pltpu.PrefetchScalarGridSpec(
            num_scalar_prefetch=1,
            grid=(1,),
            in_specs=in_specs,
            out_specs=[whole((rows, HD))] * group,
            scratch_shapes=[
                pltpu.VMEM((key_rows, HD), jnp.bfloat16),
                pltpu.VMEM((HD + 16, key_rows), jnp.bfloat16),
                pltpu.VMEM((key_rows // HD, HD), jnp.float32),
                *[pltpu.VMEM((per_block, TILE, HD), jnp.bfloat16)] * group,
                *[pltpu.VMEM((per_block, 8, TILE), jnp.float32)] * (2 * group),
                *[pltpu.VMEM((per_block, HD + 16, TILE), jnp.float32)] * group,
            ],
        ),
        out_shape=[jax.ShapeDtypeStruct((rows, HD), jnp.bfloat16)] * group,
        compiler_params=params(40),
        cost_estimate=SMALL,
        name="attend_high" if with_high else "attend_low",
    )(ctx_index, *operands)


def assemble(ctx_index, pieces, cuts):
    rows = pieces[0].shape[0]
    group = len(pieces)
    spans = list(zip(cuts[:-1], cuts[1:]))

    def kernel(ctx_ref, *refs):
        for part, (lower, upper) in enumerate(spans):
            for distance in range(group):
                column = pl.multiple_of((ctx_ref[0] ^ distance) * HD, HD)
                refs[group + part][:, pl.ds(column, HD)] = refs[distance][lower:upper, :]

    shapes = [(upper - lower, group * HD) for lower, upper in spans]
    return pl.pallas_call(
        kernel,
        grid_spec=pltpu.PrefetchScalarGridSpec(
            num_scalar_prefetch=1,
            grid=(1,),
            in_specs=[whole((rows, HD))] * group,
            out_specs=[whole(shape) for shape in shapes],
        ),
        out_shape=[jax.ShapeDtypeStruct(shape, jnp.bfloat16) for shape in shapes],
        compiler_params=params(16),
        cost_estimate=SMALL,
        name="assemble",
    )(ctx_index, *pieces)


def plain(shape):
    return pl.BlockSpec(shape, lambda step: (0,) * len(shape))


def stacked(refs):
    values = [ref[...] for ref in refs]
    return values[0] if len(values) == 1 else jnp.concatenate(values, axis=0)


def project(wanted, mine, sibling, w_mine, w_sibling):
    parts = len(mine)
    depth = mine[0].shape[1]
    columns = w_mine.shape[1] // len(TURNS)
    turns = sorted({turn for output in wanted for turn, _, _ in output})

    def kernel(*refs):
        own_rows = stacked(refs[:parts])
        other_rows = stacked(refs[parts : 2 * parts])
        weights = refs[2 * parts : 2 * parts + 2 * len(turns)]
        outs = refs[2 * parts + 2 * len(turns) :]
        for out, output in zip(outs, wanted):
            place = 0
            for turn, lower, upper in output:
                at = turns.index(turn)
                total = jnp.dot(
                    own_rows[lower:upper, :], weights[at][...], preferred_element_type=jnp.float32
                )
                total += jnp.dot(
                    other_rows[lower:upper, :],
                    weights[len(turns) + at][...],
                    preferred_element_type=jnp.float32,
                )
                out[place : place + upper - lower, :] = total.astype(jnp.bfloat16)
                place += upper - lower

    def columns_of(turn):
        return pl.BlockSpec((depth, columns), lambda step: (0, turn))

    shapes = [(sum(upper - lower for _, lower, upper in output), columns) for output in wanted]
    return pl.pallas_call(
        kernel,
        grid=(1,),
        in_specs=[plain(part.shape) for part in (*mine, *sibling)]
        + [columns_of(turn) for turn in turns] * 2,
        out_specs=[plain(shape) for shape in shapes],
        out_shape=[jax.ShapeDtypeStruct(shape, jnp.bfloat16) for shape in shapes],
        compiler_params=params(24),
        cost_estimate=SMALL,
        name="project",
    )(*mine, *sibling, *([w_mine] * len(turns)), *([w_sibling] * len(turns)))


def finish(half, rows, terms, result):
    flat = [array for term in terms for array, _ in term]
    columns = flat[0].shape[1]

    def kernel(*refs):
        refs = list(refs)
        total = None
        for term in terms:
            values = [refs.pop(0)[first:, :].astype(jnp.float32) for _, first in term]
            value = values[0] if len(values) == 1 else jnp.concatenate(values, axis=0)
            total = value if total is None else total + value
        refs[-1][...] = total.astype(jnp.bfloat16)

    in_specs = [plain(array.shape) for array in flat]
    operands = list(flat)
    aliases = {}
    if result is not None:
        in_specs.append(pl.BlockSpec(memory_space=pl.ANY))
        operands.append(result)
        aliases = {len(flat): 0}
    return pl.pallas_call(
        kernel,
        grid=(1,),
        in_specs=in_specs,
        out_specs=pl.BlockSpec((rows, columns), lambda step: (half, 0)),
        out_shape=jax.ShapeDtypeStruct((2 * rows, columns), jnp.bfloat16),
        input_output_aliases=aliases,
        compiler_params=params(16),
        cost_estimate=SMALL,
        name="finish",
    )(*operands)


def swap(value, axis, distance):
    count = lax.axis_size(axis)
    return lax.ppermute(value, axis, [(source, source ^ distance) for source in range(count)])


def add(*terms):
    total = terms[0].astype(jnp.float32)
    for term in terms[1:]:
        total = total + term.astype(jnp.float32)
    return total.astype(jnp.bfloat16)


TURNS = (3, 1, 2, 0)


def tie(*values):
    return lax.optimization_barrier(values)


def exchange_local(queries, keys, values, doc_ids, w_out):
    shard_rows = queries.shape[0]
    group = queries.shape[1] // HD
    ctx_index = lax.axis_index("ctx").astype(jnp.int32).reshape(1)
    head_index = lax.axis_index("head").astype(jnp.int32)
    places = head_index ^ (2 * jnp.array(TURNS, jnp.int32))
    docs = doc_ids.reshape(shard_rows // HD, HD)
    near = range(1, group)

    w_sibling = swap(w_out, "head", 1)
    low_out = pack(ctx_index, 0, queries, keys, values, docs)
    low_out, later = tie(low_out, (queries, keys, values))
    low = [swap(low_out[distance - 1], "ctx", distance) for distance in near]
    high_out = pack(ctx_index, 1, *later, None)
    high = [swap(high_out[distance - 1], "ctx", distance) for distance in near[:-1]]
    w_packed = pack_projection(places, w_out, w_sibling)
    low, w_packed = tie(low, w_packed)

    def send_back(pieces):
        return [swap(pieces[distance], "ctx", distance) for distance in near]

    rows = shard_rows // 2
    cuts = (0, rows // 2, rows)

    def projected(mine, sibling, *wanted):
        return list(project(wanted, mine, sibling, *w_packed))

    def to_next(part, distance):
        return swap(part, "head", 2 * distance)

    pieces = attend(ctx_index, queries, keys, values, docs, low, None)
    pieces, diagonal_out = tie(pieces, high_out[-1])
    back = send_back(pieces)
    back, high = tie(back, high)
    high = [*high, swap(diagonal_out, "ctx", near[-1])]
    mine = assemble(ctx_index, [pieces[0], *back], (0, rows))
    sibling = [swap(part, "head", 1) for part in mine]
    shares = [projected(mine, sibling, [(turn, 0, rows)])[0] for turn in range(len(TURNS))]
    far = to_next(shares[0], 1)
    near_sum = to_next(shares[1], 1)
    passed = add(shares[2], far)

    high, shares, passed = tie(high, shares, passed)
    across = to_next(passed, 2)
    pieces = attend(ctx_index, queries, keys, values, docs, low, high)
    back = send_back(pieces)
    mine = assemble(ctx_index, [pieces[0], *back], cuts)
    sibling = [swap(part, "head", 1) for part in mine]
    late = [projected(mine, sibling, [(turn, 0, rows)])[0] for turn in (0, 2, 3)]
    late[0], near_sum, across = tie(late[0], near_sum, across)
    result = finish(0, rows, [[(shares[3], 0)], [(near_sum, 0)], [(across, 0)]], None)
    far = to_next(late[0], 1)
    passed = add(late[1], far)
    across = to_next(passed, 2)
    last = projected(mine, sibling, *[[(1, *span)] for span in zip(cuts[:-1], cuts[1:])])
    last, passed = tie(last, passed)
    near_sum = [to_next(part, 1) for part in last]
    terms = [[(late[2], 0)], [(part, 0) for part in near_sum], [(across, 0)]]
    return finish(1, rows, terms, result)


def solution(mesh):
    in_specs = (P("ctx", "head"), P("ctx", "head"), P("ctx", "head"), P("ctx"), P("head", None))
    out_specs = P("ctx", "head")
    ctx_count = mesh.shape["ctx"]
    head_count = mesh.shape["head"]

    def local(queries, keys, values, doc_ids, w_out):
        heads = queries.shape[1] // HD
        exchange = heads == ctx_count and heads == 4 and head_count == 2 * len(TURNS)
        exchange = exchange and queries.shape[0] % (4 * TILE) == 0
        body = exchange_local if exchange else ring_local
        return body(queries, keys, values, doc_ids, w_out)

    return jax.shard_map(
        local, mesh=mesh, in_specs=in_specs, out_specs=out_specs, check_vma=False
    )
```

```python
import functools
import math

import jax
import jax.numpy as jnp
from jax import lax
from jax.experimental import pallas as pl
from jax.experimental.pallas import tpu as pltpu
from jax.sharding import PartitionSpec as P

HD = 128


MASKED_SCORE = -1e30
LOG2E = 1.4426950408889634


def passed_along(value, axis, steps):
    count = lax.axis_size(axis)
    pairs = [(source, (source + steps) % count) for source in range(count)]
    return lax.ppermute(value, axis, pairs)


def folded_positions(row_total, offset, shard_rows, devices_ctx):
    flat_index = offset + lax.iota(jnp.int32, row_total)
    owner_dev = flat_index // shard_rows
    within = flat_index % shard_rows
    half_rows = shard_rows // 2
    fold_block = jnp.where(within < half_rows, owner_dev, 2 * devices_ctx - 1 - owner_dev)
    return fold_block * half_rows + within % half_rows


def block_update(
    running, query, query_pos, query_doc, key_block, value_block, pos_block, doc_block
):
    largest, totals, summed = running
    query_rows = query.shape[0]
    local_heads = query.shape[1] // HD
    query_heads = query.reshape(query_rows, local_heads, HD)
    key_heads = key_block.reshape(key_block.shape[0], local_heads, HD)
    value_heads = value_block.reshape(value_block.shape[0], local_heads, HD)
    scores = jnp.einsum(
        "qhd,khd->hqk", query_heads, key_heads, preferred_element_type=jnp.float32
    ) * (1.0 / math.sqrt(HD))
    allowed = (query_doc[:, None] == doc_block[None, :]) & (
        pos_block[None, :] <= query_pos[:, None]
    )
    scores = jnp.where(allowed[None], scores, MASKED_SCORE)
    new_max = jnp.maximum(largest, jnp.max(scores, axis=2))
    weights = jnp.where(allowed[None], jnp.exp(scores - new_max[:, :, None]), 0.0)
    factor = jnp.exp(largest - new_max)
    totals = totals * factor + jnp.sum(weights, axis=2)
    product = jnp.einsum(
        "hqk,khd->qhd",
        weights.astype(jnp.bfloat16),
        value_heads,
        preferred_element_type=jnp.float32,
    )
    summed = summed * factor.T[:, :, None] + product
    return (new_max, totals, summed)


def attend_rows(running, query, query_pos, query_doc, key_rows, value_rows, key_pos, key_doc):
    row_total = key_rows.shape[0]
    block_rows = math.gcd(row_total, query.shape[0])
    block_count = row_total // block_rows
    highest = jnp.max(query_pos)

    def visit(partial_value, blocks):
        key_block, value_block, pos_block, doc_block = blocks
        masked_out = jnp.min(pos_block) > highest
        updated = lax.cond(
            masked_out,
            lambda frozen: frozen,
            lambda frozen: block_update(
                frozen, query, query_pos, query_doc, key_block, value_block, pos_block, doc_block
            ),
            partial_value,
        )
        return (updated, None)

    blocks = (
        key_rows.reshape(block_count, block_rows, key_rows.shape[1]),
        value_rows.reshape(block_count, block_rows, value_rows.shape[1]),
        key_pos.reshape(block_count, block_rows),
        key_doc.reshape(block_count, block_rows),
    )
    running, _ = lax.scan(visit, running, blocks)
    return running


def attend_shard(running, query, query_pos, query_doc, key_rows, value_rows, key_pos, key_doc):
    largest, totals, summed = running
    half_rows = query.shape[0] // 2
    new_largest = []
    new_totals = []
    new_summed = []
    for half_idx in range(2):
        lower = half_idx * half_rows
        part_state = (largest[half_idx], totals[half_idx], summed[half_idx])
        part_state = attend_rows(
            part_state,
            query[lower : lower + half_rows],
            query_pos[lower : lower + half_rows],
            query_doc[lower : lower + half_rows],
            key_rows,
            value_rows,
            key_pos,
            key_doc,
        )
        new_largest.append(part_state[0])
        new_totals.append(part_state[1])
        new_summed.append(part_state[2])
    return (jnp.stack(new_largest), jnp.stack(new_totals), jnp.stack(new_summed))


def ring_local(queries, keys, values, doc_ids, w_out):
    shard_rows = queries.shape[0]
    half_rows = shard_rows // 2
    local_heads = queries.shape[1] // HD
    devices_ctx = lax.axis_size("ctx")
    ctx_index = lax.axis_index("ctx")
    all_docs = lax.all_gather(doc_ids, "ctx", axis=0, tiled=True)
    own_pos = folded_positions(shard_rows, ctx_index * shard_rows, shard_rows, devices_ctx)
    running = (
        jnp.full((2, local_heads, half_rows), MASKED_SCORE, jnp.float32),
        jnp.zeros((2, local_heads, half_rows), jnp.float32),
        jnp.zeros((2, half_rows, local_heads, HD), jnp.float32),
    )
    travel = queries
    for hop_step in range(devices_ctx):
        anchor = (ctx_index - hop_step) % devices_ctx
        query_pos = folded_positions(shard_rows, anchor * shard_rows, shard_rows, devices_ctx)
        query_doc = lax.dynamic_slice_in_dim(all_docs, anchor * shard_rows, shard_rows, 0)
        largest, totals, summed = attend_shard(
            running, travel, query_pos, query_doc, keys, values, own_pos, doc_ids
        )
        running = (
            passed_along(largest.astype(jnp.bfloat16), "ctx", 1).astype(largest.dtype),
            passed_along(totals.astype(jnp.bfloat16), "ctx", 1).astype(totals.dtype),
            passed_along(summed.astype(jnp.bfloat16), "ctx", 1).astype(summed.dtype),
        )
        if hop_step + 1 < devices_ctx:
            travel = passed_along(travel, "ctx", 1)
    largest, totals, summed = running
    attended = summed / totals.transpose(0, 2, 1)[:, :, :, None]
    attended = attended.reshape(shard_rows, local_heads * HD).astype(jnp.bfloat16)
    partial_out = jnp.dot(attended, w_out, preferred_element_type=jnp.float32)
    return lax.psum_scatter(
        partial_out.astype(jnp.bfloat16), "head", scatter_dimension=1, tiled=True
    )


SMALL = pl.CostEstimate(flops=1024, bytes_accessed=1024, transcendentals=0)
TILE = 256
MOST_DOCS = 16


def params(mib):
    return pltpu.CompilerParams(vmem_limit_bytes=mib * 1024 * 1024)


def whole(shape):
    return pl.BlockSpec(shape, lambda step, scalars: (0,) * len(shape))


def pack(ctx_index, half, queries, keys, values, docs):
    rows = queries.shape[0] // 2
    group = queries.shape[1] // HD
    doc_rows = 0 if docs is None else 16 * pl.cdiv(docs.shape[0], 16)
    total = 3 * rows + doc_rows
    others = range(group - 1)

    def kernel(ctx_ref, query_ref, key_ref, value_ref, *refs):
        refs = list(refs)
        docs_ref = None if docs is None else refs.pop(0)
        outs = [refs.pop(0) for _ in others]
        taken, staged, taken_sem, staged_sem, out_sem = refs
        taking = []
        for place in others:
            column = pl.multiple_of((ctx_ref[0] ^ (place + 1)) * HD, HD)
            piece = (pl.ds(half * rows, rows), pl.ds(column, HD))
            copies = [
                pltpu.make_async_copy(value_ref.at[piece], taken.at[place], taken_sem.at[place])
            ]
            for part, ref in enumerate((query_ref, key_ref)):
                target = staged.at[place, pl.ds(part * rows, rows), :]
                copies.append(
                    pltpu.make_async_copy(ref.at[piece], target, staged_sem.at[place, part])
                )
            for copy in copies:
                copy.start()
            taking.append(copies)
        if docs is not None:
            mine = docs_ref[...].astype(jnp.float32)
            empty = jnp.zeros((doc_rows - mine.shape[0], HD), jnp.float32)
            mine = jnp.concatenate([mine, empty], axis=0).astype(jnp.bfloat16)
            for place in others:
                staged[place, 3 * rows :, :] = mine
        giving = []
        for place in others:
            taking[place][0].wait()
            for block in range(rows // HD):
                lower = 2 * rows + block * HD
                staged[place, lower : lower + HD, :] = jnp.transpose(
                    taken[place, block * HD : (block + 1) * HD, :]
                )
            for copy in taking[place][1:]:
                copy.wait()
            giving.append(
                pltpu.make_async_copy(staged.at[place], outs[place], out_sem.at[place])
            )
            giving[-1].start()
        for copy in giving:
            copy.wait()

    anywhere = pl.BlockSpec(memory_space=pl.ANY)
    return pl.pallas_call(
        kernel,
        grid_spec=pltpu.PrefetchScalarGridSpec(
            num_scalar_prefetch=1,
            grid=(1,),
            in_specs=[anywhere] * 3 + ([] if docs is None else [whole(docs.shape)]),
            out_specs=[anywhere] * (group - 1),
            scratch_shapes=[
                pltpu.VMEM((group - 1, rows, HD), jnp.bfloat16),
                pltpu.VMEM((group - 1, total, HD), jnp.bfloat16),
                pltpu.SemaphoreType.DMA((group - 1,)),
                pltpu.SemaphoreType.DMA((group - 1, 2)),
                pltpu.SemaphoreType.DMA((group - 1,)),
            ],
        ),
        out_shape=[jax.ShapeDtypeStruct((total, HD), jnp.bfloat16)] * (group - 1),
        compiler_params=params(56),
        cost_estimate=SMALL,
        name="pack",
    )(ctx_index, queries, keys, values, *(() if docs is None else (docs,)))


def pack_projection(places, w_mine, w_sibling):
    depth, width = w_mine.shape
    turns = len(TURNS)
    columns = width // (2 * turns)

    def kernel(places_ref, mine_in, sibling_in, mine_out, sibling_out):
        mine_out[...] = mine_in[...]
        sibling_out[...] = sibling_in[...]

    in_spec = pl.BlockSpec((depth, columns), lambda turn, at: (0, at[turn]))
    out_spec = pl.BlockSpec((depth, columns), lambda turn, at: (0, turn))
    return pl.pallas_call(
        kernel,
        grid_spec=pltpu.PrefetchScalarGridSpec(
            num_scalar_prefetch=1,
            grid=(turns,),
            in_specs=[in_spec] * 2,
            out_specs=[out_spec] * 2,
        ),
        out_shape=[jax.ShapeDtypeStruct((depth, turns * columns), w_mine.dtype)] * 2,
        compiler_params=params(56),
        cost_estimate=SMALL,
        name="pack_projection",
    )(places, w_mine, w_sibling)


def attend(ctx_index, queries, keys, values, docs, low, high):
    rows = queries.shape[0] // 2
    group = queries.shape[1] // HD
    with_high = high is not None
    per_block = rows // TILE
    lines = rows // HD
    key_rows = (2 * group if with_high else group) * rows
    key_tiles = key_rows // TILE
    scaling = LOG2E / math.sqrt(HD)

    def kernel(ctx_ref, *refs):
        refs = list(refs)
        own_low = [refs.pop(0) for _ in range(3)]
        own_high = [refs.pop(0) for _ in range(3)] if with_high else None
        own_docs = refs.pop(0)
        low_refs = [refs.pop(0) for _ in range(group - 1)]
        high_refs = [refs.pop(0) for _ in range(group - 1)] if with_high else None
        outs = [refs.pop(0) for _ in range(group)]
        key_buf, value_buf, doc_buf = refs[:3]
        query_buf, start_buf, largest_buf, summed = (
            refs[3 + kind * group : 3 + (kind + 1) * group] for kind in range(4)
        )
        ctx = ctx_ref[0]

        def part(upper, distance, index, lower=0, count=rows):
            if distance == 0:
                return (own_high if upper else own_low)[index][lower : lower + count, :]
            source = (high_refs if upper else low_refs)[distance - 1]
            return source[index * rows + lower : index * rows + lower + count, :]

        place = {}
        doc_rows = {}
        for upper in (False, True) if with_high else (False,):
            for distance in range(group):
                source = ctx ^ distance
                block = 2 * group - 1 - source if upper else source
                place[upper, distance] = block
                offset = pl.multiple_of(block * rows, rows)
                key_buf[pl.ds(offset, rows), :] = part(upper, distance, 1)
                if distance == 0:
                    both = own_docs[...].astype(jnp.float32)
                else:
                    both = low_refs[distance - 1][3 * rows :, :].astype(jnp.float32)
                begin = lines if upper else 0
                mine = []
                for line in range(lines):
                    taken = part(upper, distance, 2, line * HD, HD)
                    if distance == 0:
                        taken = jnp.transpose(taken)
                    column = pl.multiple_of(block * rows + line * HD, HD)
                    value_buf[:HD, pl.ds(column, HD)] = taken
                    mine.append(both[begin + line : begin + line + 1, :])
                    doc_buf[pl.ds(block * lines + line, 1), :] = mine[-1]
                doc_rows[upper, distance] = jnp.concatenate(mine, axis=1)
        value_buf[HD:, :] = jnp.ones((value_buf.shape[0] - HD, key_rows), jnp.bfloat16)

        all_docs = doc_buf[...]
        starts = [jnp.zeros((1, rows), jnp.float32)] * group
        for number in range(1, MOST_DOCS):
            smaller = jnp.where(all_docs < number, 1.0, 0.0)
            count = jnp.sum(jnp.sum(smaller, axis=0, keepdims=True), axis=1, keepdims=True)
            for distance in range(group):
                reached = doc_rows[with_high, distance] >= number
                starts[distance] = jnp.where(reached, count, starts[distance])

        def scores_of(query, offset):
            raw = lax.dot_general(
                key_buf[pl.ds(offset, TILE), :],
                query,
                (((1,), (1,)), ((), ())),
                preferred_element_type=jnp.float32,
            )
            return raw * scaling

        def weighted(weights, offset):
            return jnp.dot(
                value_buf[:, pl.ds(offset, TILE)],
                weights.astype(jnp.bfloat16),
                preferred_element_type=jnp.float32,
            )

        key_row = lax.broadcasted_iota(jnp.int32, (TILE, TILE), 0)
        causal = key_row <= lax.broadcasted_iota(jnp.int32, (TILE, TILE), 1)
        key_row = key_row.astype(jnp.float32)
        firsts = []
        counts = []
        for lane in range(group):
            for slot in range(per_block):
                distance = lane ^ (slot * (group - 1))
                query = part(with_high, distance, 0, slot * TILE, TILE)
                query_buf[lane][slot] = query
                start = starts[distance][:, slot * TILE : (slot + 1) * TILE]
                start_buf[lane][slot, 0:1, :] = start
                end = place[with_high, distance] * per_block + slot
                offset = pl.multiple_of(end * TILE, TILE)
                least = start - offset.astype(jnp.float32)
                scores = scores_of(query, offset)
                scores = jnp.where((key_row >= least) & causal, scores, MASKED_SCORE)
                largest = jnp.max(scores, axis=0, keepdims=True)
                largest_buf[lane][slot, 0:1, :] = largest
                summed[lane][slot] = weighted(jnp.exp2(scores - largest), offset)
                first = start[0, 0].astype(jnp.int32) // TILE
                firsts.append(first)
                counts.append(end - first)

        longest = jnp.int32(0)
        for lane in range(group):
            of_lane = counts[lane * per_block : (lane + 1) * per_block]
            longest = jnp.maximum(longest, sum(of_lane))

        def visit(step, carry):
            slots = []
            offsets = []
            beyonds = []
            for lane in range(group):
                slot = jnp.int32(0)
                index = firsts[lane * per_block] + step
                before = counts[lane * per_block]
                for later in range(1, per_block):
                    reached = step >= before
                    slot = jnp.where(reached, later, slot)
                    place_later = lane * per_block + later
                    index = jnp.where(reached, firsts[place_later] + step - before, index)
                    before = before + counts[place_later]
                offset = pl.multiple_of(jnp.minimum(index, key_tiles - 1) * TILE, TILE)
                slots.append(slot)
                offsets.append(offset)
                beyonds.append(jnp.where(step < before, -offset.astype(jnp.float32), 1e9))
            each = range(group)
            scores = [scores_of(query_buf[lane][slots[lane]], offsets[lane]) for lane in each]
            old_max = [largest_buf[lane][slots[lane], 0:1, :] for lane in each]
            new_max = []
            for lane in each:
                least = start_buf[lane][slots[lane], 0:1, :] + beyonds[lane]
                scores[lane] = jnp.where(key_row >= least, scores[lane], MASKED_SCORE)
                tile_max = jnp.max(scores[lane], axis=0, keepdims=True)
                new_max.append(jnp.maximum(old_max[lane], tile_max))
            products = [
                weighted(jnp.exp2(scores[lane] - new_max[lane]), offsets[lane]) for lane in each
            ]
            for lane in each:
                factor = jnp.exp2(old_max[lane] - new_max[lane])
                summed[lane][slots[lane]] = summed[lane][slots[lane]] * factor + products[lane]
                largest_buf[lane][slots[lane], 0:1, :] = new_max[lane]
            return carry

        lax.fori_loop(0, longest, visit, jnp.int32(0))
        for lane in range(group):
            for slot in range(per_block):
                state = summed[lane]
                attended = state[slot, :HD, :] * (1.0 / state[slot, HD : HD + 1, :])
                out = outs[lane ^ (slot * (group - 1))]
                out[slot * TILE : (slot + 1) * TILE, :] = jnp.transpose(
                    attended.astype(jnp.bfloat16)
                )

    def own(upper):
        return pl.BlockSpec((rows, HD), lambda step, ctx: (int(upper), ctx[0]))

    in_specs = [own(False)] * 3
    operands = [queries, keys, values]
    if with_high:
        in_specs += [own(True)] * 3
        operands += [queries, keys, values]
    received = [docs, *low, *(high if with_high else ())]
    operands += received
    in_specs += [whole(array.shape) for array in received]
    return pl.pallas_call(
        kernel,
        grid_spec=pltpu.PrefetchScalarGridSpec(
            num_scalar_prefetch=1,
            grid=(1,),
            in_specs=in_specs,
            out_specs=[whole((rows, HD))] * group,
            scratch_shapes=[
                pltpu.VMEM((key_rows, HD), jnp.bfloat16),
                pltpu.VMEM((HD + 16, key_rows), jnp.bfloat16),
                pltpu.VMEM((key_rows // HD, HD), jnp.float32),
                *[pltpu.VMEM((per_block, TILE, HD), jnp.bfloat16)] * group,
                *[pltpu.VMEM((per_block, 8, TILE), jnp.float32)] * (2 * group),
                *[pltpu.VMEM((per_block, HD + 16, TILE), jnp.float32)] * group,
            ],
        ),
        out_shape=[jax.ShapeDtypeStruct((rows, HD), jnp.bfloat16)] * group,
        compiler_params=params(40),
        cost_estimate=SMALL,
        name="attend_high" if with_high else "attend_low",
    )(ctx_index, *operands)


def assemble(ctx_index, pieces, cuts):
    rows = pieces[0].shape[0]
    group = len(pieces)
    spans = list(zip(cuts[:-1], cuts[1:]))

    def kernel(ctx_ref, *refs):
        for part, (lower, upper) in enumerate(spans):
            for distance in range(group):
                column = pl.multiple_of((ctx_ref[0] ^ distance) * HD, HD)
                refs[group + part][:, pl.ds(column, HD)] = refs[distance][lower:upper, :]

    shapes = [(upper - lower, group * HD) for lower, upper in spans]
    return pl.pallas_call(
        kernel,
        grid_spec=pltpu.PrefetchScalarGridSpec(
            num_scalar_prefetch=1,
            grid=(1,),
            in_specs=[whole((rows, HD))] * group,
            out_specs=[whole(shape) for shape in shapes],
        ),
        out_shape=[jax.ShapeDtypeStruct(shape, jnp.bfloat16) for shape in shapes],
        compiler_params=params(16),
        cost_estimate=SMALL,
        name="assemble",
    )(ctx_index, *pieces)


def plain(shape):
    return pl.BlockSpec(shape, lambda step: (0,) * len(shape))


def stacked(refs):
    values = [ref[...] for ref in refs]
    return values[0] if len(values) == 1 else jnp.concatenate(values, axis=0)


def project(wanted, mine, sibling, w_mine, w_sibling):
    parts = len(mine)
    depth = mine[0].shape[1]
    columns = w_mine.shape[1] // len(TURNS)
    turns = sorted({turn for output in wanted for turn, _, _ in output})

    def kernel(*refs):
        own_rows = stacked(refs[:parts])
        other_rows = stacked(refs[parts : 2 * parts])
        weights = refs[2 * parts : 2 * parts + 2 * len(turns)]
        outs = refs[2 * parts + 2 * len(turns) :]
        for out, output in zip(outs, wanted):
            place = 0
            for turn, lower, upper in output:
                at = turns.index(turn)
                total = jnp.dot(
                    own_rows[lower:upper, :], weights[at][...], preferred_element_type=jnp.float32
                )
                total += jnp.dot(
                    other_rows[lower:upper, :],
                    weights[len(turns) + at][...],
                    preferred_element_type=jnp.float32,
                )
                out[place : place + upper - lower, :] = total.astype(jnp.bfloat16)
                place += upper - lower

    def columns_of(turn):
        return pl.BlockSpec((depth, columns), lambda step: (0, turn))

    shapes = [(sum(upper - lower for _, lower, upper in output), columns) for output in wanted]
    return pl.pallas_call(
        kernel,
        grid=(1,),
        in_specs=[plain(part.shape) for part in (*mine, *sibling)]
        + [columns_of(turn) for turn in turns] * 2,
        out_specs=[plain(shape) for shape in shapes],
        out_shape=[jax.ShapeDtypeStruct(shape, jnp.bfloat16) for shape in shapes],
        compiler_params=params(24),
        cost_estimate=SMALL,
        name="project",
    )(*mine, *sibling, *([w_mine] * len(turns)), *([w_sibling] * len(turns)))


def finish(half, rows, terms, result):
    flat = [array for term in terms for array, _ in term]
    columns = flat[0].shape[1]

    def kernel(*refs):
        refs = list(refs)
        total = None
        for term in terms:
            values = [refs.pop(0)[first:, :].astype(jnp.float32) for _, first in term]
            value = values[0] if len(values) == 1 else jnp.concatenate(values, axis=0)
            total = value if total is None else total + value
        refs[-1][...] = total.astype(jnp.bfloat16)

    in_specs = [plain(array.shape) for array in flat]
    operands = list(flat)
    aliases = {}
    if result is not None:
        in_specs.append(pl.BlockSpec(memory_space=pl.ANY))
        operands.append(result)
        aliases = {len(flat): 0}
    return pl.pallas_call(
        kernel,
        grid=(1,),
        in_specs=in_specs,
        out_specs=pl.BlockSpec((rows, columns), lambda step: (half, 0)),
        out_shape=jax.ShapeDtypeStruct((2 * rows, columns), jnp.bfloat16),
        input_output_aliases=aliases,
        compiler_params=params(16),
        cost_estimate=SMALL,
        name="finish",
    )(*operands)


def swap(value, axis, distance):
    count = lax.axis_size(axis)
    return lax.ppermute(value, axis, [(source, source ^ distance) for source in range(count)])


def add(*terms):
    total = terms[0].astype(jnp.float32)
    for term in terms[1:]:
        total = total + term.astype(jnp.float32)
    return total.astype(jnp.bfloat16)


TURNS = (3, 1, 2, 0)


def tie(*values):
    return lax.optimization_barrier(values)


def exchange_local(queries, keys, values, doc_ids, w_out):
    shard_rows = queries.shape[0]
    group = queries.shape[1] // HD
    ctx_index = lax.axis_index("ctx").astype(jnp.int32).reshape(1)
    head_index = lax.axis_index("head").astype(jnp.int32)
    places = head_index ^ (2 * jnp.array(TURNS, jnp.int32))
    docs = doc_ids.reshape(shard_rows // HD, HD)
    near = range(1, group)

    w_sibling = swap(w_out, "head", 1)
    low_out = pack(ctx_index, 0, queries, keys, values, docs)
    low_out, later = tie(low_out, (queries, keys, values))
    low = [swap(low_out[distance - 1], "ctx", distance) for distance in near]
    high_out = pack(ctx_index, 1, *later, None)
    high = [swap(high_out[distance - 1], "ctx", distance) for distance in near[:-1]]
    w_packed = pack_projection(places, w_out, w_sibling)
    low, w_packed = tie(low, w_packed)

    def send_back(pieces):
        return [swap(pieces[distance], "ctx", distance) for distance in near]

    rows = shard_rows // 2
    cuts = (0, rows // 2, rows)

    def projected(mine, sibling, *wanted):
        return list(project(wanted, mine, sibling, *w_packed))

    def to_next(part, distance):
        return swap(part, "head", 2 * distance)

    pieces = attend(ctx_index, queries, keys, values, docs, low, None)
    pieces, diagonal_out = tie(pieces, high_out[-1])
    back = send_back(pieces)
    back, high = tie(back, high)
    high = [*high, swap(diagonal_out, "ctx", near[-1])]
    mine = assemble(ctx_index, [pieces[0], *back], (0, rows))
    sibling = [swap(part, "head", 1) for part in mine]
    shares = [projected(mine, sibling, [(turn, 0, rows)])[0] for turn in range(len(TURNS))]
    far = to_next(shares[0], 1)
    near_sum = to_next(shares[1], 1)
    passed = add(shares[2], far)

    high, shares, passed = tie(high, shares, passed)
    across = to_next(passed, 2)
    pieces = attend(ctx_index, queries, keys, values, docs, low, high)
    back = send_back(pieces)
    mine = assemble(ctx_index, [pieces[0], *back], cuts)
    sibling = [swap(part, "head", 1) for part in mine]
    late = [projected(mine, sibling, [(turn, 0, rows)])[0] for turn in (0, 2, 3)]
    late[0], near_sum, across = tie(late[0], near_sum, across)
    result = finish(0, rows, [[(shares[3], 0)], [(near_sum, 0)], [(across, 0)]], None)
    far = to_next(late[0], 1)
    passed = add(late[1], far)
    across = to_next(passed, 2)
    last = projected(mine, sibling, *[[(1, *span)] for span in zip(cuts[:-1], cuts[1:])])
    last, passed = tie(last, passed)
    near_sum = [to_next(part, 1) for part in last]
    terms = [[(late[2], 0)], [(part, 0) for part in near_sum], [(across, 0)]]
    return finish(1, rows, terms, result)


def solution(mesh):
    in_specs = (P("ctx", "head"), P("ctx", "head"), P("ctx", "head"), P("ctx"), P("head", None))
    out_specs = P("ctx", "head")
    ctx_count = mesh.shape["ctx"]
    head_count = mesh.shape["head"]

    def local(queries, keys, values, doc_ids, w_out):
        heads = queries.shape[1] // HD
        exchange = heads == ctx_count and heads == 4 and head_count == 2 * len(TURNS)
        exchange = exchange and queries.shape[0] % (4 * TILE) == 0
        body = exchange_local if exchange else ring_local
        return body(queries, keys, values, doc_ids, w_out)

    return jax.shard_map(
        local, mesh=mesh, in_specs=in_specs, out_specs=out_specs, check_vma=False
    )
```

```python
import functools
import math

import jax
import jax.numpy as jnp
from jax import lax
from jax.experimental import pallas as pl
from jax.experimental.pallas import tpu as pltpu
from jax.sharding import PartitionSpec as P

HD = 128


MASKED_SCORE = -1e30
LOG2E = 1.4426950408889634


def passed_along(value, axis, steps):
    count = lax.axis_size(axis)
    pairs = [(source, (source + steps) % count) for source in range(count)]
    return lax.ppermute(value, axis, pairs)


def folded_positions(row_total, offset, shard_rows, devices_ctx):
    flat_index = offset + lax.iota(jnp.int32, row_total)
    owner_dev = flat_index // shard_rows
    within = flat_index % shard_rows
    half_rows = shard_rows // 2
    fold_block = jnp.where(within < half_rows, owner_dev, 2 * devices_ctx - 1 - owner_dev)
    return fold_block * half_rows + within % half_rows


def block_update(
    running, query, query_pos, query_doc, key_block, value_block, pos_block, doc_block
):
    largest, totals, summed = running
    query_rows = query.shape[0]
    local_heads = query.shape[1] // HD
    query_heads = query.reshape(query_rows, local_heads, HD)
    key_heads = key_block.reshape(key_block.shape[0], local_heads, HD)
    value_heads = value_block.reshape(value_block.shape[0], local_heads, HD)
    scores = jnp.einsum(
        "qhd,khd->hqk", query_heads, key_heads, preferred_element_type=jnp.float32
    ) * (1.0 / math.sqrt(HD))
    allowed = (query_doc[:, None] == doc_block[None, :]) & (
        pos_block[None, :] <= query_pos[:, None]
    )
    scores = jnp.where(allowed[None], scores, MASKED_SCORE)
    new_max = jnp.maximum(largest, jnp.max(scores, axis=2))
    weights = jnp.where(allowed[None], jnp.exp(scores - new_max[:, :, None]), 0.0)
    factor = jnp.exp(largest - new_max)
    totals = totals * factor + jnp.sum(weights, axis=2)
    product = jnp.einsum(
        "hqk,khd->qhd",
        weights.astype(jnp.bfloat16),
        value_heads,
        preferred_element_type=jnp.float32,
    )
    summed = summed * factor.T[:, :, None] + product
    return (new_max, totals, summed)


def attend_rows(running, query, query_pos, query_doc, key_rows, value_rows, key_pos, key_doc):
    row_total = key_rows.shape[0]
    block_rows = math.gcd(row_total, query.shape[0])
    block_count = row_total // block_rows
    highest = jnp.max(query_pos)

    def visit(partial_value, blocks):
        key_block, value_block, pos_block, doc_block = blocks
        masked_out = jnp.min(pos_block) > highest
        updated = lax.cond(
            masked_out,
            lambda frozen: frozen,
            lambda frozen: block_update(
                frozen, query, query_pos, query_doc, key_block, value_block, pos_block, doc_block
            ),
            partial_value,
        )
        return (updated, None)

    blocks = (
        key_rows.reshape(block_count, block_rows, key_rows.shape[1]),
        value_rows.reshape(block_count, block_rows, value_rows.shape[1]),
        key_pos.reshape(block_count, block_rows),
        key_doc.reshape(block_count, block_rows),
    )
    running, _ = lax.scan(visit, running, blocks)
    return running


def attend_shard(running, query, query_pos, query_doc, key_rows, value_rows, key_pos, key_doc):
    largest, totals, summed = running
    half_rows = query.shape[0] // 2
    new_largest = []
    new_totals = []
    new_summed = []
    for half_idx in range(2):
        lower = half_idx * half_rows
        part_state = (largest[half_idx], totals[half_idx], summed[half_idx])
        part_state = attend_rows(
            part_state,
            query[lower : lower + half_rows],
            query_pos[lower : lower + half_rows],
            query_doc[lower : lower + half_rows],
            key_rows,
            value_rows,
            key_pos,
            key_doc,
        )
        new_largest.append(part_state[0])
        new_totals.append(part_state[1])
        new_summed.append(part_state[2])
    return (jnp.stack(new_largest), jnp.stack(new_totals), jnp.stack(new_summed))


def ring_local(queries, keys, values, doc_ids, w_out):
    shard_rows = queries.shape[0]
    half_rows = shard_rows // 2
    local_heads = queries.shape[1] // HD
    devices_ctx = lax.axis_size("ctx")
    ctx_index = lax.axis_index("ctx")
    all_docs = lax.all_gather(doc_ids, "ctx", axis=0, tiled=True)
    own_pos = folded_positions(shard_rows, ctx_index * shard_rows, shard_rows, devices_ctx)
    running = (
        jnp.full((2, local_heads, half_rows), MASKED_SCORE, jnp.float32),
        jnp.zeros((2, local_heads, half_rows), jnp.float32),
        jnp.zeros((2, half_rows, local_heads, HD), jnp.float32),
    )
    travel = queries
    for hop_step in range(devices_ctx):
        anchor = (ctx_index - hop_step) % devices_ctx
        query_pos = folded_positions(shard_rows, anchor * shard_rows, shard_rows, devices_ctx)
        query_doc = lax.dynamic_slice_in_dim(all_docs, anchor * shard_rows, shard_rows, 0)
        largest, totals, summed = attend_shard(
            running, travel, query_pos, query_doc, keys, values, own_pos, doc_ids
        )
        running = (
            passed_along(largest.astype(jnp.bfloat16), "ctx", 1).astype(largest.dtype),
            passed_along(totals.astype(jnp.bfloat16), "ctx", 1).astype(totals.dtype),
            passed_along(summed.astype(jnp.bfloat16), "ctx", 1).astype(summed.dtype),
        )
        if hop_step + 1 < devices_ctx:
            travel = passed_along(travel, "ctx", 1)
    largest, totals, summed = running
    attended = summed / totals.transpose(0, 2, 1)[:, :, :, None]
    attended = attended.reshape(shard_rows, local_heads * HD).astype(jnp.bfloat16)
    partial_out = jnp.dot(attended, w_out, preferred_element_type=jnp.float32)
    return lax.psum_scatter(
        partial_out.astype(jnp.bfloat16), "head", scatter_dimension=1, tiled=True
    )


SMALL = pl.CostEstimate(flops=1024, bytes_accessed=1024, transcendentals=0)
TILE = 256
MOST_DOCS = 16


def params(mib):
    return pltpu.CompilerParams(vmem_limit_bytes=mib * 1024 * 1024)


def whole(shape):
    return pl.BlockSpec(shape, lambda step, scalars: (0,) * len(shape))


def pack(ctx_index, half, queries, keys, values, docs):
    rows = queries.shape[0] // 2
    group = queries.shape[1] // HD
    doc_rows = 0 if docs is None else 16 * pl.cdiv(docs.shape[0], 16)
    total = 3 * rows + doc_rows

    def kernel(ctx_ref, *refs):
        outs = refs[len(refs) - (group - 1) :]
        if docs is not None:
            mine = refs[3 * (group - 1)][...].astype(jnp.float32)
            empty = jnp.zeros((doc_rows - mine.shape[0], HD), jnp.float32)
            mine = jnp.concatenate([mine, empty], axis=0).astype(jnp.bfloat16)
        for place in range(group - 1):
            for part in range(2):
                outs[place][part * rows : (part + 1) * rows, :] = refs[place * 3 + part][...]
            for block in range(rows // HD):
                taken = refs[place * 3 + 2][block * HD : (block + 1) * HD, :]
                lower = 2 * rows + block * HD
                outs[place][lower : lower + HD, :] = jnp.transpose(taken)
            if docs is not None:
                outs[place][3 * rows :, :] = mine

    def piece(distance):
        return pl.BlockSpec((rows, HD), lambda step, ctx: (half, ctx[0] ^ distance))

    in_specs = []
    operands = []
    for distance in range(1, group):
        for array in (queries, keys, values):
            in_specs.append(piece(distance))
            operands.append(array)
    if docs is not None:
        in_specs.append(whole(docs.shape))
        operands.append(docs)
    return pl.pallas_call(
        kernel,
        grid_spec=pltpu.PrefetchScalarGridSpec(
            num_scalar_prefetch=1,
            grid=(1,),
            in_specs=in_specs,
            out_specs=[whole((total, HD))] * (group - 1),
        ),
        out_shape=[jax.ShapeDtypeStruct((total, HD), jnp.bfloat16)] * (group - 1),
        compiler_params=params(56),
        cost_estimate=SMALL,
        name="pack",
    )(ctx_index, *operands)


def pack_projection(places, w_mine, w_sibling):
    depth, width = w_mine.shape
    turns = len(TURNS)
    columns = width // (2 * turns)

    def kernel(places_ref, mine_in, sibling_in, mine_out, sibling_out):
        mine_out[...] = mine_in[...]
        sibling_out[...] = sibling_in[...]

    in_spec = pl.BlockSpec((depth, columns), lambda turn, at: (0, at[turn]))
    out_spec = pl.BlockSpec((depth, columns), lambda turn, at: (0, turn))
    return pl.pallas_call(
        kernel,
        grid_spec=pltpu.PrefetchScalarGridSpec(
            num_scalar_prefetch=1,
            grid=(turns,),
            in_specs=[in_spec] * 2,
            out_specs=[out_spec] * 2,
        ),
        out_shape=[jax.ShapeDtypeStruct((depth, turns * columns), w_mine.dtype)] * 2,
        compiler_params=params(56),
        cost_estimate=SMALL,
        name="pack_projection",
    )(places, w_mine, w_sibling)


def attend(ctx_index, queries, keys, values, docs, low, high):
    rows = queries.shape[0] // 2
    group = queries.shape[1] // HD
    with_high = high is not None
    per_block = rows // TILE
    lines = rows // HD
    key_rows = (2 * group if with_high else group) * rows
    key_tiles = key_rows // TILE
    scaling = LOG2E / math.sqrt(HD)

    def kernel(ctx_ref, *refs):
        refs = list(refs)
        own_low = [refs.pop(0) for _ in range(3)]
        own_high = [refs.pop(0) for _ in range(3)] if with_high else None
        own_docs = refs.pop(0)
        low_refs = [refs.pop(0) for _ in range(group - 1)]
        high_refs = [refs.pop(0) for _ in range(group - 1)] if with_high else None
        outs = [refs.pop(0) for _ in range(group)]
        key_buf, value_buf, doc_buf = refs[:3]
        query_buf, start_buf, largest_buf, summed = (
            refs[3 + kind * group : 3 + (kind + 1) * group] for kind in range(4)
        )
        ctx = ctx_ref[0]

        def part(upper, distance, index, lower=0, count=rows):
            if distance == 0:
                return (own_high if upper else own_low)[index][lower : lower + count, :]
            source = (high_refs if upper else low_refs)[distance - 1]
            return source[index * rows + lower : index * rows + lower + count, :]

        place = {}
        doc_rows = {}
        for upper in (False, True) if with_high else (False,):
            for distance in range(group):
                source = ctx ^ distance
                block = 2 * group - 1 - source if upper else source
                place[upper, distance] = block
                offset = pl.multiple_of(block * rows, rows)
                key_buf[pl.ds(offset, rows), :] = part(upper, distance, 1)
                if distance == 0:
                    both = own_docs[...].astype(jnp.float32)
                else:
                    both = low_refs[distance - 1][3 * rows :, :].astype(jnp.float32)
                begin = lines if upper else 0
                mine = []
                for line in range(lines):
                    taken = part(upper, distance, 2, line * HD, HD)
                    if distance == 0:
                        taken = jnp.transpose(taken)
                    column = pl.multiple_of(block * rows + line * HD, HD)
                    value_buf[:HD, pl.ds(column, HD)] = taken
                    mine.append(both[begin + line : begin + line + 1, :])
                    doc_buf[pl.ds(block * lines + line, 1), :] = mine[-1]
                doc_rows[upper, distance] = jnp.concatenate(mine, axis=1)
        value_buf[HD:, :] = jnp.ones((value_buf.shape[0] - HD, key_rows), jnp.bfloat16)

        all_docs = doc_buf[...]
        starts = [jnp.zeros((1, rows), jnp.float32)] * group
        for number in range(1, MOST_DOCS):
            smaller = jnp.where(all_docs < number, 1.0, 0.0)
            count = jnp.sum(jnp.sum(smaller, axis=0, keepdims=True), axis=1, keepdims=True)
            for distance in range(group):
                reached = doc_rows[with_high, distance] >= number
                starts[distance] = jnp.where(reached, count, starts[distance])

        def scores_of(query, offset):
            raw = lax.dot_general(
                key_buf[pl.ds(offset, TILE), :],
                query,
                (((1,), (1,)), ((), ())),
                preferred_element_type=jnp.float32,
            )
            return raw * scaling

        def weighted(weights, offset):
            return jnp.dot(
                value_buf[:, pl.ds(offset, TILE)],
                weights.astype(jnp.bfloat16),
                preferred_element_type=jnp.float32,
            )

        key_row = lax.broadcasted_iota(jnp.int32, (TILE, TILE), 0)
        causal = key_row <= lax.broadcasted_iota(jnp.int32, (TILE, TILE), 1)
        key_row = key_row.astype(jnp.float32)
        firsts = []
        counts = []
        for lane in range(group):
            for slot in range(per_block):
                distance = lane ^ (slot * (group - 1))
                query = part(with_high, distance, 0, slot * TILE, TILE)
                query_buf[lane][slot] = query
                start = starts[distance][:, slot * TILE : (slot + 1) * TILE]
                start_buf[lane][slot, 0:1, :] = start
                end = place[with_high, distance] * per_block + slot
                offset = pl.multiple_of(end * TILE, TILE)
                least = start - offset.astype(jnp.float32)
                scores = scores_of(query, offset)
                scores = jnp.where((key_row >= least) & causal, scores, MASKED_SCORE)
                largest = jnp.max(scores, axis=0, keepdims=True)
                largest_buf[lane][slot, 0:1, :] = largest
                summed[lane][slot] = weighted(jnp.exp2(scores - largest), offset)
                first = start[0, 0].astype(jnp.int32) // TILE
                firsts.append(first)
                counts.append(end - first)

        longest = jnp.int32(0)
        for lane in range(group):
            of_lane = counts[lane * per_block : (lane + 1) * per_block]
            longest = jnp.maximum(longest, sum(of_lane))

        def visit(step, carry):
            slots = []
            offsets = []
            beyonds = []
            for lane in range(group):
                slot = jnp.int32(0)
                index = firsts[lane * per_block] + step
                before = counts[lane * per_block]
                for later in range(1, per_block):
                    reached = step >= before
                    slot = jnp.where(reached, later, slot)
                    place_later = lane * per_block + later
                    index = jnp.where(reached, firsts[place_later] + step - before, index)
                    before = before + counts[place_later]
                offset = pl.multiple_of(jnp.minimum(index, key_tiles - 1) * TILE, TILE)
                slots.append(slot)
                offsets.append(offset)
                beyonds.append(jnp.where(step < before, -offset.astype(jnp.float32), 1e9))
            each = range(group)
            scores = [scores_of(query_buf[lane][slots[lane]], offsets[lane]) for lane in each]
            old_max = [largest_buf[lane][slots[lane], 0:1, :] for lane in each]
            new_max = []
            for lane in each:
                least = start_buf[lane][slots[lane], 0:1, :] + beyonds[lane]
                scores[lane] = jnp.where(key_row >= least, scores[lane], MASKED_SCORE)
                tile_max = jnp.max(scores[lane], axis=0, keepdims=True)
                new_max.append(jnp.maximum(old_max[lane], tile_max))
            products = [
                weighted(jnp.exp2(scores[lane] - new_max[lane]), offsets[lane]) for lane in each
            ]
            for lane in each:
                factor = jnp.exp2(old_max[lane] - new_max[lane])
                summed[lane][slots[lane]] = summed[lane][slots[lane]] * factor + products[lane]
                largest_buf[lane][slots[lane], 0:1, :] = new_max[lane]
            return carry

        lax.fori_loop(0, longest, visit, jnp.int32(0))
        for lane in range(group):
            for slot in range(per_block):
                state = summed[lane]
                attended = state[slot, :HD, :] * (1.0 / state[slot, HD : HD + 1, :])
                out = outs[lane ^ (slot * (group - 1))]
                out[slot * TILE : (slot + 1) * TILE, :] = jnp.transpose(
                    attended.astype(jnp.bfloat16)
                )

    def own(upper):
        return pl.BlockSpec((rows, HD), lambda step, ctx: (int(upper), ctx[0]))

    in_specs = [own(False)] * 3
    operands = [queries, keys, values]
    if with_high:
        in_specs += [own(True)] * 3
        operands += [queries, keys, values]
    received = [docs, *low, *(high if with_high else ())]
    operands += received
    in_specs += [whole(array.shape) for array in received]
    return pl.pallas_call(
        kernel,
        grid_spec=pltpu.PrefetchScalarGridSpec(
            num_scalar_prefetch=1,
            grid=(1,),
            in_specs=in_specs,
            out_specs=[whole((rows, HD))] * group,
            scratch_shapes=[
                pltpu.VMEM((key_rows, HD), jnp.bfloat16),
                pltpu.VMEM((HD + 16, key_rows), jnp.bfloat16),
                pltpu.VMEM((key_rows // HD, HD), jnp.float32),
                *[pltpu.VMEM((per_block, TILE, HD), jnp.bfloat16)] * group,
                *[pltpu.VMEM((per_block, 8, TILE), jnp.float32)] * (2 * group),
                *[pltpu.VMEM((per_block, HD + 16, TILE), jnp.float32)] * group,
            ],
        ),
        out_shape=[jax.ShapeDtypeStruct((rows, HD), jnp.bfloat16)] * group,
        compiler_params=params(40),
        cost_estimate=SMALL,
        name="attend_high" if with_high else "attend_low",
    )(ctx_index, *operands)


def assemble(ctx_index, pieces, cuts):
    rows = pieces[0].shape[0]
    group = len(pieces)
    spans = list(zip(cuts[:-1], cuts[1:]))

    def kernel(ctx_ref, *refs):
        for part, (lower, upper) in enumerate(spans):
            for distance in range(group):
                column = pl.multiple_of((ctx_ref[0] ^ distance) * HD, HD)
                refs[group + part][:, pl.ds(column, HD)] = refs[distance][lower:upper, :]

    shapes = [(upper - lower, group * HD) for lower, upper in spans]
    return pl.pallas_call(
        kernel,
        grid_spec=pltpu.PrefetchScalarGridSpec(
            num_scalar_prefetch=1,
            grid=(1,),
            in_specs=[whole((rows, HD))] * group,
            out_specs=[whole(shape) for shape in shapes],
        ),
        out_shape=[jax.ShapeDtypeStruct(shape, jnp.bfloat16) for shape in shapes],
        compiler_params=params(16),
        cost_estimate=SMALL,
        name="assemble",
    )(ctx_index, *pieces)


def plain(shape):
    return pl.BlockSpec(shape, lambda step: (0,) * len(shape))


def stacked(refs):
    values = [ref[...] for ref in refs]
    return values[0] if len(values) == 1 else jnp.concatenate(values, axis=0)


def project(wanted, mine, sibling, w_mine, w_sibling):
    parts = len(mine)
    depth = mine[0].shape[1]
    columns = w_mine.shape[1] // len(TURNS)
    turns = sorted({turn for output in wanted for turn, _, _ in output})

    def kernel(*refs):
        own_rows = stacked(refs[:parts])
        other_rows = stacked(refs[parts : 2 * parts])
        weights = refs[2 * parts : 2 * parts + 2 * len(turns)]
        outs = refs[2 * parts + 2 * len(turns) :]
        for out, output in zip(outs, wanted):
            place = 0
            for turn, lower, upper in output:
                at = turns.index(turn)
                total = jnp.dot(
                    own_rows[lower:upper, :], weights[at][...], preferred_element_type=jnp.float32
                )
                total += jnp.dot(
                    other_rows[lower:upper, :],
                    weights[len(turns) + at][...],
                    preferred_element_type=jnp.float32,
                )
                out[place : place + upper - lower, :] = total.astype(jnp.bfloat16)
                place += upper - lower

    def columns_of(turn):
        return pl.BlockSpec((depth, columns), lambda step: (0, turn))

    shapes = [(sum(upper - lower for _, lower, upper in output), columns) for output in wanted]
    return pl.pallas_call(
        kernel,
        grid=(1,),
        in_specs=[plain(part.shape) for part in (*mine, *sibling)]
        + [columns_of(turn) for turn in turns] * 2,
        out_specs=[plain(shape) for shape in shapes],
        out_shape=[jax.ShapeDtypeStruct(shape, jnp.bfloat16) for shape in shapes],
        compiler_params=params(24),
        cost_estimate=SMALL,
        name="project",
    )(*mine, *sibling, *([w_mine] * len(turns)), *([w_sibling] * len(turns)))


def finish(half, rows, terms, result):
    flat = [array for term in terms for array, _ in term]
    columns = flat[0].shape[1]

    def kernel(*refs):
        refs = list(refs)
        total = None
        for term in terms:
            values = [refs.pop(0)[first:, :].astype(jnp.float32) for _, first in term]
            value = values[0] if len(values) == 1 else jnp.concatenate(values, axis=0)
            total = value if total is None else total + value
        refs[-1][...] = total.astype(jnp.bfloat16)

    in_specs = [plain(array.shape) for array in flat]
    operands = list(flat)
    aliases = {}
    if result is not None:
        in_specs.append(pl.BlockSpec(memory_space=pl.ANY))
        operands.append(result)
        aliases = {len(flat): 0}
    return pl.pallas_call(
        kernel,
        grid=(1,),
        in_specs=in_specs,
        out_specs=pl.BlockSpec((rows, columns), lambda step: (half, 0)),
        out_shape=jax.ShapeDtypeStruct((2 * rows, columns), jnp.bfloat16),
        input_output_aliases=aliases,
        compiler_params=params(16),
        cost_estimate=SMALL,
        name="finish",
    )(*operands)


def swap(value, axis, distance):
    count = lax.axis_size(axis)
    return lax.ppermute(value, axis, [(source, source ^ distance) for source in range(count)])


def add(*terms):
    total = terms[0].astype(jnp.float32)
    for term in terms[1:]:
        total = total + term.astype(jnp.float32)
    return total.astype(jnp.bfloat16)


TURNS = (3, 1, 2, 0)


def tie(*values):
    return lax.optimization_barrier(values)


def exchange_local(queries, keys, values, doc_ids, w_out):
    shard_rows = queries.shape[0]
    group = queries.shape[1] // HD
    ctx_index = lax.axis_index("ctx").astype(jnp.int32).reshape(1)
    head_index = lax.axis_index("head").astype(jnp.int32)
    places = head_index ^ (2 * jnp.array(TURNS, jnp.int32))
    docs = doc_ids.reshape(shard_rows // HD, HD)
    near = range(1, group)

    w_sibling = swap(w_out, "head", 1)
    low_out = pack(ctx_index, 0, queries, keys, values, docs)
    low_out, later = tie(low_out, (queries, keys, values))
    low = [swap(low_out[distance - 1], "ctx", distance) for distance in near]
    high_out = pack(ctx_index, 1, *later, None)
    high = [swap(high_out[distance - 1], "ctx", distance) for distance in near[:-1]]
    w_packed = pack_projection(places, w_out, w_sibling)
    low, w_packed = tie(low, w_packed)

    def send_back(pieces):
        return [swap(pieces[distance], "ctx", distance) for distance in near]

    rows = shard_rows // 2
    cuts = (0, rows // 2, rows)

    def projected(mine, sibling, *wanted):
        return list(project(wanted, mine, sibling, *w_packed))

    def to_next(part, distance):
        return swap(part, "head", 2 * distance)

    pieces = attend(ctx_index, queries, keys, values, docs, low, None)
    pieces, diagonal_out = tie(pieces, high_out[-1])
    back = send_back(pieces)
    back, high = tie(back, high)
    high = [*high, swap(diagonal_out, "ctx", near[-1])]
    mine = assemble(ctx_index, [pieces[0], *back], (0, rows))
    sibling = [swap(part, "head", 1) for part in mine]
    shares = [projected(mine, sibling, [(turn, 0, rows)])[0] for turn in range(len(TURNS))]
    far = to_next(shares[0], 1)
    near_sum = to_next(shares[1], 1)
    passed = add(shares[2], far)

    high, shares = tie(high, shares)
    pieces = attend(ctx_index, queries, keys, values, docs, low, high)
    back = send_back(pieces)
    pieces, passed = tie(pieces, passed)
    across = to_next(passed, 2)
    back, near_sum = tie(back, near_sum)
    mine = assemble(ctx_index, [pieces[0], *back], cuts)
    sibling = [swap(part, "head", 1) for part in mine]
    halves = list(zip(cuts[:-1], cuts[1:]))
    late = projected(mine, sibling, *[[(0, *span)] for span in halves])
    late[1], across = tie(late[1], across)
    result = finish(0, rows, [[(shares[3], 0)], [(near_sum, 0)], [(across, 0)]], None)
    far = [to_next(part, 1) for part in late]
    late = projected(mine, sibling, *[[(2, *span)] for span in halves])
    passed = [add(*both) for both in zip(late, far)]
    across = [to_next(part, 2) for part in passed]
    third = rows * 11 // 32 // 16 * 16
    thirds = ((0, third), (third, 2 * third), (2 * third, rows))
    last = projected(mine, sibling, *[[(1, *span)] for span in thirds])
    last, passed = tie(last, passed)
    near_sum = [to_next(part, 1) for part in last]
    (kept,) = projected(mine, sibling, [(3, 0, rows)])
    terms = [[(kept, 0)], [(part, 0) for part in near_sum], [(part, 0) for part in across]]
    return finish(1, rows, terms, result)


def solution(mesh):
    in_specs = (P("ctx", "head"), P("ctx", "head"), P("ctx", "head"), P("ctx"), P("head", None))
    out_specs = P("ctx", "head")
    ctx_count = mesh.shape["ctx"]
    head_count = mesh.shape["head"]

    def local(queries, keys, values, doc_ids, w_out):
        heads = queries.shape[1] // HD
        exchange = heads == ctx_count and heads == 4 and head_count == 2 * len(TURNS)
        exchange = exchange and queries.shape[0] % (4 * TILE) == 0
        body = exchange_local if exchange else ring_local
        return body(queries, keys, values, doc_ids, w_out)

    return jax.shard_map(
        local, mesh=mesh, in_specs=in_specs, out_specs=out_specs, check_vma=False
    )
```

```python
import functools
import math

import jax
import jax.numpy as jnp
from jax import lax
from jax.experimental import pallas as pl
from jax.experimental.pallas import tpu as pltpu
from jax.sharding import PartitionSpec as P

HD = 128


MASKED_SCORE = -1e30
LOG2E = 1.4426950408889634


def passed_along(value, axis, steps):
    count = lax.axis_size(axis)
    pairs = [(source, (source + steps) % count) for source in range(count)]
    return lax.ppermute(value, axis, pairs)


def folded_positions(row_total, offset, shard_rows, devices_ctx):
    flat_index = offset + lax.iota(jnp.int32, row_total)
    owner_dev = flat_index // shard_rows
    within = flat_index % shard_rows
    half_rows = shard_rows // 2
    fold_block = jnp.where(within < half_rows, owner_dev, 2 * devices_ctx - 1 - owner_dev)
    return fold_block * half_rows + within % half_rows


def block_update(
    running, query, query_pos, query_doc, key_block, value_block, pos_block, doc_block
):
    largest, totals, summed = running
    query_rows = query.shape[0]
    local_heads = query.shape[1] // HD
    query_heads = query.reshape(query_rows, local_heads, HD)
    key_heads = key_block.reshape(key_block.shape[0], local_heads, HD)
    value_heads = value_block.reshape(value_block.shape[0], local_heads, HD)
    scores = jnp.einsum(
        "qhd,khd->hqk", query_heads, key_heads, preferred_element_type=jnp.float32
    ) * (1.0 / math.sqrt(HD))
    allowed = (query_doc[:, None] == doc_block[None, :]) & (
        pos_block[None, :] <= query_pos[:, None]
    )
    scores = jnp.where(allowed[None], scores, MASKED_SCORE)
    new_max = jnp.maximum(largest, jnp.max(scores, axis=2))
    weights = jnp.where(allowed[None], jnp.exp(scores - new_max[:, :, None]), 0.0)
    factor = jnp.exp(largest - new_max)
    totals = totals * factor + jnp.sum(weights, axis=2)
    product = jnp.einsum(
        "hqk,khd->qhd",
        weights.astype(jnp.bfloat16),
        value_heads,
        preferred_element_type=jnp.float32,
    )
    summed = summed * factor.T[:, :, None] + product
    return (new_max, totals, summed)


def attend_rows(running, query, query_pos, query_doc, key_rows, value_rows, key_pos, key_doc):
    row_total = key_rows.shape[0]
    block_rows = math.gcd(row_total, query.shape[0])
    block_count = row_total // block_rows
    highest = jnp.max(query_pos)

    def visit(partial_value, blocks):
        key_block, value_block, pos_block, doc_block = blocks
        masked_out = jnp.min(pos_block) > highest
        updated = lax.cond(
            masked_out,
            lambda frozen: frozen,
            lambda frozen: block_update(
                frozen, query, query_pos, query_doc, key_block, value_block, pos_block, doc_block
            ),
            partial_value,
        )
        return (updated, None)

    blocks = (
        key_rows.reshape(block_count, block_rows, key_rows.shape[1]),
        value_rows.reshape(block_count, block_rows, value_rows.shape[1]),
        key_pos.reshape(block_count, block_rows),
        key_doc.reshape(block_count, block_rows),
    )
    running, _ = lax.scan(visit, running, blocks)
    return running


def attend_shard(running, query, query_pos, query_doc, key_rows, value_rows, key_pos, key_doc):
    largest, totals, summed = running
    half_rows = query.shape[0] // 2
    new_largest = []
    new_totals = []
    new_summed = []
    for half_idx in range(2):
        lower = half_idx * half_rows
        part_state = (largest[half_idx], totals[half_idx], summed[half_idx])
        part_state = attend_rows(
            part_state,
            query[lower : lower + half_rows],
            query_pos[lower : lower + half_rows],
            query_doc[lower : lower + half_rows],
            key_rows,
            value_rows,
            key_pos,
            key_doc,
        )
        new_largest.append(part_state[0])
        new_totals.append(part_state[1])
        new_summed.append(part_state[2])
    return (jnp.stack(new_largest), jnp.stack(new_totals), jnp.stack(new_summed))


def ring_local(queries, keys, values, doc_ids, w_out):
    shard_rows = queries.shape[0]
    half_rows = shard_rows // 2
    local_heads = queries.shape[1] // HD
    devices_ctx = lax.axis_size("ctx")
    ctx_index = lax.axis_index("ctx")
    all_docs = lax.all_gather(doc_ids, "ctx", axis=0, tiled=True)
    own_pos = folded_positions(shard_rows, ctx_index * shard_rows, shard_rows, devices_ctx)
    running = (
        jnp.full((2, local_heads, half_rows), MASKED_SCORE, jnp.float32),
        jnp.zeros((2, local_heads, half_rows), jnp.float32),
        jnp.zeros((2, half_rows, local_heads, HD), jnp.float32),
    )
    travel = queries
    for hop_step in range(devices_ctx):
        anchor = (ctx_index - hop_step) % devices_ctx
        query_pos = folded_positions(shard_rows, anchor * shard_rows, shard_rows, devices_ctx)
        query_doc = lax.dynamic_slice_in_dim(all_docs, anchor * shard_rows, shard_rows, 0)
        largest, totals, summed = attend_shard(
            running, travel, query_pos, query_doc, keys, values, own_pos, doc_ids
        )
        running = (
            passed_along(largest.astype(jnp.bfloat16), "ctx", 1).astype(largest.dtype),
            passed_along(totals.astype(jnp.bfloat16), "ctx", 1).astype(totals.dtype),
            passed_along(summed.astype(jnp.bfloat16), "ctx", 1).astype(summed.dtype),
        )
        if hop_step + 1 < devices_ctx:
            travel = passed_along(travel, "ctx", 1)
    largest, totals, summed = running
    attended = summed / totals.transpose(0, 2, 1)[:, :, :, None]
    attended = attended.reshape(shard_rows, local_heads * HD).astype(jnp.bfloat16)
    partial_out = jnp.dot(attended, w_out, preferred_element_type=jnp.float32)
    return lax.psum_scatter(
        partial_out.astype(jnp.bfloat16), "head", scatter_dimension=1, tiled=True
    )


SMALL = pl.CostEstimate(flops=1024, bytes_accessed=1024, transcendentals=0)
TILE = 256
MOST_DOCS = 16


def params(mib):
    return pltpu.CompilerParams(vmem_limit_bytes=mib * 1024 * 1024)


def whole(shape):
    return pl.BlockSpec(shape, lambda step, scalars: (0,) * len(shape))


def pack(ctx_index, half, queries, keys, values, docs):
    rows = queries.shape[0] // 2
    group = queries.shape[1] // HD
    doc_rows = 0 if docs is None else 16 * pl.cdiv(docs.shape[0], 16)
    total = 3 * rows + doc_rows

    def kernel(ctx_ref, *refs):
        outs = refs[len(refs) - (group - 1) :]
        if docs is not None:
            mine = refs[3 * (group - 1)][...].astype(jnp.float32)
            empty = jnp.zeros((doc_rows - mine.shape[0], HD), jnp.float32)
            mine = jnp.concatenate([mine, empty], axis=0).astype(jnp.bfloat16)
        for place in range(group - 1):
            for part in range(2):
                outs[place][part * rows : (part + 1) * rows, :] = refs[place * 3 + part][...]
            for block in range(rows // HD):
                taken = refs[place * 3 + 2][block * HD : (block + 1) * HD, :]
                lower = 2 * rows + block * HD
                outs[place][lower : lower + HD, :] = jnp.transpose(taken)
            if docs is not None:
                outs[place][3 * rows :, :] = mine

    def piece(distance):
        return pl.BlockSpec((rows, HD), lambda step, ctx: (half, ctx[0] ^ distance))

    in_specs = []
    operands = []
    for distance in range(1, group):
        for array in (queries, keys, values):
            in_specs.append(piece(distance))
            operands.append(array)
    if docs is not None:
        in_specs.append(whole(docs.shape))
        operands.append(docs)
    return pl.pallas_call(
        kernel,
        grid_spec=pltpu.PrefetchScalarGridSpec(
            num_scalar_prefetch=1,
            grid=(1,),
            in_specs=in_specs,
            out_specs=[whole((total, HD))] * (group - 1),
        ),
        out_shape=[jax.ShapeDtypeStruct((total, HD), jnp.bfloat16)] * (group - 1),
        compiler_params=params(56),
        cost_estimate=SMALL,
        name="pack",
    )(ctx_index, *operands)


def pack_projection(places, w_mine, w_sibling):
    depth, width = w_mine.shape
    turns = len(TURNS)
    columns = width // (2 * turns)

    def kernel(places_ref, mine_in, sibling_in, mine_out, sibling_out):
        mine_out[...] = mine_in[...]
        sibling_out[...] = sibling_in[...]

    in_spec = pl.BlockSpec((depth, columns), lambda turn, at: (0, at[turn]))
    out_spec = pl.BlockSpec((depth, columns), lambda turn, at: (0, turn))
    return pl.pallas_call(
        kernel,
        grid_spec=pltpu.PrefetchScalarGridSpec(
            num_scalar_prefetch=1,
            grid=(turns,),
            in_specs=[in_spec] * 2,
            out_specs=[out_spec] * 2,
        ),
        out_shape=[jax.ShapeDtypeStruct((depth, turns * columns), w_mine.dtype)] * 2,
        compiler_params=params(56),
        cost_estimate=SMALL,
        name="pack_projection",
    )(places, w_mine, w_sibling)


def attend(ctx_index, queries, keys, values, docs, low, high):
    rows = queries.shape[0] // 2
    group = queries.shape[1] // HD
    with_high = high is not None
    per_block = rows // TILE
    lines = rows // HD
    key_rows = (2 * group if with_high else group) * rows
    key_tiles = key_rows // TILE
    scaling = LOG2E / math.sqrt(HD)

    def kernel(ctx_ref, *refs):
        refs = list(refs)
        own_low = [refs.pop(0) for _ in range(3)]
        own_high = [refs.pop(0) for _ in range(3)] if with_high else None
        own_docs = refs.pop(0)
        low_refs = [refs.pop(0) for _ in range(group - 1)]
        high_refs = [refs.pop(0) for _ in range(group - 1)] if with_high else None
        outs = [refs.pop(0) for _ in range(group)]
        key_buf, value_buf, doc_buf = refs[:3]
        query_buf, start_buf, largest_buf, summed = (
            refs[3 + kind * group : 3 + (kind + 1) * group] for kind in range(4)
        )
        ctx = ctx_ref[0]

        def part(upper, distance, index, lower=0, count=rows):
            if distance == 0:
                return (own_high if upper else own_low)[index][lower : lower + count, :]
            source = (high_refs if upper else low_refs)[distance - 1]
            return source[index * rows + lower : index * rows + lower + count, :]

        place = {}
        doc_rows = {}
        for upper in (False, True) if with_high else (False,):
            for distance in range(group):
                source = ctx ^ distance
                block = 2 * group - 1 - source if upper else source
                place[upper, distance] = block
                offset = pl.multiple_of(block * rows, TILE)
                key_buf[pl.ds(offset + TILE, rows), :] = part(upper, distance, 1)
                if distance == 0:
                    both = own_docs[...].astype(jnp.float32)
                else:
                    both = low_refs[distance - 1][3 * rows :, :].astype(jnp.float32)
                begin = lines if upper else 0
                mine = []
                for line in range(lines):
                    taken = part(upper, distance, 2, line * HD, HD)
                    if distance == 0:
                        taken = jnp.transpose(taken)
                    column = pl.multiple_of(block * rows + line * HD + TILE, HD)
                    value_buf[:HD, pl.ds(column, HD)] = taken
                    mine.append(both[begin + line : begin + line + 1, :])
                    doc_buf[pl.ds(block * lines + line, 1), :] = mine[-1]
                doc_rows[upper, distance] = jnp.concatenate(mine, axis=1)
        value_buf[HD:, :] = jnp.ones((value_buf.shape[0] - HD, key_rows + TILE), jnp.bfloat16)
        key_buf[:TILE, :] = jnp.zeros((TILE, HD), jnp.bfloat16)
        value_buf[:HD, :TILE] = jnp.zeros((HD, TILE), jnp.bfloat16)

        all_docs = doc_buf[...]
        starts = [jnp.zeros((1, rows), jnp.float32)] * group
        for number in range(1, MOST_DOCS):
            smaller = jnp.where(all_docs < number, 1.0, 0.0)
            count = jnp.sum(jnp.sum(smaller, axis=0, keepdims=True), axis=1, keepdims=True)
            for distance in range(group):
                reached = doc_rows[with_high, distance] >= number
                starts[distance] = jnp.where(reached, count, starts[distance])

        def scores_of(query, offset, count):
            raw = lax.dot_general(
                key_buf[pl.ds(pl.multiple_of(offset + TILE, TILE), count), :],
                query,
                (((1,), (1,)), ((), ())),
                preferred_element_type=jnp.float32,
            )
            return raw * scaling

        def weighted(weights, offset, count):
            return jnp.dot(
                value_buf[:, pl.ds(pl.multiple_of(offset + TILE, TILE), count)],
                weights.astype(jnp.bfloat16),
                preferred_element_type=jnp.float32,
            )

        key_row = lax.broadcasted_iota(jnp.int32, (TILE, TILE), 0)
        causal = key_row <= lax.broadcasted_iota(jnp.int32, (TILE, TILE), 1)
        key_row = key_row.astype(jnp.float32)
        ends = []
        counts = []
        for lane in range(group):
            for slot in range(per_block):
                distance = lane ^ (slot * (group - 1))
                query = part(with_high, distance, 0, slot * TILE, TILE)
                query_buf[lane][slot] = query
                start = starts[distance][:, slot * TILE : (slot + 1) * TILE]
                start_buf[lane][slot, 0:1, :] = start
                end = place[with_high, distance] * per_block + slot
                offset = pl.multiple_of(end * TILE, TILE)
                least = start - offset.astype(jnp.float32)
                scores = scores_of(query, offset, TILE)
                scores = jnp.where((key_row >= least) & causal, scores, MASKED_SCORE)
                largest = jnp.max(scores, axis=0, keepdims=True)
                largest_buf[lane][slot, 0:1, :] = largest
                summed[lane][slot] = weighted(jnp.exp2(scores - largest), offset, TILE)
                first = start[0, 0].astype(jnp.int32) // TILE
                ends.append(end)
                counts.append((end - first + 1) // 2)

        longest = jnp.int32(0)
        for lane in range(group):
            of_lane = counts[lane * per_block : (lane + 1) * per_block]
            longest = jnp.maximum(longest, sum(of_lane))

        pair_row = lax.broadcasted_iota(jnp.int32, (2 * TILE, TILE), 0).astype(jnp.float32)

        def visit(step, carry):
            slots = []
            offsets = []
            beyonds = []
            for lane in range(group):
                slot = jnp.int32(0)
                index = ends[lane * per_block] - 2 * step - 2
                before = counts[lane * per_block]
                for later in range(1, per_block):
                    reached = step >= before
                    slot = jnp.where(reached, later, slot)
                    place_later = lane * per_block + later
                    later_index = ends[place_later] - 2 * (step - before) - 2
                    index = jnp.where(reached, later_index, index)
                    before = before + counts[place_later]
                index = jnp.minimum(jnp.maximum(index, -1), key_tiles - 2)
                offset = pl.multiple_of(index * TILE, TILE)
                slots.append(slot)
                offsets.append(offset)
                beyonds.append(jnp.where(step < before, -offset.astype(jnp.float32), 1e9))
            each = range(group)
            scores = [
                scores_of(query_buf[lane][slots[lane]], offsets[lane], 2 * TILE) for lane in each
            ]
            old_max = [largest_buf[lane][slots[lane], 0:1, :] for lane in each]
            new_max = []
            for lane in each:
                least = start_buf[lane][slots[lane], 0:1, :] + beyonds[lane]
                scores[lane] = jnp.where(pair_row >= least, scores[lane], MASKED_SCORE)
                tile_max = jnp.max(scores[lane], axis=0, keepdims=True)
                new_max.append(jnp.maximum(old_max[lane], tile_max))
            products = [
                weighted(jnp.exp2(scores[lane] - new_max[lane]), offsets[lane], 2 * TILE)
                for lane in each
            ]
            for lane in each:
                factor = jnp.exp2(old_max[lane] - new_max[lane])
                summed[lane][slots[lane]] = summed[lane][slots[lane]] * factor + products[lane]
                largest_buf[lane][slots[lane], 0:1, :] = new_max[lane]
            return carry

        lax.fori_loop(0, longest, visit, jnp.int32(0))
        for lane in range(group):
            for slot in range(per_block):
                state = summed[lane]
                attended = state[slot, :HD, :] * (1.0 / state[slot, HD : HD + 1, :])
                out = outs[lane ^ (slot * (group - 1))]
                out[slot * TILE : (slot + 1) * TILE, :] = jnp.transpose(
                    attended.astype(jnp.bfloat16)
                )

    def own(upper):
        return pl.BlockSpec((rows, HD), lambda step, ctx: (int(upper), ctx[0]))

    in_specs = [own(False)] * 3
    operands = [queries, keys, values]
    if with_high:
        in_specs += [own(True)] * 3
        operands += [queries, keys, values]
    received = [docs, *low, *(high if with_high else ())]
    operands += received
    in_specs += [whole(array.shape) for array in received]
    return pl.pallas_call(
        kernel,
        grid_spec=pltpu.PrefetchScalarGridSpec(
            num_scalar_prefetch=1,
            grid=(1,),
            in_specs=in_specs,
            out_specs=[whole((rows, HD))] * group,
            scratch_shapes=[
                pltpu.VMEM((key_rows + TILE, HD), jnp.bfloat16),
                pltpu.VMEM((HD + 16, key_rows + TILE), jnp.bfloat16),
                pltpu.VMEM((key_rows // HD, HD), jnp.float32),
                *[pltpu.VMEM((per_block, TILE, HD), jnp.bfloat16)] * group,
                *[pltpu.VMEM((per_block, 8, TILE), jnp.float32)] * (2 * group),
                *[pltpu.VMEM((per_block, HD + 16, TILE), jnp.float32)] * group,
            ],
        ),
        out_shape=[jax.ShapeDtypeStruct((rows, HD), jnp.bfloat16)] * group,
        compiler_params=params(40),
        cost_estimate=SMALL,
        name="attend_high" if with_high else "attend_low",
    )(ctx_index, *operands)


def assemble(ctx_index, pieces, parts):
    rows = pieces[0].shape[0]
    group = len(pieces)
    part_rows = rows // parts

    def kernel(ctx_ref, *refs):
        for part in range(parts):
            for distance in range(group):
                column = pl.multiple_of((ctx_ref[0] ^ distance) * HD, HD)
                taken = refs[distance][part * part_rows : (part + 1) * part_rows, :]
                refs[group + part][:, pl.ds(column, HD)] = taken

    return pl.pallas_call(
        kernel,
        grid_spec=pltpu.PrefetchScalarGridSpec(
            num_scalar_prefetch=1,
            grid=(1,),
            in_specs=[whole((rows, HD))] * group,
            out_specs=[whole((part_rows, group * HD))] * parts,
        ),
        out_shape=[jax.ShapeDtypeStruct((part_rows, group * HD), jnp.bfloat16)] * parts,
        compiler_params=params(16),
        cost_estimate=SMALL,
        name="assemble",
    )(ctx_index, *pieces)


def project(turn, mine, sibling, w_mine, w_sibling):
    parts = len(mine)
    rows, depth = mine[0].shape
    columns = w_mine.shape[1] // len(TURNS)

    def kernel(*refs):
        w_mine_ref, w_sibling_ref = refs[2 * parts : 2 * parts + 2]
        for part in range(parts):
            total = jnp.dot(refs[part][...], w_mine_ref[...], preferred_element_type=jnp.float32)
            total += jnp.dot(
                refs[parts + part][...], w_sibling_ref[...], preferred_element_type=jnp.float32
            )
            refs[2 * parts + 2 + part][...] = total.astype(jnp.bfloat16)

    weights = pl.BlockSpec((depth, columns), lambda step: (0, turn))
    attended = pl.BlockSpec((rows, depth), lambda step: (0, 0))
    return pl.pallas_call(
        kernel,
        grid=(1,),
        in_specs=[attended] * (2 * parts) + [weights] * 2,
        out_specs=[pl.BlockSpec((rows, columns), lambda step: (0, 0))] * parts,
        out_shape=[jax.ShapeDtypeStruct((rows, columns), jnp.bfloat16)] * parts,
        compiler_params=params(16),
        cost_estimate=SMALL,
        name="project",
    )(*mine, *sibling, w_mine, w_sibling)


def finish(half, terms, result):
    parts = len(terms[0])
    rows, columns = terms[0][0].shape
    flat = [part for term in terms for part in term]

    def kernel(*refs):
        for part in range(parts):
            total = refs[part][...].astype(jnp.float32)
            for term in range(1, len(terms)):
                total += refs[term * parts + part][...].astype(jnp.float32)
            refs[-1][part * rows : (part + 1) * rows, :] = total.astype(jnp.bfloat16)

    in_specs = [pl.BlockSpec((rows, columns), lambda step: (0, 0))] * len(flat)
    operands = list(flat)
    aliases = {}
    if result is not None:
        in_specs.append(pl.BlockSpec(memory_space=pl.ANY))
        operands.append(result)
        aliases = {len(flat): 0}
    return pl.pallas_call(
        kernel,
        grid=(1,),
        in_specs=in_specs,
        out_specs=pl.BlockSpec((parts * rows, columns), lambda step: (half, 0)),
        out_shape=jax.ShapeDtypeStruct((2 * parts * rows, columns), jnp.bfloat16),
        input_output_aliases=aliases,
        compiler_params=params(16),
        cost_estimate=SMALL,
        name="finish",
    )(*operands)


def swap(value, axis, distance):
    count = lax.axis_size(axis)
    return lax.ppermute(value, axis, [(source, source ^ distance) for source in range(count)])


def add(*terms):
    total = terms[0].astype(jnp.float32)
    for term in terms[1:]:
        total = total + term.astype(jnp.float32)
    return total.astype(jnp.bfloat16)


TURNS = (3, 1, 2, 0)


def tie(*values):
    return lax.optimization_barrier(values)


def exchange_local(queries, keys, values, doc_ids, w_out):
    shard_rows = queries.shape[0]
    group = queries.shape[1] // HD
    ctx_index = lax.axis_index("ctx").astype(jnp.int32).reshape(1)
    head_index = lax.axis_index("head").astype(jnp.int32)
    places = head_index ^ (2 * jnp.array(TURNS, jnp.int32))
    docs = doc_ids.reshape(shard_rows // HD, HD)
    near = range(1, group)

    w_sibling = swap(w_out, "head", 1)
    low_out = pack(ctx_index, 0, queries, keys, values, docs)
    low_out, later = tie(low_out, (queries, keys, values))
    low = [swap(low_out[distance - 1], "ctx", distance) for distance in near]
    high_out = pack(ctx_index, 1, *later, None)
    high = [swap(high_out[distance - 1], "ctx", distance) for distance in near[:-1]]
    w_packed = pack_projection(places, w_out, w_sibling)
    low, w_packed = tie(low, w_packed)

    def send_back(pieces):
        return [swap(pieces[distance], "ctx", distance) for distance in near]

    def shares_of(mine):
        sibling = [swap(part, "head", 1) for part in mine]
        return [project(turn, mine, sibling, *w_packed) for turn in range(len(TURNS))]

    def to_next(parts, distance):
        return [swap(part, "head", 2 * distance) for part in parts]

    pieces = attend(ctx_index, queries, keys, values, docs, low, None)
    pieces, diagonal_out = tie(pieces, high_out[-1])
    back = send_back(pieces)
    back, high = tie(back, high)
    high = [*high, swap(diagonal_out, "ctx", near[-1])]
    shares = shares_of(assemble(ctx_index, [pieces[0], *back], 1))
    far = to_next(shares[0], 1)
    near_sum = to_next(shares[1], 1)

    passed = [add(*both) for both in zip(shares[2], far)]
    high, shares, passed = tie(high, shares, passed)
    across = to_next(passed, 2)
    pieces = attend(ctx_index, queries, keys, values, docs, low, high)
    back = send_back(pieces)
    late = shares_of(assemble(ctx_index, [pieces[0], *back], 2))
    late[0], near_sum, across = tie(late[0], near_sum, across)
    result = finish(0, [shares[3], near_sum, across], None)
    far = to_next(late[0], 1)
    passed = [add(*both) for both in zip(late[2], far)]
    across = to_next(passed, 2)
    late[1], passed = tie(late[1], passed)
    near_sum = to_next(late[1], 1)
    return finish(1, [late[3], near_sum, across], result)


def solution(mesh):
    in_specs = (P("ctx", "head"), P("ctx", "head"), P("ctx", "head"), P("ctx"), P("head", None))
    out_specs = P("ctx", "head")
    ctx_count = mesh.shape["ctx"]
    head_count = mesh.shape["head"]

    def local(queries, keys, values, doc_ids, w_out):
        heads = queries.shape[1] // HD
        exchange = heads == ctx_count and heads == 4 and head_count == 2 * len(TURNS)
        exchange = exchange and queries.shape[0] % (4 * TILE) == 0
        body = exchange_local if exchange else ring_local
        return body(queries, keys, values, doc_ids, w_out)

    return jax.shard_map(
        local, mesh=mesh, in_specs=in_specs, out_specs=out_specs, check_vma=False
    )
```

```python
import functools
import math

import jax
import jax.numpy as jnp
from jax import lax
from jax.experimental import pallas as pl
from jax.experimental.pallas import tpu as pltpu
from jax.sharding import PartitionSpec as P

HD = 128


MASKED_SCORE = -1e30
LOG2E = 1.4426950408889634


def passed_along(value, axis, steps):
    count = lax.axis_size(axis)
    pairs = [(source, (source + steps) % count) for source in range(count)]
    return lax.ppermute(value, axis, pairs)


def folded_positions(row_total, offset, shard_rows, devices_ctx):
    flat_index = offset + lax.iota(jnp.int32, row_total)
    owner_dev = flat_index // shard_rows
    within = flat_index % shard_rows
    half_rows = shard_rows // 2
    fold_block = jnp.where(within < half_rows, owner_dev, 2 * devices_ctx - 1 - owner_dev)
    return fold_block * half_rows + within % half_rows


def block_update(
    running, query, query_pos, query_doc, key_block, value_block, pos_block, doc_block
):
    largest, totals, summed = running
    query_rows = query.shape[0]
    local_heads = query.shape[1] // HD
    query_heads = query.reshape(query_rows, local_heads, HD)
    key_heads = key_block.reshape(key_block.shape[0], local_heads, HD)
    value_heads = value_block.reshape(value_block.shape[0], local_heads, HD)
    scores = jnp.einsum(
        "qhd,khd->hqk", query_heads, key_heads, preferred_element_type=jnp.float32
    ) * (1.0 / math.sqrt(HD))
    allowed = (query_doc[:, None] == doc_block[None, :]) & (
        pos_block[None, :] <= query_pos[:, None]
    )
    scores = jnp.where(allowed[None], scores, MASKED_SCORE)
    new_max = jnp.maximum(largest, jnp.max(scores, axis=2))
    weights = jnp.where(allowed[None], jnp.exp(scores - new_max[:, :, None]), 0.0)
    factor = jnp.exp(largest - new_max)
    totals = totals * factor + jnp.sum(weights, axis=2)
    product = jnp.einsum(
        "hqk,khd->qhd",
        weights.astype(jnp.bfloat16),
        value_heads,
        preferred_element_type=jnp.float32,
    )
    summed = summed * factor.T[:, :, None] + product
    return (new_max, totals, summed)


def attend_rows(running, query, query_pos, query_doc, key_rows, value_rows, key_pos, key_doc):
    row_total = key_rows.shape[0]
    block_rows = math.gcd(row_total, query.shape[0])
    block_count = row_total // block_rows
    highest = jnp.max(query_pos)

    def visit(partial_value, blocks):
        key_block, value_block, pos_block, doc_block = blocks
        masked_out = jnp.min(pos_block) > highest
        updated = lax.cond(
            masked_out,
            lambda frozen: frozen,
            lambda frozen: block_update(
                frozen, query, query_pos, query_doc, key_block, value_block, pos_block, doc_block
            ),
            partial_value,
        )
        return (updated, None)

    blocks = (
        key_rows.reshape(block_count, block_rows, key_rows.shape[1]),
        value_rows.reshape(block_count, block_rows, value_rows.shape[1]),
        key_pos.reshape(block_count, block_rows),
        key_doc.reshape(block_count, block_rows),
    )
    running, _ = lax.scan(visit, running, blocks)
    return running


def attend_shard(running, query, query_pos, query_doc, key_rows, value_rows, key_pos, key_doc):
    largest, totals, summed = running
    half_rows = query.shape[0] // 2
    new_largest = []
    new_totals = []
    new_summed = []
    for half_idx in range(2):
        lower = half_idx * half_rows
        part_state = (largest[half_idx], totals[half_idx], summed[half_idx])
        part_state = attend_rows(
            part_state,
            query[lower : lower + half_rows],
            query_pos[lower : lower + half_rows],
            query_doc[lower : lower + half_rows],
            key_rows,
            value_rows,
            key_pos,
            key_doc,
        )
        new_largest.append(part_state[0])
        new_totals.append(part_state[1])
        new_summed.append(part_state[2])
    return (jnp.stack(new_largest), jnp.stack(new_totals), jnp.stack(new_summed))


def ring_local(queries, keys, values, doc_ids, w_out):
    shard_rows = queries.shape[0]
    half_rows = shard_rows // 2
    local_heads = queries.shape[1] // HD
    devices_ctx = lax.axis_size("ctx")
    ctx_index = lax.axis_index("ctx")
    all_docs = lax.all_gather(doc_ids, "ctx", axis=0, tiled=True)
    own_pos = folded_positions(shard_rows, ctx_index * shard_rows, shard_rows, devices_ctx)
    running = (
        jnp.full((2, local_heads, half_rows), MASKED_SCORE, jnp.float32),
        jnp.zeros((2, local_heads, half_rows), jnp.float32),
        jnp.zeros((2, half_rows, local_heads, HD), jnp.float32),
    )
    travel = queries
    for hop_step in range(devices_ctx):
        anchor = (ctx_index - hop_step) % devices_ctx
        query_pos = folded_positions(shard_rows, anchor * shard_rows, shard_rows, devices_ctx)
        query_doc = lax.dynamic_slice_in_dim(all_docs, anchor * shard_rows, shard_rows, 0)
        largest, totals, summed = attend_shard(
            running, travel, query_pos, query_doc, keys, values, own_pos, doc_ids
        )
        running = (
            passed_along(largest.astype(jnp.bfloat16), "ctx", 1).astype(largest.dtype),
            passed_along(totals.astype(jnp.bfloat16), "ctx", 1).astype(totals.dtype),
            passed_along(summed.astype(jnp.bfloat16), "ctx", 1).astype(summed.dtype),
        )
        if hop_step + 1 < devices_ctx:
            travel = passed_along(travel, "ctx", 1)
    largest, totals, summed = running
    attended = summed / totals.transpose(0, 2, 1)[:, :, :, None]
    attended = attended.reshape(shard_rows, local_heads * HD).astype(jnp.bfloat16)
    partial_out = jnp.dot(attended, w_out, preferred_element_type=jnp.float32)
    return lax.psum_scatter(
        partial_out.astype(jnp.bfloat16), "head", scatter_dimension=1, tiled=True
    )


SMALL = pl.CostEstimate(flops=1024, bytes_accessed=1024, transcendentals=0)
TILE = 256
MOST_DOCS = 16


def params(mib):
    return pltpu.CompilerParams(vmem_limit_bytes=mib * 1024 * 1024)


def whole(shape):
    return pl.BlockSpec(shape, lambda step, scalars: (0,) * len(shape))


def pack(ctx_index, half, queries, keys, values, docs):
    rows = queries.shape[0] // 2
    group = queries.shape[1] // HD
    doc_rows = 0 if docs is None else 16 * pl.cdiv(docs.shape[0], 16)
    total = 3 * rows + doc_rows

    def kernel(ctx_ref, *refs):
        outs = refs[len(refs) - (group - 1) :]
        if docs is not None:
            mine = refs[3 * (group - 1)][...].astype(jnp.float32)
            empty = jnp.zeros((doc_rows - mine.shape[0], HD), jnp.float32)
            mine = jnp.concatenate([mine, empty], axis=0).astype(jnp.bfloat16)
        for place in range(group - 1):
            for part in range(2):
                outs[place][part * rows : (part + 1) * rows, :] = refs[place * 3 + part][...]
            for block in range(rows // HD):
                taken = refs[place * 3 + 2][block * HD : (block + 1) * HD, :]
                lower = 2 * rows + block * HD
                outs[place][lower : lower + HD, :] = jnp.transpose(taken)
            if docs is not None:
                outs[place][3 * rows :, :] = mine

    def piece(distance):
        return pl.BlockSpec((rows, HD), lambda step, ctx: (half, ctx[0] ^ distance))

    in_specs = []
    operands = []
    for distance in range(1, group):
        for array in (queries, keys, values):
            in_specs.append(piece(distance))
            operands.append(array)
    if docs is not None:
        in_specs.append(whole(docs.shape))
        operands.append(docs)
    return pl.pallas_call(
        kernel,
        grid_spec=pltpu.PrefetchScalarGridSpec(
            num_scalar_prefetch=1,
            grid=(1,),
            in_specs=in_specs,
            out_specs=[whole((total, HD))] * (group - 1),
        ),
        out_shape=[jax.ShapeDtypeStruct((total, HD), jnp.bfloat16)] * (group - 1),
        compiler_params=params(56),
        cost_estimate=SMALL,
        name="pack",
    )(ctx_index, *operands)


def pack_projection(places, w_mine, w_sibling):
    depth, width = w_mine.shape
    turns = len(TURNS)
    columns = width // (2 * turns)

    def kernel(places_ref, mine_in, sibling_in, mine_out, sibling_out):
        mine_out[...] = mine_in[...]
        sibling_out[...] = sibling_in[...]

    in_spec = pl.BlockSpec((depth, columns), lambda turn, at: (0, at[turn]))
    out_spec = pl.BlockSpec((depth, columns), lambda turn, at: (0, turn))
    return pl.pallas_call(
        kernel,
        grid_spec=pltpu.PrefetchScalarGridSpec(
            num_scalar_prefetch=1,
            grid=(turns,),
            in_specs=[in_spec] * 2,
            out_specs=[out_spec] * 2,
        ),
        out_shape=[jax.ShapeDtypeStruct((depth, turns * columns), w_mine.dtype)] * 2,
        compiler_params=params(56),
        cost_estimate=SMALL,
        name="pack_projection",
    )(places, w_mine, w_sibling)


def attend(ctx_index, queries, keys, values, docs, low, high):
    rows = queries.shape[0] // 2
    group = queries.shape[1] // HD
    with_high = high is not None
    per_block = rows // TILE
    lines = rows // HD
    key_rows = (2 * group if with_high else group) * rows
    key_tiles = key_rows // TILE
    scaling = LOG2E / math.sqrt(HD)

    def kernel(ctx_ref, *refs):
        refs = list(refs)
        own_low = [refs.pop(0) for _ in range(3)]
        own_high = [refs.pop(0) for _ in range(3)] if with_high else None
        own_docs = refs.pop(0)
        low_refs = [refs.pop(0) for _ in range(group - 1)]
        high_refs = [refs.pop(0) for _ in range(group - 1)] if with_high else None
        outs = [refs.pop(0) for _ in range(group)]
        key_buf, value_buf, doc_buf = refs[:3]
        query_buf, start_buf, largest_buf, summed = (
            refs[3 + kind * group : 3 + (kind + 1) * group] for kind in range(4)
        )
        ctx = ctx_ref[0]

        def part(upper, distance, index, lower=0, count=rows):
            if distance == 0:
                return (own_high if upper else own_low)[index][lower : lower + count, :]
            source = (high_refs if upper else low_refs)[distance - 1]
            return source[index * rows + lower : index * rows + lower + count, :]

        place = {}
        doc_rows = {}
        for upper in (False, True) if with_high else (False,):
            for distance in range(group):
                source = ctx ^ distance
                block = 2 * group - 1 - source if upper else source
                place[upper, distance] = block
                offset = pl.multiple_of(block * rows, rows)
                key_buf[pl.ds(offset, rows), :] = part(upper, distance, 1)
                if distance == 0:
                    both = own_docs[...].astype(jnp.float32)
                else:
                    both = low_refs[distance - 1][3 * rows :, :].astype(jnp.float32)
                begin = lines if upper else 0
                mine = []
                for line in range(lines):
                    taken = part(upper, distance, 2, line * HD, HD)
                    if distance == 0:
                        taken = jnp.transpose(taken)
                    column = pl.multiple_of(block * rows + line * HD, HD)
                    value_buf[:HD, pl.ds(column, HD)] = taken
                    mine.append(both[begin + line : begin + line + 1, :])
                    doc_buf[pl.ds(block * lines + line, 1), :] = mine[-1]
                doc_rows[upper, distance] = jnp.concatenate(mine, axis=1)
        value_buf[HD:, :] = jnp.ones((value_buf.shape[0] - HD, key_rows), jnp.bfloat16)

        all_docs = doc_buf[...]
        starts = [jnp.zeros((1, rows), jnp.float32)] * group
        for number in range(1, MOST_DOCS):
            smaller = jnp.where(all_docs < number, 1.0, 0.0)
            count = jnp.sum(jnp.sum(smaller, axis=0, keepdims=True), axis=1, keepdims=True)
            for distance in range(group):
                reached = doc_rows[with_high, distance] >= number
                starts[distance] = jnp.where(reached, count, starts[distance])

        def scores_of(query, offset):
            raw = lax.dot_general(
                key_buf[pl.ds(offset, TILE), :],
                query,
                (((1,), (1,)), ((), ())),
                preferred_element_type=jnp.float32,
            )
            return raw * scaling

        def weighted(weights, offset):
            return jnp.dot(
                value_buf[:, pl.ds(offset, TILE)],
                weights.astype(jnp.bfloat16),
                preferred_element_type=jnp.float32,
            )

        key_row = lax.broadcasted_iota(jnp.int32, (TILE, TILE), 0)
        causal = key_row <= lax.broadcasted_iota(jnp.int32, (TILE, TILE), 1)
        key_row = key_row.astype(jnp.float32)
        firsts = []
        counts = []
        for lane in range(group):
            for slot in range(per_block):
                distance = lane ^ (slot * (group - 1))
                query = part(with_high, distance, 0, slot * TILE, TILE)
                query_buf[lane][slot] = query
                start = starts[distance][:, slot * TILE : (slot + 1) * TILE]
                start_buf[lane][slot, 0:1, :] = start
                end = place[with_high, distance] * per_block + slot
                offset = pl.multiple_of(end * TILE, TILE)
                least = start - offset.astype(jnp.float32)
                scores = scores_of(query, offset)
                scores = jnp.where((key_row >= least) & causal, scores, MASKED_SCORE)
                largest = jnp.max(scores, axis=0, keepdims=True)
                largest_buf[lane][slot, 0:1, :] = largest
                summed[lane][slot] = weighted(jnp.exp2(scores - largest), offset)
                first = start[0, 0].astype(jnp.int32) // TILE
                firsts.append(first)
                counts.append(end - first)

        longest = jnp.int32(0)
        for lane in range(group):
            of_lane = counts[lane * per_block : (lane + 1) * per_block]
            longest = jnp.maximum(longest, sum(of_lane))

        def visit(step, carry):
            slots = []
            offsets = []
            beyonds = []
            for lane in range(group):
                slot = jnp.int32(0)
                index = firsts[lane * per_block] + step
                before = counts[lane * per_block]
                for later in range(1, per_block):
                    reached = step >= before
                    slot = jnp.where(reached, later, slot)
                    place_later = lane * per_block + later
                    index = jnp.where(reached, firsts[place_later] + step - before, index)
                    before = before + counts[place_later]
                offset = pl.multiple_of(jnp.minimum(index, key_tiles - 1) * TILE, TILE)
                slots.append(slot)
                offsets.append(offset)
                beyonds.append(jnp.where(step < before, -offset.astype(jnp.float32), 1e9))
            each = range(group)
            scores = [scores_of(query_buf[lane][slots[lane]], offsets[lane]) for lane in each]
            old_max = [largest_buf[lane][slots[lane], 0:1, :] for lane in each]
            new_max = []
            for lane in each:
                least = start_buf[lane][slots[lane], 0:1, :] + beyonds[lane]
                scores[lane] = jnp.where(key_row >= least, scores[lane], MASKED_SCORE)
                tile_max = jnp.max(scores[lane], axis=0, keepdims=True)
                new_max.append(jnp.maximum(old_max[lane], tile_max))
            products = [
                weighted(jnp.exp2(scores[lane] - new_max[lane]), offsets[lane]) for lane in each
            ]
            for lane in each:
                factor = jnp.exp2(old_max[lane] - new_max[lane])
                summed[lane][slots[lane]] = summed[lane][slots[lane]] * factor + products[lane]
                largest_buf[lane][slots[lane], 0:1, :] = new_max[lane]
            return carry

        lax.fori_loop(0, longest, visit, jnp.int32(0))
        for lane in range(group):
            for slot in range(per_block):
                state = summed[lane]
                attended = state[slot, :HD, :] * (1.0 / state[slot, HD : HD + 1, :])
                out = outs[lane ^ (slot * (group - 1))]
                out[slot * TILE : (slot + 1) * TILE, :] = jnp.transpose(
                    attended.astype(jnp.bfloat16)
                )

    def own(upper):
        return pl.BlockSpec((rows, HD), lambda step, ctx: (int(upper), ctx[0]))

    in_specs = [own(False)] * 3
    operands = [queries, keys, values]
    if with_high:
        in_specs += [own(True)] * 3
        operands += [queries, keys, values]
    received = [docs, *low, *(high if with_high else ())]
    operands += received
    in_specs += [whole(array.shape) for array in received]
    return pl.pallas_call(
        kernel,
        grid_spec=pltpu.PrefetchScalarGridSpec(
            num_scalar_prefetch=1,
            grid=(1,),
            in_specs=in_specs,
            out_specs=[whole((rows, HD))] * group,
            scratch_shapes=[
                pltpu.VMEM((key_rows, HD), jnp.bfloat16),
                pltpu.VMEM((HD + 16, key_rows), jnp.bfloat16),
                pltpu.VMEM((key_rows // HD, HD), jnp.float32),
                *[pltpu.VMEM((per_block, TILE, HD), jnp.bfloat16)] * group,
                *[pltpu.VMEM((per_block, 8, TILE), jnp.float32)] * (2 * group),
                *[pltpu.VMEM((per_block, HD + 16, TILE), jnp.float32)] * group,
            ],
        ),
        out_shape=[jax.ShapeDtypeStruct((rows, HD), jnp.bfloat16)] * group,
        compiler_params=params(40),
        cost_estimate=SMALL,
        name="attend_high" if with_high else "attend_low",
    )(ctx_index, *operands)


def assemble(ctx_index, pieces, parts):
    rows = pieces[0].shape[0]
    group = len(pieces)
    part_rows = rows // parts

    def kernel(ctx_ref, *refs):
        for part in range(parts):
            for distance in range(group):
                column = pl.multiple_of((ctx_ref[0] ^ distance) * HD, HD)
                taken = refs[distance][part * part_rows : (part + 1) * part_rows, :]
                refs[group + part][:, pl.ds(column, HD)] = taken

    return pl.pallas_call(
        kernel,
        grid_spec=pltpu.PrefetchScalarGridSpec(
            num_scalar_prefetch=1,
            grid=(1,),
            in_specs=[whole((rows, HD))] * group,
            out_specs=[whole((part_rows, group * HD))] * parts,
        ),
        out_shape=[jax.ShapeDtypeStruct((part_rows, group * HD), jnp.bfloat16)] * parts,
        compiler_params=params(16),
        cost_estimate=SMALL,
        name="assemble",
    )(ctx_index, *pieces)


def project(turn, mine, sibling, w_mine, w_sibling):
    parts = len(mine)
    rows, depth = mine[0].shape
    columns = w_mine.shape[1] // len(TURNS)

    def kernel(*refs):
        w_mine_ref, w_sibling_ref = refs[2 * parts : 2 * parts + 2]
        for part in range(parts):
            total = jnp.dot(refs[part][...], w_mine_ref[...], preferred_element_type=jnp.float32)
            total += jnp.dot(
                refs[parts + part][...], w_sibling_ref[...], preferred_element_type=jnp.float32
            )
            refs[2 * parts + 2 + part][...] = total.astype(jnp.bfloat16)

    weights = pl.BlockSpec((depth, columns), lambda step: (0, turn))
    attended = pl.BlockSpec((rows, depth), lambda step: (0, 0))
    return pl.pallas_call(
        kernel,
        grid=(1,),
        in_specs=[attended] * (2 * parts) + [weights] * 2,
        out_specs=[pl.BlockSpec((rows, columns), lambda step: (0, 0))] * parts,
        out_shape=[jax.ShapeDtypeStruct((rows, columns), jnp.bfloat16)] * parts,
        compiler_params=params(16),
        cost_estimate=SMALL,
        name="project",
    )(*mine, *sibling, w_mine, w_sibling)


def finish(half, terms, result):
    parts = len(terms[0])
    rows, columns = terms[0][0].shape
    flat = [part for term in terms for part in term]

    def kernel(*refs):
        for part in range(parts):
            total = refs[part][...].astype(jnp.float32)
            for term in range(1, len(terms)):
                total += refs[term * parts + part][...].astype(jnp.float32)
            refs[-1][part * rows : (part + 1) * rows, :] = total.astype(jnp.bfloat16)

    in_specs = [pl.BlockSpec((rows, columns), lambda step: (0, 0))] * len(flat)
    operands = list(flat)
    aliases = {}
    if result is not None:
        in_specs.append(pl.BlockSpec(memory_space=pl.ANY))
        operands.append(result)
        aliases = {len(flat): 0}
    return pl.pallas_call(
        kernel,
        grid=(1,),
        in_specs=in_specs,
        out_specs=pl.BlockSpec((parts * rows, columns), lambda step: (half, 0)),
        out_shape=jax.ShapeDtypeStruct((2 * parts * rows, columns), jnp.bfloat16),
        input_output_aliases=aliases,
        compiler_params=params(16),
        cost_estimate=SMALL,
        name="finish",
    )(*operands)


def swap(value, axis, distance):
    count = lax.axis_size(axis)
    return lax.ppermute(value, axis, [(source, source ^ distance) for source in range(count)])


def add(*terms):
    total = terms[0].astype(jnp.float32)
    for term in terms[1:]:
        total = total + term.astype(jnp.float32)
    return total.astype(jnp.bfloat16)


TURNS = (3, 1, 2, 0)


def tie(*values):
    return lax.optimization_barrier(values)


def exchange_local(queries, keys, values, doc_ids, w_out):
    shard_rows = queries.shape[0]
    group = queries.shape[1] // HD
    ctx_index = lax.axis_index("ctx").astype(jnp.int32).reshape(1)
    head_index = lax.axis_index("head").astype(jnp.int32)
    places = head_index ^ (2 * jnp.array(TURNS, jnp.int32))
    docs = doc_ids.reshape(shard_rows // HD, HD)
    near = range(1, group)

    w_sibling = swap(w_out, "head", 1)
    low_out = pack(ctx_index, 0, queries, keys, values, docs)
    low_out, later = tie(low_out, (queries, keys, values))
    low = [swap(low_out[distance - 1], "ctx", distance) for distance in near]
    high_out = pack(ctx_index, 1, *later, None)
    high = [swap(high_out[distance - 1], "ctx", distance) for distance in near[:-1]]
    w_packed = pack_projection(places, w_out, w_sibling)
    low, w_packed = tie(low, w_packed)

    def send_back(pieces):
        return [swap(pieces[distance], "ctx", distance) for distance in near]

    def shares_of(mine):
        sibling = [swap(part, "head", 1) for part in mine]
        return [project(turn, mine, sibling, *w_packed) for turn in range(len(TURNS))]

    def to_next(parts, distance):
        return [swap(part, "head", 2 * distance) for part in parts]

    pieces = attend(ctx_index, queries, keys, values, docs, low, None)
    pieces, diagonal_out = tie(pieces, high_out[-1])
    back = send_back(pieces)
    back, high = tie(back, high)
    high = [*high, swap(diagonal_out, "ctx", near[-1])]
    shares = shares_of(assemble(ctx_index, [pieces[0], *back], 1))
    far = to_next(shares[0], 1)
    near_sum = to_next(shares[1], 1)

    passed = [add(*both) for both in zip(shares[2], far)]
    high, shares, passed = tie(high, shares, passed)
    across = to_next(passed, 2)
    pieces = attend(ctx_index, queries, keys, values, docs, low, high)
    back = send_back(pieces)
    late = shares_of(assemble(ctx_index, [pieces[0], *back], 2))
    late[0], near_sum, across = tie(late[0], near_sum, across)
    result = finish(0, [shares[3], near_sum, across], None)
    far = to_next(late[0], 1)
    passed = [add(*both) for both in zip(late[2], far)]
    across = to_next(passed, 2)
    late[1], passed[0] = tie(late[1], passed[0])
    near_sum = to_next(late[1], 1)
    return finish(1, [late[3], near_sum, across], result)


def solution(mesh):
    in_specs = (P("ctx", "head"), P("ctx", "head"), P("ctx", "head"), P("ctx"), P("head", None))
    out_specs = P("ctx", "head")
    ctx_count = mesh.shape["ctx"]
    head_count = mesh.shape["head"]

    def local(queries, keys, values, doc_ids, w_out):
        heads = queries.shape[1] // HD
        exchange = heads == ctx_count and heads == 4 and head_count == 2 * len(TURNS)
        exchange = exchange and queries.shape[0] % (4 * TILE) == 0
        body = exchange_local if exchange else ring_local
        return body(queries, keys, values, doc_ids, w_out)

    return jax.shard_map(
        local, mesh=mesh, in_specs=in_specs, out_specs=out_specs, check_vma=False
    )
```
